32 devices in a mesh: seq: 4 (over z), head: 8 (over y, x, core).
Axes of the slice: x: 2, y: 2, z: 4, core: 2. Of those that a mesh axis runs over, the one named last changes fastest.
Arguments:
- inputs: bfloat16 [8192, 2048], P(('seq', 'head')), may hold values from -6 to 6
- doc_lengths: int32 [3], replicated, may hold values from 65 to 6080, as said below
- first_gain: float32 [2048], replicated, may hold values from 0.5 to 1.5
- w_query: bfloat16 [2048, 2048], P(None, 'head'), may hold values from -0.125 to 0.125
- w_key: bfloat16 [2048, 2048], P(None, 'head'), may hold values from -0.125 to 0.125
- w_value: bfloat16 [2048, 4096], P(None, 'head'), may hold values from -0.125 to 0.125
- w_outgate: bfloat16 [2048, 4096], P(None, 'head'), may hold values from -0.125 to 0.125
- w_decay: bfloat16 [2048, 16], P(None, 'head'), may hold values from -0.125 to 0.125
- w_beta: bfloat16 [2048, 16], P(None, 'head'), may hold values from -0.125 to 0.125
- conv_query: float32 [4, 2048], P(None, 'head'), may hold values from -3 to 3
- conv_key: float32 [4, 2048], P(None, 'head'), may hold values from -3 to 3
- conv_value: float32 [4, 4096], P(None, 'head'), may hold values from -3 to 3
- decay_log: float32 [16], P('head'), may hold values from -4 to 1
- decay_bias: float32 [16], P('head'), may hold values from -3 to 1
- head_gain: float32 [256], replicated, may hold values from 0.5 to 1.5
- w_output: bfloat16 [4096, 2048], P('head'), may hold values from -0.09375 to 0.09375
- second_gain: float32 [2048], replicated, may hold values from 0.5 to 1.5
- w_gate: bfloat16 [2048, 5632], P(None, 'seq'), may hold values from -0.125 to 0.125
- w_up: bfloat16 [2048, 5632], P(None, 'seq'), may hold values from -0.125 to 0.125
- w_down: bfloat16 [5632, 2048], P('seq'), may hold values from -0.078125 to 0.078125
- cotangent: bfloat16 [8192, 2048], P(('seq', 'head')), may hold values from -6 to 6
Outputs:
- output: bfloat16 [8192, 2048], P(('seq', 'head'))
- grad_inputs: float32 [8192, 2048], P(('seq', 'head'))
- grad_first_gain: float32 [2048], replicated
- grad_w_query: float32 [2048, 2048], P(None, 'head')
- grad_w_key: float32 [2048, 2048], P(None, 'head')
- grad_w_value: float32 [2048, 4096], P(None, 'head')
- grad_w_outgate: float32 [2048, 4096], P(None, 'head')
- grad_w_decay: float32 [2048, 16], P(None, 'head')
- grad_w_beta: float32 [2048, 16], P(None, 'head')
- grad_conv_query: float32 [4, 2048], P(None, 'head')
- grad_conv_key: float32 [4, 2048], P(None, 'head')
- grad_conv_value: float32 [4, 4096], P(None, 'head')
- grad_decay_log: float32 [16], P('head')
- grad_decay_bias: float32 [16], P('head')
- grad_head_gain: float32 [256], replicated
- grad_w_output: float32 [4096, 2048], P('head')
- grad_second_gain: float32 [2048], replicated
- grad_w_gate: float32 [2048, 5632], P(None, 'seq')
- grad_w_up: float32 [2048, 5632], P(None, 'seq')
- grad_w_down: float32 [5632, 2048], P('seq')
The draws below stay inside these ranges and needn't reach their ends.
Inputs may be any that keep to these rules, and one draw needn't show every extreme that they name: Document i occupies a slot of doc_lengths[i] rounded up to a multiple of 64; the slots lie end to end and fill all 8192 tokens; the second document starts within the first 2048 tokens, ends within the last 2048, and is 6080 tokens long.
All inputs are finite; a program needn't handle non-finite values.
Results may differ from the reference program's by a relative error of at most 0.025.
Values may be sent and summed in bfloat16 or wider, within the bound.
A program may use at most 384 MiB of HBM per device.

```python
import jax
import jax.numpy as jnp
from jax import lax

D = 2048
HEADS = 16
DK = 128
DV = 256
FF = 5632
CONV = 4
GROUP = 64
DOCS = 3
TOK_SEQ = 2048
TOKENS = 8192


def draw_doc_lengths(key, part):
    key = jax.random.fold_in(key, 7)
    key_lead, key_padding = jax.random.split(key, 2)
    per_block = TOK_SEQ // GROUP
    all_groups = TOKENS // GROUP
    leading = jax.random.randint(key_lead, (), per_block // 2 + 1, per_block)
    trailing = per_block + 1 - leading
    slot_groups = jnp.stack([leading, all_groups - per_block - 1, trailing])
    padding = jax.random.randint(key_padding, (DOCS,), 0, GROUP) * jnp.array([1, 0, 1], jnp.int32)
    return (slot_groups * GROUP - padding).astype(jnp.int32)


def steps_of(key, dims, cuts, low, top_value):
    factor_of = 1.0
    for dim, blocks in cuts:
        heights = jax.random.uniform(jax.random.fold_in(jax.random.fold_in(key, 6), dim), (blocks,), jnp.float32, low / len(cuts), top_value / len(cuts))
        factor_of = factor_of * jnp.repeat(jnp.exp(heights), dims[dim] // blocks).reshape((-1,) + (1,) * (len(dims) - 1 - dim))
    return factor_of


def scatter_about(own_key, dims, width, reach, pieces=(), held_as=jnp.bfloat16):
    level = steps_of(own_key, dims, pieces, -0.22, 0.18) if pieces else 1.0
    values = jax.random.normal(own_key, dims, jnp.float32) * width * level
    return jnp.minimum(jnp.maximum(values, -reach), reach).astype(held_as)


def setup_inputs(seed: int = 0) -> dict:
    streams_of = jax.random.split(jax.random.key(seed), 22)
    inputs = scatter_about(streams_of[0], (TOKENS, D), 1.0, 6.0, ((0, 32),))
    doc_lengths = draw_doc_lengths(jax.random.fold_in(streams_of[21], 71), 0)
    first_gain = jnp.clip(1.0 + 0.1 * jax.random.normal(streams_of[2], (D,), jnp.float32), 0.5, 1.5)
    w_query = scatter_about(streams_of[3], (D, HEADS * DK), D ** -0.5, 0.125, ((1, 8),))
    w_key = scatter_about(streams_of[4], (D, HEADS * DK), D ** -0.5, 0.125, ((1, 8),))
    w_value = scatter_about(streams_of[5], (D, HEADS * DV), D ** -0.5, 0.125, ((1, 8),))
    w_outgate = scatter_about(streams_of[6], (D, HEADS * DV), D ** -0.5, 0.125, ((1, 8),))
    w_decay = scatter_about(streams_of[7], (D, HEADS), D ** -0.5, 0.125, ((1, 8),))
    w_beta = scatter_about(streams_of[8], (D, HEADS), D ** -0.5, 0.125, ((1, 8),))
    conv_query = scatter_about(streams_of[9], (CONV, HEADS * DK), 0.5, 3.0, ((1, 8),), jnp.float32)
    conv_key = scatter_about(streams_of[10], (CONV, HEADS * DK), 0.5, 3.0, ((1, 8),), jnp.float32)
    conv_value = scatter_about(streams_of[11], (CONV, HEADS * DV), 0.5, 3.0, ((1, 8),), jnp.float32)
    decay_log = jnp.clip(-4.0 + 5.0 * jax.random.uniform(streams_of[12], (HEADS,), jnp.float32) ** steps_of(streams_of[12], (HEADS,), ((0, 8),), -0.2, 0.2), -4.0, 1.0)
    decay_bias = jnp.clip(-3.0 + 4.0 * jax.random.uniform(streams_of[13], (HEADS,), jnp.float32) ** steps_of(streams_of[13], (HEADS,), ((0, 8),), -0.2, 0.2), -3.0, 1.0)
    head_gain = jnp.clip(1.0 + 0.1 * jax.random.normal(streams_of[14], (DV,), jnp.float32), 0.5, 1.5)
    w_output = scatter_about(streams_of[15], (HEADS * DV, D), (HEADS * DV) ** -0.5, 0.09375, ((0, 8),))
    second_gain = jnp.clip(1.0 + 0.1 * jax.random.normal(streams_of[16], (D,), jnp.float32), 0.5, 1.5)
    w_gate = scatter_about(streams_of[17], (D, FF), D ** -0.5, 0.125, ((1, 4),))
    w_up = scatter_about(streams_of[18], (D, FF), D ** -0.5, 0.125, ((1, 4),))
    w_down = scatter_about(streams_of[19], (FF, D), FF ** -0.5, 0.078125, ((0, 4),))
    cotangent = scatter_about(streams_of[20], (TOKENS, D), 1.0, 6.0, ((0, 32),))
    return {"inputs": inputs, "doc_lengths": doc_lengths, "first_gain": first_gain, "w_query": w_query, "w_key": w_key, "w_value": w_value, "w_outgate": w_outgate, "w_decay": w_decay, "w_beta": w_beta, "conv_query": conv_query, "conv_key": conv_key, "conv_value": conv_value, "decay_log": decay_log, "decay_bias": decay_bias, "head_gain": head_gain, "w_output": w_output, "second_gain": second_gain, "w_gate": w_gate, "w_up": w_up, "w_down": w_down, "cotangent": cotangent}


epsilon = 1e-06
highest_precision = lax.Precision.HIGHEST

@jax.custom_vjp
def low(v):
    return lax.optimization_barrier(v.astype(jnp.bfloat16)).astype(jnp.float32)

@jax.custom_vjp
def low_back(v):
    return v

def low_keep(v):
    return (low(v), None)

def low_pass(kept, grad):
    return (grad,)

def back_keep(v):
    return (v, None)

def back_low(kept, grad):
    return (low(grad),)
low.defvjp(low_keep, low_pass)
low_back.defvjp(back_keep, back_low)

def matmul(left, right):
    return jnp.dot(left, right, precision=highest_precision, preferred_element_type=jnp.float32)

def layout(doc_lengths, first_row, row_total):
    slot_sizes = (doc_lengths + (GROUP - 1)) // GROUP * GROUP
    starts = jnp.cumsum(slot_sizes, dtype=jnp.int32) - slot_sizes
    places = first_row + jnp.arange(row_total, dtype=jnp.int32)
    owners = lax.optimization_barrier(jnp.sum((places[:, None] >= starts[None, 1:]).astype(jnp.int32), axis=1, dtype=jnp.int32))
    picked = (owners[:, None] == jnp.arange(DOCS, dtype=jnp.int32)[None, :]).astype(jnp.int32)
    begins = lax.optimization_barrier(jnp.sum(picked * starts[None, :], axis=1, dtype=jnp.int32))
    length = lax.optimization_barrier(jnp.sum(picked * doc_lengths[None, :], axis=1, dtype=jnp.int32))
    offset = places - begins
    return (offset, offset < length)

def rms_scale(values, gain):
    return values * lax.rsqrt(lax.optimization_barrier(jnp.mean(values * values, axis=-1, keepdims=True)) + epsilon) * gain

def unit_rows(values):
    return values * lax.rsqrt(lax.optimization_barrier(jnp.sum(values * values, axis=-1, keepdims=True)) + epsilon)

def causal_conv(pre, kernel, offset):
    summed = jnp.zeros_like(pre)
    for lag_at in range(kernel.shape[0]):
        moved = jnp.concatenate([jnp.zeros((lag_at, pre.shape[1]), pre.dtype), pre[:pre.shape[0] - lag_at]], axis=0)
        summed = summed + kernel[lag_at] * moved * (offset >= lag_at).astype(pre.dtype)[:, None]
    return summed

def delta_core(queries, key_rows, values, decay, strength, resets):
    tokens_all = queries.shape[0]
    blocks = tokens_all // GROUP

    def token_step(memory_state, item):
        query_at_step, key_at_step, value_t, decay_t, strength_t, reset_t = item
        memory_state = memory_state * (1.0 - reset_t)
        recalled_values = jnp.einsum('bs,bsz->bz', key_at_step, memory_state, precision=highest_precision)
        memory_state = jnp.exp(decay_t)[:, None, None] * (memory_state - strength_t[:, None, None] * key_at_step[:, :, None] * recalled_values[:, None, :]) + strength_t[:, None, None] * key_at_step[:, :, None] * value_t[:, None, :]
        return (memory_state, jnp.einsum('bs,bsz->bz', query_at_step, memory_state, precision=highest_precision))

    @jax.checkpoint
    def block_step(memory_state, block):
        return lax.scan(token_step, memory_state, block)

    def split_blocks(array):
        return array.reshape((blocks, GROUP) + array.shape[1:])
    items = tuple((split_blocks(array) for array in (queries, key_rows, values, decay, strength, resets)))
    state_zero = jnp.zeros((HEADS, DK, DV), jnp.float32)
    _, outs = lax.scan(block_step, state_zero, items)
    return outs.reshape(tokens_all, HEADS, DV)

def reference(inputs, doc_lengths, first_gain, w_query, w_key, w_value, w_outgate, w_decay, w_beta, conv_query, conv_key, conv_value, decay_log, decay_bias, head_gain, w_output, second_gain, w_gate, w_up, w_down, cotangent):
    offset, valid = layout(doc_lengths, 0, TOKENS)
    resets = (offset == 0).astype(jnp.float32)

    def layer(x_in, gain_one, wq_in, wk_in, wv_in, wg_in, wd_in, wb_in, cq_in, ck_in, cv_in, dlog_in, dbias_in, hgain_in, wo_in, gain_two, wgate_in, wup_in, wdown_in):
        normed = low(rms_scale(x_in, gain_one))
        pre_q = low_back(matmul(normed, wq_in))
        pre_k = low_back(matmul(normed, wk_in))
        pre_v = low_back(matmul(normed, wv_in))
        pre_gate = low_back(matmul(normed, wg_in))
        pre_decay = low_back(matmul(normed, wd_in))
        pre_beta = low_back(matmul(normed, wb_in))
        act_q = jax.nn.silu(causal_conv(pre_q, cq_in, offset)).reshape(TOKENS, HEADS, DK)
        act_k = jax.nn.silu(causal_conv(pre_k, ck_in, offset)).reshape(TOKENS, HEADS, DK)
        act_v = jax.nn.silu(causal_conv(pre_v, cv_in, offset)).reshape(TOKENS, HEADS, DV)
        queries = low(unit_rows(act_q) * DK ** (-0.5))
        key_rows = low(unit_rows(act_k))
        values = low(act_v)
        strength = jax.nn.sigmoid(pre_beta)
        decay = -jnp.exp(dlog_in) * jax.nn.softplus(pre_decay + dbias_in)
        core = delta_core(queries, key_rows, values, decay, strength, resets)
        head_normed = rms_scale(core, hgain_in)
        gated = low((head_normed * jax.nn.silu(pre_gate.reshape(TOKENS, HEADS, DV))).reshape(TOKENS, HEADS * DV))
        mixed = low_back(matmul(gated, wo_in))
        hidden_in = x_in + mixed
        normed_two = low(rms_scale(hidden_in, gain_two))
        gate_pre = low_back(matmul(normed_two, wgate_in))
        up_pre = low_back(matmul(normed_two, wup_in))
        hidden = low(jax.nn.silu(gate_pre) * up_pre)
        feed = low_back(matmul(hidden, wdown_in))
        return hidden_in + feed
    primals = tuple((array.astype(jnp.float32) for array in (inputs, first_gain, w_query, w_key, w_value, w_outgate, w_decay, w_beta, conv_query, conv_key, conv_value, decay_log, decay_bias, head_gain, w_output, second_gain, w_gate, w_up, w_down)))
    result, pullback = jax.vjp(layer, *primals)
    grads = pullback(cotangent.astype(jnp.float32) * valid.astype(jnp.float32)[:, None])
    return (result.astype(jnp.bfloat16), grads[0], grads[1], grads[2], grads[3], grads[4], grads[5], grads[6], grads[7], grads[8], grads[9], grads[10], grads[11], grads[12], grads[13], grads[14], grads[15], grads[16], grads[17], grads[18])
```

```python
import functools

import jax
import jax.numpy as jnp
from jax import lax
from jax.experimental import pallas as pl
from jax.experimental.pallas import tpu as pltpu
from jax.sharding import PartitionSpec as P

GROUP = 64
BLOCK = 256
LANES = 128
HALO = 8

epsilon = 1e-06
f32 = jnp.float32
bf16 = jnp.bfloat16
VMEM_LIMIT = 56 * 1024 * 1024


def dot(left, right):
    return jnp.dot(left, right, preferred_element_type=f32)


def dot_tn(left, right):
    return lax.dot_general(left, right, (((0,), (0,)), ((), ())), preferred_element_type=f32)


def dot_nt(left, right):
    return lax.dot_general(left, right, (((1,), (1,)), ((), ())), preferred_element_type=f32)


def halves(values):
    top = values.astype(bf16)
    return top, (values - top.astype(f32)).astype(bf16)


def exact_left(left, right):
    top = right.astype(bf16)
    rest = right - top.astype(f32)
    middle = rest.astype(bf16)
    low = (rest - middle.astype(f32)).astype(bf16)
    return dot(left, top) + dot(left, middle) + dot(left, low)


def dot_fine(left, right):
    left_top, left_low = halves(left)
    right_top, right_low = halves(right)
    return dot(left_top, right_top) + (dot(left_top, right_low) + dot(left_low, right_top))


def sigmoid(values):
    return jax.nn.sigmoid(values)


def silu_slope(values):
    sigma = sigmoid(values)
    return sigma * (1.0 + values * (1.0 - sigma))


def softplus(values):
    return jnp.maximum(values, 0.0) + jnp.log1p(jnp.exp(-jnp.abs(values)))


def slot_starts(doc_lengths):
    slot_sizes = (doc_lengths + (GROUP - 1)) // GROUP * GROUP
    return jnp.cumsum(slot_sizes, dtype=jnp.int32) - slot_sizes


def layout(doc_lengths, first_row, row_total):
    starts = slot_starts(doc_lengths)
    places = first_row + jnp.arange(row_total, dtype=jnp.int32)
    owners = jnp.sum(
        (places[:, None] >= starts[None, 1:]).astype(jnp.int32), axis=1, dtype=jnp.int32
    )
    picked = (owners[:, None] == jnp.arange(doc_lengths.shape[0], dtype=jnp.int32)[None, :]).astype(
        jnp.int32
    )
    begins = jnp.sum(picked * starts[None, :], axis=1, dtype=jnp.int32)
    length = jnp.sum(picked * doc_lengths[None, :], axis=1, dtype=jnp.int32)
    offset = places - begins
    return (offset, offset < length)


def rms_scale(values, gain):
    return values * lax.rsqrt(jnp.mean(values * values, axis=-1, keepdims=True) + epsilon) * gain


def rms_back(values, gain, grad_in):
    scale = lax.rsqrt(jnp.mean(values * values, axis=-1, keepdims=True) + epsilon)
    weighted = grad_in * gain
    grad_values = scale * weighted - values * scale**3 * jnp.mean(
        weighted * values, axis=-1, keepdims=True
    )
    grad_gain = jnp.sum((grad_in * values * scale).reshape(-1, values.shape[-1]), axis=0)
    return (grad_values, grad_gain)


def owner_of(meta, docs, places):
    total = jnp.zeros_like(places)
    for doc in range(1, docs):
        total = total + jnp.where(places >= meta[1 + doc], 1, 0)
    return total


def offset_of(meta, docs, places):
    begin = jnp.zeros_like(places)
    for doc in range(1, docs):
        begin = jnp.where(places >= meta[1 + doc], meta[1 + doc], begin)
    return places - begin


class Masks:
    def __init__(self, meta, docs, chunk):
        base = meta[0] + chunk * BLOCK
        rows = lax.broadcasted_iota(jnp.int32, (BLOCK, BLOCK), 0)
        cols = lax.broadcasted_iota(jnp.int32, (BLOCK, BLOCK), 1)
        same = owner_of(meta, docs, base + rows) == owner_of(meta, docs, base + cols)
        self.inclusive = same & (rows >= cols)
        self.strictly = same & (rows > cols)
        self.level = rows ^ cols
        self.lower = jnp.where(rows >= cols, 1.0, 0.0).astype(bf16)
        self.upper = jnp.where(rows <= cols, 1.0, 0.0).astype(bf16)
        self.eye = jnp.where(rows == cols, 1.0, 0.0)
        place = base + lax.broadcasted_iota(jnp.int32, (BLOCK, 1), 0)
        owner = owner_of(meta, docs, place)
        before = jnp.int32(0)
        last = jnp.int32(0)
        for doc in range(1, docs):
            before = before + jnp.where(base - 1 >= meta[1 + doc], 1, 0)
            last = last + jnp.where(base + BLOCK - 1 >= meta[1 + doc], 1, 0)
        self.enters = jnp.where(owner == before, 1.0, 0.0)
        self.leaves = jnp.where(owner == last, 1.0, 0.0)
        self.through = jnp.where(before == last, 1.0, 0.0).astype(f32)
        self.offset = offset_of(meta, docs, place)


def decays(masks, scal, scal_t, head):
    column = scal[:, head : head + 1]
    row = scal_t[head : head + 1, :]
    within = jnp.where(masks.inclusive, jnp.exp(jnp.minimum(column - row, 0.0)), 0.0)
    last = column[BLOCK - 1 : BLOCK, :]
    entry = jnp.exp(column) * masks.enters
    leave = jnp.exp(last - column) * masks.leaves
    through = jnp.exp(last) * masks.through
    return within, entry, leave, through


def unit_lower_inverse(masks, system):
    inverse = masks.eye - jnp.where(masks.level == 1, system, 0.0)
    width = 2
    while width < BLOCK:
        part = jnp.where((masks.level >= width) & (masks.level < 2 * width), system, 0.0)
        low = inverse.astype(bf16)
        inverse = inverse - dot(low, dot(part.astype(bf16), low).astype(bf16))
        width *= 2
    return inverse


def forward_kernel(
    heads, key_width, value_width, docs, taps,
    meta, rows_ref, tail_ref, w_ref, conv_ref, dvec_ref,
    pre_ref, act_ref, gate_ref, small_ref, scal_ref, qkv_ref, inv_ref, w_out_ref, u_ref, starts_ref, drop_ref, map_ref,
    ext, state,
):
    chunk = pl.program_id(0)
    qw, vw = heads * key_width, heads * value_width
    mixed = 2 * qw + vw
    masks = Masks(meta, docs, chunk)
    rows = rows_ref[...]

    @pl.when(chunk == 0)
    def _():
        halo = dot(tail_ref[...], w_ref[:, :mixed])
        ext[0:HALO, :] = halo[HALO : 2 * HALO, :]
        ident = jnp.where(
            lax.broadcasted_iota(jnp.int32, (key_width, key_width + value_width), 0)
            == lax.broadcasted_iota(jnp.int32, (key_width, key_width + value_width), 1),
            1.0, 0.0,
        )
        for head in range(heads):
            state[head] = ident

    @pl.when(chunk > 0)
    def _():
        ext[0:HALO, :] = ext[BLOCK : BLOCK + HALO, :]

    pre = dot(rows, w_ref[...])
    ext[HALO : HALO + BLOCK, :] = pre[:, :mixed]
    pre_ref[...] = pre[:, :mixed]
    gate_ref[...] = pre[:, mixed : mixed + vw]
    small = pre[:, mixed + vw :]
    small_ref[...] = small

    conv = jnp.zeros((BLOCK, mixed), f32)
    for lag in range(taps):
        keep = jnp.where(masks.offset >= lag, 1.0, 0.0)
        conv = conv + conv_ref[lag : lag + 1, :] * (ext[HALO - lag : HALO - lag + BLOCK, :] * keep)
    act_ref[...] = conv
    act = conv * sigmoid(conv)

    lane = lax.broadcasted_iota(jnp.int32, (BLOCK, LANES), 1)
    decay = dvec_ref[1:2, :] * softplus(small + dvec_ref[0:1, :])
    cumul = exact_left(masks.lower, decay)
    scal = jnp.where(lane < heads, cumul, sigmoid(small))
    scal_ref[...] = scal
    scal_t = scal.T

    for head in range(heads):
        act_q = act[:, head * key_width : (head + 1) * key_width]
        act_k = act[:, qw + head * key_width : qw + (head + 1) * key_width]
        value = act[:, 2 * qw + head * value_width : 2 * qw + (head + 1) * value_width].astype(bf16)
        norm_q = lax.rsqrt(jnp.sum(act_q * act_q, axis=1, keepdims=True) + epsilon)
        norm_k = lax.rsqrt(jnp.sum(act_k * act_k, axis=1, keepdims=True) + epsilon)
        query = (act_q * norm_q * key_width ** (-0.5)).astype(bf16)
        key = (act_k * norm_k).astype(bf16)
        qkv_ref[:, head * key_width : (head + 1) * key_width] = query
        qkv_ref[:, qw + head * key_width : qw + (head + 1) * key_width] = key
        qkv_ref[:, 2 * qw + head * value_width : 2 * qw + (head + 1) * value_width] = value
        within, entry, leave, through = decays(masks, scal, scal_t, head)
        beta = scal[:, heads + head : heads + head + 1]
        system = jnp.where(masks.strictly, beta * dot_nt(key, key) * within, 0.0)
        inverse = unit_lower_inverse(masks, system).astype(bf16)
        inv_ref[0, head] = inverse
        key_f = key.astype(f32)
        w_part = dot(inverse, (beta * entry * key_f).astype(bf16)).astype(bf16)
        u_part = dot(inverse, (beta * value.astype(f32)).astype(bf16))
        w_out_ref[0, head] = w_part
        u_ref[0, head] = u_part
        tail_key = (leave * key_f).astype(bf16)
        drop = dot_tn(tail_key, w_part)
        added = dot_tn(tail_key, u_part.astype(bf16))
        drop_ref[0, head] = drop
        before = state[head]
        starts_ref[0, head] = before
        after = through * before - dot(drop.astype(bf16), before.astype(bf16))
        after = after + jnp.concatenate([jnp.zeros((key_width, key_width), f32), added], axis=1)
        state[head] = after
        map_ref[head] = after


def output_kernel(
    heads, key_width, value_width, docs, others,
    meta, maps_ref, starts_ref, w_in_ref, u_ref, qkv_ref, scal_ref, gate_ref, gain_ref, w_output_ref,
    core_ref, gated_ref, mixed_ref, fresh_ref, state_ref,
    incoming,
):
    chunk = pl.program_id(0)
    qw = heads * key_width

    @pl.when(chunk == 0)
    def _():
        for head in range(heads):
            state = jnp.zeros((key_width, value_width), f32)
            for other in range(others):
                passing = maps_ref[other, head, :, :key_width]
                top, low = halves(state)
                state = dot(passing, top) + dot(passing, low) + maps_ref[other, head, :, key_width:].astype(f32)
            incoming[head] = state

    masks = Masks(meta, docs, chunk)
    scal = scal_ref[...]
    scal_t = scal.T
    gain = gain_ref[...]
    for head in range(heads):
        query = qkv_ref[:, head * key_width : (head + 1) * key_width]
        key = qkv_ref[:, qw + head * key_width : qw + (head + 1) * key_width]
        within, entry, leave, through = decays(masks, scal, scal_t, head)
        begun = starts_ref[0, head]
        state = dot_fine(begun[:, :key_width], incoming[head]) + begun[:, key_width:]
        state_ref[0, head] = state
        state_low = state.astype(bf16)
        fresh = (u_ref[0, head] - dot(w_in_ref[0, head], state_low)).astype(bf16)
        fresh_ref[0, head] = fresh
        scores = (dot_nt(query, key) * within).astype(bf16)
        core = dot((query.astype(f32) * entry).astype(bf16), state_low) + dot(scores, fresh)
        span = slice(head * value_width, (head + 1) * value_width)
        core_ref[:, span] = core
        scale = lax.rsqrt(jnp.mean(core * core, axis=1, keepdims=True) + epsilon)
        gate = gate_ref[:, span]
        gated_ref[:, span] = (core * scale * gain * (gate * sigmoid(gate))).astype(bf16)
    mixed_ref[...] = dot(gated_ref[...], w_output_ref[...]).astype(bf16)


def core_grad_kernel(
    heads, key_width, value_width, docs, chunks,
    meta, grad_ref, w_output_ref, core_ref, gate_ref, gain_ref, qkv_ref, scal_ref, w_in_ref, drop_ref,
    grad_core_ref, inner_ref, pull_ref, grad_gate_ref, grad_gain_ref, total_ref,
):
    step = pl.program_id(0)
    chunk = chunks - 1 - step
    qw = heads * key_width
    masks = Masks(meta, docs, chunk)
    scal = scal_ref[...]
    scal_t = scal.T
    gain = gain_ref[...]

    @pl.when(step == 0)
    def _():
        grad_gain_ref[...] = jnp.zeros_like(grad_gain_ref)
        total_ref[...] = jnp.zeros_like(total_ref)

    grad_gated = dot_nt(grad_ref[...], w_output_ref[...])
    for head in range(heads):
        span = slice(head * value_width, (head + 1) * value_width)
        core = core_ref[:, span]
        gate = gate_ref[:, span]
        grad_in = grad_gated[:, span]
        scale = lax.rsqrt(jnp.mean(core * core, axis=1, keepdims=True) + epsilon)
        sigma = sigmoid(gate)
        normed = core * scale
        grad_gate_ref[:, span] = (
            grad_in * (normed * gain) * (sigma * (1.0 + gate * (1.0 - sigma)))
        ).astype(bf16)
        grad_normed = grad_in * (gate * sigma)
        weighted = grad_normed * gain
        grad_core = scale * (weighted - normed * jnp.mean(weighted * normed, axis=1, keepdims=True))
        grad_gain_ref[0:1, :] += jnp.sum(grad_normed * normed, axis=0, keepdims=True)
        grad_core = grad_core.astype(bf16)
        grad_core_ref[0, head] = grad_core
        query = qkv_ref[:, head * key_width : (head + 1) * key_width]
        key = qkv_ref[:, qw + head * key_width : qw + (head + 1) * key_width]
        within, entry, leave, through = decays(masks, scal, scal_t, head)
        scores = (dot_nt(query, key) * within).astype(bf16)
        inner = dot_tn(scores, grad_core)
        inner_ref[0, head] = inner
        pull = dot_tn((query.astype(f32) * entry).astype(bf16), grad_core) - dot_tn(
            w_in_ref[0, head], inner.astype(bf16)
        )
        pull_ref[0, head] = pull
        total = total_ref[head]
        total_ref[head] = (
            through * total - dot_tn(drop_ref[0, head].astype(bf16), total.astype(bf16)) + pull
        )


def backward_kernel(
    heads, key_width, value_width, docs, chunks, others,
    meta, maps_ref, qkv_ref, act_ref, scal_ref, small_ref, inv_ref, fresh_ref, state_ref,
    grad_core_ref, inner_ref, pull_ref, drop_ref, dvec_ref,
    grad_conv_ref, grad_small_ref, sums_ref,
    carried,
):
    step = pl.program_id(0)
    chunk = chunks - 1 - step
    qw = heads * key_width

    @pl.when(step == 0)
    def _():
        sums_ref[...] = jnp.zeros_like(sums_ref)
        for head in range(heads):
            state = jnp.zeros((key_width, value_width), f32)
            for other in range(others):
                passing = maps_ref[other, head, :, :key_width]
                top, low = halves(state)
                state = dot_tn(passing, top) + dot_tn(passing, low) + maps_ref[other, head, :, key_width:].astype(f32)
            carried[head] = state

    masks = Masks(meta, docs, chunk)
    scal = scal_ref[...]
    scal_t = scal.T
    lane = lax.broadcasted_iota(jnp.int32, (BLOCK, LANES), 1)
    slopes = jnp.zeros((BLOCK, LANES), f32)
    tails = jnp.zeros((1, LANES), f32)
    betas = jnp.zeros((BLOCK, LANES), f32)
    for head in range(heads):
        q_span = slice(head * key_width, (head + 1) * key_width)
        k_span = slice(qw + head * key_width, qw + (head + 1) * key_width)
        v_span = slice(2 * qw + head * value_width, 2 * qw + (head + 1) * value_width)
        query, key, value = qkv_ref[:, q_span], qkv_ref[:, k_span], qkv_ref[:, v_span]
        query_f, key_f = query.astype(f32), key.astype(f32)
        within, entry, leave, through = decays(masks, scal, scal_t, head)
        beta = scal[:, heads + head : heads + head + 1]
        later = carried[head]
        later_low = later.astype(bf16)
        state = state_ref[0, head]
        state_low = state.astype(bf16)
        grad_core = grad_core_ref[0, head]
        fresh = fresh_ref[0, head]
        carried[head] = through * later - dot_tn(drop_ref[0, head].astype(bf16), later_low) + pull_ref[0, head]
        grad_fresh = inner_ref[0, head] + dot((leave * key_f).astype(bf16), later_low)
        grad_x = dot_tn(inv_ref[0, head], grad_fresh.astype(bf16))
        grad_x_low = grad_x.astype(bf16)
        grad_x_beta = beta * grad_x
        recalled = dot(key, state_low)
        grad_beta = jnp.sum(grad_x * (value.astype(f32) - entry * recalled), axis=1, keepdims=True)
        from_state_q = dot_nt(grad_core, state_low)
        from_state_k = dot_nt(grad_x_beta.astype(bf16), state_low)
        grad_scores = (dot_nt(grad_core, fresh) * within).astype(bf16)
        gram = dot_nt(key, key)
        grad_system = jnp.where(masks.strictly, dot_nt(grad_x_low, fresh) * within, 0.0)
        grad_beta = grad_beta - jnp.sum(grad_system * gram, axis=1, keepdims=True)
        grad_gram = (-beta * grad_system).astype(bf16)
        grad_query = dot(grad_scores, key) + entry * from_state_q
        grad_row = dot(grad_gram, key) - entry * from_state_k
        passed = leave * dot_nt(fresh, later_low)
        grad_col = dot_tn(grad_gram, key) + dot_tn(grad_scores, query) + passed
        slope = jnp.sum(query_f * grad_query + key_f * (grad_row - grad_col), axis=1, keepdims=True)
        kept = jnp.sum(jnp.sum(state * later, axis=1, keepdims=True), axis=0, keepdims=True)
        moved = jnp.sum(jnp.sum(key_f * passed, axis=1, keepdims=True), axis=0, keepdims=True)
        tail = through * kept + moved
        slopes = jnp.where(lane == head, slope, slopes)
        tails = jnp.where(lane[0:1, :] == head, tail, tails)
        betas = jnp.where(lane == heads + head, grad_beta, betas)

        conv_q, conv_k, conv_v = act_ref[:, q_span], act_ref[:, k_span], act_ref[:, v_span]
        for span, conv, grad, factor in (
            (q_span, conv_q, grad_query, key_width ** (-0.5)),
            (k_span, conv_k, grad_row + grad_col, 1.0),
        ):
            sigma = sigmoid(conv)
            act = conv * sigma
            norm = lax.rsqrt(jnp.sum(act * act, axis=1, keepdims=True) + epsilon)
            unit = act * norm
            grad_act = (factor * norm) * (grad - unit * jnp.sum(grad * unit, axis=1, keepdims=True))
            grad_conv_ref[:, span] = grad_act * (sigma * (1.0 + conv * (1.0 - sigma)))
        grad_conv_ref[:, v_span] = grad_x_beta * silu_slope(conv_v)

    grad_decay = jnp.where(lane < heads, exact_left(masks.upper, slopes) + tails, 0.0)
    shifted = small_ref[...] + dvec_ref[0:1, :]
    rate = dvec_ref[1:2, :]
    grad_z = grad_decay * rate * sigmoid(shifted)
    sums_ref[0:1, :] += jnp.sum(grad_z, axis=0, keepdims=True)
    sums_ref[1:2, :] += jnp.sum(grad_decay * (rate * softplus(shifted)), axis=0, keepdims=True)
    strength = sigmoid(small_ref[...])
    grad_small_ref[...] = jnp.where(lane < heads, grad_z, betas * strength * (1.0 - strength)).astype(bf16)


def projection_grad_kernel(
    mixed, docs, chunks, taps,
    meta, grad_conv_ref, later_ref, edge_ref, pre_ref, grad_gate_ref, grad_small_ref, conv_ref, w_ref,
    grad_pre_ref, grad_taps_ref, grad_rows_ref,
    ext,
):
    chunk = pl.program_id(0)

    @pl.when(chunk == 0)
    def _():
        grad_taps_ref[...] = jnp.zeros_like(grad_taps_ref)

    ext[0:BLOCK, :] = grad_conv_ref[...]

    @pl.when(chunk == chunks - 1)
    def _():
        ext[BLOCK : BLOCK + HALO, :] = edge_ref[...]

    @pl.when(chunk < chunks - 1)
    def _():
        ext[BLOCK : BLOCK + HALO, :] = later_ref[...]

    place = meta[0] + chunk * BLOCK + lax.broadcasted_iota(jnp.int32, (BLOCK, 1), 0)
    pre = pre_ref[...]
    total = jnp.zeros((BLOCK, mixed), f32)
    for lag in range(taps):
        keep = jnp.where(offset_of(meta, docs, place + lag) >= lag, 1.0, 0.0)
        moved = ext[lag : lag + BLOCK, :] * keep
        total = total + conv_ref[lag : lag + 1, :] * moved
        grad_taps_ref[lag : lag + 1, :] += jnp.sum(pre * moved, axis=0, keepdims=True)
    width = grad_gate_ref.shape[1]
    grad_pre_ref[:, :mixed] = total.astype(bf16)
    grad_pre_ref[:, mixed : mixed + width] = grad_gate_ref[...]
    grad_pre_ref[:, mixed + width :] = grad_small_ref[...]
    grad_rows_ref[...] = dot_nt(grad_pre_ref[...], w_ref[...]).astype(bf16)


def whole(shape):
    zeros = (0,) * len(shape)
    return pl.BlockSpec(tuple(shape), lambda step: zeros)


def by_rows(width, chunks=None):
    if chunks is None:
        return pl.BlockSpec((BLOCK, width), lambda step: (step, 0))
    return pl.BlockSpec((BLOCK, width), lambda step: (chunks - 1 - step, 0))


def by_chunk(shape, chunks=None):
    rest = (0,) * len(shape)
    if chunks is None:
        return pl.BlockSpec((1,) + tuple(shape), lambda step: (step,) + rest)
    return pl.BlockSpec((1,) + tuple(shape), lambda step: (chunks - 1 - step,) + rest)


SCALARS = pl.BlockSpec(memory_space=pltpu.SMEM)


def params():
    return pltpu.CompilerParams(dimension_semantics=("arbitrary",), vmem_limit_bytes=VMEM_LIMIT)


def struct(shape, dtype):
    return jax.ShapeDtypeStruct(tuple(shape), dtype)


def from_earlier(array, axis):
    devices = lax.axis_size(axis)
    parts = [
        lax.ppermute(array, axis, [(i, i + by) for i in range(devices - by)])
        for by in range(devices - 1, 0, -1)
    ]
    return jnp.stack(parts) if parts else jnp.zeros((1,) + array.shape, array.dtype)


def from_later(array, axis):
    devices = lax.axis_size(axis)
    parts = [
        lax.ppermute(array, axis, [(i + by, i) for i in range(devices - by)])
        for by in range(devices - 1, 0, -1)
    ]
    return jnp.stack(parts) if parts else jnp.zeros((1,) + array.shape, array.dtype)


def shards(
    inputs,
    doc_lengths,
    first_gain,
    w_query,
    w_key,
    w_value,
    w_outgate,
    w_decay,
    w_beta,
    conv_query,
    conv_key,
    conv_value,
    decay_log,
    decay_bias,
    head_gain,
    w_output,
    second_gain,
    w_gate,
    w_up,
    w_down,
    cotangent,
):
    row_count, model_width = inputs.shape
    heads = decay_log.shape[0]
    qw, vw = w_query.shape[1], w_value.shape[1]
    key_width, value_width = qw // heads, vw // heads
    mixed_width = 2 * qw + vw
    taps = conv_query.shape[0]
    docs = doc_lengths.shape[0]
    seq_index = lax.axis_index("seq")
    head_index = lax.axis_index("head")
    head_total = lax.axis_size("head")
    seq_rows = row_count * head_total
    chunks = seq_rows // BLOCK
    others = max(lax.axis_size("seq") - 1, 1)
    sizes = (heads, key_width, value_width, docs)

    inputs_f = inputs.astype(f32)
    normed = rms_scale(inputs_f, first_gain).astype(bf16)
    block_rows = lax.all_gather(normed, "head", axis=0, tiled=True)
    tail = from_previous(block_rows[seq_rows - 2 * HALO :])
    meta = jnp.concatenate(
        [(seq_index * seq_rows).astype(jnp.int32)[None], slot_starts(doc_lengths)]
    )
    _, own_valid = layout(doc_lengths, (seq_index * head_total + head_index) * row_count, row_count)

    w_all = jnp.concatenate(
        [
            w_query, w_key, w_value, w_outgate, w_decay, w_beta,
            jnp.zeros((model_width, LANES - 2 * heads), bf16),
        ],
        axis=1,
    )
    all_width = w_all.shape[1]
    conv_all = jnp.concatenate([conv_query, conv_key, conv_value], axis=1)
    dvec = jnp.zeros((8, LANES), f32)
    dvec = dvec.at[0, :heads].set(decay_bias).at[1, :heads].set(-jnp.exp(decay_log))
    map_shape = (heads, key_width, key_width + value_width)

    (pre, conv, gate, small, scal, qkv, inverse, w_part, u_part, starts, drop, block_map) = pl.pallas_call(
        functools.partial(forward_kernel, *sizes, taps),
        grid=(chunks,),
        in_specs=[
            SCALARS, by_rows(model_width), whole((2 * HALO, model_width)),
            whole(w_all.shape), whole(conv_all.shape), whole(dvec.shape),
        ],
        out_specs=[
            by_rows(mixed_width), by_rows(mixed_width), by_rows(vw), by_rows(LANES), by_rows(LANES),
            by_rows(mixed_width),
            by_chunk((heads, BLOCK, BLOCK)), by_chunk((heads, BLOCK, key_width)),
            by_chunk((heads, BLOCK, value_width)), by_chunk(map_shape),
            by_chunk((heads, key_width, key_width)), whole(map_shape),
        ],
        out_shape=[
            struct((seq_rows, mixed_width), f32), struct((seq_rows, mixed_width), f32),
            struct((seq_rows, vw), f32), struct((seq_rows, LANES), f32), struct((seq_rows, LANES), f32),
            struct((seq_rows, mixed_width), bf16),
            struct((chunks, heads, BLOCK, BLOCK), bf16), struct((chunks, heads, BLOCK, key_width), bf16),
            struct((chunks, heads, BLOCK, value_width), f32), struct((chunks,) + map_shape, f32),
            struct((chunks, heads, key_width, key_width), f32), struct(map_shape, f32),
        ],
        scratch_shapes=[pltpu.VMEM((BLOCK + HALO, mixed_width), f32), pltpu.VMEM(map_shape, f32)],
        compiler_params=params(),
        name="mixer_forward",
    )(meta, block_rows, tail, w_all, conv_all, dvec)

    earlier = from_earlier(block_map.astype(bf16), "seq")
    gain_row = head_gain[None, :]
    core, gated, mixed_part, fresh, states = pl.pallas_call(
        functools.partial(output_kernel, *sizes, others),
        grid=(chunks,),
        in_specs=[
            SCALARS, whole(earlier.shape), by_chunk(map_shape), by_chunk((heads, BLOCK, key_width)),
            by_chunk((heads, BLOCK, value_width)), by_rows(mixed_width), by_rows(LANES), by_rows(vw),
            whole(gain_row.shape), whole(w_output.shape),
        ],
        out_specs=[
            by_rows(vw), by_rows(vw), by_rows(model_width), by_chunk((heads, BLOCK, value_width)),
            by_chunk((heads, key_width, value_width)),
        ],
        out_shape=[
            struct((seq_rows, vw), f32), struct((seq_rows, vw), bf16), struct((seq_rows, model_width), bf16),
            struct((chunks, heads, BLOCK, value_width), bf16),
            struct((chunks, heads, key_width, value_width), f32),
        ],
        scratch_shapes=[pltpu.VMEM((heads, key_width, value_width), f32)],
        compiler_params=params(),
        name="mixer_output",
    )(meta, earlier, starts, w_part, u_part, qkv, scal, gate, gain_row, w_output)

    mixer_out = lax.psum_scatter(mixed_part, "head", scatter_dimension=0, tiled=True).astype(f32)
    hidden_in = inputs_f + mixer_out
    normed_two = rms_scale(hidden_in, second_gain).astype(bf16)
    mlp_block = lax.all_gather(normed_two, "seq", axis=0, tiled=True)
    gate_pre = dot(mlp_block, w_gate)
    up_pre = dot(mlp_block, w_up)
    hidden = (jax.nn.silu(gate_pre) * up_pre).astype(bf16)
    mlp_out = lax.psum_scatter(
        dot(hidden, w_down).astype(bf16), "seq", scatter_dimension=0, tiled=True
    ).astype(f32)
    output = (hidden_in + mlp_out).astype(bf16)
    grad_out = cotangent.astype(f32) * own_valid.astype(f32)[:, None]
    grad_low = grad_out.astype(bf16)
    grad_block_two = lax.all_gather(grad_low, "seq", axis=0, tiled=True)
    grad_hidden = dot_nt(grad_block_two, w_down)
    grad_w_down = dot_tn(hidden, grad_block_two)
    grad_gate = (grad_hidden * up_pre * silu_slope(gate_pre)).astype(bf16)
    grad_up = (grad_hidden * jax.nn.silu(gate_pre)).astype(bf16)
    grad_normed_two = lax.psum_scatter(
        (dot_nt(grad_gate, w_gate) + dot_nt(grad_up, w_up)).astype(bf16),
        "seq",
        scatter_dimension=0,
        tiled=True,
    ).astype(f32)
    grad_w_gate = dot_tn(mlp_block, grad_gate)
    grad_w_up = dot_tn(mlp_block, grad_up)
    grad_hidden_norm, grad_second = rms_back(hidden_in, second_gain, grad_normed_two)
    grad_hidden_in = grad_out + grad_hidden_norm
    grad_mix = grad_hidden_in.astype(bf16)
    grad_block = lax.all_gather(grad_mix, "head", axis=0, tiled=True)

    grad_core, inner, pull, grad_gate_pre, grad_head, pulled = pl.pallas_call(
        functools.partial(core_grad_kernel, *sizes, chunks),
        grid=(chunks,),
        in_specs=[
            SCALARS, by_rows(model_width, chunks), whole(w_output.shape), by_rows(vw, chunks), by_rows(vw, chunks),
            whole(gain_row.shape), by_rows(mixed_width, chunks), by_rows(LANES, chunks),
            by_chunk((heads, BLOCK, key_width), chunks), by_chunk((heads, key_width, key_width), chunks),
        ],
        out_specs=[
            by_chunk((heads, BLOCK, value_width), chunks), by_chunk((heads, BLOCK, value_width), chunks),
            by_chunk((heads, key_width, value_width), chunks), by_rows(vw, chunks),
            whole((8, value_width)), whole((heads, key_width, value_width)),
        ],
        out_shape=[
            struct((chunks, heads, BLOCK, value_width), bf16), struct((chunks, heads, BLOCK, value_width), f32),
            struct((chunks, heads, key_width, value_width), f32), struct((seq_rows, vw), bf16),
            struct((8, value_width), f32), struct((heads, key_width, value_width), f32),
        ],
        compiler_params=params(),
        name="mixer_core_grad",
    )(meta, grad_block, w_output, core, gate, gain_row, qkv, scal, w_part, drop)
    grad_w_output = dot_tn(gated, grad_block)

    later = from_later(
        jnp.concatenate([block_map[:, :, :key_width], pulled], axis=2).astype(bf16), "seq"
    )
    grad_conv, grad_small, sums = pl.pallas_call(
        functools.partial(backward_kernel, *sizes, chunks, others),
        grid=(chunks,),
        in_specs=[
            SCALARS, whole(later.shape), by_rows(mixed_width, chunks), by_rows(mixed_width, chunks),
            by_rows(LANES, chunks), by_rows(LANES, chunks), by_chunk((heads, BLOCK, BLOCK), chunks),
            by_chunk((heads, BLOCK, value_width), chunks), by_chunk((heads, key_width, value_width), chunks),
            by_chunk((heads, BLOCK, value_width), chunks), by_chunk((heads, BLOCK, value_width), chunks),
            by_chunk((heads, key_width, value_width), chunks), by_chunk((heads, key_width, key_width), chunks),
            whole(dvec.shape),
        ],
        out_specs=[by_rows(mixed_width, chunks), by_rows(LANES, chunks), whole((8, LANES))],
        out_shape=[
            struct((seq_rows, mixed_width), f32), struct((seq_rows, LANES), bf16), struct((8, LANES), f32),
        ],
        scratch_shapes=[pltpu.VMEM((heads, key_width, value_width), f32)],
        compiler_params=params(),
        name="mixer_backward",
    )(meta, later, qkv, conv, scal, small, inverse, fresh, states, grad_core, inner, pull, drop, dvec)

    edge = from_next(grad_conv[:HALO])
    step_rows = BLOCK // HALO
    last_halo = seq_rows // HALO - 1
    grad_pre, grad_taps, grad_rows = pl.pallas_call(
        functools.partial(projection_grad_kernel, mixed_width, docs, chunks, taps),
        grid=(chunks,),
        in_specs=[
            SCALARS, by_rows(mixed_width),
            pl.BlockSpec(
                (HALO, mixed_width), lambda step: (jnp.minimum((step + 1) * step_rows, last_halo), 0)
            ),
            whole(edge.shape), by_rows(mixed_width), by_rows(vw), by_rows(LANES),
            whole(conv_all.shape), whole(w_all.shape),
        ],
        out_specs=[by_rows(all_width), whole((8, mixed_width)), by_rows(model_width)],
        out_shape=[
            struct((seq_rows, all_width), bf16), struct((8, mixed_width), f32),
            struct((seq_rows, model_width), bf16),
        ],
        scratch_shapes=[pltpu.VMEM((BLOCK + HALO, mixed_width), f32)],
        compiler_params=params(),
        name="projection_grad",
    )(meta, grad_conv, grad_conv, edge, pre, grad_gate_pre, grad_small, conv_all, w_all)

    grad_normed = lax.psum_scatter(grad_rows, "head", scatter_dimension=0, tiled=True).astype(f32)
    grad_input_norm, grad_first = rms_back(inputs_f, first_gain, grad_normed)
    grad_inputs = grad_hidden_in + grad_input_norm
    grad_w_all = dot_tn(block_rows, grad_pre).astype(bf16)

    grad_w_gate, grad_w_up, grad_w_down, first_part, second_part, head_part = (
        lax.psum(grad_w_gate.astype(bf16), "head").astype(f32),
        lax.psum(grad_w_up.astype(bf16), "head").astype(f32),
        lax.psum(grad_w_down.astype(bf16), "head").astype(f32),
        lax.psum(grad_first.astype(bf16), "head").astype(f32),
        lax.psum(grad_second.astype(bf16), "head").astype(f32),
        lax.psum(grad_head[0].astype(bf16), "head").astype(f32),
    )
    grad_w_all, grad_w_output, grad_taps, sums, first_part, second_part, head_part = (
        lax.psum(part.astype(bf16), "seq").astype(f32)
        for part in (
            grad_w_all, grad_w_output, grad_taps[:taps], sums[:2, :heads], first_part, second_part, head_part,
        )
    )
    gate_at = mixed_width
    small_at = mixed_width + vw
    return (
        output,
        grad_inputs,
        first_part,
        grad_w_all[:, :qw],
        grad_w_all[:, qw : 2 * qw],
        grad_w_all[:, 2 * qw : gate_at],
        grad_w_all[:, gate_at:small_at],
        grad_w_all[:, small_at : small_at + heads],
        grad_w_all[:, small_at + heads : small_at + 2 * heads],
        grad_taps[:, :qw],
        grad_taps[:, qw : 2 * qw],
        grad_taps[:, 2 * qw :],
        sums[1],
        sums[0],
        head_part,
        grad_w_output,
        second_part,
        grad_w_gate,
        grad_w_up,
        grad_w_down,
    )


def from_previous(array):
    devices = lax.axis_size("seq")
    return lax.ppermute(array, "seq", [(i, i + 1) for i in range(devices - 1)])


def from_next(array):
    devices = lax.axis_size("seq")
    return lax.ppermute(array, "seq", [(i + 1, i) for i in range(devices - 1)])


def solution(mesh):
    in_specs = (
        P(("seq", "head"), None),
        P(),
        P(),
        P(None, "head"),
        P(None, "head"),
        P(None, "head"),
        P(None, "head"),
        P(None, "head"),
        P(None, "head"),
        P(None, "head"),
        P(None, "head"),
        P(None, "head"),
        P("head"),
        P("head"),
        P(),
        P("head", None),
        P(),
        P(None, "seq"),
        P(None, "seq"),
        P("seq", None),
        P(("seq", "head"), None),
    )
    out_specs = (
        P(("seq", "head"), None),
        P(("seq", "head"), None),
        P(),
        P(None, "head"),
        P(None, "head"),
        P(None, "head"),
        P(None, "head"),
        P(None, "head"),
        P(None, "head"),
        P(None, "head"),
        P(None, "head"),
        P(None, "head"),
        P("head"),
        P("head"),
        P(),
        P("head", None),
        P(),
        P(None, "seq"),
        P(None, "seq"),
        P("seq", None),
    )
    return jax.shard_map(shards, mesh=mesh, in_specs=in_specs, out_specs=out_specs, check_vma=False)
```

```python
import functools

import jax
import jax.numpy as jnp
from jax import lax
from jax.experimental import pallas as pl
from jax.experimental.pallas import tpu as pltpu
from jax.sharding import PartitionSpec as P

GROUP = 64
BLOCK = 256
LANES = 128
HALO = 8

epsilon = 1e-06
f32 = jnp.float32
bf16 = jnp.bfloat16
VMEM_LIMIT = 56 * 1024 * 1024


def dot(left, right):
    return jnp.dot(left, right, preferred_element_type=f32)


def dot_tn(left, right):
    return lax.dot_general(left, right, (((0,), (0,)), ((), ())), preferred_element_type=f32)


def dot_nt(left, right):
    return lax.dot_general(left, right, (((1,), (1,)), ((), ())), preferred_element_type=f32)


def halves(values):
    top = values.astype(bf16)
    return top, (values - top.astype(f32)).astype(bf16)


def exact_left(left, right):
    top = right.astype(bf16)
    rest = right - top.astype(f32)
    middle = rest.astype(bf16)
    low = (rest - middle.astype(f32)).astype(bf16)
    return dot(left, top) + dot(left, middle) + dot(left, low)


def dot_fine(left, right):
    left_top, left_low = halves(left)
    right_top, right_low = halves(right)
    return dot(left_top, right_top) + (dot(left_top, right_low) + dot(left_low, right_top))


def sigmoid(values):
    return jax.nn.sigmoid(values)


def silu_slope(values):
    sigma = sigmoid(values)
    return sigma * (1.0 + values * (1.0 - sigma))


def softplus(values):
    return jnp.maximum(values, 0.0) + jnp.log1p(jnp.exp(-jnp.abs(values)))


def slot_starts(doc_lengths):
    slot_sizes = (doc_lengths + (GROUP - 1)) // GROUP * GROUP
    return jnp.cumsum(slot_sizes, dtype=jnp.int32) - slot_sizes


def layout(doc_lengths, first_row, row_total):
    starts = slot_starts(doc_lengths)
    places = first_row + jnp.arange(row_total, dtype=jnp.int32)
    owners = jnp.sum(
        (places[:, None] >= starts[None, 1:]).astype(jnp.int32), axis=1, dtype=jnp.int32
    )
    picked = (owners[:, None] == jnp.arange(doc_lengths.shape[0], dtype=jnp.int32)[None, :]).astype(
        jnp.int32
    )
    begins = jnp.sum(picked * starts[None, :], axis=1, dtype=jnp.int32)
    length = jnp.sum(picked * doc_lengths[None, :], axis=1, dtype=jnp.int32)
    offset = places - begins
    return (offset, offset < length)


def rms_scale(values, gain):
    return values * lax.rsqrt(jnp.mean(values * values, axis=-1, keepdims=True) + epsilon) * gain


def rms_back(values, gain, grad_in):
    scale = lax.rsqrt(jnp.mean(values * values, axis=-1, keepdims=True) + epsilon)
    weighted = grad_in * gain
    grad_values = scale * weighted - values * scale**3 * jnp.mean(
        weighted * values, axis=-1, keepdims=True
    )
    grad_gain = jnp.sum((grad_in * values * scale).reshape(-1, values.shape[-1]), axis=0)
    return (grad_values, grad_gain)


def owner_of(meta, docs, places):
    total = jnp.zeros_like(places)
    for doc in range(1, docs):
        total = total + jnp.where(places >= meta[1 + doc], 1, 0)
    return total


def offset_of(meta, docs, places):
    begin = jnp.zeros_like(places)
    for doc in range(1, docs):
        begin = jnp.where(places >= meta[1 + doc], meta[1 + doc], begin)
    return places - begin


class Masks:
    def __init__(self, meta, docs, chunk):
        base = meta[0] + chunk * BLOCK
        rows = lax.broadcasted_iota(jnp.int32, (BLOCK, BLOCK), 0)
        cols = lax.broadcasted_iota(jnp.int32, (BLOCK, BLOCK), 1)
        same = owner_of(meta, docs, base + rows) == owner_of(meta, docs, base + cols)
        self.inclusive = same & (rows >= cols)
        self.strictly = same & (rows > cols)
        self.level = rows ^ cols
        self.lower = jnp.where(rows >= cols, 1.0, 0.0).astype(bf16)
        self.upper = jnp.where(rows <= cols, 1.0, 0.0).astype(bf16)
        self.eye = jnp.where(rows == cols, 1.0, 0.0)
        place = base + lax.broadcasted_iota(jnp.int32, (BLOCK, 1), 0)
        owner = owner_of(meta, docs, place)
        before = jnp.int32(0)
        last = jnp.int32(0)
        for doc in range(1, docs):
            before = before + jnp.where(base - 1 >= meta[1 + doc], 1, 0)
            last = last + jnp.where(base + BLOCK - 1 >= meta[1 + doc], 1, 0)
        self.enters = jnp.where(owner == before, 1.0, 0.0)
        self.leaves = jnp.where(owner == last, 1.0, 0.0)
        self.through = jnp.where(before == last, 1.0, 0.0).astype(f32)
        self.offset = offset_of(meta, docs, place)


def decays(masks, scal, scal_t, head):
    column = scal[:, head : head + 1]
    row = scal_t[head : head + 1, :]
    within = jnp.where(masks.inclusive, jnp.exp(jnp.minimum(column - row, 0.0)), 0.0)
    last = column[BLOCK - 1 : BLOCK, :]
    entry = jnp.exp(column) * masks.enters
    leave = jnp.exp(last - column) * masks.leaves
    through = jnp.exp(last) * masks.through
    return within, entry, leave, through


def unit_lower_inverse(masks, system):
    inverse = masks.eye - jnp.where(masks.level == 1, system, 0.0)
    width = 2
    while width < BLOCK:
        part = jnp.where((masks.level >= width) & (masks.level < 2 * width), system, 0.0)
        low = inverse.astype(bf16)
        inverse = inverse - dot(low, dot(part.astype(bf16), low).astype(bf16))
        width *= 2
    return inverse


def forward_kernel(
    heads, key_width, value_width, docs, taps, chunks,
    meta, rows_ref, tail_ref, wq_ref, wk_ref, wv_ref, wg_ref, ws_ref, conv_ref, dvec_ref, block_ref,
    pre_ref, act_ref, gate_ref, small_ref, scal_ref, qkv_ref, inv_ref, w_out_ref, u_ref, starts_ref, drop_ref, map_ref, blocks_ref,
    ext, state, own_sem, send_sem, recv_sem,
):
    chunk = pl.program_id(0)
    gather = LineGather("seq", block_ref, blocks_ref, own_sem, send_sem, recv_sem)

    @pl.when(chunk == 0)
    def _():
        gather.enter()
        gather.advance(0)

    for hop in range(1, gather.devices):
        @pl.when(chunk == min(hop * chunks // gather.devices + 1, chunks - 1))
        def _():
            gather.advance(hop)

    qw, vw = heads * key_width, heads * value_width
    mixed = 2 * qw + vw
    masks = Masks(meta, docs, chunk)
    rows = rows_ref[...]
    mixed_weights = ((slice(0, qw), wq_ref), (slice(qw, 2 * qw), wk_ref), (slice(2 * qw, mixed), wv_ref))

    @pl.when(chunk == 0)
    def _():
        for span, ref in mixed_weights:
            ext[0:HALO, span] = dot(tail_ref[...], ref[...])[HALO : 2 * HALO, :]

        ident = jnp.where(
            lax.broadcasted_iota(jnp.int32, (key_width, key_width + value_width), 0)
            == lax.broadcasted_iota(jnp.int32, (key_width, key_width + value_width), 1),
            1.0, 0.0,
        )
        for head in range(heads):
            state[head] = ident

    @pl.when(chunk > 0)
    def _():
        ext[0:HALO, :] = ext[BLOCK : BLOCK + HALO, :]

    for span, ref in mixed_weights:
        pre = dot(rows, ref[...])
        ext[HALO : HALO + BLOCK, span] = pre
        pre_ref[:, span] = pre
    gate_ref[...] = dot(rows, wg_ref[...])
    small = dot(rows, ws_ref[...])
    small_ref[...] = small

    conv = jnp.zeros((BLOCK, mixed), f32)
    for lag in range(taps):
        keep = jnp.where(masks.offset >= lag, 1.0, 0.0)
        conv = conv + conv_ref[lag : lag + 1, :] * (ext[HALO - lag : HALO - lag + BLOCK, :] * keep)
    act_ref[...] = conv
    act = conv * sigmoid(conv)

    lane = lax.broadcasted_iota(jnp.int32, (BLOCK, LANES), 1)
    decay = dvec_ref[1:2, :] * softplus(small + dvec_ref[0:1, :])
    cumul = exact_left(masks.lower, decay)
    scal = jnp.where(lane < heads, cumul, sigmoid(small))
    scal_ref[...] = scal
    scal_t = scal.T

    for head in range(heads):
        act_q = act[:, head * key_width : (head + 1) * key_width]
        act_k = act[:, qw + head * key_width : qw + (head + 1) * key_width]
        value = act[:, 2 * qw + head * value_width : 2 * qw + (head + 1) * value_width].astype(bf16)
        norm_q = lax.rsqrt(jnp.sum(act_q * act_q, axis=1, keepdims=True) + epsilon)
        norm_k = lax.rsqrt(jnp.sum(act_k * act_k, axis=1, keepdims=True) + epsilon)
        query = (act_q * norm_q * key_width ** (-0.5)).astype(bf16)
        key = (act_k * norm_k).astype(bf16)
        qkv_ref[:, head * key_width : (head + 1) * key_width] = query
        qkv_ref[:, qw + head * key_width : qw + (head + 1) * key_width] = key
        qkv_ref[:, 2 * qw + head * value_width : 2 * qw + (head + 1) * value_width] = value
        within, entry, leave, through = decays(masks, scal, scal_t, head)
        beta = scal[:, heads + head : heads + head + 1]
        system = jnp.where(masks.strictly, beta * dot_nt(key, key) * within, 0.0)
        inverse = unit_lower_inverse(masks, system).astype(bf16)
        inv_ref[0, head] = inverse
        key_f = key.astype(f32)
        w_part = dot(inverse, (beta * entry * key_f).astype(bf16)).astype(bf16)
        u_part = dot(inverse, (beta * value.astype(f32)).astype(bf16))
        w_out_ref[0, head] = w_part
        u_ref[0, head] = u_part
        tail_key = (leave * key_f).astype(bf16)
        drop = dot_tn(tail_key, w_part)
        added = dot_tn(tail_key, u_part.astype(bf16))
        drop_ref[0, head] = drop
        before = state[head]
        starts_ref[0, head] = before
        after = through * before - dot(drop.astype(bf16), before.astype(bf16))
        after = after + jnp.concatenate([jnp.zeros((key_width, key_width), f32), added], axis=1)
        state[head] = after
        map_ref[head] = after

    @pl.when(chunk == chunks - 1)
    def _():
        gather.leave()


def output_kernel(
    heads, key_width, value_width, docs, others,
    meta, maps_ref, starts_ref, w_in_ref, u_ref, qkv_ref, scal_ref, gate_ref, gain_ref, w_output_ref,
    core_ref, gated_ref, mixed_ref, fresh_ref, state_ref,
    incoming,
):
    chunk = pl.program_id(0)
    qw = heads * key_width

    @pl.when(chunk == 0)
    def _():
        for head in range(heads):
            state = jnp.zeros((key_width, value_width), f32)
            for other in range(others):
                passing = maps_ref[other, head, :, :key_width]
                top, low = halves(state)
                state = dot(passing, top) + dot(passing, low) + maps_ref[other, head, :, key_width:].astype(f32)
            incoming[head] = state

    masks = Masks(meta, docs, chunk)
    scal = scal_ref[...]
    scal_t = scal.T
    gain = gain_ref[...]
    for head in range(heads):
        query = qkv_ref[:, head * key_width : (head + 1) * key_width]
        key = qkv_ref[:, qw + head * key_width : qw + (head + 1) * key_width]
        within, entry, leave, through = decays(masks, scal, scal_t, head)
        begun = starts_ref[0, head]
        state = dot_fine(begun[:, :key_width], incoming[head]) + begun[:, key_width:]
        state_ref[0, head] = state
        state_low = state.astype(bf16)
        fresh = (u_ref[0, head] - dot(w_in_ref[0, head], state_low)).astype(bf16)
        fresh_ref[0, head] = fresh
        scores = (dot_nt(query, key) * within).astype(bf16)
        core = dot((query.astype(f32) * entry).astype(bf16), state_low) + dot(scores, fresh)
        span = slice(head * value_width, (head + 1) * value_width)
        core_ref[:, span] = core
        scale = lax.rsqrt(jnp.mean(core * core, axis=1, keepdims=True) + epsilon)
        gate = gate_ref[:, span]
        gated_ref[:, span] = (core * scale * gain * (gate * sigmoid(gate))).astype(bf16)
    mixed_ref[...] = dot(gated_ref[...], w_output_ref[...]).astype(bf16)


def core_grad_kernel(
    heads, key_width, value_width, docs, chunks,
    meta, grad_ref, w_output_ref, core_ref, gate_ref, gain_ref, qkv_ref, scal_ref, w_in_ref, drop_ref,
    grad_core_ref, inner_ref, pull_ref, grad_gate_ref, grad_gain_ref, total_ref,
):
    step = pl.program_id(0)
    chunk = chunks - 1 - step
    qw = heads * key_width
    masks = Masks(meta, docs, chunk)
    scal = scal_ref[...]
    scal_t = scal.T
    gain = gain_ref[...]

    @pl.when(step == 0)
    def _():
        grad_gain_ref[...] = jnp.zeros_like(grad_gain_ref)
        total_ref[...] = jnp.zeros_like(total_ref)

    grad_gated = dot_nt(grad_ref[...], w_output_ref[...])
    for head in range(heads):
        span = slice(head * value_width, (head + 1) * value_width)
        core = core_ref[:, span]
        gate = gate_ref[:, span]
        grad_in = grad_gated[:, span]
        scale = lax.rsqrt(jnp.mean(core * core, axis=1, keepdims=True) + epsilon)
        sigma = sigmoid(gate)
        normed = core * scale
        grad_gate_ref[:, span] = (
            grad_in * (normed * gain) * (sigma * (1.0 + gate * (1.0 - sigma)))
        ).astype(bf16)
        grad_normed = grad_in * (gate * sigma)
        weighted = grad_normed * gain
        grad_core = scale * (weighted - normed * jnp.mean(weighted * normed, axis=1, keepdims=True))
        grad_gain_ref[0:1, :] += jnp.sum(grad_normed * normed, axis=0, keepdims=True)
        grad_core = grad_core.astype(bf16)
        grad_core_ref[0, head] = grad_core
        query = qkv_ref[:, head * key_width : (head + 1) * key_width]
        key = qkv_ref[:, qw + head * key_width : qw + (head + 1) * key_width]
        within, entry, leave, through = decays(masks, scal, scal_t, head)
        scores = (dot_nt(query, key) * within).astype(bf16)
        inner = dot_tn(scores, grad_core)
        inner_ref[0, head] = inner
        pull = dot_tn((query.astype(f32) * entry).astype(bf16), grad_core) - dot_tn(
            w_in_ref[0, head], inner.astype(bf16)
        )
        pull_ref[0, head] = pull
        total = total_ref[head]
        total_ref[head] = (
            through * total - dot_tn(drop_ref[0, head].astype(bf16), total.astype(bf16)) + pull
        )


def backward_kernel(
    heads, key_width, value_width, docs, chunks, others,
    meta, maps_ref, qkv_ref, act_ref, scal_ref, small_ref, inv_ref, fresh_ref, state_ref,
    grad_core_ref, inner_ref, pull_ref, drop_ref, dvec_ref,
    grad_conv_ref, grad_small_ref, sums_ref,
    carried,
):
    step = pl.program_id(0)
    chunk = chunks - 1 - step
    qw = heads * key_width

    @pl.when(step == 0)
    def _():
        sums_ref[...] = jnp.zeros_like(sums_ref)
        for head in range(heads):
            state = jnp.zeros((key_width, value_width), f32)
            for other in range(others):
                passing = maps_ref[other, head, :, :key_width]
                top, low = halves(state)
                state = dot_tn(passing, top) + dot_tn(passing, low) + maps_ref[other, head, :, key_width:].astype(f32)
            carried[head] = state

    masks = Masks(meta, docs, chunk)
    scal = scal_ref[...]
    scal_t = scal.T
    lane = lax.broadcasted_iota(jnp.int32, (BLOCK, LANES), 1)
    slopes = jnp.zeros((BLOCK, LANES), f32)
    tails = jnp.zeros((1, LANES), f32)
    betas = jnp.zeros((BLOCK, LANES), f32)
    for head in range(heads):
        q_span = slice(head * key_width, (head + 1) * key_width)
        k_span = slice(qw + head * key_width, qw + (head + 1) * key_width)
        v_span = slice(2 * qw + head * value_width, 2 * qw + (head + 1) * value_width)
        query, key, value = qkv_ref[:, q_span], qkv_ref[:, k_span], qkv_ref[:, v_span]
        query_f, key_f = query.astype(f32), key.astype(f32)
        within, entry, leave, through = decays(masks, scal, scal_t, head)
        beta = scal[:, heads + head : heads + head + 1]
        later = carried[head]
        later_low = later.astype(bf16)
        state = state_ref[0, head]
        state_low = state.astype(bf16)
        grad_core = grad_core_ref[0, head]
        fresh = fresh_ref[0, head]
        carried[head] = through * later - dot_tn(drop_ref[0, head].astype(bf16), later_low) + pull_ref[0, head]
        grad_fresh = inner_ref[0, head] + dot((leave * key_f).astype(bf16), later_low)
        grad_x = dot_tn(inv_ref[0, head], grad_fresh.astype(bf16))
        grad_x_low = grad_x.astype(bf16)
        grad_x_beta = beta * grad_x
        recalled = dot(key, state_low)
        grad_beta = jnp.sum(grad_x * (value.astype(f32) - entry * recalled), axis=1, keepdims=True)
        from_state_q = dot_nt(grad_core, state_low)
        from_state_k = dot_nt(grad_x_beta.astype(bf16), state_low)
        grad_scores = (dot_nt(grad_core, fresh) * within).astype(bf16)
        gram = dot_nt(key, key)
        grad_system = jnp.where(masks.strictly, dot_nt(grad_x_low, fresh) * within, 0.0)
        grad_beta = grad_beta - jnp.sum(grad_system * gram, axis=1, keepdims=True)
        grad_gram = (-beta * grad_system).astype(bf16)
        grad_query = dot(grad_scores, key) + entry * from_state_q
        grad_row = dot(grad_gram, key) - entry * from_state_k
        passed = leave * dot_nt(fresh, later_low)
        grad_col = dot_tn(grad_gram, key) + dot_tn(grad_scores, query) + passed
        slope = jnp.sum(query_f * grad_query + key_f * (grad_row - grad_col), axis=1, keepdims=True)
        kept = jnp.sum(jnp.sum(state * later, axis=1, keepdims=True), axis=0, keepdims=True)
        moved = jnp.sum(jnp.sum(key_f * passed, axis=1, keepdims=True), axis=0, keepdims=True)
        tail = through * kept + moved
        slopes = jnp.where(lane == head, slope, slopes)
        tails = jnp.where(lane[0:1, :] == head, tail, tails)
        betas = jnp.where(lane == heads + head, grad_beta, betas)

        conv_q, conv_k, conv_v = act_ref[:, q_span], act_ref[:, k_span], act_ref[:, v_span]
        for span, conv, grad, factor in (
            (q_span, conv_q, grad_query, key_width ** (-0.5)),
            (k_span, conv_k, grad_row + grad_col, 1.0),
        ):
            sigma = sigmoid(conv)
            act = conv * sigma
            norm = lax.rsqrt(jnp.sum(act * act, axis=1, keepdims=True) + epsilon)
            unit = act * norm
            grad_act = (factor * norm) * (grad - unit * jnp.sum(grad * unit, axis=1, keepdims=True))
            grad_conv_ref[:, span] = grad_act * (sigma * (1.0 + conv * (1.0 - sigma)))
        grad_conv_ref[:, v_span] = grad_x_beta * silu_slope(conv_v)

    grad_decay = jnp.where(lane < heads, exact_left(masks.upper, slopes) + tails, 0.0)
    shifted = small_ref[...] + dvec_ref[0:1, :]
    rate = dvec_ref[1:2, :]
    grad_z = grad_decay * rate * sigmoid(shifted)
    sums_ref[0:1, :] += jnp.sum(grad_z, axis=0, keepdims=True)
    sums_ref[1:2, :] += jnp.sum(grad_decay * (rate * softplus(shifted)), axis=0, keepdims=True)
    strength = sigmoid(small_ref[...])
    grad_small_ref[...] = jnp.where(lane < heads, grad_z, betas * strength * (1.0 - strength)).astype(bf16)


def projection_grad_kernel(
    mixed, docs, chunks, taps,
    meta, grad_conv_ref, later_ref, edge_ref, pre_ref, grad_gate_ref, grad_small_ref, conv_ref, rows_ref,
    wq_ref, wk_ref, wv_ref, wg_ref, ws_ref,
    grad_pre_ref, grad_taps_ref, grad_rows_ref, gain_sum_ref,
    ext,
):
    chunk = pl.program_id(0)

    @pl.when(chunk == 0)
    def _():
        grad_taps_ref[...] = jnp.zeros_like(grad_taps_ref)
        gain_sum_ref[...] = jnp.zeros_like(gain_sum_ref)

    ext[0:BLOCK, :] = grad_conv_ref[...]

    @pl.when(chunk == chunks - 1)
    def _():
        ext[BLOCK : BLOCK + HALO, :] = edge_ref[...]

    @pl.when(chunk < chunks - 1)
    def _():
        ext[BLOCK : BLOCK + HALO, :] = later_ref[...]

    place = meta[0] + chunk * BLOCK + lax.broadcasted_iota(jnp.int32, (BLOCK, 1), 0)
    pre = pre_ref[...]
    total = jnp.zeros((BLOCK, mixed), f32)
    for lag in range(taps):
        keep = jnp.where(offset_of(meta, docs, place + lag) >= lag, 1.0, 0.0)
        moved = ext[lag : lag + BLOCK, :] * keep
        total = total + conv_ref[lag : lag + 1, :] * moved
        grad_taps_ref[lag : lag + 1, :] += jnp.sum(pre * moved, axis=0, keepdims=True)
    width = grad_gate_ref.shape[1]
    grad_pre_ref[:, :mixed] = total.astype(bf16)
    grad_pre_ref[:, mixed : mixed + width] = grad_gate_ref[...]
    grad_pre_ref[:, mixed + width :] = grad_small_ref[...]
    grad = jnp.zeros(grad_rows_ref.shape, f32)
    begin = 0
    for ref in (wq_ref, wk_ref, wv_ref, wg_ref, ws_ref):
        grad = grad + dot_nt(grad_pre_ref[:, begin : begin + ref.shape[1]], ref[...])
        begin += ref.shape[1]
    grad_rows_ref[...] = grad.astype(bf16)
    gain_sum_ref[0:1, :] += jnp.sum(grad * rows_ref[...].astype(f32), axis=0, keepdims=True)


MESH = pl.DeviceIdType.MESH
ANYWHERE = pl.BlockSpec(memory_space=pl.ANY)


def line_barrier(axis):
    devices, place = lax.axis_size(axis), lax.axis_index(axis)
    barrier = pltpu.get_barrier_semaphore()

    @pl.when(place > 0)
    def _():
        pl.semaphore_signal(barrier, inc=1, device_id={axis: place - 1}, device_id_type=MESH)

    @pl.when(place < devices - 1)
    def _():
        pl.semaphore_signal(barrier, inc=1, device_id={axis: place + 1}, device_id_type=MESH)

    @pl.when((place > 0) & (place < devices - 1))
    def _():
        pl.semaphore_wait(barrier, 2)

    @pl.when((place == 0) | (place == devices - 1))
    def _():
        pl.semaphore_wait(barrier, 1)


def line_sum_kernel(axis, counts, depths, *refs):
    total = len(counts)
    parts, sums = refs[:total], refs[total : 2 * total]
    arrived, passed = refs[2 * total : 3 * total], refs[3 * total : 4 * total]
    semaphores = refs[4 * total :]
    devices = lax.axis_size(axis)
    place = lax.axis_index(axis)

    line_barrier(axis)

    def rows_of(index, half, at):
        return pl.ds(pl.multiple_of((half * counts[index] + at) * depths[index], depths[index]), depths[index])

    def copy(index, half, at, target, back):
        rows = rows_of(index, half, at)
        slot = half * counts[index] + at
        sent = semaphores[4 * index + 2 * back].at[slot]
        received = semaphores[4 * index + 2 * back + 1].at[slot]
        source, landing = (sums, sums) if back else (passed, arrived)
        return pltpu.make_async_remote_copy(
            source[index].at[rows, :], landing[index].at[rows, :], sent, received,
            device_id={axis: target}, device_id_type=MESH,
        )

    def each(step, handle):
        for half in range(2):
            first, last = (devices - 1, 0) if half == 0 else (0, devices - 1)
            toward = place - 1 if half == 0 else place + 1
            away = place + 1 if half == 0 else place - 1
            for index in range(total):
                handle(half, index, step, toward, away, place == first, place == last)

    steps = max(counts)
    skew = 2
    window = 2

    def send(half, index, at, target, back):
        @pl.when(at >= window)
        def _():
            copy(index, half, at - window, target, back).wait_send()

        copy(index, half, at, target, back).start()

    def reduce_step(step, carry):
        def handle(half, index, step, toward, away, begin, end):
            at = step - skew * ((devices - 1 - place) if half == 0 else place)

            @pl.when((at >= 0) & (at < counts[index]))
            def _():
                rows = rows_of(index, half, at)

                @pl.when(begin)
                def _():
                    passed[index][rows, :] = parts[index][rows, :]
                    send(half, index, at, toward, 0)

                @pl.when(jnp.logical_not(begin))
                def _():
                    copy(index, half, at, toward, 0).wait_recv()
                    added = (parts[index][rows, :].astype(f32) + arrived[index][rows, :].astype(f32)).astype(bf16)

                    @pl.when(jnp.logical_not(end))
                    def _():
                        passed[index][rows, :] = added
                        send(half, index, at, toward, 0)

                    @pl.when(end)
                    def _():
                        sums[index][rows, :] = added

        each(step, handle)
        return carry

    lax.fori_loop(0, steps + skew * (devices - 1), reduce_step, 0)

    def back_step(step, carry):
        def handle(half, index, step, toward, away, begin, end):
            at = step - skew * (place if half == 0 else (devices - 1 - place))

            @pl.when((at >= 0) & (at < counts[index]))
            def _():
                @pl.when(jnp.logical_not(end))
                def _():
                    copy(index, half, at, away, 1).wait_recv()

                @pl.when(jnp.logical_not(begin))
                def _():
                    send(half, index, at, away, 1)

        each(step, handle)
        return carry

    lax.fori_loop(0, steps + skew * (devices - 1), back_step, 0)

    def last_step(step, carry):
        def handle(half, index, step, toward, away, begin, end):
            at = counts[index] - min(window, counts[index]) + step

            @pl.when(at < counts[index])
            def _():
                @pl.when(jnp.logical_not(end))
                def _():
                    copy(index, half, at, toward, 0).wait_send()

                @pl.when(jnp.logical_not(begin))
                def _():
                    copy(index, half, at, away, 1).wait_send()

        each(step, handle)
        return carry

    lax.fori_loop(0, window, last_step, 0)


def line_sum(arrays, depths, axis, collective_id):
    if lax.axis_size(axis) == 1:
        return arrays
    counts = tuple(array.shape[0] // (2 * depth) for array, depth in zip(arrays, depths))
    vmem = pl.BlockSpec(memory_space=pltpu.VMEM)
    scratch = [pltpu.VMEM(array.shape, bf16) for array in arrays] * 2
    for count in counts:
        scratch += [pltpu.SemaphoreType.DMA((2 * count,))] * 4
    return pl.pallas_call(
        functools.partial(line_sum_kernel, axis, counts, tuple(depths)),
        in_specs=[vmem] * len(arrays),
        out_specs=[vmem] * len(arrays),
        out_shape=[struct(array.shape, bf16) for array in arrays],
        scratch_shapes=scratch,
        compiler_params=pltpu.CompilerParams(
            collective_id=collective_id, has_side_effects=True, vmem_limit_bytes=VMEM_LIMIT
        ),
        cost_estimate=pl.CostEstimate(flops=10**8, bytes_accessed=600 * 10**6, transcendentals=0),
        name="line_sum",
    )(*arrays)


class LineGather:
    def __init__(self, axis, block, blocks, own_sem, send_sem, recv_sem):
        self.axis, self.block, self.blocks = axis, block, blocks
        self.own_sem, self.send_sem, self.recv_sem = own_sem, send_sem, recv_sem
        self.devices, self.place = lax.axis_size(axis), lax.axis_index(axis)
        self.rows = block.shape[0]

    def at(self, owner):
        return self.blocks.at[pl.ds(pl.multiple_of(owner * self.rows, self.rows), self.rows), :]

    def enter(self):
        line_barrier(self.axis)

    def copy(self, hop, way):
        owner = self.place - hop if way == 0 else self.place + hop
        target = self.place + 1 if way == 0 else self.place - 1
        slot = 2 * hop + way
        return pltpu.make_async_remote_copy(
            self.block if hop == 0 else self.at(owner), self.at(owner),
            self.send_sem.at[slot], self.recv_sem.at[slot],
            device_id={self.axis: target}, device_id_type=MESH,
        )

    def arrival(self, hop, way):
        owner = self.place - hop if way == 0 else self.place + hop
        target = self.place + 1 if way == 0 else self.place - 1
        slot = 2 * (hop - 1) + way
        return pltpu.make_async_remote_copy(
            self.at(owner), self.at(owner), self.send_sem.at[slot], self.recv_sem.at[slot],
            device_id={self.axis: target}, device_id_type=MESH,
        )

    def sends(self, hop, way):
        if way == 0:
            return (self.place >= hop) & (self.place < self.devices - 1)
        return (self.place + hop < self.devices) & (self.place > 0)

    def comes(self, hop, way):
        return self.place >= hop if way == 0 else self.place + hop < self.devices

    def own(self):
        return pltpu.make_async_copy(self.block, self.at(self.place), self.own_sem)

    def advance(self, hop):
        if hop == 0:
            self.own().start()
        for way in range(2):
            if hop:
                @pl.when(self.comes(hop, way))
                def _():
                    self.arrival(hop, way).wait_recv()

            if hop < self.devices - 1:
                @pl.when(self.sends(hop, way))
                def _():
                    self.copy(hop, way).start()

    def leave(self):
        self.own().wait()
        for hop in range(self.devices - 1):
            for way in range(2):
                @pl.when(self.sends(hop, way))
                def _():
                    self.copy(hop, way).wait_send()


def whole(shape):
    zeros = (0,) * len(shape)
    return pl.BlockSpec(tuple(shape), lambda step: zeros)


def by_rows(width, chunks=None):
    if chunks is None:
        return pl.BlockSpec((BLOCK, width), lambda step: (step, 0))
    return pl.BlockSpec((BLOCK, width), lambda step: (chunks - 1 - step, 0))


def by_chunk(shape, chunks=None):
    rest = (0,) * len(shape)
    if chunks is None:
        return pl.BlockSpec((1,) + tuple(shape), lambda step: (step,) + rest)
    return pl.BlockSpec((1,) + tuple(shape), lambda step: (chunks - 1 - step,) + rest)


SCALARS = pl.BlockSpec(memory_space=pltpu.SMEM)


def feed_kernel(
    axis, devices, rows,
    own_ref, grad_hidden_ref, w_gate_ref, w_up_ref,
    blocks_ref, hidden_ref, grad_gate_ref, grad_up_ref, total_ref,
    parts, arrived, gather_send, gather_recv, chain_send, chain_recv,
):
    place = lax.axis_index(axis)
    piece = rows // 2
    line_barrier(axis)

    def span(block, half):
        return pl.ds(pl.multiple_of(block * rows + half * piece, piece), piece)

    def full(block):
        return pl.ds(pl.multiple_of(block * rows, rows), rows)

    def gather(owner, hop, way, half):
        target = place + 1 - 2 * way
        slot = (hop * 2 + way) * 2 + half
        return pltpu.make_async_remote_copy(
            blocks_ref.at[span(owner, half), :], blocks_ref.at[span(owner, half), :],
            gather_send.at[slot], gather_recv.at[slot], device_id={axis: target}, device_id_type=MESH,
        )

    def chain(block, way, half, at):
        target = at + 1 - 2 * way
        landing = jnp.where((block == target) & (way == 0), devices, block)
        slot = (way * devices + block) * 2 + half
        return pltpu.make_async_remote_copy(
            parts.at[span(block, half), :], arrived.at[span(landing, half), :],
            chain_send.at[slot], chain_recv.at[slot], device_id={axis: target}, device_id_type=MESH,
        )

    blocks_ref[full(place), :] = own_ref[...]

    def event(step, carry):
        hop = (step + 1) // 2
        way = (step + 1) % 2
        owner = jnp.where(way == 0, place - hop, place + hop)
        target = place + 1 - 2 * way

        @pl.when(step == 0)
        def _():
            for side in range(2):
                @pl.when((place + 1 - 2 * side >= 0) & (place + 1 - 2 * side < devices))
                def _():
                    for half in range(2):
                        gather(place, 0, side, half).start()

        @pl.when((owner >= 0) & (owner < devices))
        def _():
            @pl.when(step > 0)
            def _():
                for half in range(2):
                    gather(owner, hop - 1, way, half).wait_recv()

                    @pl.when((target >= 0) & (target < devices))
                    def _():
                        gather(owner, hop, way, half).start()

            here = full(owner)
            block = blocks_ref[here, :]
            gate_pre = dot(block, w_gate_ref[...])
            up_pre = dot(block, w_up_ref[...])
            sigma = sigmoid(gate_pre)
            act = gate_pre * sigma
            hidden_ref[here, :] = (act * up_pre).astype(bf16)
            grad_hidden = grad_hidden_ref[here, :]
            grad_gate_ref[here, :] = (grad_hidden * up_pre * (sigma * (1.0 + gate_pre * (1.0 - sigma)))).astype(bf16)
            grad_up_ref[here, :] = (grad_hidden * act).astype(bf16)
            grad = dot_nt(grad_gate_ref[here, :], w_gate_ref[...]) + dot_nt(grad_up_ref[here, :], w_up_ref[...])

            @pl.when(step == 0)
            def _():
                total_ref[...] = grad

            @pl.when(step > 0)
            def _():
                parts[here, :] = grad.astype(bf16)

        @pl.when((way == 1) & (step > 0))
        def _():
            for side in (1, 0):
                block = devices - 1 - hop if side == 1 else hop
                begins = place == devices - 1 if side == 1 else place == 0
                valid = (block >= 0) & (block < place) if side == 1 else (block < devices) & (block > place)

                @pl.when(valid)
                def _():
                    for half in range(2):
                        @pl.when(jnp.logical_not(begins))
                        def _():
                            chain(block, side, half, place + 2 * side - 1).wait_recv()
                            at = span(block, half)
                            parts[at, :] = (parts[at, :].astype(f32) + arrived[at, :].astype(f32)).astype(bf16)

                        chain(block, side, half, place).start()

        return carry

    lax.fori_loop(0, 2 * devices - 1, event, 0)

    for side, landing, comes in ((1, place, place < devices - 1), (0, devices, place > 0)):
        @pl.when(comes)
        def _():
            for half in range(2):
                chain(place, side, half, place + 2 * side - 1).wait_recv()
                at = pl.ds(half * piece, piece)
                total_ref[at, :] += arrived[span(landing, half), :].astype(f32)

    def gather_end(step, carry):
        hop = step // 2
        way = step % 2
        owner = jnp.where(way == 0, place - hop, place + hop)
        target = place + 1 - 2 * way

        @pl.when((owner >= 0) & (owner < devices) & (target >= 0) & (target < devices))
        def _():
            for half in range(2):
                gather(owner, hop, way, half).wait_send()

        return carry

    lax.fori_loop(0, 2 * (devices - 1), gather_end, 0)

    def chain_end(block, carry):
        @pl.when(block < place)
        def _():
            for half in range(2):
                chain(block, 1, half, place).wait_send()

        @pl.when(block > place)
        def _():
            for half in range(2):
                chain(block, 0, half, place).wait_send()

        return carry

    lax.fori_loop(0, devices, chain_end, 0)


def feed(own, grad_hidden, w_gate, w_up, axis, collective_id):
    devices = lax.axis_size(axis)
    rows, width = own.shape
    units = w_gate.shape[1]
    vmem = pl.BlockSpec(memory_space=pltpu.VMEM)
    moves = pltpu.SemaphoreType.DMA((4 * devices,))
    return pl.pallas_call(
        functools.partial(feed_kernel, axis, devices, rows),
        in_specs=[vmem] * 4,
        out_specs=[vmem] * 5,
        out_shape=[struct((devices * rows, width), bf16)]
        + [struct((devices * rows, units), bf16)] * 3
        + [struct((rows, width), f32)],
        scratch_shapes=[
            pltpu.VMEM((devices * rows, width), bf16), pltpu.VMEM(((devices + 1) * rows, width), bf16),
            moves, moves, moves, moves,
        ],
        compiler_params=pltpu.CompilerParams(
            collective_id=collective_id, has_side_effects=True, vmem_limit_bytes=60 * 1024 * 1024
        ),
        name="feed",
    )(own, grad_hidden, w_gate, w_up)


def flip(index, mask):
    for bit in (1, 2, 4):
        if mask & bit:
            index = index + bit * (1 - 2 * ((index // bit) % 2))
    return index


def cube_barrier(axis, place):
    barrier = pltpu.get_barrier_semaphore()
    for mask in (1, 2, 4):
        pl.semaphore_signal(barrier, inc=1, device_id={axis: flip(place, mask)}, device_id_type=MESH)
    pl.semaphore_wait(barrier, 3)


class CubeGather:
    FIRST = ((0, 0, 2), (0, 1, 4), (0, 1, 2), (0, 0, 4), (0, 0, 1), (0, 1, 1))
    SECOND = ((2, 0, 4), (4, 1, 2), (2, 0, 1), (4, 1, 1))
    THIRD = ((2, 1, 1), (4, 0, 1))
    FOURTH = ((6, 0, 1), (6, 1, 1))

    def __init__(self, axis, own_ref, all_ref, own_sem, send_sem, recv_sem):
        self.axis, self.own_ref, self.all_ref = axis, own_ref, all_ref
        self.own_sem, self.send_sem, self.recv_sem = own_sem, send_sem, recv_sem
        self.place = lax.axis_index(axis)
        self.rows = own_ref.shape[0]
        self.piece = self.rows // 2

    def part(self, mask, half):
        start = flip(self.place, mask) * self.rows + half * self.piece
        return self.all_ref.at[pl.ds(pl.multiple_of(start, self.piece), self.piece), :]

    def copy(self, mask, half, toward):
        source = self.part(mask, half) if mask else self.own_ref.at[pl.ds(half * self.piece, self.piece), :]
        return pltpu.make_async_remote_copy(
            source, self.part(mask, half),
            self.send_sem.at[toward * 2 + half, mask // 2], self.recv_sem.at[(mask ^ toward) * 2 + half],
            device_id={self.axis: flip(self.place, toward)}, device_id_type=MESH,
        )

    def wait(self, mask, half):
        pltpu.make_async_remote_copy(
            self.part(mask, half), self.part(mask, half), self.send_sem.at[0, 0], self.recv_sem.at[mask * 2 + half],
            device_id={self.axis: flip(self.place, 1)}, device_id_type=MESH,
        ).wait_recv()

    def own(self):
        start = pl.multiple_of(self.place * self.rows, self.rows)
        return pltpu.make_async_copy(self.own_ref, self.all_ref.at[pl.ds(start, self.rows), :], self.own_sem)

    def first(self):
        cube_barrier(self.axis, self.place)
        for move in self.FIRST:
            self.copy(*move).start()
        self.own().start()

    def second(self):
        self.wait(2, 0)
        self.copy(*self.SECOND[0]).start()
        self.wait(4, 1)
        for move in self.SECOND[1:]:
            self.copy(*move).start()

    def third(self):
        for move in self.THIRD:
            self.wait(*move[:2])
            self.copy(*move).start()

    def fourth(self):
        for move in self.FOURTH:
            self.wait(*move[:2])
            self.copy(*move).start()

    def last(self):
        for mask in (1, 3, 5, 7):
            for half in range(2):
                self.wait(mask, half)
        self.own().wait()
        for move in self.FIRST + self.SECOND + self.THIRD + self.FOURTH:
            self.copy(*move).wait_send()


CUBE_SEMAPHORES = [pltpu.SemaphoreType.DMA, pltpu.SemaphoreType.DMA((10, 4)), pltpu.SemaphoreType.DMA((16,))]


def cube_gather_kernel(axis, own_ref, all_ref, *semaphores):
    gather = CubeGather(axis, own_ref, all_ref, *semaphores)
    gather.first()
    gather.second()
    gather.third()
    gather.fourth()
    gather.last()


def cube_gather(own, axis, collective_id):
    if lax.axis_size(axis) != 8:
        return lax.all_gather(own, axis, axis=0, tiled=True)
    rows, width = own.shape
    return pl.pallas_call(
        functools.partial(cube_gather_kernel, axis),
        in_specs=[ANYWHERE],
        out_specs=ANYWHERE,
        out_shape=struct((8 * rows, width), own.dtype),
        scratch_shapes=CUBE_SEMAPHORES,
        compiler_params=pltpu.CompilerParams(
            collective_id=collective_id, has_side_effects=True, vmem_limit_bytes=VMEM_LIMIT
        ),
        name="cube_gather",
    )(own)


def feed_grads_kernel(
    axis, cube,
    own_ref, blocks_ref, grads_ref, w_down_ref, hidden_ref, grad_gate_ref, grad_up_ref,
    *refs,
):
    outs = refs[: 5 if cube else 4]
    down_ref, gate_ref, up_ref, part_ref = outs[:4]
    step = pl.program_id(0)
    steps = pl.num_programs(0)
    if cube:
        gather = CubeGather(axis, own_ref, outs[4], *refs[5:])
        for at, phase in ((0, gather.first), (2, gather.second), (4, gather.third), (6, gather.fourth)):
            @pl.when(step == at)
            def _():
                phase()

    gate_ref[...] = dot_tn(blocks_ref[...], grad_gate_ref[...]).astype(bf16)
    up_ref[...] = dot_tn(blocks_ref[...], grad_up_ref[...]).astype(bf16)
    down_ref[...] = dot_tn(hidden_ref[...], grads_ref[...]).astype(bf16)
    part_ref[...] = dot(hidden_ref[...], w_down_ref[...]).astype(bf16)
    if cube:
        @pl.when(step == steps - 1)
        def _():
            gather.last()


def feed_grads(own, blocks, grads, w_down, hidden, grad_gate, grad_up, axis, collective_id):
    cube = lax.axis_size(axis) == 8
    rows, width = blocks.shape
    units = hidden.shape[1]
    tall = pl.BlockSpec((rows, BLOCK), lambda step: (0, step))
    down = pl.BlockSpec((units, BLOCK), lambda step: (0, step))
    flat = pl.BlockSpec((BLOCK, units), lambda step: (step, 0))
    held = pl.BlockSpec((rows, units), lambda step: (0, 0), pipeline_mode=pl.Buffered(1))
    *results, gathered = pl.pallas_call(
        functools.partial(feed_grads_kernel, axis, cube),
        grid=(width // BLOCK,),
        in_specs=[ANYWHERE, tall, tall, down, held, held, held],
        out_specs=[down, flat, flat, tall] + [ANYWHERE] * cube,
        out_shape=[
            struct((units, width), bf16), struct((width, units), bf16), struct((width, units), bf16),
            struct((rows, width), bf16),
        ] + [struct((8 * own.shape[0], width), bf16)] * cube,
        scratch_shapes=CUBE_SEMAPHORES if cube else [],
        compiler_params=params(collective_id if cube else None),
        name="feed_grads",
    )(own, blocks, grads, w_down, hidden, grad_gate, grad_up)
    if not cube:
        results, gathered = [*results, gathered], lax.all_gather(own, axis, axis=0, tiled=True)
    return (*results, gathered)


def cube_sum_kernel(axis, part_ref, total_ref, held, arrived, send_sem, recv_sem):
    place = lax.axis_index(axis)
    cube_barrier(axis, place)
    held[0] = part_ref[...]
    for stage, mask in enumerate((1, 2, 4)):
        copy = pltpu.make_async_remote_copy(
            held.at[stage], arrived.at[stage], send_sem.at[stage], recv_sem.at[stage],
            device_id={axis: flip(place, mask)}, device_id_type=MESH,
        )
        copy.start()
        copy.wait()
        if stage < 2:
            held[stage + 1] = held[stage] + arrived[stage]
        else:
            total_ref[...] = held[stage] + arrived[stage]


def cube_sum(part, axis, collective_id):
    if lax.axis_size(axis) != 8:
        return lax.psum(part, axis)
    vmem = pl.BlockSpec(memory_space=pltpu.VMEM)
    return pl.pallas_call(
        functools.partial(cube_sum_kernel, axis),
        in_specs=[vmem],
        out_specs=vmem,
        out_shape=struct(part.shape, f32),
        scratch_shapes=[
            pltpu.VMEM((3,) + part.shape, f32), pltpu.VMEM((3,) + part.shape, f32),
            pltpu.SemaphoreType.DMA((3,)), pltpu.SemaphoreType.DMA((3,)),
        ],
        compiler_params=pltpu.CompilerParams(collective_id=collective_id, has_side_effects=True),
        name="cube_sum",
    )(part)


def cube_scatter_kernel(axis, rows, parts_ref, total_ref, other, leaving, coming, send_sem, recv_sem):
    place = lax.axis_index(axis)
    piece = rows // 2

    def span(mask, half):
        return pl.ds(pl.multiple_of(flip(place, mask) * rows + half * piece, piece), piece)

    def slot(index, half):
        return pl.ds((2 * index + half) * piece, piece)

    def core_copy(mask, half):
        return pltpu.make_async_remote_copy(
            parts_ref.at[span(mask, half), :], other.at[slot(mask // 2, half), :],
            send_sem.at[0, mask // 2, half], recv_sem.at[0, mask // 2, half],
            device_id={axis: flip(place, 1)}, device_id_type=MESH,
        )

    def chip_copy(index, half, toward):
        landing = (toward // 2 - 1) * 2 + (1 if index else 0)
        return pltpu.make_async_remote_copy(
            leaving.at[slot(index, half), :], coming.at[slot(landing, half), :],
            send_sem.at[toward // 2, index, half], recv_sem.at[toward // 2, 1 if index else 0, half],
            device_id={axis: flip(place, toward)}, device_id_type=MESH,
        )

    cube_barrier(axis, place)
    for mask in (7, 3, 5, 1):
        for half in range(2):
            core_copy(mask, half).start()

    def chip_part(mask, half):
        core_copy(mask + 1, half).wait_recv()
        return parts_ref[span(mask, half), :].astype(f32) + other[slot(mask // 2, half), :].astype(f32)

    def arrived(index, half, toward):
        chip_copy(index, half, toward).wait_recv()
        landing = (toward // 2 - 1) * 2 + (1 if index else 0)
        return coming[slot(landing, half), :].astype(f32)

    leaving[slot(0, 0), :] = chip_part(6, 0).astype(bf16)
    chip_copy(0, 0, 2).start()
    leaving[slot(0, 1), :] = chip_part(6, 1).astype(bf16)
    chip_copy(0, 1, 4).start()
    leaving[slot(1, 0), :] = chip_part(2, 0).astype(bf16)
    chip_copy(1, 0, 2).start()
    leaving[slot(2, 1), :] = chip_part(4, 1).astype(bf16)
    chip_copy(2, 1, 4).start()
    by_x = chip_part(2, 1)
    leaving[slot(1, 1), :] = (by_x + arrived(0, 1, 4)).astype(bf16)
    chip_copy(1, 1, 2).start()
    by_y = chip_part(4, 0)
    leaving[slot(2, 0), :] = (by_y + arrived(0, 0, 2)).astype(bf16)
    chip_copy(2, 0, 4).start()
    for half in range(2):
        total_ref[half * piece : (half + 1) * piece, :] = chip_part(0, half)
    for half in (0, 1):
        at = slice(half * piece, (half + 1) * piece)
        if half == 0:
            total_ref[at, :] += arrived(1, 0, 2)
            total_ref[at, :] += arrived(2, 0, 4)
        else:
            total_ref[at, :] += arrived(2, 1, 4)
            total_ref[at, :] += arrived(1, 1, 2)
    for mask in (7, 3, 5, 1):
        for half in range(2):
            core_copy(mask, half).wait_send()
    for index, half, toward in ((0, 0, 2), (0, 1, 4), (1, 0, 2), (2, 1, 4), (1, 1, 2), (2, 0, 4)):
        chip_copy(index, half, toward).wait_send()


def cube_scatter(parts, axis, collective_id):
    if lax.axis_size(axis) != 8:
        return lax.psum_scatter(parts, axis, scatter_dimension=0, tiled=True).astype(f32)
    rows, width = parts.shape[0] // 8, parts.shape[1]
    vmem = pl.BlockSpec(memory_space=pltpu.VMEM)
    return pl.pallas_call(
        functools.partial(cube_scatter_kernel, axis, rows),
        in_specs=[vmem],
        out_specs=vmem,
        out_shape=struct((rows, width), f32),
        scratch_shapes=[
            pltpu.VMEM((4 * rows, width), bf16), pltpu.VMEM((3 * rows, width), bf16),
            pltpu.VMEM((4 * rows, width), bf16),
            pltpu.SemaphoreType.DMA((3, 4, 2)), pltpu.SemaphoreType.DMA((3, 4, 2)),
        ],
        compiler_params=pltpu.CompilerParams(
            collective_id=collective_id, has_side_effects=True, vmem_limit_bytes=VMEM_LIMIT
        ),
        name="cube_scatter",
    )(parts)


def params(collective_id=None):
    return pltpu.CompilerParams(
        dimension_semantics=("arbitrary",),
        vmem_limit_bytes=VMEM_LIMIT,
        collective_id=collective_id,
        has_side_effects=collective_id is not None,
    )


def struct(shape, dtype):
    return jax.ShapeDtypeStruct(tuple(shape), dtype)


def from_earlier(array, axis):
    devices = lax.axis_size(axis)
    parts = [
        lax.ppermute(array, axis, [(i, i + by) for i in range(devices - by)])
        for by in range(devices - 1, 0, -1)
    ]
    return jnp.stack(parts) if parts else jnp.zeros((1,) + array.shape, array.dtype)


def from_later(array, axis):
    devices = lax.axis_size(axis)
    parts = [
        lax.ppermute(array, axis, [(i + by, i) for i in range(devices - by)])
        for by in range(devices - 1, 0, -1)
    ]
    return jnp.stack(parts) if parts else jnp.zeros((1,) + array.shape, array.dtype)


def shards(
    inputs,
    doc_lengths,
    first_gain,
    w_query,
    w_key,
    w_value,
    w_outgate,
    w_decay,
    w_beta,
    conv_query,
    conv_key,
    conv_value,
    decay_log,
    decay_bias,
    head_gain,
    w_output,
    second_gain,
    w_gate,
    w_up,
    w_down,
    cotangent,
):
    row_count, model_width = inputs.shape
    heads = decay_log.shape[0]
    qw, vw = w_query.shape[1], w_value.shape[1]
    key_width, value_width = qw // heads, vw // heads
    mixed_width = 2 * qw + vw
    taps = conv_query.shape[0]
    docs = doc_lengths.shape[0]
    seq_index = lax.axis_index("seq")
    head_index = lax.axis_index("head")
    head_total = lax.axis_size("head")
    seq_rows = row_count * head_total
    chunks = seq_rows // BLOCK
    others = max(lax.axis_size("seq") - 1, 1)
    sizes = (heads, key_width, value_width, docs)

    inputs_f = inputs.astype(f32)
    normed = rms_scale(inputs_f, first_gain).astype(bf16)
    block_rows = cube_gather(normed, "head", 4)
    tail = from_previous(block_rows[seq_rows - 2 * HALO :])
    meta = jnp.concatenate(
        [(seq_index * seq_rows).astype(jnp.int32)[None], slot_starts(doc_lengths)]
    )
    _, own_valid = layout(doc_lengths, (seq_index * head_total + head_index) * row_count, row_count)

    grad_out = cotangent.astype(f32) * own_valid.astype(f32)[:, None]
    grad_low = grad_out.astype(bf16)
    w_small = jnp.concatenate([w_decay, w_beta, jnp.zeros((model_width, LANES - 2 * heads), bf16)], axis=1)
    weights = (w_query, w_key, w_value, w_outgate, w_small)
    all_width = mixed_width + vw + LANES
    conv_all = jnp.concatenate([conv_query, conv_key, conv_value], axis=1)
    dvec = jnp.zeros((8, LANES), f32)
    dvec = dvec.at[0, :heads].set(decay_bias).at[1, :heads].set(-jnp.exp(decay_log))
    map_shape = (heads, key_width, key_width + value_width)

    (pre, conv, gate, small, scal, qkv, inverse, w_part, u_part, starts, drop, block_map, grad_block_two) = pl.pallas_call(
        functools.partial(forward_kernel, *sizes, taps, chunks),
        grid=(chunks,),
        in_specs=[
            SCALARS, by_rows(model_width), whole((2 * HALO, model_width)),
            *(whole(weight.shape) for weight in weights), whole(conv_all.shape), whole(dvec.shape), ANYWHERE,
        ],
        out_specs=[
            by_rows(mixed_width), by_rows(mixed_width), by_rows(vw), by_rows(LANES), by_rows(LANES),
            by_rows(mixed_width),
            by_chunk((heads, BLOCK, BLOCK)), by_chunk((heads, BLOCK, key_width)),
            by_chunk((heads, BLOCK, value_width)), by_chunk(map_shape),
            by_chunk((heads, key_width, key_width)), whole(map_shape), ANYWHERE,
        ],
        out_shape=[
            struct((seq_rows, mixed_width), f32), struct((seq_rows, mixed_width), f32),
            struct((seq_rows, vw), f32), struct((seq_rows, LANES), f32), struct((seq_rows, LANES), f32),
            struct((seq_rows, mixed_width), bf16),
            struct((chunks, heads, BLOCK, BLOCK), bf16), struct((chunks, heads, BLOCK, key_width), bf16),
            struct((chunks, heads, BLOCK, value_width), f32), struct((chunks,) + map_shape, f32),
            struct((chunks, heads, key_width, key_width), f32), struct(map_shape, f32),
            struct((lax.axis_size("seq") * row_count, model_width), bf16),
        ],
        scratch_shapes=[
            pltpu.VMEM((BLOCK + HALO, mixed_width), f32), pltpu.VMEM(map_shape, f32), pltpu.SemaphoreType.DMA,
            pltpu.SemaphoreType.DMA((2 * lax.axis_size("seq"),)), pltpu.SemaphoreType.DMA((2 * lax.axis_size("seq"),)),
        ],
        compiler_params=params(2),
        name="mixer_forward",
    )(meta, block_rows, tail, *weights, conv_all, dvec, grad_low)

    earlier = from_earlier(block_map.astype(bf16), "seq")
    gain_row = head_gain[None, :]
    core, gated, mixed_part, fresh, states = pl.pallas_call(
        functools.partial(output_kernel, *sizes, others),
        grid=(chunks,),
        in_specs=[
            SCALARS, whole(earlier.shape), by_chunk(map_shape), by_chunk((heads, BLOCK, key_width)),
            by_chunk((heads, BLOCK, value_width)), by_rows(mixed_width), by_rows(LANES), by_rows(vw),
            whole(gain_row.shape), whole(w_output.shape),
        ],
        out_specs=[
            by_rows(vw), by_rows(vw), by_rows(model_width), by_chunk((heads, BLOCK, value_width)),
            by_chunk((heads, key_width, value_width)),
        ],
        out_shape=[
            struct((seq_rows, vw), f32), struct((seq_rows, vw), bf16), struct((seq_rows, model_width), bf16),
            struct((chunks, heads, BLOCK, value_width), bf16),
            struct((chunks, heads, key_width, value_width), f32),
        ],
        scratch_shapes=[pltpu.VMEM((heads, key_width, value_width), f32)],
        compiler_params=params(),
        name="mixer_output",
    )(meta, earlier, starts, w_part, u_part, qkv, scal, gate, gain_row, w_output)

    mixer_out = cube_scatter(mixed_part, "head", 5)
    hidden_in = inputs_f + mixer_out
    normed_two = rms_scale(hidden_in, second_gain).astype(bf16)
    grad_hidden = dot_nt(grad_block_two, w_down)
    mlp_block, hidden, grad_gate, grad_up, grad_normed_two = feed(
        normed_two, grad_hidden, w_gate, w_up, "seq", 3
    )
    grad_hidden_norm, grad_second = rms_back(hidden_in, second_gain, grad_normed_two)
    grad_hidden_in = grad_out + grad_hidden_norm
    grad_mix = grad_hidden_in.astype(bf16)
    *ff_grads, mlp_part, grad_block = feed_grads(
        grad_mix, mlp_block, grad_block_two, w_down, hidden, grad_gate, grad_up, "head", 6
    )
    grad_core, inner, pull, grad_gate_pre, grad_head, pulled = pl.pallas_call(
        functools.partial(core_grad_kernel, *sizes, chunks),
        grid=(chunks,),
        in_specs=[
            SCALARS, by_rows(model_width, chunks), whole(w_output.shape), by_rows(vw, chunks), by_rows(vw, chunks),
            whole(gain_row.shape), by_rows(mixed_width, chunks), by_rows(LANES, chunks),
            by_chunk((heads, BLOCK, key_width), chunks), by_chunk((heads, key_width, key_width), chunks),
        ],
        out_specs=[
            by_chunk((heads, BLOCK, value_width), chunks), by_chunk((heads, BLOCK, value_width), chunks),
            by_chunk((heads, key_width, value_width), chunks), by_rows(vw, chunks),
            whole((8, value_width)), whole((heads, key_width, value_width)),
        ],
        out_shape=[
            struct((chunks, heads, BLOCK, value_width), bf16), struct((chunks, heads, BLOCK, value_width), f32),
            struct((chunks, heads, key_width, value_width), f32), struct((seq_rows, vw), bf16),
            struct((8, value_width), f32), struct((heads, key_width, value_width), f32),
        ],
        compiler_params=params(),
        name="mixer_core_grad",
    )(meta, grad_block, w_output, core, gate, gain_row, qkv, scal, w_part, drop)
    grad_w_output = dot_tn(gated, grad_block).astype(bf16)

    later = from_later(
        jnp.concatenate([block_map[:, :, :key_width], pulled], axis=2).astype(bf16), "seq"
    )
    mlp_part, later = lax.optimization_barrier((mlp_part, later))
    mlp_out = lax.psum_scatter(mlp_part, "seq", scatter_dimension=0, tiled=True)
    grad_conv, grad_small, sums = pl.pallas_call(
        functools.partial(backward_kernel, *sizes, chunks, others),
        grid=(chunks,),
        in_specs=[
            SCALARS, whole(later.shape), by_rows(mixed_width, chunks), by_rows(mixed_width, chunks),
            by_rows(LANES, chunks), by_rows(LANES, chunks), by_chunk((heads, BLOCK, BLOCK), chunks),
            by_chunk((heads, BLOCK, value_width), chunks), by_chunk((heads, key_width, value_width), chunks),
            by_chunk((heads, BLOCK, value_width), chunks), by_chunk((heads, BLOCK, value_width), chunks),
            by_chunk((heads, key_width, value_width), chunks), by_chunk((heads, key_width, key_width), chunks),
            whole(dvec.shape),
        ],
        out_specs=[by_rows(mixed_width, chunks), by_rows(LANES, chunks), whole((8, LANES))],
        out_shape=[
            struct((seq_rows, mixed_width), f32), struct((seq_rows, LANES), bf16), struct((8, LANES), f32),
        ],
        scratch_shapes=[pltpu.VMEM((heads, key_width, value_width), f32)],
        compiler_params=params(),
        name="mixer_backward",
    )(meta, later, qkv, conv, scal, small, inverse, fresh, states, grad_core, inner, pull, drop, dvec)

    edge = from_next(grad_conv[:HALO])
    step_rows = BLOCK // HALO
    last_halo = seq_rows // HALO - 1
    grad_pre, grad_taps, grad_rows, gain_sum = pl.pallas_call(
        functools.partial(projection_grad_kernel, mixed_width, docs, chunks, taps),
        grid=(chunks,),
        in_specs=[
            SCALARS, by_rows(mixed_width),
            pl.BlockSpec(
                (HALO, mixed_width), lambda step: (jnp.minimum((step + 1) * step_rows, last_halo), 0)
            ),
            whole(edge.shape), by_rows(mixed_width), by_rows(vw), by_rows(LANES),
            whole(conv_all.shape), by_rows(model_width), *(whole(weight.shape) for weight in weights),
        ],
        out_specs=[by_rows(all_width), whole((8, mixed_width)), by_rows(model_width), whole((8, model_width))],
        out_shape=[
            struct((seq_rows, all_width), bf16), struct((8, mixed_width), f32),
            struct((seq_rows, model_width), bf16), struct((8, model_width), f32),
        ],
        scratch_shapes=[pltpu.VMEM((BLOCK + HALO, mixed_width), f32)],
        compiler_params=params(),
        name="projection_grad",
    )(meta, grad_conv, grad_conv, edge, pre, grad_gate_pre, grad_small, conv_all, block_rows, *weights)

    grad_normed = lax.psum_scatter(grad_rows, "head", scatter_dimension=0, tiled=True).astype(f32)
    grad_input_norm, _ = rms_back(inputs_f, first_gain, grad_normed)
    grad_inputs = grad_hidden_in + grad_input_norm
    grad_w_all = dot_tn(block_rows, grad_pre).astype(bf16)

    gains = cube_sum(
        jnp.concatenate([gain_sum[0] / first_gain, grad_second, grad_head[0]]).reshape(2, -1).repeat(4, axis=0),
        "head",
        7,
    )
    mlp_out, *ff_grads = lax.optimization_barrier((mlp_out, *ff_grads))
    ff_grads = [lax.psum(part, "head") for part in ff_grads]
    grad_w_all, grad_w_output, small_sums, gains = line_sum(
        (
            grad_w_all,
            grad_w_output,
            jnp.pad(
                jnp.concatenate([grad_taps, sums], axis=1), ((0, 24), (0, all_width - mixed_width - LANES))
            ).astype(bf16),
            jnp.pad(gains, ((0, 24), (0, 0))).astype(bf16),
        ),
        (32, 16, 16, 16),
        "seq",
        1,
    )
    gains = jnp.concatenate([gains[0], gains[4]]).astype(f32)
    first_part, second_part = gains[:model_width], gains[model_width : 2 * model_width]
    head_part = gains[2 * model_width :]
    grad_w_all, *ff_grads = lax.optimization_barrier((grad_w_all, *ff_grads))
    grad_w_down, grad_w_gate, grad_w_up = (part.astype(f32) for part in ff_grads)
    grad_w_all = grad_w_all.astype(f32)
    grad_w_output = grad_w_output.astype(f32)
    grad_taps = small_sums[:taps, :mixed_width].astype(f32)
    sums = small_sums[:2, mixed_width : mixed_width + heads].astype(f32)
    output = (hidden_in + mlp_out.astype(f32)).astype(bf16)
    gate_at = mixed_width
    small_at = mixed_width + vw
    return (
        output,
        grad_inputs,
        first_part,
        grad_w_all[:, :qw],
        grad_w_all[:, qw : 2 * qw],
        grad_w_all[:, 2 * qw : gate_at],
        grad_w_all[:, gate_at:small_at],
        grad_w_all[:, small_at : small_at + heads],
        grad_w_all[:, small_at + heads : small_at + 2 * heads],
        grad_taps[:, :qw],
        grad_taps[:, qw : 2 * qw],
        grad_taps[:, 2 * qw :],
        sums[1],
        sums[0],
        head_part,
        grad_w_output,
        second_part,
        grad_w_gate,
        grad_w_up,
        grad_w_down,
    )


def from_previous(array):
    devices = lax.axis_size("seq")
    return lax.ppermute(array, "seq", [(i, i + 1) for i in range(devices - 1)])


def from_next(array):
    devices = lax.axis_size("seq")
    return lax.ppermute(array, "seq", [(i + 1, i) for i in range(devices - 1)])


def solution(mesh):
    in_specs = (
        P(("seq", "head"), None),
        P(),
        P(),
        P(None, "head"),
        P(None, "head"),
        P(None, "head"),
        P(None, "head"),
        P(None, "head"),
        P(None, "head"),
        P(None, "head"),
        P(None, "head"),
        P(None, "head"),
        P("head"),
        P("head"),
        P(),
        P("head", None),
        P(),
        P(None, "seq"),
        P(None, "seq"),
        P("seq", None),
        P(("seq", "head"), None),
    )
    out_specs = (
        P(("seq", "head"), None),
        P(("seq", "head"), None),
        P(),
        P(None, "head"),
        P(None, "head"),
        P(None, "head"),
        P(None, "head"),
        P(None, "head"),
        P(None, "head"),
        P(None, "head"),
        P(None, "head"),
        P(None, "head"),
        P("head"),
        P("head"),
        P(),
        P("head", None),
        P(),
        P(None, "seq"),
        P(None, "seq"),
        P("seq", None),
    )
    return jax.shard_map(shards, mesh=mesh, in_specs=in_specs, out_specs=out_specs, check_vma=False)
```

```python
import functools

import jax
import jax.numpy as jnp
from jax import lax
from jax.experimental import pallas as pl
from jax.experimental.pallas import tpu as pltpu
from jax.sharding import PartitionSpec as P

GROUP = 64
BLOCK = 256
LANES = 128
HALO = 8

epsilon = 1e-06
f32 = jnp.float32
bf16 = jnp.bfloat16
VMEM_LIMIT = 56 * 1024 * 1024


def dot(left, right):
    return jnp.dot(left, right, preferred_element_type=f32)


def dot_tn(left, right):
    return lax.dot_general(left, right, (((0,), (0,)), ((), ())), preferred_element_type=f32)


def dot_nt(left, right):
    return lax.dot_general(left, right, (((1,), (1,)), ((), ())), preferred_element_type=f32)


def halves(values):
    top = values.astype(bf16)
    return top, (values - top.astype(f32)).astype(bf16)


def exact_left(left, right):
    top = right.astype(bf16)
    rest = right - top.astype(f32)
    middle = rest.astype(bf16)
    low = (rest - middle.astype(f32)).astype(bf16)
    return dot(left, top) + dot(left, middle) + dot(left, low)


def dot_fine(left, right):
    left_top, left_low = halves(left)
    right_top, right_low = halves(right)
    return dot(left_top, right_top) + (dot(left_top, right_low) + dot(left_low, right_top))


def sigmoid(values):
    return jax.nn.sigmoid(values)


def silu_slope(values):
    sigma = sigmoid(values)
    return sigma * (1.0 + values * (1.0 - sigma))


def softplus(values):
    return jnp.maximum(values, 0.0) + jnp.log1p(jnp.exp(-jnp.abs(values)))


def slot_starts(doc_lengths):
    slot_sizes = (doc_lengths + (GROUP - 1)) // GROUP * GROUP
    return jnp.cumsum(slot_sizes, dtype=jnp.int32) - slot_sizes


def layout(doc_lengths, first_row, row_total):
    starts = slot_starts(doc_lengths)
    places = first_row + jnp.arange(row_total, dtype=jnp.int32)
    owners = jnp.sum(
        (places[:, None] >= starts[None, 1:]).astype(jnp.int32), axis=1, dtype=jnp.int32
    )
    picked = (owners[:, None] == jnp.arange(doc_lengths.shape[0], dtype=jnp.int32)[None, :]).astype(
        jnp.int32
    )
    begins = jnp.sum(picked * starts[None, :], axis=1, dtype=jnp.int32)
    length = jnp.sum(picked * doc_lengths[None, :], axis=1, dtype=jnp.int32)
    offset = places - begins
    return (offset, offset < length)


def rms_scale(values, gain):
    return values * lax.rsqrt(jnp.mean(values * values, axis=-1, keepdims=True) + epsilon) * gain


def rms_back(values, gain, grad_in):
    scale = lax.rsqrt(jnp.mean(values * values, axis=-1, keepdims=True) + epsilon)
    weighted = grad_in * gain
    grad_values = scale * weighted - values * scale**3 * jnp.mean(
        weighted * values, axis=-1, keepdims=True
    )
    grad_gain = jnp.sum((grad_in * values * scale).reshape(-1, values.shape[-1]), axis=0)
    return (grad_values, grad_gain)


def owner_of(meta, docs, places):
    total = jnp.zeros_like(places)
    for doc in range(1, docs):
        total = total + jnp.where(places >= meta[1 + doc], 1, 0)
    return total


def offset_of(meta, docs, places):
    begin = jnp.zeros_like(places)
    for doc in range(1, docs):
        begin = jnp.where(places >= meta[1 + doc], meta[1 + doc], begin)
    return places - begin


class Masks:
    def __init__(self, meta, docs, chunk):
        base = meta[0] + chunk * BLOCK
        rows = lax.broadcasted_iota(jnp.int32, (BLOCK, BLOCK), 0)
        cols = lax.broadcasted_iota(jnp.int32, (BLOCK, BLOCK), 1)
        same = owner_of(meta, docs, base + rows) == owner_of(meta, docs, base + cols)
        self.inclusive = same & (rows >= cols)
        self.strictly = same & (rows > cols)
        self.level = rows ^ cols
        self.lower = jnp.where(rows >= cols, 1.0, 0.0).astype(bf16)
        self.upper = jnp.where(rows <= cols, 1.0, 0.0).astype(bf16)
        self.eye = jnp.where(rows == cols, 1.0, 0.0)
        place = base + lax.broadcasted_iota(jnp.int32, (BLOCK, 1), 0)
        owner = owner_of(meta, docs, place)
        before = jnp.int32(0)
        last = jnp.int32(0)
        for doc in range(1, docs):
            before = before + jnp.where(base - 1 >= meta[1 + doc], 1, 0)
            last = last + jnp.where(base + BLOCK - 1 >= meta[1 + doc], 1, 0)
        self.enters = jnp.where(owner == before, 1.0, 0.0)
        self.leaves = jnp.where(owner == last, 1.0, 0.0)
        self.through = jnp.where(before == last, 1.0, 0.0).astype(f32)
        self.offset = offset_of(meta, docs, place)


def decays(masks, scal, scal_t, head):
    column = scal[:, head : head + 1]
    row = scal_t[head : head + 1, :]
    within = jnp.where(masks.inclusive, jnp.exp(jnp.minimum(column - row, 0.0)), 0.0)
    last = column[BLOCK - 1 : BLOCK, :]
    entry = jnp.exp(column) * masks.enters
    leave = jnp.exp(last - column) * masks.leaves
    through = jnp.exp(last) * masks.through
    return within, entry, leave, through


def unit_lower_inverses(systems):
    half = BLOCK // 2
    rows = lax.broadcasted_iota(jnp.int32, (half, half), 0)
    cols = lax.broadcasted_iota(jnp.int32, (half, half), 1)
    level = rows ^ cols
    eye = jnp.where(rows == cols, 1.0, 0.0)
    parts = [system[at : at + half, at : at + half] for system in systems for at in (0, half)]
    solved = [eye - jnp.where(level == 1, part, 0.0) for part in parts]
    width = 2
    while width < half:
        keep = (level >= width) & (level < 2 * width)
        low = [inverse.astype(bf16) for inverse in solved]
        moved = [dot(jnp.where(keep, part, 0.0).astype(bf16), inverse) for part, inverse in zip(parts, low)]
        solved = [
            whole_part - dot(inverse, part.astype(bf16))
            for whole_part, inverse, part in zip(solved, low, moved)
        ]
        width *= 2
    solved = [inverse.astype(bf16) for inverse in solved]
    results = []
    for index, system in enumerate(systems):
        upper, lower = solved[2 * index], solved[2 * index + 1]
        corner = -dot(lower, dot(system[half:, :half].astype(bf16), upper).astype(bf16))
        results.append((upper, corner.astype(bf16), lower))
    return results


LEAD = 2 * HALO
STRIDE = BLOCK + LEAD


def cube_order(axis, step):
    place = lax.axis_index(axis)
    chunk = 0
    for bit in (1, 2, 4):
        chunk = chunk + bit * ((place // bit + step // bit) % 2)
    return chunk


class EdgeRows:
    def __init__(self, line, axis, own_ref, rows_ref, edge_ref, line_sem, send_sem, recv_sem):
        self.line, self.axis = line, axis
        self.group, self.place = lax.axis_index(line), lax.axis_index(axis)
        self.groups, self.last = lax.axis_size(line), lax.axis_size(axis) - 1
        self.own_ref, self.rows_ref, self.edge_ref = own_ref, rows_ref, edge_ref
        self.line_sem, self.send_sem, self.recv_sem = line_sem, send_sem, recv_sem

    def enter(self):
        barrier = pltpu.get_barrier_semaphore()
        for mask in (1, 2, 4, 6):
            pl.semaphore_signal(barrier, inc=1, device_id={self.axis: flip(self.place, mask)}, device_id_type=MESH)

        @pl.when(self.receives())
        def _():
            pl.semaphore_signal(barrier, inc=1, device_id={self.line: self.group - 1}, device_id_type=MESH)

        @pl.when(self.hands_on())
        def _():
            pl.semaphore_wait(barrier, 5)

        @pl.when(jnp.logical_not(self.hands_on()))
        def _():
            pl.semaphore_wait(barrier, 4)

    def hands_on(self):
        return (self.place == self.last) & (self.group < self.groups - 1)

    def receives(self):
        return (self.place == self.last) & (self.group > 0)

    def landing(self, mask):
        block = lax.rem(flip(self.place, mask) + 1, self.last + 1)
        return self.rows_ref.at[pl.ds(pl.multiple_of(block * STRIDE, LEAD), LEAD), :]

    def onward(self):
        return pltpu.make_async_remote_copy(
            self.own_ref.at[pl.ds(BLOCK - LEAD, LEAD), :], self.edge_ref, self.line_sem.at[0], self.line_sem.at[1],
            device_id={self.line: self.group + 1}, device_id_type=MESH,
        )

    def copy(self, mask, toward):
        return pltpu.make_async_remote_copy(
            self.landing(mask) if mask else self.edge_ref, self.landing(mask),
            self.send_sem.at[mask + toward if mask else toward], self.recv_sem.at[mask ^ toward],
            device_id={self.axis: flip(self.place, toward)}, device_id_type=MESH,
        )

    def wait(self, mask):
        pltpu.make_async_remote_copy(
            self.landing(mask), self.landing(mask), self.send_sem.at[0], self.recv_sem.at[mask],
            device_id={self.axis: flip(self.place, 1)}, device_id_type=MESH,
        ).wait_recv()

    def start(self):
        @pl.when(self.hands_on())
        def _():
            self.onward().start()

        @pl.when(self.place < self.last)
        def _():
            self.edge_ref[...] = self.own_ref[BLOCK - LEAD :, :]

        @pl.when((self.place == self.last) & (self.group == 0))
        def _():
            self.edge_ref[...] = jnp.zeros(self.edge_ref.shape, bf16)

        @pl.when(self.receives())
        def _():
            pltpu.make_async_remote_copy(
                self.edge_ref, self.edge_ref, self.line_sem.at[0], self.line_sem.at[1],
                device_id={self.line: self.group - 1}, device_id_type=MESH,
            ).wait_recv()

        for toward in (6, 2, 4, 1):
            self.copy(0, toward).start()
        self.landing(0)[...] = self.edge_ref[...]

    def spread(self):
        for mask in (2, 4, 6):
            self.wait(mask)
            self.copy(mask, 1).start()
        for mask in (1, 3, 5, 7):
            self.wait(mask)

    def end(self):
        @pl.when(self.hands_on())
        def _():
            self.onward().wait_send()

        for toward in (6, 2, 4, 1):
            self.copy(0, toward).wait_send()
        for mask in (2, 4, 6):
            self.copy(mask, 1).wait_send()


def forward_kernel(
    heads, key_width, value_width, docs, taps, chunks, cube,
    meta, rows_ref, wq_ref, wk_ref, wv_ref, wg_ref, ws_ref, conv_ref, dvec_ref,
    pre_ref, act_ref, gate_ref, small_ref, scal_ref, qkv_ref, inv_ref, w_out_ref, u_ref, drop_ref,
    starts_ref, map_ref, *refs,
):
    step = pl.program_id(0)
    ext, state, drops, adds, throughs = refs[cube : cube + 5]
    if cube:
        all_ref = refs[0]
        held, copy_sem, edge_ref, line_sem, edge_send, edge_recv, cube_send, cube_recv = refs[6:]
        chunk = cube_order("head", step)
        rows_in = CubeGather("head", rows_ref, held, None, cube_send, cube_recv, STRIDE, LEAD)
        edges = EdgeRows("seq", "head", rows_ref, held, edge_ref, line_sem, edge_send, edge_recv)

        def kept(block):
            start = pl.multiple_of(block * STRIDE + LEAD, LEAD)
            return pltpu.make_async_copy(
                held.at[pl.ds(start, BLOCK), :],
                all_ref.at[pl.ds(pl.multiple_of(block * BLOCK, BLOCK), BLOCK), :],
                copy_sem.at[block],
            )

        @pl.when(step == 0)
        def _():
            edges.enter()
            edges.start()
            rows_in.first()
            held[pl.ds(pl.multiple_of(chunk * STRIDE + LEAD, LEAD), BLOCK), :] = rows_ref[...]

        @pl.when(step == 2)
        def _():
            rows_in.second()
            rows_in.third()

        @pl.when(step == 4)
        def _():
            rows_in.fourth()

        for odd in (1, 3, 5, 7):
            @pl.when(step == odd)
            def _():
                for half in range(2):
                    rows_in.wait(odd, half)

        kept(chunk).start()
        rows = held[pl.ds(pl.multiple_of(chunk * STRIDE + LEAD, LEAD), BLOCK), :]
    else:
        chunk = step
        rows = rows_ref[LEAD:, :]

    qw, vw = heads * key_width, heads * value_width
    mixed = 2 * qw + vw
    masks = Masks(meta, docs, chunk)
    gate_ref[...] = dot(rows, wg_ref[...])
    small = dot(rows, ws_ref[...])
    small_ref[...] = small
    if cube:
        @pl.when(step == 0)
        def _():
            edges.spread()

        rows_ext = held[pl.ds(pl.multiple_of(chunk * STRIDE, LEAD), STRIDE), :]
    else:
        rows_ext = rows_ref[...]
    for span, ref in ((slice(0, qw), wq_ref), (slice(qw, 2 * qw), wk_ref), (slice(2 * qw, mixed), wv_ref)):
        pre = dot(rows_ext, ref[...])
        ext[:, span] = pre
        pre_ref[:, span] = pre[LEAD:, :]

    conv = jnp.zeros((BLOCK, mixed), f32)
    for lag in range(taps):
        keep = jnp.where(masks.offset >= lag, 1.0, 0.0)
        conv = conv + conv_ref[lag : lag + 1, :] * (ext[LEAD - lag : LEAD - lag + BLOCK, :] * keep)
    act_ref[...] = conv
    act = conv * sigmoid(conv)

    lane = lax.broadcasted_iota(jnp.int32, (BLOCK, LANES), 1)
    decay = dvec_ref[1:2, :] * softplus(small + dvec_ref[0:1, :])
    cumul = exact_left(masks.lower, decay)
    scal = jnp.where(lane < heads, cumul, sigmoid(small))
    scal_ref[...] = scal
    scal_t = scal.T

    held_heads = []
    for head in range(heads):
        act_q = act[:, head * key_width : (head + 1) * key_width]
        act_k = act[:, qw + head * key_width : qw + (head + 1) * key_width]
        value = act[:, 2 * qw + head * value_width : 2 * qw + (head + 1) * value_width].astype(bf16)
        norm_q = lax.rsqrt(jnp.sum(act_q * act_q, axis=1, keepdims=True) + epsilon)
        norm_k = lax.rsqrt(jnp.sum(act_k * act_k, axis=1, keepdims=True) + epsilon)
        query = (act_q * norm_q * key_width ** (-0.5)).astype(bf16)
        key = (act_k * norm_k).astype(bf16)
        qkv_ref[:, head * key_width : (head + 1) * key_width] = query
        qkv_ref[:, qw + head * key_width : qw + (head + 1) * key_width] = key
        qkv_ref[:, 2 * qw + head * value_width : 2 * qw + (head + 1) * value_width] = value
        within, entry, leave, through = decays(masks, scal, scal_t, head)
        beta = scal[:, heads + head : heads + head + 1]
        system = jnp.where(masks.strictly, beta * dot_nt(key, key) * within, 0.0)
        held_heads.append((system, key, value, beta, entry, leave, through))

    half = BLOCK // 2
    inverses = unit_lower_inverses([part[0] for part in held_heads])
    for head, (upper, corner, lower) in enumerate(inverses):
        inv_ref[0, head, :half, :half] = upper
        inv_ref[0, head, :half, half:] = jnp.zeros((half, half), bf16)
        inv_ref[0, head, half:, :half] = corner
        inv_ref[0, head, half:, half:] = lower
    for head, (_, key, value, beta, entry, leave, through) in enumerate(held_heads):
        inverse = inv_ref[0, head]
        key_f = key.astype(f32)
        w_part = dot(inverse, (beta * entry * key_f).astype(bf16)).astype(bf16)
        u_part = dot(inverse, (beta * value.astype(f32)).astype(bf16))
        w_out_ref[0, head] = w_part
        u_ref[0, head] = u_part
        tail_key = (leave * key_f).astype(bf16)
        drop = dot_tn(tail_key, w_part)
        drop_ref[0, head] = drop
        drops[chunk, head] = drop.astype(bf16)
        adds[chunk, head] = dot_tn(tail_key, u_part.astype(bf16))
        throughs[chunk, head] = jnp.broadcast_to(through, (8, LANES))

    @pl.when(step == chunks - 1)
    def _():
        shape = (key_width, key_width + value_width)
        ident = jnp.where(lax.broadcasted_iota(jnp.int32, shape, 0) == lax.broadcasted_iota(jnp.int32, shape, 1), 1.0, 0.0)
        for head in range(heads):
            state[head] = ident

        def pass_on(at, carry):
            for head in range(heads):
                before = state[head]
                starts_ref[at, head] = before
                after = throughs[at, head][0:1, 0:1] * before - dot(drops[at, head], before.astype(bf16))
                state[head] = after + jnp.concatenate(
                    [jnp.zeros((key_width, key_width), f32), adds[at, head]], axis=1
                )
            return carry

        lax.fori_loop(0, chunks, pass_on, 0)
        for head in range(heads):
            map_ref[head] = state[head]
        if cube:
            rows_in.last()
            edges.end()
            for block in range(chunks):
                kept(block).wait()


def output_kernel(
    heads, key_width, value_width, docs, others, cube,
    meta, maps_ref, starts_ref, w_in_ref, u_ref, qkv_ref, scal_ref, gate_ref, gain_ref, w_output_ref,
    core_ref, gated_ref, fresh_ref, state_ref, mixed_ref,
    incoming, *refs,
):
    step = pl.program_id(0)
    chunk = cube_order("head", 7 - step) if cube else step
    qw = heads * key_width

    @pl.when(step == 0)
    def _():
        for head in range(heads):
            state = jnp.zeros((key_width, value_width), f32)
            for other in range(others):
                passing = maps_ref[other, head, :, :key_width]
                top, low = halves(state)
                state = dot(passing, top) + dot(passing, low) + maps_ref[other, head, :, key_width:].astype(f32)
            incoming[head] = state

    masks = Masks(meta, docs, chunk)
    scal = scal_ref[...]
    scal_t = scal.T
    gain = gain_ref[...]
    for head in range(heads):
        query = qkv_ref[:, head * key_width : (head + 1) * key_width]
        key = qkv_ref[:, qw + head * key_width : qw + (head + 1) * key_width]
        within, entry, leave, through = decays(masks, scal, scal_t, head)
        begun = starts_ref[0, head]
        state = dot_fine(begun[:, :key_width], incoming[head]) + begun[:, key_width:]
        state_ref[0, head] = state
        state_low = state.astype(bf16)
        fresh = (u_ref[0, head] - dot(w_in_ref[0, head], state_low)).astype(bf16)
        fresh_ref[0, head] = fresh
        scores = (dot_nt(query, key) * within).astype(bf16)
        core = dot((query.astype(f32) * entry).astype(bf16), state_low) + dot(scores, fresh)
        span = slice(head * value_width, (head + 1) * value_width)
        core_ref[:, span] = core
        scale = lax.rsqrt(jnp.mean(core * core, axis=1, keepdims=True) + epsilon)
        gate = gate_ref[:, span]
        gated_ref[:, span] = (core * scale * gain * (gate * sigmoid(gate))).astype(bf16)
    mixed = dot(gated_ref[...], w_output_ref[...])
    if not cube:
        mixed_ref[...] = mixed.astype(bf16)
        return

    scatter_block(step, CubeScatter("head", mixed_ref, *refs), mixed)


def core_grad_kernel(
    heads, key_width, value_width, docs, chunks,
    meta, grad_ref, w_output_ref, core_ref, gate_ref, gain_ref, qkv_ref, scal_ref, w_in_ref, drop_ref,
    grad_core_ref, inner_ref, pull_ref, grad_gate_ref, grad_gain_ref, total_ref,
):
    step = pl.program_id(0)
    chunk = chunks - 1 - step
    qw = heads * key_width
    masks = Masks(meta, docs, chunk)
    scal = scal_ref[...]
    scal_t = scal.T
    gain = gain_ref[...]

    @pl.when(step == 0)
    def _():
        grad_gain_ref[...] = jnp.zeros_like(grad_gain_ref)
        total_ref[...] = jnp.zeros_like(total_ref)

    grad_gated = dot_nt(grad_ref[...], w_output_ref[...])
    for head in range(heads):
        span = slice(head * value_width, (head + 1) * value_width)
        core = core_ref[:, span]
        gate = gate_ref[:, span]
        grad_in = grad_gated[:, span]
        scale = lax.rsqrt(jnp.mean(core * core, axis=1, keepdims=True) + epsilon)
        sigma = sigmoid(gate)
        normed = core * scale
        grad_gate_ref[:, span] = (
            grad_in * (normed * gain) * (sigma * (1.0 + gate * (1.0 - sigma)))
        ).astype(bf16)
        grad_normed = grad_in * (gate * sigma)
        weighted = grad_normed * gain
        grad_core = scale * (weighted - normed * jnp.mean(weighted * normed, axis=1, keepdims=True))
        grad_gain_ref[0:1, :] += jnp.sum(grad_normed * normed, axis=0, keepdims=True)
        grad_core = grad_core.astype(bf16)
        grad_core_ref[0, head] = grad_core
        query = qkv_ref[:, head * key_width : (head + 1) * key_width]
        key = qkv_ref[:, qw + head * key_width : qw + (head + 1) * key_width]
        within, entry, leave, through = decays(masks, scal, scal_t, head)
        scores = (dot_nt(query, key) * within).astype(bf16)
        inner = dot_tn(scores, grad_core)
        inner_ref[0, head] = inner
        pull = dot_tn((query.astype(f32) * entry).astype(bf16), grad_core) - dot_tn(
            w_in_ref[0, head], inner.astype(bf16)
        )
        pull_ref[0, head] = pull
        total = total_ref[head]
        total_ref[head] = (
            through * total - dot_tn(drop_ref[0, head].astype(bf16), total.astype(bf16)) + pull
        )


def backward_kernel(
    heads, key_width, value_width, docs, chunks, others,
    meta, maps_ref, qkv_ref, act_ref, scal_ref, small_ref, inv_ref, fresh_ref, state_ref,
    grad_core_ref, inner_ref, pull_ref, drop_ref, dvec_ref,
    grad_conv_ref, grad_small_ref, sums_ref,
    carried,
):
    step = pl.program_id(0)
    chunk = chunks - 1 - step
    qw = heads * key_width

    @pl.when(step == 0)
    def _():
        sums_ref[...] = jnp.zeros_like(sums_ref)
        for head in range(heads):
            state = jnp.zeros((key_width, value_width), f32)
            for other in range(others):
                passing = maps_ref[other, head, :, :key_width]
                top, low = halves(state)
                state = dot_tn(passing, top) + dot_tn(passing, low) + maps_ref[other, head, :, key_width:].astype(f32)
            carried[head] = state

    masks = Masks(meta, docs, chunk)
    scal = scal_ref[...]
    scal_t = scal.T
    lane = lax.broadcasted_iota(jnp.int32, (BLOCK, LANES), 1)
    slopes = jnp.zeros((BLOCK, LANES), f32)
    tails = jnp.zeros((1, LANES), f32)
    betas = jnp.zeros((BLOCK, LANES), f32)
    for head in range(heads):
        q_span = slice(head * key_width, (head + 1) * key_width)
        k_span = slice(qw + head * key_width, qw + (head + 1) * key_width)
        v_span = slice(2 * qw + head * value_width, 2 * qw + (head + 1) * value_width)
        query, key, value = qkv_ref[:, q_span], qkv_ref[:, k_span], qkv_ref[:, v_span]
        query_f, key_f = query.astype(f32), key.astype(f32)
        within, entry, leave, through = decays(masks, scal, scal_t, head)
        beta = scal[:, heads + head : heads + head + 1]
        later = carried[head]
        later_low = later.astype(bf16)
        state = state_ref[0, head]
        state_low = state.astype(bf16)
        grad_core = grad_core_ref[0, head]
        fresh = fresh_ref[0, head]
        carried[head] = through * later - dot_tn(drop_ref[0, head].astype(bf16), later_low) + pull_ref[0, head]
        grad_fresh = inner_ref[0, head] + dot((leave * key_f).astype(bf16), later_low)
        grad_x = dot_tn(inv_ref[0, head], grad_fresh.astype(bf16))
        grad_x_low = grad_x.astype(bf16)
        grad_x_beta = beta * grad_x
        recalled = dot(key, state_low)
        grad_beta = jnp.sum(grad_x * (value.astype(f32) - entry * recalled), axis=1, keepdims=True)
        from_state_q = dot_nt(grad_core, state_low)
        from_state_k = dot_nt(grad_x_beta.astype(bf16), state_low)
        grad_scores = (dot_nt(grad_core, fresh) * within).astype(bf16)
        gram = dot_nt(key, key)
        grad_system = jnp.where(masks.strictly, dot_nt(grad_x_low, fresh) * within, 0.0)
        grad_beta = grad_beta - jnp.sum(grad_system * gram, axis=1, keepdims=True)
        grad_gram = (-beta * grad_system).astype(bf16)
        grad_query = dot(grad_scores, key) + entry * from_state_q
        grad_row = dot(grad_gram, key) - entry * from_state_k
        passed = leave * dot_nt(fresh, later_low)
        grad_col = dot_tn(grad_gram, key) + dot_tn(grad_scores, query) + passed
        slope = jnp.sum(query_f * grad_query + key_f * (grad_row - grad_col), axis=1, keepdims=True)
        kept = jnp.sum(jnp.sum(state * later, axis=1, keepdims=True), axis=0, keepdims=True)
        moved = jnp.sum(jnp.sum(key_f * passed, axis=1, keepdims=True), axis=0, keepdims=True)
        tail = through * kept + moved
        slopes = jnp.where(lane == head, slope, slopes)
        tails = jnp.where(lane[0:1, :] == head, tail, tails)
        betas = jnp.where(lane == heads + head, grad_beta, betas)

        conv_q, conv_k, conv_v = act_ref[:, q_span], act_ref[:, k_span], act_ref[:, v_span]
        for span, conv, grad, factor in (
            (q_span, conv_q, grad_query, key_width ** (-0.5)),
            (k_span, conv_k, grad_row + grad_col, 1.0),
        ):
            sigma = sigmoid(conv)
            act = conv * sigma
            norm = lax.rsqrt(jnp.sum(act * act, axis=1, keepdims=True) + epsilon)
            unit = act * norm
            grad_act = (factor * norm) * (grad - unit * jnp.sum(grad * unit, axis=1, keepdims=True))
            grad_conv_ref[:, span] = grad_act * (sigma * (1.0 + conv * (1.0 - sigma)))
        grad_conv_ref[:, v_span] = grad_x_beta * silu_slope(conv_v)

    grad_decay = jnp.where(lane < heads, exact_left(masks.upper, slopes) + tails, 0.0)
    shifted = small_ref[...] + dvec_ref[0:1, :]
    rate = dvec_ref[1:2, :]
    grad_z = grad_decay * rate * sigmoid(shifted)
    sums_ref[0:1, :] += jnp.sum(grad_z, axis=0, keepdims=True)
    sums_ref[1:2, :] += jnp.sum(grad_decay * (rate * softplus(shifted)), axis=0, keepdims=True)
    strength = sigmoid(small_ref[...])
    grad_small_ref[...] = jnp.where(lane < heads, grad_z, betas * strength * (1.0 - strength)).astype(bf16)


def projection_grad_kernel(
    mixed, docs, chunks, taps, cube,
    meta, grad_conv_ref, later_ref, edge_ref, pre_ref, grad_gate_ref, grad_small_ref, conv_ref, rows_ref,
    wq_ref, wk_ref, wv_ref, wg_ref, ws_ref,
    grad_pre_ref, grad_taps_ref, grad_rows_ref, gain_sum_ref,
    ext, *refs,
):
    step = pl.program_id(0)
    chunk = cube_order("head", 7 - step) if cube else step

    @pl.when(step == 0)
    def _():
        grad_taps_ref[...] = jnp.zeros_like(grad_taps_ref)
        gain_sum_ref[...] = jnp.zeros_like(gain_sum_ref)

    ext[0:BLOCK, :] = grad_conv_ref[...]

    @pl.when(chunk == chunks - 1)
    def _():
        ext[BLOCK : BLOCK + HALO, :] = edge_ref[...]

    @pl.when(chunk < chunks - 1)
    def _():
        ext[BLOCK : BLOCK + HALO, :] = later_ref[...]

    place = meta[0] + chunk * BLOCK + lax.broadcasted_iota(jnp.int32, (BLOCK, 1), 0)
    pre = pre_ref[...]
    total = jnp.zeros((BLOCK, mixed), f32)
    for lag in range(taps):
        keep = jnp.where(offset_of(meta, docs, place + lag) >= lag, 1.0, 0.0)
        moved = ext[lag : lag + BLOCK, :] * keep
        total = total + conv_ref[lag : lag + 1, :] * moved
        grad_taps_ref[lag : lag + 1, :] += jnp.sum(pre * moved, axis=0, keepdims=True)
    width = grad_gate_ref.shape[1]
    grad_pre_ref[:, :mixed] = total.astype(bf16)
    grad_pre_ref[:, mixed : mixed + width] = grad_gate_ref[...]
    grad_pre_ref[:, mixed + width :] = grad_small_ref[...]
    grad = jnp.zeros(grad_rows_ref.shape, f32)
    begin = 0
    for ref in (wq_ref, wk_ref, wv_ref, wg_ref, ws_ref):
        grad = grad + dot_nt(grad_pre_ref[:, begin : begin + ref.shape[1]], ref[...])
        begin += ref.shape[1]
    gain_sum_ref[0:1, :] += jnp.sum(grad * rows_ref[...].astype(f32), axis=0, keepdims=True)
    if cube:
        scatter_block(step, CubeScatter("head", grad_rows_ref, *refs), grad)
    else:
        grad_rows_ref[...] = grad.astype(bf16)


MESH = pl.DeviceIdType.MESH
ANYWHERE = pl.BlockSpec(memory_space=pl.ANY)


def line_barrier(axis, cube=None):
    devices, place = lax.axis_size(axis), lax.axis_index(axis)
    barrier = pltpu.get_barrier_semaphore()

    @pl.when(place > 0)
    def _():
        pl.semaphore_signal(barrier, inc=1, device_id={axis: place - 1}, device_id_type=MESH)

    @pl.when(place < devices - 1)
    def _():
        pl.semaphore_signal(barrier, inc=1, device_id={axis: place + 1}, device_id_type=MESH)

    more = 0
    if cube is not None:
        for mask in (1, 2, 4):
            pl.semaphore_signal(
                barrier, inc=1, device_id={cube: flip(lax.axis_index(cube), mask)}, device_id_type=MESH
            )
        more = 3

    @pl.when((place > 0) & (place < devices - 1))
    def _():
        pl.semaphore_wait(barrier, 2 + more)

    @pl.when((place == 0) | (place == devices - 1))
    def _():
        pl.semaphore_wait(barrier, 1 + more)


class LineSum:
    skew = 2
    window = 4

    def __init__(self, axis, counts, depths, parts, passed, arrived, sums, reduce_sems, back_sems):
        self.axis, self.counts, self.depths = axis, counts, depths
        self.parts, self.passed, self.arrived, self.sums = parts, passed, arrived, sums
        self.sems = (reduce_sems, back_sems)
        self.devices, self.place = lax.axis_size(axis), lax.axis_index(axis)
        self.steps = max(counts) + self.skew * (self.devices - 1)

    def rows_of(self, half, index, at):
        depth = self.depths[index]
        return pl.ds(pl.multiple_of((half * self.counts[index] + at) * depth, depth), depth)

    def copy(self, half, index, at, target, back):
        rows = self.rows_of(half, index, at)
        slot = half * self.counts[index] + at
        source, landing = (self.sums, self.sums) if back else (self.passed, self.arrived)
        sent, received = self.sems[back][2 * index], self.sems[back][2 * index + 1]
        return pltpu.make_async_remote_copy(
            source[index].at[rows, :], landing[index].at[rows, :], sent.at[slot], received.at[slot],
            device_id={self.axis: target}, device_id_type=MESH,
        )

    def send(self, half, index, at, target, back):
        @pl.when(at >= self.window)
        def _():
            self.copy(half, index, at - self.window, target, back).wait_send()

        self.copy(half, index, at, target, back).start()

    def each(self, handle):
        place, last = self.place, self.devices - 1
        for half in range(2):
            ends = (last, 0) if half == 0 else (0, last)
            toward = place - 1 if half == 0 else place + 1
            away = place + 1 if half == 0 else place - 1
            for index in range(len(self.counts)):
                handle(half, index, toward, away, place == ends[0], place == ends[1])

    def reduce(self, step):
        def handle(half, index, toward, away, begin, end):
            late = (self.devices - 1 - self.place) if half == 0 else self.place
            at = step - self.skew * late

            @pl.when((at >= 0) & (at < self.counts[index]))
            def _():
                rows = self.rows_of(half, index, at)

                @pl.when(begin)
                def _():
                    self.passed[index][rows, :] = self.parts[index][rows, :]
                    self.send(half, index, at, toward, 0)

                @pl.when(jnp.logical_not(begin))
                def _():
                    self.copy(half, index, at, toward, 0).wait_recv()
                    added = (
                        self.parts[index][rows, :].astype(f32) + self.arrived[index][rows, :].astype(f32)
                    ).astype(bf16)

                    @pl.when(jnp.logical_not(end))
                    def _():
                        self.passed[index][rows, :] = added
                        self.send(half, index, at, toward, 0)

                    @pl.when(end)
                    def _():
                        self.sums[index][rows, :] = added

        self.each(handle)

    def back(self, step, given=None):
        def handle(half, index, toward, away, begin, end):
            late = self.place if half == 0 else (self.devices - 1 - self.place)
            at = step - self.skew * late

            @pl.when((at >= 0) & (at < self.counts[index]))
            def _():
                if given is not None:
                    @pl.when(end)
                    def _():
                        rows = self.rows_of(half, index, at)
                        self.sums[index][rows, :] = given[index][rows, :]

                @pl.when(jnp.logical_not(end))
                def _():
                    self.copy(half, index, at, away, 1).wait_recv()

                @pl.when(jnp.logical_not(begin))
                def _():
                    self.send(half, index, at, away, 1)

        self.each(handle)

    def settle(self, back):
        def handle(half, index, toward, away, begin, end):
            count = self.counts[index]
            for at in range(max(count - self.window, 0), count):
                @pl.when(jnp.logical_not(begin if back else end))
                def _():
                    self.copy(half, index, at, away if back else toward, back).wait_send()

        self.each(handle)


def line_sum_kernel(axis, cube, counts, depths, *refs):
    total = len(counts)
    rows_ref, grads_ref, *refs = refs
    parts, sums, refs = refs[: total - 1], refs[total - 1 : 2 * total - 1], refs[2 * total - 1 :]
    if cube:
        whole_ref, refs = refs[0], refs[1:]
    product, *refs = refs
    parts = (product, *parts)
    arrived, passed, refs = refs[:total], refs[total : 2 * total], refs[2 * total :]
    share = BLOCK // depths[0]
    tiles = counts[0] // share
    line = LineSum(axis, counts, depths, parts, passed, arrived, sums, refs[: 2 * total], refs[2 * total : 4 * total])
    line_barrier(axis, "head" if cube else None)

    begin = max(counts)
    final = CubeTotal(*refs[4 * total :]) if cube else None

    def step_on(step, carry):
        @pl.when((step % share == 0) & (step < tiles * share))
        def _():
            for half in range(2):
                columns = pl.ds(pl.multiple_of((half * tiles + step // share) * BLOCK, BLOCK), BLOCK)
                product[columns, :] = dot_tn(rows_ref[:, columns], grads_ref[...]).astype(bf16)

        @pl.when(step < line.steps)
        def _():
            line.reduce(step)

        @pl.when(step >= begin)
        def _():
            line.back(step - begin)

        if cube:
            after = begin + line.skew * line.devices
            for stage in range(4):
                @pl.when(step == after + 3 * stage)
                def _():
                    if stage:
                        final.end(stage - 1, whole_ref)
                    else:
                        final.held[0] = sums[-1][: whole_ref.shape[0], :].astype(f32)
                    if stage < 3:
                        final.copy(stage).start()

        return carry

    lax.fori_loop(0, begin + line.steps, step_on, 0)
    line.settle(0)
    line.settle(1)


class CubeTotal:
    def __init__(self, held, arrived, send_sem, recv_sem):
        self.held, self.arrived, self.send_sem, self.recv_sem = held, arrived, send_sem, recv_sem

    def copy(self, stage):
        return pltpu.make_async_remote_copy(
            self.held.at[stage], self.arrived.at[stage], self.send_sem.at[stage], self.recv_sem.at[stage],
            device_id={"head": flip(lax.axis_index("head"), (1, 2, 4)[stage])}, device_id_type=MESH,
        )

    def end(self, stage, total_ref):
        self.copy(stage).wait()
        if stage < 2:
            self.held[stage + 1] = self.held[stage] + self.arrived[stage]
        else:
            total_ref[...] = self.held[stage] + self.arrived[stage]


def line_scratch(arrays, depths, moves):
    counts = tuple(array.shape[0] // (2 * depth) for array, depth in zip(arrays, depths))
    semaphores = []
    for count in counts:
        semaphores += [pltpu.SemaphoreType.DMA((2 * count,))] * 2
    return counts, semaphores * moves


def line_sum(rows, grads, given, depths, axis, collective_id):
    cube = lax.axis_size("head") == 8
    arrays = (struct((rows.shape[1], grads.shape[1]), bf16), *given)
    counts, semaphores = line_scratch(arrays, depths, 2)
    vmem = pl.BlockSpec(memory_space=pltpu.VMEM)
    scratch = [pltpu.VMEM(array.shape, bf16) for array in (arrays[0], *arrays, *arrays)] + semaphores
    total = (8, arrays[-1].shape[1])
    if cube:
        scratch += [pltpu.VMEM((3,) + total, f32)] * 2 + [pltpu.SemaphoreType.DMA((3,))] * 2
    results = pl.pallas_call(
        functools.partial(line_sum_kernel, axis, cube, counts, tuple(depths)),
        in_specs=[vmem] * (len(arrays) + 1),
        out_specs=[vmem] * (len(arrays) + cube),
        out_shape=[struct(array.shape, bf16) for array in arrays] + [struct(total, f32)] * cube,
        scratch_shapes=scratch,
        compiler_params=pltpu.CompilerParams(
            collective_id=collective_id, has_side_effects=True, vmem_limit_bytes=VMEM_LIMIT
        ),
        cost_estimate=pl.CostEstimate(flops=10**8, bytes_accessed=40 * 10**6, transcendentals=0),
        name="line_sum",
    )(rows, grads, *given)
    if not cube:
        results = [*results, lax.psum(results[-1][:8].astype(f32), "head")]
    return results


def whole(shape):
    zeros = (0,) * len(shape)
    return pl.BlockSpec(tuple(shape), lambda step: zeros)


def held(shape):
    zeros = (0,) * len(shape)
    return pl.BlockSpec(tuple(shape), lambda step: zeros, pipeline_mode=pl.Buffered(1))


def by_rows(width, chunks=None):
    if chunks is None:
        return pl.BlockSpec((BLOCK, width), lambda step: (step, 0))
    return pl.BlockSpec((BLOCK, width), lambda step: (chunks - 1 - step, 0))


def by_chunk(shape, chunks=None):
    rest = (0,) * len(shape)
    if chunks is None:
        return pl.BlockSpec((1,) + tuple(shape), lambda step: (step,) + rest)
    return pl.BlockSpec((1,) + tuple(shape), lambda step: (chunks - 1 - step,) + rest)


SCALARS = pl.BlockSpec(memory_space=pltpu.SMEM)


def feed_kernel(
    axis, devices, rows,
    own_ref, *refs,
):
    given, kept, refs = refs[:4], refs[4:9], refs[9:]
    total_ref, *refs = refs
    inside, refs = refs[:8], refs[8:]
    inside = (*inside, inside[0])
    grads_ref, w_gate_ref, w_up_ref, w_down_ref = inside[:4]
    blocks_ref, hidden_ref, grad_gate_ref, grad_up_ref, part_ref = inside[4:]
    parts, arrived, gather_send, gather_recv, chain_send, chain_recv, load_sem, store_sem = refs
    place = lax.axis_index(axis)
    piece = rows // 2

    def load(index):
        return pltpu.make_async_copy(given[index], inside[index], load_sem.at[index])

    def store(index):
        return pltpu.make_async_copy(inside[4 + index], kept[index], store_sem.at[index])

    for index in (3, 0, 1, 2):
        load(index).start()
    line_barrier(axis)

    def span(block, half):
        return pl.ds(pl.multiple_of(block * rows + half * piece, piece), piece)

    def full(block):
        return pl.ds(pl.multiple_of(block * rows, rows), rows)

    def gather(owner, hop, way, half):
        target = place + 1 - 2 * way
        slot = (hop * 2 + way) * 2 + half
        return pltpu.make_async_remote_copy(
            blocks_ref.at[span(owner, half), :], blocks_ref.at[span(owner, half), :],
            gather_send.at[slot], gather_recv.at[slot], device_id={axis: target}, device_id_type=MESH,
        )

    def quarter(block, part):
        return pl.ds(pl.multiple_of(block * rows + part * (rows // 4), rows // 4), rows // 4)

    def chain(block, way, part, at):
        target = at + 1 - 2 * way
        landing = jnp.where((block == target) & (way == 0), devices, block)
        slot = (way * devices + block) * 4 + part
        return pltpu.make_async_remote_copy(
            parts.at[quarter(block, part), :], arrived.at[quarter(landing, part), :],
            chain_send.at[slot], chain_recv.at[slot], device_id={axis: target}, device_id_type=MESH,
        )

    blocks_ref[full(place), :] = own_ref[...]

    def event(step, carry):
        hop = (step + 1) // 2
        way = (step + 1) % 2
        owner = jnp.where(way == 0, place - hop, place + hop)
        target = place + 1 - 2 * way

        @pl.when(step == 0)
        def _():
            for side in range(2):
                @pl.when((place + 1 - 2 * side >= 0) & (place + 1 - 2 * side < devices))
                def _():
                    for half in range(2):
                        gather(place, 0, side, half).start()

            for index in range(4):
                load(index).wait()

        @pl.when((owner >= 0) & (owner < devices))
        def _():
            here = full(owner)
            grad_hidden = dot_nt(grads_ref[here, :], w_down_ref[...])

            @pl.when(step > 0)
            def _():
                for half in range(2):
                    gather(owner, hop - 1, way, half).wait_recv()

                    @pl.when((target >= 0) & (target < devices))
                    def _():
                        gather(owner, hop, way, half).start()

            block = blocks_ref[here, :]
            gate_pre = dot(block, w_gate_ref[...])
            up_pre = dot(block, w_up_ref[...])
            sigma = sigmoid(gate_pre)
            act = gate_pre * sigma
            hidden_ref[here, :] = (act * up_pre).astype(bf16)
            grad_gate_ref[here, :] = (grad_hidden * up_pre * (sigma * (1.0 + gate_pre * (1.0 - sigma)))).astype(bf16)
            grad_up_ref[here, :] = (grad_hidden * act).astype(bf16)
            grad = dot_nt(grad_gate_ref[here, :], w_gate_ref[...]) + dot_nt(grad_up_ref[here, :], w_up_ref[...])

            @pl.when(step == 0)
            def _():
                total_ref[...] = grad

            @pl.when(step > 0)
            def _():
                parts[here, :] = grad.astype(bf16)

        @pl.when((way == 1) & (step > 0))
        def _():
            for turn in range(2):
                side = jnp.where(2 * place < devices, turn, 1 - turn)
                block = jnp.where(side == 1, devices - 1 - hop, hop)
                begins = place == jnp.where(side == 1, devices - 1, 0)
                valid = jnp.where(side == 1, block < place, block > place)

                @pl.when(valid)
                def _():
                    for part in range(4):
                        @pl.when(jnp.logical_not(begins))
                        def _():
                            chain(block, side, part, place + 2 * side - 1).wait_recv()
                            at = quarter(block, part)
                            parts[at, :] = (parts[at, :].astype(f32) + arrived[at, :].astype(f32)).astype(bf16)

                        chain(block, side, part, place).start()

        return carry

    lax.fori_loop(0, 2 * devices - 1, event, 0)

    for index in range(4):
        store(index).start()

    def feed_part(block, carry):
        part_ref[full(block), :] = dot(hidden_ref[full(block), :], w_down_ref[...]).astype(bf16)
        return carry

    lax.fori_loop(0, devices, feed_part, 0)
    store(4).start()

    for side, landing, comes in ((1, place, place < devices - 1), (0, devices, place > 0)):
        @pl.when(comes)
        def _():
            for part in range(4):
                chain(place, side, part, place + 2 * side - 1).wait_recv()
                at = pl.ds(part * (rows // 4), rows // 4)
                total_ref[at, :] += arrived[quarter(landing, part), :].astype(f32)

    def gather_end(step, carry):
        hop = step // 2
        way = step % 2
        owner = jnp.where(way == 0, place - hop, place + hop)
        target = place + 1 - 2 * way

        @pl.when((owner >= 0) & (owner < devices) & (target >= 0) & (target < devices))
        def _():
            for half in range(2):
                gather(owner, hop, way, half).wait_send()

        return carry

    lax.fori_loop(0, 2 * (devices - 1), gather_end, 0)

    def chain_end(block, carry):
        @pl.when(block < place)
        def _():
            for part in range(4):
                chain(block, 1, part, place).wait_send()

        @pl.when(block > place)
        def _():
            for part in range(4):
                chain(block, 0, part, place).wait_send()

        return carry

    lax.fori_loop(0, devices, chain_end, 0)
    for index in range(5):
        store(index).wait()


def feed(own, grads, w_gate, w_up, w_down, axis, collective_id):
    devices = lax.axis_size(axis)
    rows, width = own.shape
    units = w_gate.shape[1]
    vmem = pl.BlockSpec(memory_space=pltpu.VMEM)
    moves = pltpu.SemaphoreType.DMA((4 * devices,))
    chains = pltpu.SemaphoreType.DMA((8 * devices,))
    given = (grads, w_gate, w_up, w_down)
    kept = [struct((devices * rows, width), bf16)] + [struct((devices * rows, units), bf16)] * 3
    kept += [struct((devices * rows, width), bf16)]
    return pl.pallas_call(
        functools.partial(feed_kernel, axis, devices, rows),
        in_specs=[vmem] + [ANYWHERE] * 4,
        out_specs=[ANYWHERE] * 5 + [vmem],
        out_shape=kept + [struct((rows, width), f32)],
        scratch_shapes=[
            *(pltpu.VMEM(array.shape, array.dtype) for array in (*given, *kept[:4])),
            pltpu.VMEM((devices * rows, width), bf16), pltpu.VMEM(((devices + 1) * rows, width), bf16),
            moves, moves, chains, chains, pltpu.SemaphoreType.DMA((4,)), pltpu.SemaphoreType.DMA((5,)),
        ],
        compiler_params=pltpu.CompilerParams(
            collective_id=collective_id, has_side_effects=True, vmem_limit_bytes=61 * 1024 * 1024
        ),
        name="feed",
    )(own, grads, w_gate, w_up, w_down)


def flip(index, mask):
    for bit in (1, 2, 4):
        if mask & bit:
            index = index + bit * (1 - 2 * ((index // bit) % 2))
    return index


def cube_barrier(axis, place):
    barrier = pltpu.get_barrier_semaphore()
    for mask in (1, 2, 4):
        pl.semaphore_signal(barrier, inc=1, device_id={axis: flip(place, mask)}, device_id_type=MESH)
    pl.semaphore_wait(barrier, 3)


class CubeGather:
    FIRST = ((0, 0, 2), (0, 1, 4), (0, 1, 2), (0, 0, 4), (0, 0, 1), (0, 1, 1))
    SECOND = ((2, 0, 4), (4, 1, 2), (2, 0, 1), (4, 1, 1))
    THIRD = ((2, 1, 1), (4, 0, 1))
    FOURTH = ((6, 0, 1), (6, 1, 1))

    def __init__(self, axis, own_ref, all_ref, own_sem, send_sem, recv_sem, stride=None, lead=0):
        self.axis, self.own_ref, self.all_ref = axis, own_ref, all_ref
        self.stride, self.lead = stride or own_ref.shape[0], lead
        self.own_sem, self.send_sem, self.recv_sem = own_sem, send_sem, recv_sem
        self.place = lax.axis_index(axis)
        self.rows = own_ref.shape[0]
        self.piece = self.rows // 2

    def part(self, mask, half):
        start = flip(self.place, mask) * self.stride + self.lead + half * self.piece
        return self.all_ref.at[pl.ds(pl.multiple_of(start, LEAD), self.piece), :]

    def copy(self, mask, half, toward):
        source = self.part(mask, half) if mask else self.own_ref.at[pl.ds(half * self.piece, self.piece), :]
        return pltpu.make_async_remote_copy(
            source, self.part(mask, half),
            self.send_sem.at[toward * 2 + half, mask // 2], self.recv_sem.at[(mask ^ toward) * 2 + half],
            device_id={self.axis: flip(self.place, toward)}, device_id_type=MESH,
        )

    def wait(self, mask, half):
        pltpu.make_async_remote_copy(
            self.part(mask, half), self.part(mask, half), self.send_sem.at[0, 0], self.recv_sem.at[mask * 2 + half],
            device_id={self.axis: flip(self.place, 1)}, device_id_type=MESH,
        ).wait_recv()

    def own(self):
        start = pl.multiple_of(self.place * self.rows, self.rows)
        return pltpu.make_async_copy(self.own_ref, self.all_ref.at[pl.ds(start, self.rows), :], self.own_sem)

    def first(self):
        if self.own_sem is not None:
            cube_barrier(self.axis, self.place)
            self.own().start()
        for move in self.FIRST:
            self.copy(*move).start()

    def second(self):
        self.wait(2, 0)
        self.copy(*self.SECOND[0]).start()
        self.wait(4, 1)
        for move in self.SECOND[1:]:
            self.copy(*move).start()

    def third(self):
        for move in self.THIRD:
            self.wait(*move[:2])
            self.copy(*move).start()

    def fourth(self):
        for move in self.FOURTH:
            self.wait(*move[:2])
            self.copy(*move).start()

    def last(self):
        if self.own_sem is not None:
            for mask in (1, 3, 5, 7):
                for half in range(2):
                    self.wait(mask, half)
            self.own().wait()
        for move in self.FIRST + self.SECOND + self.THIRD + self.FOURTH:
            self.copy(*move).wait_send()


CUBE_SEMAPHORES = [pltpu.SemaphoreType.DMA, pltpu.SemaphoreType.DMA((10, 4)), pltpu.SemaphoreType.DMA((16,))]


def cube_gather_kernel(axis, own_ref, all_ref, *semaphores):
    gather = CubeGather(axis, own_ref, all_ref, *semaphores)
    gather.first()
    gather.second()
    gather.third()
    gather.fourth()
    gather.last()


def cube_gather(own, axis, collective_id):
    if lax.axis_size(axis) != 8:
        return lax.all_gather(own, axis, axis=0, tiled=True)
    rows, width = own.shape
    return pl.pallas_call(
        functools.partial(cube_gather_kernel, axis),
        in_specs=[ANYWHERE],
        out_specs=ANYWHERE,
        out_shape=struct((8 * rows, width), own.dtype),
        scratch_shapes=CUBE_SEMAPHORES,
        compiler_params=pltpu.CompilerParams(
            collective_id=collective_id, has_side_effects=True, vmem_limit_bytes=VMEM_LIMIT
        ),
        name="cube_gather",
    )(own)


def feed_grads_kernel(
    axis, cube,
    own_ref, blocks_ref, grads_ref, hidden_ref, grad_gate_ref, grad_up_ref,
    *refs,
):
    down_ref, gate_ref, up_ref = refs[:3]
    step = pl.program_id(0)
    steps = pl.num_programs(0)
    if cube:
        gather = CubeGather(axis, own_ref, refs[3], *refs[4:])
        for at, phase in ((0, gather.first), (2, gather.second), (4, gather.third), (6, gather.fourth)):
            @pl.when(step == at)
            def _():
                phase()

    gate_ref[...] = dot_tn(blocks_ref[...], grad_gate_ref[...]).astype(bf16)
    up_ref[...] = dot_tn(blocks_ref[...], grad_up_ref[...]).astype(bf16)
    down_ref[...] = dot_tn(hidden_ref[...], grads_ref[...]).astype(bf16)
    if cube:
        @pl.when(step == steps - 1)
        def _():
            gather.last()


def feed_grads(own, blocks, grads, hidden, grad_gate, grad_up, axis, collective_id):
    cube = lax.axis_size(axis) == 8
    rows, width = blocks.shape
    units = hidden.shape[1]
    tall = pl.BlockSpec((rows, BLOCK), lambda step: (0, step))
    down = pl.BlockSpec((units, BLOCK), lambda step: (0, step))
    flat = pl.BlockSpec((BLOCK, units), lambda step: (step, 0))
    fixed = held((rows, units))
    results = pl.pallas_call(
        functools.partial(feed_grads_kernel, axis, cube),
        grid=(width // BLOCK,),
        in_specs=[ANYWHERE, tall, tall, fixed, fixed, fixed],
        out_specs=[down, flat, flat] + [ANYWHERE] * cube,
        out_shape=[
            struct((units, width), bf16), struct((width, units), bf16), struct((width, units), bf16),
        ] + [struct((8 * own.shape[0], width), bf16)] * cube,
        scratch_shapes=CUBE_SEMAPHORES if cube else [],
        compiler_params=params(collective_id if cube else None),
        name="feed_grads",
    )(own, blocks, grads, hidden, grad_gate, grad_up)
    return results if cube else (*results, lax.all_gather(own, axis, axis=0, tiled=True))


class CubeScatter:
    def __init__(self, axis, total_ref, given, other, leaving, coming, waiting, send_sem, recv_sem):
        self.axis, self.total_ref = axis, total_ref
        self.given, self.other, self.leaving, self.coming, self.waiting = given, other, leaving, coming, waiting
        self.send_sem, self.recv_sem = send_sem, recv_sem
        self.place = lax.axis_index(axis)
        self.piece = total_ref.shape[0] // 2

    def slot(self, index, half):
        return pl.ds((2 * index + half) * self.piece, self.piece)

    def core_copy(self, mask, half):
        at = self.slot(mask // 2, half)
        return pltpu.make_async_remote_copy(
            self.given.at[at, :], self.other.at[at, :],
            self.send_sem.at[0, mask // 2, half], self.recv_sem.at[0, mask // 2, half],
            device_id={self.axis: flip(self.place, 1)}, device_id_type=MESH,
        )

    def landing(self, index, toward):
        return (toward // 2 - 1) * 2 + (1 if index else 0)

    def chip_copy(self, index, half, toward):
        return pltpu.make_async_remote_copy(
            self.leaving.at[self.slot(index, half), :],
            self.coming.at[self.slot(self.landing(index, toward), half), :],
            self.send_sem.at[toward // 2, index, half], self.recv_sem.at[toward // 2, 1 if index else 0, half],
            device_id={self.axis: flip(self.place, toward)}, device_id_type=MESH,
        )

    def arrived(self, index, half, toward):
        self.chip_copy(index, half, toward).wait_recv()
        return self.coming[self.slot(self.landing(index, toward), half), :].astype(f32)

    def send(self, index, half, toward, values):
        self.leaving[self.slot(index, half), :] = values.astype(bf16)
        self.chip_copy(index, half, toward).start()

    def take(self, mask, block):
        piece = self.piece
        if mask % 2:
            self.given[pl.ds(mask // 2 * 2 * piece, 2 * piece), :] = block.astype(bf16)
            for half in range(2):
                self.core_copy(mask, half).start()
            return
        parts = []
        for half in range(2):
            self.core_copy(mask + 1, half).wait_recv()
            parts.append(
                block[half * piece : (half + 1) * piece, :]
                + self.other[self.slot(mask // 2, half), :].astype(f32)
            )
        if mask == 6:
            self.send(0, 0, 2, parts[0])
            self.send(0, 1, 4, parts[1])
        elif mask == 4:
            self.send(2, 1, 4, parts[1])
            self.waiting[0] = parts[0]
        elif mask == 2:
            self.send(1, 0, 2, parts[0])
            self.waiting[1] = parts[1]
        else:
            self.total_ref[0:piece, :] = parts[0]
            self.total_ref[piece:, :] = parts[1]

    def finish(self):
        piece = self.piece
        self.send(2, 0, 4, self.waiting[0] + self.arrived(0, 0, 2))
        self.send(1, 1, 2, self.waiting[1] + self.arrived(0, 1, 4))
        self.total_ref[0:piece, :] += self.arrived(1, 0, 2)
        self.total_ref[piece:, :] += self.arrived(2, 1, 4)
        self.total_ref[0:piece, :] += self.arrived(2, 0, 4)
        self.total_ref[piece:, :] += self.arrived(1, 1, 2)
        for mask in (7, 5, 3, 1):
            for half in range(2):
                self.core_copy(mask, half).wait_send()
        for index, half, toward in ((0, 0, 2), (0, 1, 4), (1, 0, 2), (2, 1, 4), (1, 1, 2), (2, 0, 4)):
            self.chip_copy(index, half, toward).wait_send()


def scatter_block(step, scatter, block):
    @pl.when(step == 0)
    def _():
        cube_barrier("head", scatter.place)

    for mask in range(8):
        @pl.when(step == 7 - mask)
        def _():
            scatter.take(mask, block)

    @pl.when(step == 7)
    def _():
        scatter.finish()


def cube_scatter_scratch(rows, width):
    return [
        pltpu.VMEM((4 * rows, width), bf16), pltpu.VMEM((4 * rows, width), bf16),
        pltpu.VMEM((3 * rows, width), bf16), pltpu.VMEM((4 * rows, width), bf16),
        pltpu.VMEM((2, rows // 2, width), f32),
        pltpu.SemaphoreType.DMA((3, 4, 2)), pltpu.SemaphoreType.DMA((3, 4, 2)),
    ]


def params(collective_id=None):
    return pltpu.CompilerParams(
        dimension_semantics=("arbitrary",),
        vmem_limit_bytes=VMEM_LIMIT,
        collective_id=collective_id,
        has_side_effects=collective_id is not None,
    )


def widen_kernel(cuts, down_in, gate_in, up_in, all_in, output_in, down, gate, up, *refs):
    *columns, output = refs
    for source, result in ((down_in, down), (gate_in, gate), (up_in, up), (output_in, output)):
        result[...] = source[...].astype(f32)
    begin = 0
    for cut, result in zip(cuts, columns):
        result[...] = all_in[:, begin : begin + cut].astype(f32)
        begin += cut


def widen(ff_grads, grad_w_all, cuts, grad_w_output):
    sources = (*ff_grads, grad_w_all, grad_w_output)
    steps = 8 if ff_grads[0].shape[0] % 128 == 0 else 4
    shapes = [array.shape for array in ff_grads] + [(grad_w_all.shape[0], cut) for cut in cuts] + [grad_w_output.shape]

    def part(shape):
        return pl.BlockSpec((shape[0] // steps, shape[1]), lambda step: (step, 0))

    return pl.pallas_call(
        functools.partial(widen_kernel, cuts),
        grid=(steps,),
        in_specs=[part(array.shape) for array in sources],
        out_specs=[part(shape) for shape in shapes],
        out_shape=[struct(shape, f32) for shape in shapes],
        compiler_params=params(),
        name="widen",
    )(*sources)


def struct(shape, dtype):
    return jax.ShapeDtypeStruct(tuple(shape), dtype)


def from_earlier(array, axis):
    devices = lax.axis_size(axis)
    parts = [
        lax.ppermute(array, axis, [(i, i + by) for i in range(devices - by)])
        for by in range(devices - 1, 0, -1)
    ]
    return jnp.stack(parts) if parts else jnp.zeros((1,) + array.shape, array.dtype)


def from_later(array, axis):
    devices = lax.axis_size(axis)
    parts = [
        lax.ppermute(array, axis, [(i + by, i) for i in range(devices - by)])
        for by in range(devices - 1, 0, -1)
    ]
    return jnp.stack(parts) if parts else jnp.zeros((1,) + array.shape, array.dtype)


def shards(
    inputs,
    doc_lengths,
    first_gain,
    w_query,
    w_key,
    w_value,
    w_outgate,
    w_decay,
    w_beta,
    conv_query,
    conv_key,
    conv_value,
    decay_log,
    decay_bias,
    head_gain,
    w_output,
    second_gain,
    w_gate,
    w_up,
    w_down,
    cotangent,
):
    row_count, model_width = inputs.shape
    heads = decay_log.shape[0]
    qw, vw = w_query.shape[1], w_value.shape[1]
    key_width, value_width = qw // heads, vw // heads
    mixed_width = 2 * qw + vw
    taps = conv_query.shape[0]
    docs = doc_lengths.shape[0]
    seq_index = lax.axis_index("seq")
    head_index = lax.axis_index("head")
    head_total = lax.axis_size("head")
    seq_rows = row_count * head_total
    chunks = seq_rows // BLOCK
    others = max(lax.axis_size("seq") - 1, 1)
    sizes = (heads, key_width, value_width, docs)

    inputs_f = inputs.astype(f32)
    normed = rms_scale(inputs_f, first_gain).astype(bf16)
    meta = jnp.concatenate(
        [(seq_index * seq_rows).astype(jnp.int32)[None], slot_starts(doc_lengths)]
    )
    _, own_valid = layout(doc_lengths, (seq_index * head_total + head_index) * row_count, row_count)

    grad_out = cotangent.astype(f32) * own_valid.astype(f32)[:, None]
    grad_low = grad_out.astype(bf16)
    w_small = jnp.concatenate([w_decay, w_beta, jnp.zeros((model_width, LANES - 2 * heads), bf16)], axis=1)
    weights = (w_query, w_key, w_value, w_outgate, w_small)
    all_width = mixed_width + vw + LANES
    conv_all = jnp.concatenate([conv_query, conv_key, conv_value], axis=1)
    dvec = jnp.zeros((8, LANES), f32)
    dvec = dvec.at[0, :heads].set(decay_bias).at[1, :heads].set(-jnp.exp(decay_log))
    map_shape = (heads, key_width, key_width + value_width)

    cube = head_total == 8 and chunks == 8 and row_count == BLOCK
    if cube:
        rows_given, rows_spec = normed, held(normed.shape)

        def at_step(step):
            return cube_order("head", step)
    else:
        block_rows = lax.all_gather(normed, "head", axis=0, tiled=True)
        tail = from_previous(block_rows[seq_rows - LEAD :])
        blocks = block_rows.reshape(chunks, BLOCK, model_width)
        leads = jnp.concatenate([tail[None], blocks[:-1, BLOCK - LEAD :]], axis=0)
        rows_given = jnp.concatenate([leads, blocks], axis=1).reshape(chunks * STRIDE, model_width)
        rows_spec = pl.BlockSpec((STRIDE, model_width), lambda step: (step, 0))

        def at_step(step):
            return step

    def rows_out(width):
        return pl.BlockSpec((BLOCK, width), lambda step: (at_step(step), 0))

    def chunk_out(shape):
        return pl.BlockSpec((1,) + tuple(shape), lambda step: (at_step(step),) + (0,) * len(shape))

    results = pl.pallas_call(
        functools.partial(forward_kernel, *sizes, taps, chunks, cube),
        grid=(chunks,),
        in_specs=[
            SCALARS, rows_spec, *(held(weight.shape) for weight in weights), whole(conv_all.shape),
            whole(dvec.shape),
        ],
        out_specs=[
            rows_out(mixed_width), rows_out(mixed_width), rows_out(vw), rows_out(LANES), rows_out(LANES),
            rows_out(mixed_width),
            chunk_out((heads, BLOCK, BLOCK)), chunk_out((heads, BLOCK, key_width)),
            chunk_out((heads, BLOCK, value_width)), chunk_out((heads, key_width, key_width)),
            whole((chunks,) + map_shape), whole(map_shape),
        ] + [ANYWHERE] * cube,
        out_shape=[
            struct((seq_rows, mixed_width), f32), struct((seq_rows, mixed_width), f32),
            struct((seq_rows, vw), f32), struct((seq_rows, LANES), f32), struct((seq_rows, LANES), f32),
            struct((seq_rows, mixed_width), bf16),
            struct((chunks, heads, BLOCK, BLOCK), bf16), struct((chunks, heads, BLOCK, key_width), bf16),
            struct((chunks, heads, BLOCK, value_width), f32),
            struct((chunks, heads, key_width, key_width), f32),
            struct((chunks,) + map_shape, f32), struct(map_shape, f32),
        ] + [struct((seq_rows, model_width), bf16)] * cube,
        scratch_shapes=[
            pltpu.VMEM((STRIDE, mixed_width), f32), pltpu.VMEM(map_shape, f32),
            pltpu.VMEM((chunks, heads, key_width, key_width), bf16),
            pltpu.VMEM((chunks, heads, key_width, value_width), f32),
            pltpu.VMEM((chunks, heads, 8, LANES), f32),
        ] + [
            pltpu.VMEM((chunks * STRIDE, model_width), bf16), pltpu.SemaphoreType.DMA((chunks,)),
            pltpu.VMEM((LEAD, model_width), bf16), pltpu.SemaphoreType.DMA((2,)),
            pltpu.SemaphoreType.DMA((8,)), pltpu.SemaphoreType.DMA((8,)), *CUBE_SEMAPHORES[1:],
        ] * cube,
        compiler_params=params(2 if cube else None),
        name="mixer_forward",
    )(meta, rows_given, *weights, conv_all, dvec)
    (pre, conv, gate, small, scal, qkv, inverse, w_part, u_part, drop, starts, block_map) = results[:12]
    if cube:
        block_rows = results[12]

    earlier = from_earlier(block_map.astype(bf16), "seq")
    grad_block_two = lax.all_gather(grad_low, "seq", axis=0, tiled=True)
    gain_row = head_gain[None, :]
    def last_first(step):
        return cube_order("head", 7 - step) if cube else step

    def rows_back(width):
        return pl.BlockSpec((BLOCK, width), lambda step: (last_first(step), 0))

    def chunk_back(shape):
        return pl.BlockSpec((1,) + tuple(shape), lambda step: (last_first(step),) + (0,) * len(shape))

    core, gated, fresh, states, mixed_part = pl.pallas_call(
        functools.partial(output_kernel, *sizes, others, cube),
        grid=(chunks,),
        in_specs=[
            SCALARS, whole(earlier.shape), chunk_back(map_shape), chunk_back((heads, BLOCK, key_width)),
            chunk_back((heads, BLOCK, value_width)), rows_back(mixed_width), rows_back(LANES), rows_back(vw),
            whole(gain_row.shape), held(w_output.shape),
        ],
        out_specs=[
            rows_back(vw), rows_back(vw), chunk_back((heads, BLOCK, value_width)),
            chunk_back((heads, key_width, value_width)),
            whole((row_count, model_width)) if cube else rows_back(model_width),
        ],
        out_shape=[
            struct((seq_rows, vw), f32), struct((seq_rows, vw), bf16),
            struct((chunks, heads, BLOCK, value_width), bf16),
            struct((chunks, heads, key_width, value_width), f32),
            struct((row_count, model_width), f32) if cube else struct((seq_rows, model_width), bf16),
        ],
        scratch_shapes=[pltpu.VMEM((heads, key_width, value_width), f32)]
        + (cube_scatter_scratch(row_count, model_width) if cube else []),
        compiler_params=params(5 if cube else None),
        name="mixer_output",
    )(meta, earlier, starts, w_part, u_part, qkv, scal, gate, gain_row, w_output)
    if cube:
        mixer_out = mixed_part
    else:
        mixer_out = lax.psum_scatter(mixed_part, "head", scatter_dimension=0, tiled=True).astype(f32)

    hidden_in = inputs_f + mixer_out
    normed_two = rms_scale(hidden_in, second_gain).astype(bf16)
    mlp_block, hidden, grad_gate, grad_up, mlp_part, grad_normed_two = feed(
        normed_two, grad_block_two, w_gate, w_up, w_down, "seq", 3
    )
    mlp_out = lax.psum_scatter(mlp_part, "seq", scatter_dimension=0, tiled=True)
    grad_hidden_norm, grad_second = rms_back(hidden_in, second_gain, grad_normed_two)
    grad_hidden_in = grad_out + grad_hidden_norm
    grad_mix = grad_hidden_in.astype(bf16)
    *ff_grads, grad_block = feed_grads(
        grad_mix, mlp_block, grad_block_two, hidden, grad_gate, grad_up, "head", 6
    )
    grad_core, inner, pull, grad_gate_pre, grad_head, pulled = pl.pallas_call(
        functools.partial(core_grad_kernel, *sizes, chunks),
        grid=(chunks,),
        in_specs=[
            SCALARS, by_rows(model_width, chunks), whole(w_output.shape), by_rows(vw, chunks), by_rows(vw, chunks),
            whole(gain_row.shape), by_rows(mixed_width, chunks), by_rows(LANES, chunks),
            by_chunk((heads, BLOCK, key_width), chunks), by_chunk((heads, key_width, key_width), chunks),
        ],
        out_specs=[
            by_chunk((heads, BLOCK, value_width), chunks), by_chunk((heads, BLOCK, value_width), chunks),
            by_chunk((heads, key_width, value_width), chunks), by_rows(vw, chunks),
            whole((8, value_width)), whole((heads, key_width, value_width)),
        ],
        out_shape=[
            struct((chunks, heads, BLOCK, value_width), bf16), struct((chunks, heads, BLOCK, value_width), f32),
            struct((chunks, heads, key_width, value_width), f32), struct((seq_rows, vw), bf16),
            struct((8, value_width), f32), struct((heads, key_width, value_width), f32),
        ],
        compiler_params=params(),
        name="mixer_core_grad",
    )(meta, grad_block, w_output, core, gate, gain_row, qkv, scal, w_part, drop)
    grad_w_output = dot_tn(gated, grad_block).astype(bf16)

    later = from_later(
        jnp.concatenate([block_map[:, :, :key_width], pulled], axis=2).astype(bf16), "seq"
    )
    grad_conv, grad_small, sums = pl.pallas_call(
        functools.partial(backward_kernel, *sizes, chunks, others),
        grid=(chunks,),
        in_specs=[
            SCALARS, whole(later.shape), by_rows(mixed_width, chunks), by_rows(mixed_width, chunks),
            by_rows(LANES, chunks), by_rows(LANES, chunks), by_chunk((heads, BLOCK, BLOCK), chunks),
            by_chunk((heads, BLOCK, value_width), chunks), by_chunk((heads, key_width, value_width), chunks),
            by_chunk((heads, BLOCK, value_width), chunks), by_chunk((heads, BLOCK, value_width), chunks),
            by_chunk((heads, key_width, value_width), chunks), by_chunk((heads, key_width, key_width), chunks),
            whole(dvec.shape),
        ],
        out_specs=[by_rows(mixed_width, chunks), by_rows(LANES, chunks), whole((8, LANES))],
        out_shape=[
            struct((seq_rows, mixed_width), f32), struct((seq_rows, LANES), bf16), struct((8, LANES), f32),
        ],
        scratch_shapes=[pltpu.VMEM((heads, key_width, value_width), f32)],
        compiler_params=params(),
        name="mixer_backward",
    )(meta, later, qkv, conv, scal, small, inverse, fresh, states, grad_core, inner, pull, drop, dvec)

    edge = from_next(grad_conv[:HALO])
    step_rows = BLOCK // HALO
    last_halo = seq_rows // HALO - 1
    later_rows = pl.BlockSpec(
        (HALO, mixed_width), lambda step: (jnp.minimum((last_first(step) + 1) * step_rows, last_halo), 0)
    )
    grad_pre, grad_taps, grad_rows, gain_sum = pl.pallas_call(
        functools.partial(projection_grad_kernel, mixed_width, docs, chunks, taps, cube),
        grid=(chunks,),
        in_specs=[
            SCALARS, rows_back(mixed_width), later_rows, whole(edge.shape), rows_back(mixed_width), rows_back(vw),
            rows_back(LANES), whole(conv_all.shape), rows_back(model_width),
            *(held(weight.shape) for weight in weights),
        ],
        out_specs=[
            rows_back(all_width), whole((8, mixed_width)),
            whole((row_count, model_width)) if cube else rows_back(model_width), whole((8, model_width)),
        ],
        out_shape=[
            struct((seq_rows, all_width), bf16), struct((8, mixed_width), f32),
            struct((row_count, model_width), f32) if cube else struct((seq_rows, model_width), bf16),
            struct((8, model_width), f32),
        ],
        scratch_shapes=[pltpu.VMEM((BLOCK + HALO, mixed_width), f32)]
        + (cube_scatter_scratch(row_count, model_width) if cube else []),
        compiler_params=params(8 if cube else None),
        name="projection_grad",
    )(meta, grad_conv, grad_conv, edge, pre, grad_gate_pre, grad_small, conv_all, block_rows, *weights)

    grad_pre, *ff_grads = lax.optimization_barrier((grad_pre, *ff_grads))
    ff_grads = [lax.psum(part, "head") for part in ff_grads]
    if cube:
        grad_normed = grad_rows
    else:
        grad_normed = lax.psum_scatter(grad_rows, "head", scatter_dimension=0, tiled=True).astype(f32)
    grad_input_norm, _ = rms_back(inputs_f, first_gain, grad_normed)
    grad_inputs = grad_hidden_in + grad_input_norm
    gains = jnp.concatenate([gain_sum[0] / first_gain, grad_second, grad_head[0]]).reshape(2, -1)
    grad_w_all, grad_w_output, small_sums, _, gains = line_sum(
        block_rows,
        grad_pre,
        (
            grad_w_output,
            jnp.pad(
                jnp.concatenate([grad_taps, sums], axis=1), ((0, 24), (0, 0))
            ).astype(bf16),
            jnp.pad(gains, ((0, 30), (0, 0))).astype(bf16),
        ),
        (32, 16, 16, 16),
        "seq",
        1,
    )
    gains = gains[:2].reshape(-1)
    first_part, second_part = gains[:model_width], gains[model_width : 2 * model_width]
    head_part = gains[2 * model_width :]
    grad_w_all, mlp_out, *ff_grads = lax.optimization_barrier((grad_w_all, mlp_out, *ff_grads))
    grad_w_down, grad_w_gate, grad_w_up, grad_w_query, grad_w_key, grad_w_value, grad_w_outgate, grad_w_output = widen(
        ff_grads, grad_w_all, (qw, qw, vw, vw), grad_w_output
    )
    grad_w_small = grad_w_all[:, mixed_width + vw :].astype(f32)
    grad_taps = small_sums[:taps, :mixed_width].astype(f32)
    sums = small_sums[:2, mixed_width : mixed_width + heads].astype(f32)
    output = (hidden_in + mlp_out.astype(f32)).astype(bf16)
    return (
        output,
        grad_inputs,
        first_part,
        grad_w_query,
        grad_w_key,
        grad_w_value,
        grad_w_outgate,
        grad_w_small[:, :heads],
        grad_w_small[:, heads : 2 * heads],
        grad_taps[:, :qw],
        grad_taps[:, qw : 2 * qw],
        grad_taps[:, 2 * qw :],
        sums[1],
        sums[0],
        head_part,
        grad_w_output,
        second_part,
        grad_w_gate,
        grad_w_up,
        grad_w_down,
    )


def from_previous(array):
    devices = lax.axis_size("seq")
    return lax.ppermute(array, "seq", [(i, i + 1) for i in range(devices - 1)])


def from_next(array):
    devices = lax.axis_size("seq")
    return lax.ppermute(array, "seq", [(i + 1, i) for i in range(devices - 1)])


def solution(mesh):
    in_specs = (
        P(("seq", "head"), None),
        P(),
        P(),
        P(None, "head"),
        P(None, "head"),
        P(None, "head"),
        P(None, "head"),
        P(None, "head"),
        P(None, "head"),
        P(None, "head"),
        P(None, "head"),
        P(None, "head"),
        P("head"),
        P("head"),
        P(),
        P("head", None),
        P(),
        P(None, "seq"),
        P(None, "seq"),
        P("seq", None),
        P(("seq", "head"), None),
    )
    out_specs = (
        P(("seq", "head"), None),
        P(("seq", "head"), None),
        P(),
        P(None, "head"),
        P(None, "head"),
        P(None, "head"),
        P(None, "head"),
        P(None, "head"),
        P(None, "head"),
        P(None, "head"),
        P(None, "head"),
        P(None, "head"),
        P("head"),
        P("head"),
        P(),
        P("head", None),
        P(),
        P(None, "seq"),
        P(None, "seq"),
        P("seq", None),
    )
    return jax.shard_map(shards, mesh=mesh, in_specs=in_specs, out_specs=out_specs, check_vma=False)
```

```python
import functools

import jax
import jax.numpy as jnp
from jax import lax
from jax.experimental import pallas as pl
from jax.experimental.pallas import tpu as pltpu
from jax.sharding import PartitionSpec as P

GROUP = 64
BLOCK = 256
LANES = 128
HALO = 8

epsilon = 1e-06
f32 = jnp.float32
bf16 = jnp.bfloat16
VMEM_LIMIT = 56 * 1024 * 1024


def dot(left, right):
    return jnp.dot(left, right, preferred_element_type=f32)


def dot_tn(left, right):
    return lax.dot_general(left, right, (((0,), (0,)), ((), ())), preferred_element_type=f32)


def dot_nt(left, right):
    return lax.dot_general(left, right, (((1,), (1,)), ((), ())), preferred_element_type=f32)


def halves(values):
    top = values.astype(bf16)
    return top, (values - top.astype(f32)).astype(bf16)


def exact_left(left, right):
    top = right.astype(bf16)
    rest = right - top.astype(f32)
    middle = rest.astype(bf16)
    low = (rest - middle.astype(f32)).astype(bf16)
    return dot(left, top) + dot(left, middle) + dot(left, low)


def dot_fine(left, right):
    left_top, left_low = halves(left)
    right_top, right_low = halves(right)
    return dot(left_top, right_top) + (dot(left_top, right_low) + dot(left_low, right_top))


def sigmoid(values):
    return jax.nn.sigmoid(values)


def silu_slope(values):
    sigma = sigmoid(values)
    return sigma * (1.0 + values * (1.0 - sigma))


def softplus(values):
    return jnp.maximum(values, 0.0) + jnp.log1p(jnp.exp(-jnp.abs(values)))


def slot_starts(doc_lengths):
    slot_sizes = (doc_lengths + (GROUP - 1)) // GROUP * GROUP
    return jnp.cumsum(slot_sizes, dtype=jnp.int32) - slot_sizes


def layout(doc_lengths, first_row, row_total):
    starts = slot_starts(doc_lengths)
    places = first_row + jnp.arange(row_total, dtype=jnp.int32)
    owners = jnp.sum(
        (places[:, None] >= starts[None, 1:]).astype(jnp.int32), axis=1, dtype=jnp.int32
    )
    picked = (owners[:, None] == jnp.arange(doc_lengths.shape[0], dtype=jnp.int32)[None, :]).astype(
        jnp.int32
    )
    begins = jnp.sum(picked * starts[None, :], axis=1, dtype=jnp.int32)
    length = jnp.sum(picked * doc_lengths[None, :], axis=1, dtype=jnp.int32)
    offset = places - begins
    return (offset, offset < length)


def rms_scale(values, gain):
    return values * lax.rsqrt(jnp.mean(values * values, axis=-1, keepdims=True) + epsilon) * gain


def rms_back(values, gain, grad_in):
    scale = lax.rsqrt(jnp.mean(values * values, axis=-1, keepdims=True) + epsilon)
    weighted = grad_in * gain
    grad_values = scale * weighted - values * scale**3 * jnp.mean(
        weighted * values, axis=-1, keepdims=True
    )
    grad_gain = jnp.sum((grad_in * values * scale).reshape(-1, values.shape[-1]), axis=0)
    return (grad_values, grad_gain)


def owner_of(meta, docs, places):
    total = jnp.zeros_like(places)
    for doc in range(1, docs):
        total = total + jnp.where(places >= meta[1 + doc], 1, 0)
    return total


def offset_of(meta, docs, places):
    begin = jnp.zeros_like(places)
    for doc in range(1, docs):
        begin = jnp.where(places >= meta[1 + doc], meta[1 + doc], begin)
    return places - begin


class Masks:
    def __init__(self, meta, docs, chunk):
        base = meta[0] + chunk * BLOCK
        rows = lax.broadcasted_iota(jnp.int32, (BLOCK, BLOCK), 0)
        cols = lax.broadcasted_iota(jnp.int32, (BLOCK, BLOCK), 1)
        same = owner_of(meta, docs, base + rows) == owner_of(meta, docs, base + cols)
        self.inclusive = same & (rows >= cols)
        self.strictly = same & (rows > cols)
        self.level = rows ^ cols
        self.lower = jnp.where(rows >= cols, 1.0, 0.0).astype(bf16)
        self.upper = jnp.where(rows <= cols, 1.0, 0.0).astype(bf16)
        self.eye = jnp.where(rows == cols, 1.0, 0.0)
        place = base + lax.broadcasted_iota(jnp.int32, (BLOCK, 1), 0)
        owner = owner_of(meta, docs, place)
        before = jnp.int32(0)
        last = jnp.int32(0)
        for doc in range(1, docs):
            before = before + jnp.where(base - 1 >= meta[1 + doc], 1, 0)
            last = last + jnp.where(base + BLOCK - 1 >= meta[1 + doc], 1, 0)
        self.enters = jnp.where(owner == before, 1.0, 0.0)
        self.leaves = jnp.where(owner == last, 1.0, 0.0)
        self.through = jnp.where(before == last, 1.0, 0.0).astype(f32)
        self.offset = offset_of(meta, docs, place)


def decays(masks, scal, scal_t, head):
    column = scal[:, head : head + 1]
    row = scal_t[head : head + 1, :]
    within = jnp.where(masks.inclusive, jnp.exp(jnp.minimum(column - row, 0.0)), 0.0)
    last = column[BLOCK - 1 : BLOCK, :]
    entry = jnp.exp(column) * masks.enters
    leave = jnp.exp(last - column) * masks.leaves
    through = jnp.exp(last) * masks.through
    return within, entry, leave, through


def unit_lower_inverses(systems):
    half = BLOCK // 2
    rows = lax.broadcasted_iota(jnp.int32, (half, half), 0)
    cols = lax.broadcasted_iota(jnp.int32, (half, half), 1)
    level = rows ^ cols
    eye = jnp.where(rows == cols, 1.0, 0.0)
    parts = [system[at : at + half, at : at + half] for system in systems for at in (0, half)]
    solved = [eye - jnp.where(level == 1, part, 0.0) for part in parts]
    width = 2
    while width < half:
        keep = (level >= width) & (level < 2 * width)
        low = [inverse.astype(bf16) for inverse in solved]
        moved = [dot(jnp.where(keep, part, 0.0).astype(bf16), inverse) for part, inverse in zip(parts, low)]
        solved = [
            whole_part - dot(inverse, part.astype(bf16))
            for whole_part, inverse, part in zip(solved, low, moved)
        ]
        width *= 2
    solved = [inverse.astype(bf16) for inverse in solved]
    results = []
    for index, system in enumerate(systems):
        upper, lower = solved[2 * index], solved[2 * index + 1]
        corner = -dot(lower, dot(system[half:, :half].astype(bf16), upper).astype(bf16))
        results.append((upper, corner.astype(bf16), lower))
    return results


LEAD = 2 * HALO
STRIDE = BLOCK + LEAD


def cube_order(axis, step):
    place = lax.axis_index(axis)
    chunk = 0
    for bit in (1, 2, 4):
        chunk = chunk + bit * ((place // bit + step // bit) % 2)
    return chunk


class EdgeRows:
    def __init__(self, line, axis, own_ref, rows_ref, edge_ref, line_sem, send_sem, recv_sem):
        self.line, self.axis = line, axis
        self.group, self.place = lax.axis_index(line), lax.axis_index(axis)
        self.groups, self.last = lax.axis_size(line), lax.axis_size(axis) - 1
        self.own_ref, self.rows_ref, self.edge_ref = own_ref, rows_ref, edge_ref
        self.line_sem, self.send_sem, self.recv_sem = line_sem, send_sem, recv_sem

    def enter(self):
        barrier = pltpu.get_barrier_semaphore()
        for mask in (1, 2, 4, 6):
            pl.semaphore_signal(barrier, inc=1, device_id={self.axis: flip(self.place, mask)}, device_id_type=MESH)
        for by in range(1, self.groups):
            other = lax.rem(self.group + by, self.groups)
            pl.semaphore_signal(barrier, inc=1, device_id={self.line: other}, device_id_type=MESH)
        pl.semaphore_wait(barrier, 3 + self.groups)

    def hands_on(self):
        return (self.place == self.last) & (self.group < self.groups - 1)

    def receives(self):
        return (self.place == self.last) & (self.group > 0)

    def landing(self, mask):
        block = lax.rem(flip(self.place, mask) + 1, self.last + 1)
        return self.rows_ref.at[pl.ds(pl.multiple_of(block * STRIDE, LEAD), LEAD), :]

    def onward(self):
        return pltpu.make_async_remote_copy(
            self.own_ref.at[pl.ds(BLOCK - LEAD, LEAD), :], self.edge_ref, self.line_sem.at[0], self.line_sem.at[1],
            device_id={self.line: self.group + 1}, device_id_type=MESH,
        )

    def copy(self, mask, toward):
        return pltpu.make_async_remote_copy(
            self.landing(mask) if mask else self.edge_ref, self.landing(mask),
            self.send_sem.at[mask + toward if mask else toward], self.recv_sem.at[mask ^ toward],
            device_id={self.axis: flip(self.place, toward)}, device_id_type=MESH,
        )

    def wait(self, mask):
        pltpu.make_async_remote_copy(
            self.landing(mask), self.landing(mask), self.send_sem.at[0], self.recv_sem.at[mask],
            device_id={self.axis: flip(self.place, 1)}, device_id_type=MESH,
        ).wait_recv()

    def start(self):
        @pl.when(self.hands_on())
        def _():
            self.onward().start()

        @pl.when(self.place < self.last)
        def _():
            self.edge_ref[...] = self.own_ref[BLOCK - LEAD :, :]

        @pl.when((self.place == self.last) & (self.group == 0))
        def _():
            self.edge_ref[...] = jnp.zeros(self.edge_ref.shape, bf16)

        @pl.when(self.receives())
        def _():
            pltpu.make_async_remote_copy(
                self.edge_ref, self.edge_ref, self.line_sem.at[0], self.line_sem.at[1],
                device_id={self.line: self.group - 1}, device_id_type=MESH,
            ).wait_recv()

        for toward in (6, 2, 4, 1):
            self.copy(0, toward).start()
        self.landing(0)[...] = self.edge_ref[...]

    def spread(self):
        for mask in (2, 4, 6):
            self.wait(mask)
            self.copy(mask, 1).start()
        for mask in (1, 3, 5, 7):
            self.wait(mask)

    def end(self):
        @pl.when(self.hands_on())
        def _():
            self.onward().wait_send()

        for toward in (6, 2, 4, 1):
            self.copy(0, toward).wait_send()
        for mask in (2, 4, 6):
            self.copy(mask, 1).wait_send()


def forward_kernel(
    heads, key_width, value_width, docs, taps, chunks, cube,
    meta, rows_ref, wq_ref, wk_ref, wv_ref, wg_ref, ws_ref, conv_ref, dvec_ref,
    pre_ref, act_ref, gate_ref, small_ref, scal_ref, qkv_ref, inv_ref, w_out_ref, u_ref, drop_ref,
    starts_ref, map_ref, *refs,
):
    step = pl.program_id(0)
    ext, state, drops, adds, throughs = refs[2 * cube : 2 * cube + 5]
    if cube:
        all_ref = refs[0]
        earlier_ref, *refs = refs[1:]
        held, copy_sem, edge_ref, line_sem, edge_send, edge_recv, cube_send, cube_recv = refs[5:13]
        going, coming, map_sem = refs[13:]
        chunk = cube_order("head", step)
        rows_in = CubeGather("head", rows_ref, held, None, cube_send, cube_recv, STRIDE, LEAD)
        edges = EdgeRows("seq", "head", rows_ref, held, edge_ref, line_sem, edge_send, edge_recv)

        def kept(block):
            start = pl.multiple_of(block * STRIDE + LEAD, LEAD)
            return pltpu.make_async_copy(
                held.at[pl.ds(start, BLOCK), :],
                all_ref.at[pl.ds(pl.multiple_of(block * BLOCK, BLOCK), BLOCK), :],
                copy_sem.at[block],
            )

        @pl.when(step == 0)
        def _():
            edges.enter()
            edges.start()
            rows_in.first()
            held[pl.ds(pl.multiple_of(chunk * STRIDE + LEAD, LEAD), BLOCK), :] = rows_ref[...]

        @pl.when(step == 2)
        def _():
            rows_in.second()
            rows_in.third()

        @pl.when(step == 4)
        def _():
            rows_in.fourth()

        for odd in (1, 3, 5, 7):
            @pl.when(step == odd)
            def _():
                for half in range(2):
                    rows_in.wait(odd, half)

        kept(chunk).start()
        rows = held[pl.ds(pl.multiple_of(chunk * STRIDE + LEAD, LEAD), BLOCK), :]
    else:
        chunk = step
        rows = rows_ref[LEAD:, :]

    qw, vw = heads * key_width, heads * value_width
    mixed = 2 * qw + vw
    masks = Masks(meta, docs, chunk)
    gate_ref[...] = dot(rows, wg_ref[...])
    small = dot(rows, ws_ref[...])
    small_ref[...] = small
    if cube:
        @pl.when(step == 0)
        def _():
            edges.spread()

        rows_ext = held[pl.ds(pl.multiple_of(chunk * STRIDE, LEAD), STRIDE), :]
    else:
        rows_ext = rows_ref[...]
    for span, ref in ((slice(0, qw), wq_ref), (slice(qw, 2 * qw), wk_ref), (slice(2 * qw, mixed), wv_ref)):
        pre = dot(rows_ext, ref[...])
        ext[:, span] = pre
        pre_ref[:, span] = pre[LEAD:, :]

    conv = jnp.zeros((BLOCK, mixed), f32)
    for lag in range(taps):
        keep = jnp.where(masks.offset >= lag, 1.0, 0.0)
        conv = conv + conv_ref[lag : lag + 1, :] * (ext[LEAD - lag : LEAD - lag + BLOCK, :] * keep)
    act_ref[...] = conv
    act = conv * sigmoid(conv)

    lane = lax.broadcasted_iota(jnp.int32, (BLOCK, LANES), 1)
    decay = dvec_ref[1:2, :] * softplus(small + dvec_ref[0:1, :])
    cumul = exact_left(masks.lower, decay)
    scal = jnp.where(lane < heads, cumul, sigmoid(small))
    scal_ref[...] = scal
    scal_t = scal.T

    held_heads = []
    for head in range(heads):
        act_q = act[:, head * key_width : (head + 1) * key_width]
        act_k = act[:, qw + head * key_width : qw + (head + 1) * key_width]
        value = act[:, 2 * qw + head * value_width : 2 * qw + (head + 1) * value_width].astype(bf16)
        norm_q = lax.rsqrt(jnp.sum(act_q * act_q, axis=1, keepdims=True) + epsilon)
        norm_k = lax.rsqrt(jnp.sum(act_k * act_k, axis=1, keepdims=True) + epsilon)
        query = (act_q * norm_q * key_width ** (-0.5)).astype(bf16)
        key = (act_k * norm_k).astype(bf16)
        qkv_ref[:, head * key_width : (head + 1) * key_width] = query
        qkv_ref[:, qw + head * key_width : qw + (head + 1) * key_width] = key
        qkv_ref[:, 2 * qw + head * value_width : 2 * qw + (head + 1) * value_width] = value
        within, entry, leave, through = decays(masks, scal, scal_t, head)
        beta = scal[:, heads + head : heads + head + 1]
        system = jnp.where(masks.strictly, beta * dot_nt(key, key) * within, 0.0)
        held_heads.append((system, key, value, beta, entry, leave, through))

    half = BLOCK // 2
    inverses = unit_lower_inverses([part[0] for part in held_heads])
    for head, (upper, corner, lower) in enumerate(inverses):
        inv_ref[0, head, :half, :half] = upper
        inv_ref[0, head, :half, half:] = jnp.zeros((half, half), bf16)
        inv_ref[0, head, half:, :half] = corner
        inv_ref[0, head, half:, half:] = lower
    for head, (_, key, value, beta, entry, leave, through) in enumerate(held_heads):
        inverse = inv_ref[0, head]
        key_f = key.astype(f32)
        w_part = dot(inverse, (beta * entry * key_f).astype(bf16)).astype(bf16)
        u_part = dot(inverse, (beta * value.astype(f32)).astype(bf16))
        w_out_ref[0, head] = w_part
        u_ref[0, head] = u_part
        tail_key = (leave * key_f).astype(bf16)
        drop = dot_tn(tail_key, w_part)
        drop_ref[0, head] = drop
        drops[chunk, head] = drop.astype(bf16)
        adds[chunk, head] = dot_tn(tail_key, u_part.astype(bf16))
        throughs[chunk, head] = jnp.broadcast_to(through, (8, LANES))

    @pl.when(step == chunks - 1)
    def _():
        shape = (key_width, key_width + value_width)
        ident = jnp.where(lax.broadcasted_iota(jnp.int32, shape, 0) == lax.broadcasted_iota(jnp.int32, shape, 1), 1.0, 0.0)
        for head in range(heads):
            state[head] = ident

        def pass_on(at, carry):
            for head in range(heads):
                before = state[head]
                starts_ref[at, head] = before
                after = throughs[at, head][0:1, 0:1] * before - dot(drops[at, head], before.astype(bf16))
                state[head] = after + jnp.concatenate(
                    [jnp.zeros((key_width, key_width), f32), adds[at, head]], axis=1
                )
            return carry

        lax.fori_loop(0, chunks, pass_on, 0)
        for head in range(heads):
            map_ref[head] = state[head]
        if cube:
            groups, group = lax.axis_size("seq"), lax.axis_index("seq")

            def hand_on(by, target):
                slot = groups - 1 - by
                return pltpu.make_async_remote_copy(
                    going, coming.at[slot], map_sem.at[0, slot], map_sem.at[1, slot],
                    device_id={"seq": target}, device_id_type=MESH,
                )

            for head in range(heads):
                going[head] = state[head].astype(bf16)
            for by in range(groups - 1, 0, -1):
                @pl.when(group + by < groups)
                def _():
                    hand_on(by, group + by).start()

            for by in range(groups - 1, 0, -1):
                slot = groups - 1 - by

                @pl.when(group >= by)
                def _():
                    hand_on(by, group - by).wait_recv()
                    earlier_ref[slot] = coming[slot]

                @pl.when(group < by)
                def _():
                    earlier_ref[slot] = jnp.zeros(earlier_ref.shape[1:], bf16)

            for by in range(groups - 1, 0, -1):
                @pl.when(group + by < groups)
                def _():
                    hand_on(by, group + by).wait_send()

            rows_in.last()
            edges.end()
            for block in range(chunks):
                kept(block).wait()


def output_kernel(
    heads, key_width, value_width, docs, others, cube,
    meta, maps_ref, starts_ref, w_in_ref, u_ref, qkv_ref, scal_ref, gate_ref, gain_ref, w_output_ref,
    core_ref, gated_ref, fresh_ref, state_ref, mixed_ref,
    incoming, *refs,
):
    step = pl.program_id(0)
    chunk = cube_order("head", 7 - step) if cube else step
    qw = heads * key_width

    @pl.when(step == 0)
    def _():
        for head in range(heads):
            state = jnp.zeros((key_width, value_width), f32)
            for other in range(others):
                passing = maps_ref[other, head, :, :key_width]
                top, low = halves(state)
                state = dot(passing, top) + dot(passing, low) + maps_ref[other, head, :, key_width:].astype(f32)
            incoming[head] = state

    masks = Masks(meta, docs, chunk)
    scal = scal_ref[...]
    scal_t = scal.T
    gain = gain_ref[...]
    for head in range(heads):
        query = qkv_ref[:, head * key_width : (head + 1) * key_width]
        key = qkv_ref[:, qw + head * key_width : qw + (head + 1) * key_width]
        within, entry, leave, through = decays(masks, scal, scal_t, head)
        begun = starts_ref[0, head]
        state = dot_fine(begun[:, :key_width], incoming[head]) + begun[:, key_width:]
        state_ref[0, head] = state
        state_low = state.astype(bf16)
        fresh = (u_ref[0, head] - dot(w_in_ref[0, head], state_low)).astype(bf16)
        fresh_ref[0, head] = fresh
        scores = (dot_nt(query, key) * within).astype(bf16)
        core = dot((query.astype(f32) * entry).astype(bf16), state_low) + dot(scores, fresh)
        span = slice(head * value_width, (head + 1) * value_width)
        core_ref[:, span] = core
        scale = lax.rsqrt(jnp.mean(core * core, axis=1, keepdims=True) + epsilon)
        gate = gate_ref[:, span]
        gated_ref[:, span] = (core * scale * gain * (gate * sigmoid(gate))).astype(bf16)
    mixed = dot(gated_ref[...], w_output_ref[...])
    if not cube:
        mixed_ref[...] = mixed.astype(bf16)
        return

    scatter_block(step, CubeScatter("head", mixed_ref, *refs), mixed)


def core_grad_kernel(
    heads, key_width, value_width, docs, chunks,
    meta, grad_ref, w_output_ref, core_ref, gate_ref, gain_ref, qkv_ref, scal_ref, w_in_ref, drop_ref,
    grad_core_ref, inner_ref, pull_ref, grad_gate_ref, grad_gain_ref, total_ref, chunk=None, later=None,
):
    step = pl.program_id(0)
    chunk = chunks - 1 - step if chunk is None else chunk
    qw = heads * key_width
    masks = Masks(meta, docs, chunk)
    scal = scal_ref[...]
    scal_t = scal.T
    gain = gain_ref[...]

    @pl.when(step == 0)
    def _():
        grad_gain_ref[...] = jnp.zeros_like(grad_gain_ref)
        total_ref[...] = jnp.zeros_like(total_ref)

    grad_gated = dot_nt(grad_ref[...], w_output_ref[...])
    for head in range(heads):
        span = slice(head * value_width, (head + 1) * value_width)
        core = core_ref[:, span]
        gate = gate_ref[:, span]
        grad_in = grad_gated[:, span]
        scale = lax.rsqrt(jnp.mean(core * core, axis=1, keepdims=True) + epsilon)
        sigma = sigmoid(gate)
        normed = core * scale
        grad_gate_ref[:, span] = (
            grad_in * (normed * gain) * (sigma * (1.0 + gate * (1.0 - sigma)))
        ).astype(bf16)
        grad_normed = grad_in * (gate * sigma)
        weighted = grad_normed * gain
        grad_core = scale * (weighted - normed * jnp.mean(weighted * normed, axis=1, keepdims=True))
        grad_gain_ref[0:1, :] += jnp.sum(grad_normed * normed, axis=0, keepdims=True)
        grad_core = grad_core.astype(bf16)
        grad_core_ref[0, head] = grad_core
        query = qkv_ref[:, head * key_width : (head + 1) * key_width]
        key = qkv_ref[:, qw + head * key_width : qw + (head + 1) * key_width]
        within, entry, leave, through = decays(masks, scal, scal_t, head)
        scores = (dot_nt(query, key) * within).astype(bf16)
        inner = dot_tn(scores, grad_core)
        inner_ref[0, head] = inner
        pull = dot_tn((query.astype(f32) * entry).astype(bf16), grad_core) - dot_tn(
            w_in_ref[0, head], inner.astype(bf16)
        )
        pull_ref[0, head] = pull
        if later is not None:
            pulls, drops, throughs = later
            pulls[chunk, head] = pull
            drops[chunk, head] = drop_ref[0, head].astype(bf16)
            throughs[chunk, head] = jnp.broadcast_to(through, (8, LANES))
            continue
        total = total_ref[head]
        total_ref[head] = (
            through * total - dot_tn(drop_ref[0, head].astype(bf16), total.astype(bf16)) + pull
        )


def backward_kernel(
    heads, key_width, value_width, docs, chunks, others,
    meta, maps_ref, qkv_ref, act_ref, scal_ref, small_ref, inv_ref, fresh_ref, state_ref,
    grad_core_ref, inner_ref, pull_ref, drop_ref, dvec_ref,
    grad_conv_ref, grad_small_ref, sums_ref, edge_ref,
    carried, edge_out, edge_in, edge_sem,
):
    step = pl.program_id(0)
    chunk = chunks - 1 - step
    groups, group = lax.axis_size("seq"), lax.axis_index("seq")
    edge = pltpu.make_async_remote_copy(
        edge_out, edge_in, edge_sem.at[0], edge_sem.at[1],
        device_id={"seq": jnp.maximum(group - 1, 0)}, device_id_type=MESH,
    )

    @pl.when(step == 0)
    def _():
        line_barrier("seq")
    qw = heads * key_width

    @pl.when(step == 0)
    def _():
        sums_ref[...] = jnp.zeros_like(sums_ref)
        for head in range(heads):
            state = jnp.zeros((key_width, value_width), f32)
            for other in range(others):
                passing = maps_ref[other, head, :, :key_width]
                top, low = halves(state)
                state = dot_tn(passing, top) + dot_tn(passing, low) + maps_ref[other, head, :, key_width:].astype(f32)
            carried[head] = state

    masks = Masks(meta, docs, chunk)
    scal = scal_ref[...]
    scal_t = scal.T
    lane = lax.broadcasted_iota(jnp.int32, (BLOCK, LANES), 1)
    slopes = jnp.zeros((BLOCK, LANES), f32)
    tails = jnp.zeros((1, LANES), f32)
    betas = jnp.zeros((BLOCK, LANES), f32)
    for head in range(heads):
        q_span = slice(head * key_width, (head + 1) * key_width)
        k_span = slice(qw + head * key_width, qw + (head + 1) * key_width)
        v_span = slice(2 * qw + head * value_width, 2 * qw + (head + 1) * value_width)
        query, key, value = qkv_ref[:, q_span], qkv_ref[:, k_span], qkv_ref[:, v_span]
        query_f, key_f = query.astype(f32), key.astype(f32)
        within, entry, leave, through = decays(masks, scal, scal_t, head)
        beta = scal[:, heads + head : heads + head + 1]
        later = carried[head]
        later_low = later.astype(bf16)
        state = state_ref[0, head]
        state_low = state.astype(bf16)
        grad_core = grad_core_ref[0, head]
        fresh = fresh_ref[0, head]
        carried[head] = through * later - dot_tn(drop_ref[0, head].astype(bf16), later_low) + pull_ref[0, head]
        grad_fresh = inner_ref[0, head] + dot((leave * key_f).astype(bf16), later_low)
        grad_x = dot_tn(inv_ref[0, head], grad_fresh.astype(bf16))
        grad_x_low = grad_x.astype(bf16)
        grad_x_beta = beta * grad_x
        recalled = dot(key, state_low)
        grad_beta = jnp.sum(grad_x * (value.astype(f32) - entry * recalled), axis=1, keepdims=True)
        from_state_q = dot_nt(grad_core, state_low)
        from_state_k = dot_nt(grad_x_beta.astype(bf16), state_low)
        grad_scores = (dot_nt(grad_core, fresh) * within).astype(bf16)
        gram = dot_nt(key, key)
        grad_system = jnp.where(masks.strictly, dot_nt(grad_x_low, fresh) * within, 0.0)
        grad_beta = grad_beta - jnp.sum(grad_system * gram, axis=1, keepdims=True)
        grad_gram = (-beta * grad_system).astype(bf16)
        grad_query = dot(grad_scores, key) + entry * from_state_q
        grad_row = dot(grad_gram, key) - entry * from_state_k
        passed = leave * dot_nt(fresh, later_low)
        grad_col = dot_tn(grad_gram, key) + dot_tn(grad_scores, query) + passed
        slope = jnp.sum(query_f * grad_query + key_f * (grad_row - grad_col), axis=1, keepdims=True)
        kept = jnp.sum(jnp.sum(state * later, axis=1, keepdims=True), axis=0, keepdims=True)
        moved = jnp.sum(jnp.sum(key_f * passed, axis=1, keepdims=True), axis=0, keepdims=True)
        tail = through * kept + moved
        slopes = jnp.where(lane == head, slope, slopes)
        tails = jnp.where(lane[0:1, :] == head, tail, tails)
        betas = jnp.where(lane == heads + head, grad_beta, betas)

        conv_q, conv_k, conv_v = act_ref[:, q_span], act_ref[:, k_span], act_ref[:, v_span]
        for span, conv, grad, factor in (
            (q_span, conv_q, grad_query, key_width ** (-0.5)),
            (k_span, conv_k, grad_row + grad_col, 1.0),
        ):
            sigma = sigmoid(conv)
            act = conv * sigma
            norm = lax.rsqrt(jnp.sum(act * act, axis=1, keepdims=True) + epsilon)
            unit = act * norm
            grad_act = (factor * norm) * (grad - unit * jnp.sum(grad * unit, axis=1, keepdims=True))
            grad_conv_ref[:, span] = grad_act * (sigma * (1.0 + conv * (1.0 - sigma)))
        grad_conv_ref[:, v_span] = grad_x_beta * silu_slope(conv_v)

    grad_decay = jnp.where(lane < heads, exact_left(masks.upper, slopes) + tails, 0.0)
    shifted = small_ref[...] + dvec_ref[0:1, :]
    rate = dvec_ref[1:2, :]
    grad_z = grad_decay * rate * sigmoid(shifted)
    sums_ref[0:1, :] += jnp.sum(grad_z, axis=0, keepdims=True)
    sums_ref[1:2, :] += jnp.sum(grad_decay * (rate * softplus(shifted)), axis=0, keepdims=True)
    strength = sigmoid(small_ref[...])
    grad_small_ref[...] = jnp.where(lane < heads, grad_z, betas * strength * (1.0 - strength)).astype(bf16)

    @pl.when(step == chunks - 1)
    def _():
        edge_out[...] = grad_conv_ref[0:HALO, :]

        @pl.when(group > 0)
        def _():
            edge.start()

        @pl.when(group < groups - 1)
        def _():
            edge.wait_recv()
            edge_ref[...] = edge_in[...]

        @pl.when(group == groups - 1)
        def _():
            edge_ref[...] = jnp.zeros(edge_ref.shape, f32)

        @pl.when(group > 0)
        def _():
            edge.wait_send()


def projection_grad_kernel(
    mixed, docs, chunks, taps, cube,
    meta, grad_conv_ref, later_ref, edge_ref, pre_ref, grad_gate_ref, grad_small_ref, conv_ref, rows_ref,
    wq_ref, wk_ref, wv_ref, wg_ref, ws_ref,
    grad_pre_ref, grad_taps_ref, grad_rows_ref, gain_sum_ref,
    ext, *refs,
):
    step = pl.program_id(0)
    chunk = cube_order("head", 7 - step) if cube else step

    @pl.when(step == 0)
    def _():
        grad_taps_ref[...] = jnp.zeros_like(grad_taps_ref)
        gain_sum_ref[...] = jnp.zeros_like(gain_sum_ref)

    ext[0:BLOCK, :] = grad_conv_ref[...]

    @pl.when(chunk == chunks - 1)
    def _():
        ext[BLOCK : BLOCK + HALO, :] = edge_ref[...]

    @pl.when(chunk < chunks - 1)
    def _():
        ext[BLOCK : BLOCK + HALO, :] = later_ref[...]

    place = meta[0] + chunk * BLOCK + lax.broadcasted_iota(jnp.int32, (BLOCK, 1), 0)
    pre = pre_ref[...]
    total = jnp.zeros((BLOCK, mixed), f32)
    for lag in range(taps):
        keep = jnp.where(offset_of(meta, docs, place + lag) >= lag, 1.0, 0.0)
        moved = ext[lag : lag + BLOCK, :] * keep
        total = total + conv_ref[lag : lag + 1, :] * moved
        grad_taps_ref[lag : lag + 1, :] += jnp.sum(pre * moved, axis=0, keepdims=True)
    grad_pre_ref[:, :mixed] = total.astype(bf16)
    grad_pre_ref[:, mixed:] = grad_small_ref[...]
    grad = jnp.zeros(grad_rows_ref.shape, f32)
    begin = 0
    for ref in (wq_ref, wk_ref, wv_ref, ws_ref):
        grad = grad + dot_nt(grad_pre_ref[:, begin : begin + ref.shape[1]], ref[...])
        begin += ref.shape[1]
    grad = grad + dot_nt(grad_gate_ref[...], wg_ref[...])
    gain_sum_ref[0:1, :] += jnp.sum(grad * rows_ref[...].astype(f32), axis=0, keepdims=True)
    if cube:
        scatter_block(step, CubeScatter("head", grad_rows_ref, *refs), grad)
    else:
        grad_rows_ref[...] = grad.astype(bf16)


MESH = pl.DeviceIdType.MESH
ANYWHERE = pl.BlockSpec(memory_space=pl.ANY)


def line_barrier(axis, cube=None):
    devices, place = lax.axis_size(axis), lax.axis_index(axis)
    barrier = pltpu.get_barrier_semaphore()

    @pl.when(place > 0)
    def _():
        pl.semaphore_signal(barrier, inc=1, device_id={axis: place - 1}, device_id_type=MESH)

    @pl.when(place < devices - 1)
    def _():
        pl.semaphore_signal(barrier, inc=1, device_id={axis: place + 1}, device_id_type=MESH)

    more = 0
    if cube is not None:
        for mask in (1, 2, 4):
            pl.semaphore_signal(
                barrier, inc=1, device_id={cube: flip(lax.axis_index(cube), mask)}, device_id_type=MESH
            )
        more = 3

    @pl.when((place > 0) & (place < devices - 1))
    def _():
        pl.semaphore_wait(barrier, 2 + more)

    @pl.when((place == 0) | (place == devices - 1))
    def _():
        pl.semaphore_wait(barrier, 1 + more)


class LineSum:
    skew = 2
    window = 4

    def __init__(self, axis, counts, depths, parts, passed, arrived, sums, reduce_sems, back_sems):
        self.axis, self.counts, self.depths = axis, counts, depths
        self.parts, self.passed, self.arrived, self.sums = parts, passed, arrived, sums
        self.sems = (reduce_sems, back_sems)
        self.devices, self.place = lax.axis_size(axis), lax.axis_index(axis)
        self.steps = max(counts) + self.skew * (self.devices - 1)

    def rows_of(self, half, index, at):
        depth = self.depths[index]
        return pl.ds(pl.multiple_of((half * self.counts[index] + at) * depth, depth), depth)

    def copy(self, half, index, at, target, back):
        rows = self.rows_of(half, index, at)
        slot = half * self.counts[index] + at
        source, landing = (self.sums, self.sums) if back else (self.passed, self.arrived)
        sent, received = self.sems[back][2 * index], self.sems[back][2 * index + 1]
        return pltpu.make_async_remote_copy(
            source[index].at[rows, :], landing[index].at[rows, :], sent.at[slot], received.at[slot],
            device_id={self.axis: target}, device_id_type=MESH,
        )

    def send(self, half, index, at, target, back):
        @pl.when(at >= self.window)
        def _():
            self.copy(half, index, at - self.window, target, back).wait_send()

        self.copy(half, index, at, target, back).start()

    def each(self, handle):
        place, last = self.place, self.devices - 1
        for half in range(2):
            ends = (last, 0) if half == 0 else (0, last)
            toward = place - 1 if half == 0 else place + 1
            away = place + 1 if half == 0 else place - 1
            for index in range(len(self.counts)):
                handle(half, index, toward, away, place == ends[0], place == ends[1])

    def reduce(self, step):
        def handle(half, index, toward, away, begin, end):
            late = (self.devices - 1 - self.place) if half == 0 else self.place
            at = step - self.skew * late

            @pl.when((at >= 0) & (at < self.counts[index]))
            def _():
                rows = self.rows_of(half, index, at)

                @pl.when(begin)
                def _():
                    self.passed[index][rows, :] = self.parts[index][rows, :]
                    self.send(half, index, at, toward, 0)

                @pl.when(jnp.logical_not(begin))
                def _():
                    self.copy(half, index, at, toward, 0).wait_recv()
                    added = (
                        self.parts[index][rows, :].astype(f32) + self.arrived[index][rows, :].astype(f32)
                    ).astype(bf16)

                    @pl.when(jnp.logical_not(end))
                    def _():
                        self.passed[index][rows, :] = added
                        self.send(half, index, at, toward, 0)

                    @pl.when(end)
                    def _():
                        self.sums[index][rows, :] = added

        self.each(handle)

    def back(self, step, given=None):
        def handle(half, index, toward, away, begin, end):
            late = self.place if half == 0 else (self.devices - 1 - self.place)
            at = step - self.skew * late

            @pl.when((at >= 0) & (at < self.counts[index]))
            def _():
                if given is not None:
                    @pl.when(end)
                    def _():
                        rows = self.rows_of(half, index, at)
                        self.sums[index][rows, :] = given[index][rows, :]

                @pl.when(jnp.logical_not(end))
                def _():
                    self.copy(half, index, at, away, 1).wait_recv()

                @pl.when(jnp.logical_not(begin))
                def _():
                    self.send(half, index, at, away, 1)

        self.each(handle)

    def settle(self, back):
        def handle(half, index, toward, away, begin, end):
            count = self.counts[index]
            for at in range(max(count - self.window, 0), count):
                @pl.when(jnp.logical_not(begin if back else end))
                def _():
                    self.copy(half, index, at, away if back else toward, back).wait_send()

        self.each(handle)


def line_sum_kernel(axis, cube, counts, depths, *refs):
    total = len(counts)
    rows_ref, grads_ref, *refs = refs
    parts, sums, refs = refs[: total - 1], refs[total - 1 : 2 * total - 1], refs[2 * total - 1 :]
    if cube:
        whole_ref, refs = refs[0], refs[1:]
    product, *refs = refs
    parts = (product, *parts)
    arrived, passed, refs = refs[:total], refs[total : 2 * total], refs[2 * total :]
    share = BLOCK // depths[0]
    tiles = counts[0] // share
    line = LineSum(axis, counts, depths, parts, passed, arrived, sums, refs[: 2 * total], refs[2 * total : 4 * total])
    line_barrier(axis, "head" if cube else None)

    begin = max(counts)
    final = CubeTotal(*refs[4 * total :]) if cube else None

    def step_on(step, carry):
        @pl.when((step % share == 0) & (step < tiles * share))
        def _():
            for half in range(2):
                columns = pl.ds(pl.multiple_of((half * tiles + step // share) * BLOCK, BLOCK), BLOCK)
                product[columns, :] = dot_tn(rows_ref[:, columns], grads_ref[...]).astype(bf16)

        @pl.when(step < line.steps)
        def _():
            line.reduce(step)

        @pl.when(step >= begin)
        def _():
            line.back(step - begin)

        if cube:
            after = begin + line.skew * line.devices
            for stage in range(4):
                @pl.when(step == after + 3 * stage)
                def _():
                    if stage:
                        final.end(stage - 1, whole_ref)
                    else:
                        final.held[0] = sums[-1][: whole_ref.shape[0], :].astype(f32)
                    if stage < 3:
                        final.copy(stage).start()

        return carry

    lax.fori_loop(0, begin + line.steps, step_on, 0)
    line.settle(0)
    line.settle(1)


class CubeTotal:
    def __init__(self, held, arrived, send_sem, recv_sem):
        self.held, self.arrived, self.send_sem, self.recv_sem = held, arrived, send_sem, recv_sem

    def copy(self, stage):
        return pltpu.make_async_remote_copy(
            self.held.at[stage], self.arrived.at[stage], self.send_sem.at[stage], self.recv_sem.at[stage],
            device_id={"head": flip(lax.axis_index("head"), (1, 2, 4)[stage])}, device_id_type=MESH,
        )

    def end(self, stage, total_ref):
        self.copy(stage).wait()
        if stage < 2:
            self.held[stage + 1] = self.held[stage] + self.arrived[stage]
        else:
            total_ref[...] = self.held[stage] + self.arrived[stage]


def line_scratch(arrays, depths, moves):
    counts = tuple(array.shape[0] // (2 * depth) for array, depth in zip(arrays, depths))
    semaphores = []
    for count in counts:
        semaphores += [pltpu.SemaphoreType.DMA((2 * count,))] * 2
    return counts, semaphores * moves


def line_sum(rows, grads, given, depths, axis, collective_id):
    cube = lax.axis_size("head") == 8
    arrays = (struct((rows.shape[1], grads.shape[1]), bf16), *given)
    counts, semaphores = line_scratch(arrays, depths, 2)
    vmem = pl.BlockSpec(memory_space=pltpu.VMEM)
    scratch = [pltpu.VMEM(array.shape, bf16) for array in (arrays[0], *arrays, *arrays)] + semaphores
    total = (8, arrays[-1].shape[1])
    if cube:
        scratch += [pltpu.VMEM((3,) + total, f32)] * 2 + [pltpu.SemaphoreType.DMA((3,))] * 2
    results = pl.pallas_call(
        functools.partial(line_sum_kernel, axis, cube, counts, tuple(depths)),
        in_specs=[vmem] * (len(arrays) + 1),
        out_specs=[vmem] * (len(arrays) + cube),
        out_shape=[struct(array.shape, bf16) for array in arrays] + [struct(total, f32)] * cube,
        scratch_shapes=scratch,
        compiler_params=pltpu.CompilerParams(
            collective_id=collective_id, has_side_effects=True, vmem_limit_bytes=VMEM_LIMIT
        ),
        cost_estimate=pl.CostEstimate(flops=10**8, bytes_accessed=40 * 10**6, transcendentals=0),
        name="line_sum",
    )(rows, grads, *given)
    if not cube:
        results = [*results, lax.psum(results[-1][:8].astype(f32), "head")]
    return results


def whole(shape):
    zeros = (0,) * len(shape)
    return pl.BlockSpec(tuple(shape), lambda step: zeros)


def held(shape):
    zeros = (0,) * len(shape)
    return pl.BlockSpec(tuple(shape), lambda step: zeros, pipeline_mode=pl.Buffered(1))


def by_rows(width, chunks=None):
    if chunks is None:
        return pl.BlockSpec((BLOCK, width), lambda step: (step, 0))
    return pl.BlockSpec((BLOCK, width), lambda step: (chunks - 1 - step, 0))


def by_chunk(shape, chunks=None):
    rest = (0,) * len(shape)
    if chunks is None:
        return pl.BlockSpec((1,) + tuple(shape), lambda step: (step,) + rest)
    return pl.BlockSpec((1,) + tuple(shape), lambda step: (chunks - 1 - step,) + rest)


SCALARS = pl.BlockSpec(memory_space=pltpu.SMEM)


def feed_kernel(
    axis, devices, rows,
    own_ref, *refs,
):
    given, kept, refs = refs[:4], refs[4:9], refs[9:]
    total_ref, *refs = refs
    hidden_ref, *refs = refs
    inside, refs = refs[:8], refs[8:]
    inside = (*inside, inside[0])
    grads_ref, w_gate_ref, w_up_ref, w_down_ref = inside[:4]
    blocks_ref, turned_ref, grad_gate_ref, grad_up_ref, part_ref = inside[4:]
    parts, arrived, gather_send, gather_recv, chain_send, chain_recv, load_sem, store_sem = refs
    place = lax.axis_index(axis)
    piece = rows // 2

    def load(index):
        return pltpu.make_async_copy(given[index], inside[index], load_sem.at[index])

    def store(index):
        return pltpu.make_async_copy(inside[4 + index], kept[index], store_sem.at[index])

    for index in (3, 0, 1, 2):
        load(index).start()
    line_barrier(axis)

    def span(block, half):
        return pl.ds(pl.multiple_of(block * rows + half * piece, piece), piece)

    def full(block):
        return pl.ds(pl.multiple_of(block * rows, rows), rows)

    def gather(owner, hop, way, half):
        target = place + 1 - 2 * way
        slot = (hop * 2 + way) * 2 + half
        return pltpu.make_async_remote_copy(
            blocks_ref.at[span(owner, half), :], blocks_ref.at[span(owner, half), :],
            gather_send.at[slot], gather_recv.at[slot], device_id={axis: target}, device_id_type=MESH,
        )

    def quarter(block, part):
        return pl.ds(pl.multiple_of(block * rows + part * (rows // 4), rows // 4), rows // 4)

    def chain(block, way, part, at):
        target = at + 1 - 2 * way
        landing = jnp.where((block == target) & (way == 0), devices, block)
        slot = (way * devices + block) * 4 + part
        return pltpu.make_async_remote_copy(
            parts.at[quarter(block, part), :], arrived.at[quarter(landing, part), :],
            chain_send.at[slot], chain_recv.at[slot], device_id={axis: target}, device_id_type=MESH,
        )

    blocks_ref[full(place), :] = own_ref[...]

    def event(step, carry):
        hop = (step + 1) // 2
        way = (step + 1) % 2
        owner = jnp.where(way == 0, place - hop, place + hop)

        @pl.when(step == 0)
        def _():
            for side in range(2):
                @pl.when((place + 1 - 2 * side >= 0) & (place + 1 - 2 * side < devices))
                def _():
                    for half in range(2):
                        gather(place, 0, side, half).start()

            for index in range(4):
                load(index).wait()

        @pl.when((step > 0) & (way == 0))
        def _():
            for side in range(2):
                come = place - hop if side == 0 else place + hop
                goes = place + 1 if side == 0 else place - 1

                @pl.when((come >= 0) & (come < devices))
                def _():
                    for half in range(2):
                        gather(come, hop - 1, side, half).wait_recv()

                        @pl.when((goes >= 0) & (goes < devices))
                        def _():
                            gather(come, hop, side, half).start()

        @pl.when((owner >= 0) & (owner < devices))
        def _():
            here = full(owner)
            grad_hidden = dot_nt(grads_ref[here, :], w_down_ref[...])

            block = blocks_ref[here, :]
            gate_pre = dot(block, w_gate_ref[...])
            up_pre = dot(block, w_up_ref[...])
            sigma = sigmoid(gate_pre)
            act = gate_pre * sigma
            hidden = (act * up_pre).astype(bf16)
            hidden_ref[here, :] = hidden
            turned_ref[:, full(owner)] = hidden.T
            grad_gate_ref[here, :] = (grad_hidden * up_pre * (sigma * (1.0 + gate_pre * (1.0 - sigma)))).astype(bf16)
            grad_up_ref[here, :] = (grad_hidden * act).astype(bf16)
            grad = dot_nt(grad_gate_ref[here, :], w_gate_ref[...]) + dot_nt(grad_up_ref[here, :], w_up_ref[...])

            @pl.when(step == 0)
            def _():
                total_ref[...] = grad

            @pl.when(step > 0)
            def _():
                parts[here, :] = grad.astype(bf16)

        @pl.when((way == 1) & (step > 0))
        def _():
            for turn in range(2):
                side = jnp.where(2 * place < devices, turn, 1 - turn)
                block = jnp.where(side == 1, devices - 1 - hop, hop)
                begins = place == jnp.where(side == 1, devices - 1, 0)
                valid = jnp.where(side == 1, block < place, block > place)

                @pl.when(valid)
                def _():
                    for part in range(4):
                        @pl.when(jnp.logical_not(begins))
                        def _():
                            chain(block, side, part, place + 2 * side - 1).wait_recv()
                            at = quarter(block, part)
                            parts[at, :] = (parts[at, :].astype(f32) + arrived[at, :].astype(f32)).astype(bf16)

                        chain(block, side, part, place).start()

        return carry

    lax.fori_loop(0, 2 * devices - 1, event, 0)

    for index in range(4):
        store(index).start()

    def feed_part(block, carry):
        part_ref[full(block), :] = dot(hidden_ref[full(block), :], w_down_ref[...]).astype(bf16)
        return carry

    lax.fori_loop(0, devices, feed_part, 0)
    store(4).start()

    for side, landing, comes in ((1, place, place < devices - 1), (0, devices, place > 0)):
        @pl.when(comes)
        def _():
            for part in range(4):
                chain(place, side, part, place + 2 * side - 1).wait_recv()
                at = pl.ds(part * (rows // 4), rows // 4)
                total_ref[at, :] += arrived[quarter(landing, part), :].astype(f32)

    def gather_end(step, carry):
        hop = step // 2
        way = step % 2
        owner = jnp.where(way == 0, place - hop, place + hop)
        target = place + 1 - 2 * way

        @pl.when((owner >= 0) & (owner < devices) & (target >= 0) & (target < devices))
        def _():
            for half in range(2):
                gather(owner, hop, way, half).wait_send()

        return carry

    lax.fori_loop(0, 2 * (devices - 1), gather_end, 0)

    def chain_end(block, carry):
        @pl.when(block < place)
        def _():
            for part in range(4):
                chain(block, 1, part, place).wait_send()

        @pl.when(block > place)
        def _():
            for part in range(4):
                chain(block, 0, part, place).wait_send()

        return carry

    lax.fori_loop(0, devices, chain_end, 0)
    for index in range(5):
        store(index).wait()


def feed(own, grads, w_gate, w_up, w_down, axis, collective_id):
    devices = lax.axis_size(axis)
    rows, width = own.shape
    units = w_gate.shape[1]
    vmem = pl.BlockSpec(memory_space=pltpu.VMEM)
    moves = pltpu.SemaphoreType.DMA((4 * devices,))
    chains = pltpu.SemaphoreType.DMA((8 * devices,))
    given = (grads, w_gate, w_up, w_down)
    kept = [struct((devices * rows, width), bf16), struct((units, devices * rows), bf16)]
    kept += [struct((devices * rows, units), bf16)] * 2
    kept += [struct((devices * rows, width), bf16)]
    return pl.pallas_call(
        functools.partial(feed_kernel, axis, devices, rows),
        in_specs=[vmem] + [ANYWHERE] * 4,
        out_specs=[ANYWHERE] * 5 + [vmem],
        out_shape=kept + [struct((rows, width), f32)],
        scratch_shapes=[
            pltpu.VMEM((devices * rows, units), bf16),
            *(pltpu.VMEM(array.shape, array.dtype) for array in (*given, *kept[:4])),
            pltpu.VMEM((devices * rows, width), bf16), pltpu.VMEM(((devices + 1) * rows, width), bf16),
            moves, moves, chains, chains, pltpu.SemaphoreType.DMA((4,)), pltpu.SemaphoreType.DMA((5,)),
        ],
        compiler_params=pltpu.CompilerParams(
            collective_id=collective_id, has_side_effects=True, vmem_limit_bytes=61 * 1024 * 1024
        ),
        name="feed",
    )(own, grads, w_gate, w_up, w_down)


def flip(index, mask):
    for bit in (1, 2, 4):
        if mask & bit:
            index = index + bit * (1 - 2 * ((index // bit) % 2))
    return index


def cube_barrier(axis, place):
    barrier = pltpu.get_barrier_semaphore()
    for mask in (1, 2, 4):
        pl.semaphore_signal(barrier, inc=1, device_id={axis: flip(place, mask)}, device_id_type=MESH)
    pl.semaphore_wait(barrier, 3)


class CubeGather:
    FIRST = ((0, 0, 2), (0, 1, 4), (0, 1, 2), (0, 0, 4), (0, 0, 1), (0, 1, 1))
    SECOND = ((2, 0, 4), (4, 1, 2), (2, 0, 1), (4, 1, 1))
    THIRD = ((2, 1, 1), (4, 0, 1))
    FOURTH = ((6, 0, 1), (6, 1, 1))

    def __init__(self, axis, own_ref, all_ref, own_sem, send_sem, recv_sem, stride=None, lead=0):
        self.axis, self.own_ref, self.all_ref = axis, own_ref, all_ref
        self.stride, self.lead = stride or own_ref.shape[0], lead
        self.own_sem, self.send_sem, self.recv_sem = own_sem, send_sem, recv_sem
        self.place = lax.axis_index(axis)
        self.rows = own_ref.shape[0]
        self.piece = self.rows // 2

    def part(self, mask, half):
        start = flip(self.place, mask) * self.stride + self.lead + half * self.piece
        return self.all_ref.at[pl.ds(pl.multiple_of(start, LEAD), self.piece), :]

    def copy(self, mask, half, toward):
        source = self.part(mask, half) if mask else self.own_ref.at[pl.ds(half * self.piece, self.piece), :]
        return pltpu.make_async_remote_copy(
            source, self.part(mask, half),
            self.send_sem.at[toward * 2 + half, mask // 2], self.recv_sem.at[(mask ^ toward) * 2 + half],
            device_id={self.axis: flip(self.place, toward)}, device_id_type=MESH,
        )

    def wait(self, mask, half):
        pltpu.make_async_remote_copy(
            self.part(mask, half), self.part(mask, half), self.send_sem.at[0, 0], self.recv_sem.at[mask * 2 + half],
            device_id={self.axis: flip(self.place, 1)}, device_id_type=MESH,
        ).wait_recv()

    def own(self):
        start = pl.multiple_of(self.place * self.rows, self.rows)
        return pltpu.make_async_copy(self.own_ref, self.all_ref.at[pl.ds(start, self.rows), :], self.own_sem)

    def first(self):
        if self.own_sem is not None:
            cube_barrier(self.axis, self.place)
            self.own().start()
        for move in self.FIRST:
            self.copy(*move).start()

    def second(self):
        self.wait(2, 0)
        self.copy(*self.SECOND[0]).start()
        self.wait(4, 1)
        for move in self.SECOND[1:]:
            self.copy(*move).start()

    def third(self):
        for move in self.THIRD:
            self.wait(*move[:2])
            self.copy(*move).start()

    def fourth(self):
        for move in self.FOURTH:
            self.wait(*move[:2])
            self.copy(*move).start()

    def last(self):
        if self.own_sem is not None:
            for mask in (1, 3, 5, 7):
                for half in range(2):
                    self.wait(mask, half)
            self.own().wait()
        for move in self.FIRST + self.SECOND + self.THIRD + self.FOURTH:
            self.copy(*move).wait_send()


CUBE_SEMAPHORES = [pltpu.SemaphoreType.DMA, pltpu.SemaphoreType.DMA((10, 4)), pltpu.SemaphoreType.DMA((16,))]


def feed_grads_kernel(
    blocks_ref, grads_ref, hidden_ref, grad_gate_ref, grad_up_ref, down_ref, gate_ref, up_ref,
):
    gate_ref[...] = dot_tn(blocks_ref[...], grad_gate_ref[...]).astype(bf16)
    up_ref[...] = dot_tn(blocks_ref[...], grad_up_ref[...]).astype(bf16)
    down_ref[...] = dot(hidden_ref[...], grads_ref[...]).astype(bf16)


def feed_grads(own, blocks, grads, hidden, grad_gate, grad_up, axis):
    rows, width = blocks.shape
    units = hidden.shape[0]
    tall = pl.BlockSpec((rows, BLOCK), lambda step: (0, step))
    down = pl.BlockSpec((units, BLOCK), lambda step: (0, step))
    flat = pl.BlockSpec((BLOCK, units), lambda step: (step, 0))
    fixed = held((rows, units))
    results = pl.pallas_call(
        feed_grads_kernel,
        grid=(width // BLOCK,),
        in_specs=[tall, tall, held(hidden.shape), fixed, fixed],
        out_specs=[down, flat, flat],
        out_shape=[
            struct((units, width), bf16), struct((width, units), bf16), struct((width, units), bf16),
        ],
        compiler_params=params(),
        name="feed_grads",
    )(blocks, grads, hidden, grad_gate, grad_up)
    return (*results, lax.all_gather(own, axis, axis=0, tiled=True))


def feed_core_kernel(
    sizes, chunks, axis, tiles,
    meta, own_ref, blocks_ref, grads_ref, hidden_ref, feed_gate_ref, feed_up_ref,
    w_output_ref, core_ref, gate_ref, gain_ref, qkv_ref, scal_ref, w_in_ref, drop_ref,
    down_out, gate_out, up_out, all_ref, *refs,
):
    outs, (rows_ref, copy_sem, send_sem, recv_sem, *later) = refs[:6], refs[6:]
    step = pl.program_id(0)
    gather = CubeGather(axis, own_ref, rows_ref, None, send_sem, recv_sem)
    rows = own_ref.shape[0]

    @pl.when(step == 0)
    def _():
        cube_barrier(axis, gather.place)
        gather.first()
        rows_ref[pl.ds(pl.multiple_of(gather.place * rows, rows), rows), :] = own_ref[...]

    @pl.when(step == tiles - 1)
    def _():
        gather.second()
        gather.third()

    @pl.when(step == tiles + 3)
    def _():
        gather.fourth()

    for mask in (1, 3, 5, 7):
        @pl.when(step == (1 if mask == 1 else tiles + mask))
        def _():
            for half in range(2):
                gather.wait(mask, half)

    @pl.when((step >= 2) & (step < tiles + 2))
    def _():
        turned = blocks_ref[...].T
        gate_out[...] = dot(turned, feed_gate_ref[...]).astype(bf16)
        up_out[...] = dot(turned, feed_up_ref[...]).astype(bf16)
        down_out[...] = dot(hidden_ref[...], grads_ref[...]).astype(bf16)

    @pl.when((step < 2) | (step >= tiles + 2))
    def _():
        chunk = core_order(axis, step, tiles)
        core_grad_kernel(
            *sizes, chunks,
            meta, rows_ref.at[pl.ds(pl.multiple_of(chunk * BLOCK, BLOCK), BLOCK), :], w_output_ref,
            core_ref, gate_ref, gain_ref, qkv_ref, scal_ref, w_in_ref, drop_ref, *outs, chunk=chunk, later=later,
        )

    @pl.when(step == tiles + chunks - 1)
    def _():
        kept = pltpu.make_async_copy(rows_ref, all_ref, copy_sem)
        kept.start()
        total_ref = outs[5]
        pulls, drops, throughs = later

        def pass_on(at, carry):
            chunk = chunks - 1 - at
            for head in range(sizes[0]):
                total = total_ref[head]
                total_ref[head] = (
                    throughs[chunk, head][0:1, 0:1] * total
                    - dot_tn(drops[chunk, head], total.astype(bf16)) + pulls[chunk, head]
                )
            return carry

        lax.fori_loop(0, chunks, pass_on, 0)
        gather.last()
        kept.wait()


def core_order(axis, step, tiles):
    return cube_order(axis, jnp.where(step < 2, step, jnp.maximum(step - tiles, 1)))


class CubeScatter:
    def __init__(self, axis, total_ref, given, other, leaving, coming, waiting, send_sem, recv_sem):
        self.axis, self.total_ref = axis, total_ref
        self.given, self.other, self.leaving, self.coming, self.waiting = given, other, leaving, coming, waiting
        self.send_sem, self.recv_sem = send_sem, recv_sem
        self.place = lax.axis_index(axis)
        self.piece = total_ref.shape[0] // 2

    def slot(self, index, half):
        return pl.ds((2 * index + half) * self.piece, self.piece)

    def core_copy(self, mask, half):
        at = self.slot(mask // 2, half)
        return pltpu.make_async_remote_copy(
            self.given.at[at, :], self.other.at[at, :],
            self.send_sem.at[0, mask // 2, half], self.recv_sem.at[0, mask // 2, half],
            device_id={self.axis: flip(self.place, 1)}, device_id_type=MESH,
        )

    def landing(self, index, toward):
        return (toward // 2 - 1) * 2 + (1 if index else 0)

    def chip_copy(self, index, half, toward):
        return pltpu.make_async_remote_copy(
            self.leaving.at[self.slot(index, half), :],
            self.coming.at[self.slot(self.landing(index, toward), half), :],
            self.send_sem.at[toward // 2, index, half], self.recv_sem.at[toward // 2, 1 if index else 0, half],
            device_id={self.axis: flip(self.place, toward)}, device_id_type=MESH,
        )

    def arrived(self, index, half, toward):
        self.chip_copy(index, half, toward).wait_recv()
        return self.coming[self.slot(self.landing(index, toward), half), :].astype(f32)

    def send(self, index, half, toward, values):
        self.leaving[self.slot(index, half), :] = values.astype(bf16)
        self.chip_copy(index, half, toward).start()

    def take(self, mask, block):
        piece = self.piece
        if mask % 2:
            self.given[pl.ds(mask // 2 * 2 * piece, 2 * piece), :] = block.astype(bf16)
            for half in range(2):
                self.core_copy(mask, half).start()
            return
        parts = []
        for half in range(2):
            self.core_copy(mask + 1, half).wait_recv()
            parts.append(
                block[half * piece : (half + 1) * piece, :]
                + self.other[self.slot(mask // 2, half), :].astype(f32)
            )
        if mask == 6:
            self.send(0, 0, 2, parts[0])
            self.send(0, 1, 4, parts[1])
        elif mask == 4:
            self.send(2, 1, 4, parts[1])
            self.waiting[0] = parts[0]
        elif mask == 2:
            self.send(1, 0, 2, parts[0])
            self.waiting[1] = parts[1]
        else:
            self.total_ref[0:piece, :] = parts[0]
            self.total_ref[piece:, :] = parts[1]

    def finish(self):
        piece = self.piece
        self.send(2, 0, 4, self.waiting[0] + self.arrived(0, 0, 2))
        self.send(1, 1, 2, self.waiting[1] + self.arrived(0, 1, 4))
        self.total_ref[0:piece, :] += self.arrived(1, 0, 2)
        self.total_ref[piece:, :] += self.arrived(2, 1, 4)
        self.total_ref[0:piece, :] += self.arrived(2, 0, 4)
        self.total_ref[piece:, :] += self.arrived(1, 1, 2)
        for mask in (7, 5, 3, 1):
            for half in range(2):
                self.core_copy(mask, half).wait_send()
        for index, half, toward in ((0, 0, 2), (0, 1, 4), (1, 0, 2), (2, 1, 4), (1, 1, 2), (2, 0, 4)):
            self.chip_copy(index, half, toward).wait_send()


def scatter_block(step, scatter, block):
    @pl.when(step == 0)
    def _():
        cube_barrier("head", scatter.place)

    for mask in range(8):
        @pl.when(step == 7 - mask)
        def _():
            scatter.take(mask, block)

    @pl.when(step == 7)
    def _():
        scatter.finish()


def cube_scatter_scratch(rows, width):
    return [
        pltpu.VMEM((4 * rows, width), bf16), pltpu.VMEM((4 * rows, width), bf16),
        pltpu.VMEM((3 * rows, width), bf16), pltpu.VMEM((4 * rows, width), bf16),
        pltpu.VMEM((2, rows // 2, width), f32),
        pltpu.SemaphoreType.DMA((3, 4, 2)), pltpu.SemaphoreType.DMA((3, 4, 2)),
    ]


def params(collective_id=None):
    return pltpu.CompilerParams(
        dimension_semantics=("arbitrary",),
        vmem_limit_bytes=VMEM_LIMIT,
        collective_id=collective_id,
        has_side_effects=collective_id is not None,
    )


def widen_kernel(cuts, total, *refs):
    given, refs = refs[:total], refs[total:]
    if cuts:
        all_in, *refs = refs
        begin = 0
        for cut, result in zip(cuts, refs):
            result[...] = all_in[:, begin : begin + cut].astype(f32)
            begin += cut
        refs = refs[len(cuts) :]
        refs[-1][...] = all_in[:, begin:].astype(f32).T
    for source, result in zip(given, refs):
        result[...] = source[...].astype(f32)


def widen(given, columns=None, cuts=()):
    steps = 8 if given[0].shape[0] % 128 == 0 else 4
    sources = list(given)
    shapes = [array.shape for array in given]

    def part(shape):
        return pl.BlockSpec((shape[0] // steps, shape[1]), lambda step: (step, 0))

    specs = [part(shape) for shape in shapes]
    if cuts:
        sources.append(columns)
        rows, width = columns.shape
        rest = width - sum(cuts)
        cut_shapes = [(rows, cut) for cut in cuts]
        specs = [part(shape) for shape in cut_shapes] + specs
        specs.append(pl.BlockSpec((rest, rows // steps), lambda step: (0, step)))
        shapes = cut_shapes + shapes + [(rest, rows)]
    return pl.pallas_call(
        functools.partial(widen_kernel, cuts, len(given)),
        grid=(steps,),
        in_specs=[part(array.shape) for array in sources],
        out_specs=specs,
        out_shape=[struct(shape, f32) for shape in shapes],
        compiler_params=params(),
        name="widen",
    )(*sources)


def struct(shape, dtype):
    return jax.ShapeDtypeStruct(tuple(shape), dtype)


def from_earlier(array, axis):
    devices = lax.axis_size(axis)
    parts = [
        lax.ppermute(array, axis, [(i, i + by) for i in range(devices - by)])
        for by in range(devices - 1, 0, -1)
    ]
    return jnp.stack(parts) if parts else jnp.zeros((1,) + array.shape, array.dtype)


def from_later(array, axis):
    devices = lax.axis_size(axis)
    parts = [
        lax.ppermute(array, axis, [(i + by, i) for i in range(devices - by)])
        for by in range(devices - 1, 0, -1)
    ]
    return jnp.stack(parts) if parts else jnp.zeros((1,) + array.shape, array.dtype)


def shards(
    inputs,
    doc_lengths,
    first_gain,
    w_query,
    w_key,
    w_value,
    w_outgate,
    w_decay,
    w_beta,
    conv_query,
    conv_key,
    conv_value,
    decay_log,
    decay_bias,
    head_gain,
    w_output,
    second_gain,
    w_gate,
    w_up,
    w_down,
    cotangent,
):
    row_count, model_width = inputs.shape
    heads = decay_log.shape[0]
    qw, vw = w_query.shape[1], w_value.shape[1]
    key_width, value_width = qw // heads, vw // heads
    mixed_width = 2 * qw + vw
    taps = conv_query.shape[0]
    docs = doc_lengths.shape[0]
    seq_index = lax.axis_index("seq")
    head_index = lax.axis_index("head")
    head_total = lax.axis_size("head")
    seq_rows = row_count * head_total
    chunks = seq_rows // BLOCK
    others = max(lax.axis_size("seq") - 1, 1)
    sizes = (heads, key_width, value_width, docs)

    inputs_f = inputs.astype(f32)
    normed = rms_scale(inputs_f, first_gain).astype(bf16)
    meta = jnp.concatenate(
        [(seq_index * seq_rows).astype(jnp.int32)[None], slot_starts(doc_lengths)]
    )
    _, own_valid = layout(doc_lengths, (seq_index * head_total + head_index) * row_count, row_count)

    grad_out = cotangent.astype(f32) * own_valid.astype(f32)[:, None]
    grad_low = grad_out.astype(bf16)
    w_small = jnp.concatenate([w_decay, w_beta, jnp.zeros((model_width, LANES - 2 * heads), bf16)], axis=1)
    weights = (w_query, w_key, w_value, w_outgate, w_small)
    all_width = mixed_width + LANES
    conv_all = jnp.concatenate([conv_query, conv_key, conv_value], axis=1)
    dvec = jnp.zeros((8, LANES), f32)
    dvec = dvec.at[0, :heads].set(decay_bias).at[1, :heads].set(-jnp.exp(decay_log))
    map_shape = (heads, key_width, key_width + value_width)

    cube = head_total == 8 and chunks == 8 and row_count == BLOCK
    if cube:
        rows_given, rows_spec = normed, held(normed.shape)

        def at_step(step):
            return cube_order("head", step)
    else:
        block_rows = lax.all_gather(normed, "head", axis=0, tiled=True)
        tail = from_previous(block_rows[seq_rows - LEAD :])
        blocks = block_rows.reshape(chunks, BLOCK, model_width)
        leads = jnp.concatenate([tail[None], blocks[:-1, BLOCK - LEAD :]], axis=0)
        rows_given = jnp.concatenate([leads, blocks], axis=1).reshape(chunks * STRIDE, model_width)
        rows_spec = pl.BlockSpec((STRIDE, model_width), lambda step: (step, 0))

        def at_step(step):
            return step

    def rows_out(width):
        return pl.BlockSpec((BLOCK, width), lambda step: (at_step(step), 0))

    def chunk_out(shape):
        return pl.BlockSpec((1,) + tuple(shape), lambda step: (at_step(step),) + (0,) * len(shape))

    results = pl.pallas_call(
        functools.partial(forward_kernel, *sizes, taps, chunks, cube),
        grid=(chunks,),
        in_specs=[
            SCALARS, rows_spec, *(held(weight.shape) for weight in weights), whole(conv_all.shape),
            whole(dvec.shape),
        ],
        out_specs=[
            rows_out(mixed_width), rows_out(mixed_width), rows_out(vw), rows_out(LANES), rows_out(LANES),
            rows_out(mixed_width),
            chunk_out((heads, BLOCK, BLOCK)), chunk_out((heads, BLOCK, key_width)),
            chunk_out((heads, BLOCK, value_width)), chunk_out((heads, key_width, key_width)),
            whole((chunks,) + map_shape), whole(map_shape),
        ] + [ANYWHERE, whole((others,) + map_shape)] * cube,
        out_shape=[
            struct((seq_rows, mixed_width), f32), struct((seq_rows, mixed_width), f32),
            struct((seq_rows, vw), f32), struct((seq_rows, LANES), f32), struct((seq_rows, LANES), f32),
            struct((seq_rows, mixed_width), bf16),
            struct((chunks, heads, BLOCK, BLOCK), bf16), struct((chunks, heads, BLOCK, key_width), bf16),
            struct((chunks, heads, BLOCK, value_width), f32),
            struct((chunks, heads, key_width, key_width), f32),
            struct((chunks,) + map_shape, f32), struct(map_shape, f32),
        ] + [struct((seq_rows, model_width), bf16), struct((others,) + map_shape, bf16)] * cube,
        scratch_shapes=[
            pltpu.VMEM((STRIDE, mixed_width), f32), pltpu.VMEM(map_shape, f32),
            pltpu.VMEM((chunks, heads, key_width, key_width), bf16),
            pltpu.VMEM((chunks, heads, key_width, value_width), f32),
            pltpu.VMEM((chunks, heads, 8, LANES), f32),
        ] + [
            pltpu.VMEM((chunks * STRIDE, model_width), bf16), pltpu.SemaphoreType.DMA((chunks,)),
            pltpu.VMEM((LEAD, model_width), bf16), pltpu.SemaphoreType.DMA((2,)),
            pltpu.SemaphoreType.DMA((8,)), pltpu.SemaphoreType.DMA((8,)), *CUBE_SEMAPHORES[1:],
            pltpu.VMEM(map_shape, bf16), pltpu.VMEM((others,) + map_shape, bf16),
            pltpu.SemaphoreType.DMA((2, others)),
        ] * cube,
        compiler_params=params(2 if cube else None),
        name="mixer_forward",
    )(meta, rows_given, *weights, conv_all, dvec)
    (pre, conv, gate, small, scal, qkv, inverse, w_part, u_part, drop, starts, block_map) = results[:12]
    if cube:
        block_rows, earlier = results[12:]
    else:
        earlier = from_earlier(block_map.astype(bf16), "seq")

    grad_block_two = lax.all_gather(grad_low, "seq", axis=0, tiled=True)
    gain_row = head_gain[None, :]
    def last_first(step):
        return cube_order("head", 7 - step) if cube else step

    def rows_back(width):
        return pl.BlockSpec((BLOCK, width), lambda step: (last_first(step), 0))

    def chunk_back(shape):
        return pl.BlockSpec((1,) + tuple(shape), lambda step: (last_first(step),) + (0,) * len(shape))

    core, gated, fresh, states, mixed_part = pl.pallas_call(
        functools.partial(output_kernel, *sizes, others, cube),
        grid=(chunks,),
        in_specs=[
            SCALARS, whole(earlier.shape), chunk_back(map_shape), chunk_back((heads, BLOCK, key_width)),
            chunk_back((heads, BLOCK, value_width)), rows_back(mixed_width), rows_back(LANES), rows_back(vw),
            whole(gain_row.shape), held(w_output.shape),
        ],
        out_specs=[
            rows_back(vw), rows_back(vw), chunk_back((heads, BLOCK, value_width)),
            chunk_back((heads, key_width, value_width)),
            whole((row_count, model_width)) if cube else rows_back(model_width),
        ],
        out_shape=[
            struct((seq_rows, vw), f32), struct((seq_rows, vw), bf16),
            struct((chunks, heads, BLOCK, value_width), bf16),
            struct((chunks, heads, key_width, value_width), f32),
            struct((row_count, model_width), f32) if cube else struct((seq_rows, model_width), bf16),
        ],
        scratch_shapes=[pltpu.VMEM((heads, key_width, value_width), f32)]
        + (cube_scatter_scratch(row_count, model_width) if cube else []),
        compiler_params=params(5 if cube else None),
        name="mixer_output",
    )(meta, earlier, starts, w_part, u_part, qkv, scal, gate, gain_row, w_output)
    if cube:
        mixer_out = mixed_part
    else:
        mixer_out = lax.psum_scatter(mixed_part, "head", scatter_dimension=0, tiled=True).astype(f32)

    hidden_in = inputs_f + mixer_out
    normed_two = rms_scale(hidden_in, second_gain).astype(bf16)
    mlp_block, hidden, grad_gate, grad_up, mlp_part, grad_normed_two = feed(
        normed_two, grad_block_two, w_gate, w_up, w_down, "seq", 3
    )
    mlp_out = lax.psum_scatter(mlp_part, "seq", scatter_dimension=0, tiled=True)
    grad_hidden_norm, grad_second = rms_back(hidden_in, second_gain, grad_normed_two)
    grad_hidden_in = grad_out + grad_hidden_norm
    grad_mix = grad_hidden_in.astype(bf16)
    core_shapes = [
        struct((chunks, heads, BLOCK, value_width), bf16), struct((chunks, heads, BLOCK, value_width), f32),
        struct((chunks, heads, key_width, value_width), f32), struct((seq_rows, vw), bf16),
        struct((8, value_width), f32), struct((heads, key_width, value_width), f32),
    ]
    if cube:
        tiles = model_width // BLOCK
        units, mlp_rows = hidden.shape

        def tile(step):
            return jnp.clip(step - 2, 0, tiles - 1)

        def core_chunk(step):
            return core_order("head", step, tiles)

        def core_rows(width):
            return pl.BlockSpec((BLOCK, width), lambda step: (core_chunk(step), 0))

        def core_blocks(shape):
            return pl.BlockSpec((1,) + tuple(shape), lambda step: (core_chunk(step),) + (0,) * len(shape))

        tall = pl.BlockSpec((mlp_rows, BLOCK), lambda step: (0, tile(step)))
        down = pl.BlockSpec((units, BLOCK), lambda step: (0, tile(step)))
        flat = pl.BlockSpec((BLOCK, units), lambda step: (tile(step), 0))
        results = pl.pallas_call(
            functools.partial(feed_core_kernel, sizes, chunks, "head", tiles),
            grid=(tiles + chunks,),
            in_specs=[
                SCALARS, held(grad_mix.shape), tall, tall, *(held(array.shape) for array in (hidden, grad_gate, grad_up)),
                held(w_output.shape), core_rows(vw), core_rows(vw), whole(gain_row.shape), core_rows(mixed_width),
                core_rows(LANES), core_blocks((heads, BLOCK, key_width)), core_blocks((heads, key_width, key_width)),
            ],
            out_specs=[
                down, flat, flat, ANYWHERE,
                core_blocks((heads, BLOCK, value_width)), core_blocks((heads, BLOCK, value_width)),
                core_blocks((heads, key_width, value_width)), core_rows(vw),
                whole((8, value_width)), whole((heads, key_width, value_width)),
            ],
            out_shape=[
                struct((units, model_width), bf16), struct((model_width, units), bf16),
                struct((model_width, units), bf16), struct((seq_rows, model_width), bf16), *core_shapes,
            ],
            scratch_shapes=[
                pltpu.VMEM((seq_rows, model_width), bf16), pltpu.SemaphoreType.DMA, *CUBE_SEMAPHORES[1:],
                pltpu.VMEM((chunks, heads, key_width, value_width), f32),
                pltpu.VMEM((chunks, heads, key_width, key_width), bf16),
                pltpu.VMEM((chunks, heads, 8, LANES), f32),
            ],
            compiler_params=params(6),
            name="feed_core",
        )(
            meta, grad_mix, mlp_block, grad_block_two, hidden, grad_gate, grad_up,
            w_output, core, gate, gain_row, qkv, scal, w_part, drop,
        )
        ff_grads, grad_block = results[:3], results[3]
        grad_core, inner, pull, grad_gate_pre, grad_head, pulled = results[4:]
    else:
        *ff_grads, grad_block = feed_grads(
            grad_mix, mlp_block, grad_block_two, hidden, grad_gate, grad_up, "head"
        )
        grad_core, inner, pull, grad_gate_pre, grad_head, pulled = pl.pallas_call(
            functools.partial(core_grad_kernel, *sizes, chunks),
            grid=(chunks,),
            in_specs=[
                SCALARS, by_rows(model_width, chunks), whole(w_output.shape), by_rows(vw, chunks), by_rows(vw, chunks),
                whole(gain_row.shape), by_rows(mixed_width, chunks), by_rows(LANES, chunks),
                by_chunk((heads, BLOCK, key_width), chunks), by_chunk((heads, key_width, key_width), chunks),
            ],
            out_specs=[
                by_chunk((heads, BLOCK, value_width), chunks), by_chunk((heads, BLOCK, value_width), chunks),
                by_chunk((heads, key_width, value_width), chunks), by_rows(vw, chunks),
                whole((8, value_width)), whole((heads, key_width, value_width)),
            ],
            out_shape=core_shapes,
            compiler_params=params(),
            name="mixer_core_grad",
        )(meta, grad_block, w_output, core, gate, gain_row, qkv, scal, w_part, drop)
    grad_w_output = dot_tn(gated, grad_block).astype(bf16)
    grad_w_outgate = dot_tn(block_rows, grad_gate_pre).astype(bf16)

    later = from_later(
        jnp.concatenate([block_map[:, :, :key_width], pulled], axis=2).astype(bf16), "seq"
    )
    later, grad_w_output, grad_w_outgate = lax.optimization_barrier((later, grad_w_output, grad_w_outgate))
    mlp_out, grad_w_outgate = lax.optimization_barrier((mlp_out, grad_w_outgate))
    grad_w_outgate = lax.psum(grad_w_outgate, "seq")
    grad_conv, grad_small, sums, edge = pl.pallas_call(
        functools.partial(backward_kernel, *sizes, chunks, others),
        grid=(chunks,),
        in_specs=[
            SCALARS, whole(later.shape), by_rows(mixed_width, chunks), by_rows(mixed_width, chunks),
            by_rows(LANES, chunks), by_rows(LANES, chunks), by_chunk((heads, BLOCK, BLOCK), chunks),
            by_chunk((heads, BLOCK, value_width), chunks), by_chunk((heads, key_width, value_width), chunks),
            by_chunk((heads, BLOCK, value_width), chunks), by_chunk((heads, BLOCK, value_width), chunks),
            by_chunk((heads, key_width, value_width), chunks), by_chunk((heads, key_width, key_width), chunks),
            whole(dvec.shape),
        ],
        out_specs=[
            by_rows(mixed_width, chunks), by_rows(LANES, chunks), whole((8, LANES)), whole((HALO, mixed_width)),
        ],
        out_shape=[
            struct((seq_rows, mixed_width), f32), struct((seq_rows, LANES), bf16), struct((8, LANES), f32),
            struct((HALO, mixed_width), f32),
        ],
        scratch_shapes=[
            pltpu.VMEM((heads, key_width, value_width), f32), pltpu.VMEM((HALO, mixed_width), f32),
            pltpu.VMEM((HALO, mixed_width), f32), pltpu.SemaphoreType.DMA((2,)),
        ],
        compiler_params=params(9),
        name="mixer_backward",
    )(meta, later, qkv, conv, scal, small, inverse, fresh, states, grad_core, inner, pull, drop, dvec)

    grad_small, *ff_grads = lax.optimization_barrier((grad_small, *ff_grads))
    ff_grads = [lax.psum(part, "head") for part in ff_grads]
    step_rows = BLOCK // HALO
    last_halo = seq_rows // HALO - 1
    later_rows = pl.BlockSpec(
        (HALO, mixed_width), lambda step: (jnp.minimum((last_first(step) + 1) * step_rows, last_halo), 0)
    )
    grad_pre, grad_taps, grad_rows, gain_sum = pl.pallas_call(
        functools.partial(projection_grad_kernel, mixed_width, docs, chunks, taps, cube),
        grid=(chunks,),
        in_specs=[
            SCALARS, rows_back(mixed_width), later_rows, whole(edge.shape), rows_back(mixed_width), rows_back(vw),
            rows_back(LANES), whole(conv_all.shape), rows_back(model_width),
            *(held(weight.shape) for weight in weights),
        ],
        out_specs=[
            rows_back(all_width), whole((8, mixed_width)),
            whole((row_count, model_width)) if cube else rows_back(model_width), whole((8, model_width)),
        ],
        out_shape=[
            struct((seq_rows, all_width), bf16), struct((8, mixed_width), f32),
            struct((row_count, model_width), f32) if cube else struct((seq_rows, model_width), bf16),
            struct((8, model_width), f32),
        ],
        scratch_shapes=[pltpu.VMEM((BLOCK + HALO, mixed_width), f32)]
        + (cube_scatter_scratch(row_count, model_width) if cube else []),
        compiler_params=params(8 if cube else None),
        name="projection_grad",
    )(meta, grad_conv, grad_conv, edge, pre, grad_gate_pre, grad_small, conv_all, block_rows, *weights)

    if cube:
        grad_normed = grad_rows
    else:
        grad_normed = lax.psum_scatter(grad_rows, "head", scatter_dimension=0, tiled=True).astype(f32)
    grad_input_norm, _ = rms_back(inputs_f, first_gain, grad_normed)
    grad_inputs = grad_hidden_in + grad_input_norm
    gains = jnp.concatenate([gain_sum[0] / first_gain, grad_second, grad_head[0]]).reshape(2, -1)
    grad_w_all, grad_w_output, small_sums, _, gains = line_sum(
        block_rows,
        grad_pre,
        (
            grad_w_output,
            jnp.pad(
                jnp.concatenate([grad_taps, sums], axis=1), ((0, 24), (0, 0))
            ).astype(bf16),
            jnp.pad(gains, ((0, 30), (0, 0))).astype(bf16),
        ),
        (32, 16, 16, 16),
        "seq",
        1,
    )
    gains = gains[:2].reshape(-1)
    first_part, second_part = gains[:model_width], gains[model_width : 2 * model_width]
    head_part = gains[2 * model_width :]
    grad_w_query, grad_w_key, grad_w_value, grad_w_outgate, grad_w_output, grad_w_small = widen(
        (grad_w_outgate, grad_w_output), grad_w_all, (qw, qw, vw)
    )
    grad_inputs, grad_w_query, mlp_out, *ff_grads = lax.optimization_barrier(
        (grad_inputs, grad_w_query, mlp_out, *ff_grads)
    )
    grad_w_down, grad_w_gate, grad_w_up = widen(ff_grads)
    grad_taps = small_sums[:taps, :mixed_width].astype(f32)
    sums = small_sums[:2, mixed_width : mixed_width + heads].astype(f32)
    output = (hidden_in + mlp_out.astype(f32)).astype(bf16)
    return (
        output,
        grad_inputs,
        first_part,
        grad_w_query,
        grad_w_key,
        grad_w_value,
        grad_w_outgate,
        grad_w_small[:heads].T,
        grad_w_small[heads : 2 * heads].T,
        grad_taps[:, :qw],
        grad_taps[:, qw : 2 * qw],
        grad_taps[:, 2 * qw :],
        sums[1],
        sums[0],
        head_part,
        grad_w_output,
        second_part,
        grad_w_gate,
        grad_w_up,
        grad_w_down,
    )


def from_previous(array):
    devices = lax.axis_size("seq")
    return lax.ppermute(array, "seq", [(i, i + 1) for i in range(devices - 1)])


def solution(mesh):
    in_specs = (
        P(("seq", "head"), None),
        P(),
        P(),
        P(None, "head"),
        P(None, "head"),
        P(None, "head"),
        P(None, "head"),
        P(None, "head"),
        P(None, "head"),
        P(None, "head"),
        P(None, "head"),
        P(None, "head"),
        P("head"),
        P("head"),
        P(),
        P("head", None),
        P(),
        P(None, "seq"),
        P(None, "seq"),
        P("seq", None),
        P(("seq", "head"), None),
    )
    out_specs = (
        P(("seq", "head"), None),
        P(("seq", "head"), None),
        P(),
        P(None, "head"),
        P(None, "head"),
        P(None, "head"),
        P(None, "head"),
        P(None, "head"),
        P(None, "head"),
        P(None, "head"),
        P(None, "head"),
        P(None, "head"),
        P("head"),
        P("head"),
        P(),
        P("head", None),
        P(),
        P(None, "seq"),
        P(None, "seq"),
        P("seq", None),
    )
    return jax.shard_map(shards, mesh=mesh, in_specs=in_specs, out_specs=out_specs, check_vma=False)
```

```python
import functools

import jax
import jax.numpy as jnp
from jax import lax
from jax.experimental import pallas as pl
from jax.experimental.pallas import tpu as pltpu
from jax.sharding import PartitionSpec as P

GROUP = 64
BLOCK = 256
LANES = 128
HALO = 8

epsilon = 1e-06
f32 = jnp.float32
bf16 = jnp.bfloat16
VMEM_LIMIT = 56 * 1024 * 1024


def dot(left, right):
    return jnp.dot(left, right, preferred_element_type=f32)


def dot_tn(left, right):
    return lax.dot_general(left, right, (((0,), (0,)), ((), ())), preferred_element_type=f32)


def dot_nt(left, right):
    return lax.dot_general(left, right, (((1,), (1,)), ((), ())), preferred_element_type=f32)


def halves(values):
    top = values.astype(bf16)
    return top, (values - top.astype(f32)).astype(bf16)


def exact_left(left, right):
    top = right.astype(bf16)
    rest = right - top.astype(f32)
    middle = rest.astype(bf16)
    low = (rest - middle.astype(f32)).astype(bf16)
    return dot(left, top) + dot(left, middle) + dot(left, low)


def dot_fine(left, right):
    left_top, left_low = halves(left)
    right_top, right_low = halves(right)
    return dot(left_top, right_top) + (dot(left_top, right_low) + dot(left_low, right_top))


def sigmoid(values):
    return jax.nn.sigmoid(values)


def silu_slope(values):
    sigma = sigmoid(values)
    return sigma * (1.0 + values * (1.0 - sigma))


def softplus(values):
    return jnp.maximum(values, 0.0) + jnp.log1p(jnp.exp(-jnp.abs(values)))


def slot_starts(doc_lengths):
    slot_sizes = (doc_lengths + (GROUP - 1)) // GROUP * GROUP
    return jnp.cumsum(slot_sizes, dtype=jnp.int32) - slot_sizes


def layout(doc_lengths, first_row, row_total):
    starts = slot_starts(doc_lengths)
    places = first_row + jnp.arange(row_total, dtype=jnp.int32)
    owners = jnp.sum(
        (places[:, None] >= starts[None, 1:]).astype(jnp.int32), axis=1, dtype=jnp.int32
    )
    picked = (owners[:, None] == jnp.arange(doc_lengths.shape[0], dtype=jnp.int32)[None, :]).astype(
        jnp.int32
    )
    begins = jnp.sum(picked * starts[None, :], axis=1, dtype=jnp.int32)
    length = jnp.sum(picked * doc_lengths[None, :], axis=1, dtype=jnp.int32)
    offset = places - begins
    return (offset, offset < length)


def rms_scale(values, gain):
    return values * lax.rsqrt(jnp.mean(values * values, axis=-1, keepdims=True) + epsilon) * gain


def rms_back(values, gain, grad_in):
    scale = lax.rsqrt(jnp.mean(values * values, axis=-1, keepdims=True) + epsilon)
    weighted = grad_in * gain
    grad_values = scale * weighted - values * scale**3 * jnp.mean(
        weighted * values, axis=-1, keepdims=True
    )
    grad_gain = jnp.sum((grad_in * values * scale).reshape(-1, values.shape[-1]), axis=0)
    return (grad_values, grad_gain)


def owner_of(meta, docs, places):
    total = jnp.zeros_like(places)
    for doc in range(1, docs):
        total = total + jnp.where(places >= meta[1 + doc], 1, 0)
    return total


def offset_of(meta, docs, places):
    begin = jnp.zeros_like(places)
    for doc in range(1, docs):
        begin = jnp.where(places >= meta[1 + doc], meta[1 + doc], begin)
    return places - begin


class Masks:
    def __init__(self, meta, docs, chunk):
        base = meta[0] + chunk * BLOCK
        rows = lax.broadcasted_iota(jnp.int32, (BLOCK, BLOCK), 0)
        cols = lax.broadcasted_iota(jnp.int32, (BLOCK, BLOCK), 1)
        same = owner_of(meta, docs, base + rows) == owner_of(meta, docs, base + cols)
        self.inclusive = same & (rows >= cols)
        self.strictly = same & (rows > cols)
        self.level = rows ^ cols
        self.lower = jnp.where(rows >= cols, 1.0, 0.0).astype(bf16)
        self.upper = jnp.where(rows <= cols, 1.0, 0.0).astype(bf16)
        self.eye = jnp.where(rows == cols, 1.0, 0.0)
        place = base + lax.broadcasted_iota(jnp.int32, (BLOCK, 1), 0)
        owner = owner_of(meta, docs, place)
        before = jnp.int32(0)
        last = jnp.int32(0)
        for doc in range(1, docs):
            before = before + jnp.where(base - 1 >= meta[1 + doc], 1, 0)
            last = last + jnp.where(base + BLOCK - 1 >= meta[1 + doc], 1, 0)
        self.enters = jnp.where(owner == before, 1.0, 0.0)
        self.leaves = jnp.where(owner == last, 1.0, 0.0)
        self.through = jnp.where(before == last, 1.0, 0.0).astype(f32)
        self.offset = offset_of(meta, docs, place)


def decays(masks, scal, scal_t, head):
    column = scal[:, head : head + 1]
    row = scal_t[head : head + 1, :]
    within = jnp.where(masks.inclusive, jnp.exp(jnp.minimum(column - row, 0.0)), 0.0)
    last = column[BLOCK - 1 : BLOCK, :]
    entry = jnp.exp(column) * masks.enters
    leave = jnp.exp(last - column) * masks.leaves
    through = jnp.exp(last) * masks.through
    return within, entry, leave, through


def unit_lower_inverses(systems):
    half = BLOCK // 2
    rows = lax.broadcasted_iota(jnp.int32, (half, half), 0)
    cols = lax.broadcasted_iota(jnp.int32, (half, half), 1)
    level = rows ^ cols
    eye = jnp.where(rows == cols, 1.0, 0.0)
    parts = [system[at : at + half, at : at + half] for system in systems for at in (0, half)]
    solved = [eye - jnp.where(level == 1, part, 0.0) for part in parts]
    width = 2
    while width < half:
        keep = (level >= width) & (level < 2 * width)
        low = [inverse.astype(bf16) for inverse in solved]
        moved = [dot(jnp.where(keep, part, 0.0).astype(bf16), inverse) for part, inverse in zip(parts, low)]
        solved = [
            whole_part - dot(inverse, part.astype(bf16))
            for whole_part, inverse, part in zip(solved, low, moved)
        ]
        width *= 2
    solved = [inverse.astype(bf16) for inverse in solved]
    results = []
    for index, system in enumerate(systems):
        upper, lower = solved[2 * index], solved[2 * index + 1]
        corner = -dot(lower, dot(system[half:, :half].astype(bf16), upper).astype(bf16))
        results.append((upper, corner.astype(bf16), lower))
    return results


LEAD = 2 * HALO
STRIDE = BLOCK + LEAD


def cube_order(axis, step):
    place = lax.axis_index(axis)
    chunk = 0
    for bit in (1, 2, 4):
        chunk = chunk + bit * ((place // bit + step // bit) % 2)
    return chunk


class EdgeRows:
    def __init__(self, line, axis, own_ref, rows_ref, edge_ref, line_sem, send_sem, recv_sem):
        self.line, self.axis = line, axis
        self.group, self.place = lax.axis_index(line), lax.axis_index(axis)
        self.groups, self.last = lax.axis_size(line), lax.axis_size(axis) - 1
        self.own_ref, self.rows_ref, self.edge_ref = own_ref, rows_ref, edge_ref
        self.line_sem, self.send_sem, self.recv_sem = line_sem, send_sem, recv_sem

    def enter(self):
        barrier = pltpu.get_barrier_semaphore()
        for mask in (1, 2, 4, 6):
            pl.semaphore_signal(barrier, inc=1, device_id={self.axis: flip(self.place, mask)}, device_id_type=MESH)
        for by in range(1, self.groups):
            other = lax.rem(self.group + by, self.groups)
            pl.semaphore_signal(barrier, inc=1, device_id={self.line: other}, device_id_type=MESH)
        pl.semaphore_wait(barrier, 3 + self.groups)

    def hands_on(self):
        return (self.place == self.last) & (self.group < self.groups - 1)

    def receives(self):
        return (self.place == self.last) & (self.group > 0)

    def landing(self, mask):
        block = lax.rem(flip(self.place, mask) + 1, self.last + 1)
        return self.rows_ref.at[pl.ds(pl.multiple_of(block * STRIDE, LEAD), LEAD), :]

    def onward(self):
        return pltpu.make_async_remote_copy(
            self.own_ref.at[pl.ds(BLOCK - LEAD, LEAD), :], self.edge_ref, self.line_sem.at[0], self.line_sem.at[1],
            device_id={self.line: self.group + 1}, device_id_type=MESH,
        )

    def copy(self, mask, toward):
        return pltpu.make_async_remote_copy(
            self.landing(mask) if mask else self.edge_ref, self.landing(mask),
            self.send_sem.at[mask + toward if mask else toward], self.recv_sem.at[mask ^ toward],
            device_id={self.axis: flip(self.place, toward)}, device_id_type=MESH,
        )

    def wait(self, mask):
        pltpu.make_async_remote_copy(
            self.landing(mask), self.landing(mask), self.send_sem.at[0], self.recv_sem.at[mask],
            device_id={self.axis: flip(self.place, 1)}, device_id_type=MESH,
        ).wait_recv()

    def start(self):
        @pl.when(self.hands_on())
        def _():
            self.onward().start()

        @pl.when(self.place < self.last)
        def _():
            self.edge_ref[...] = self.own_ref[BLOCK - LEAD :, :]

        @pl.when((self.place == self.last) & (self.group == 0))
        def _():
            self.edge_ref[...] = jnp.zeros(self.edge_ref.shape, bf16)

        @pl.when(self.receives())
        def _():
            pltpu.make_async_remote_copy(
                self.edge_ref, self.edge_ref, self.line_sem.at[0], self.line_sem.at[1],
                device_id={self.line: self.group - 1}, device_id_type=MESH,
            ).wait_recv()

        for toward in (6, 2, 4, 1):
            self.copy(0, toward).start()
        self.landing(0)[...] = self.edge_ref[...]

    def spread(self):
        for mask in (2, 4, 6):
            self.wait(mask)
            self.copy(mask, 1).start()
        for mask in (1, 3, 5, 7):
            self.wait(mask)

    def end(self):
        @pl.when(self.hands_on())
        def _():
            self.onward().wait_send()

        for toward in (6, 2, 4, 1):
            self.copy(0, toward).wait_send()
        for mask in (2, 4, 6):
            self.copy(mask, 1).wait_send()


def forward_kernel(
    heads, key_width, value_width, docs, taps, chunks, cube,
    meta, rows_ref, wq_ref, wk_ref, wv_ref, wg_ref, ws_ref, conv_ref, dvec_ref,
    pre_ref, act_ref, gate_ref, small_ref, scal_ref, qkv_ref, inv_ref, w_out_ref, u_ref, drop_ref,
    starts_ref, map_ref, *refs,
):
    step = pl.program_id(0)
    ext, state, drops, adds, throughs = refs[2 * cube : 2 * cube + 5]
    if cube:
        all_ref = refs[0]
        earlier_ref, *refs = refs[1:]
        held, copy_sem, edge_ref, line_sem, edge_send, edge_recv, cube_send, cube_recv = refs[5:13]
        going, coming, map_sem = refs[13:]
        chunk = cube_order("head", step)
        rows_in = CubeGather("head", rows_ref, held, None, cube_send, cube_recv, STRIDE, LEAD)
        edges = EdgeRows("seq", "head", rows_ref, held, edge_ref, line_sem, edge_send, edge_recv)

        def kept(block):
            start = pl.multiple_of(block * STRIDE + LEAD, LEAD)
            return pltpu.make_async_copy(
                held.at[pl.ds(start, BLOCK), :],
                all_ref.at[pl.ds(pl.multiple_of(block * BLOCK, BLOCK), BLOCK), :],
                copy_sem.at[block],
            )

        @pl.when(step == 0)
        def _():
            edges.enter()
            edges.start()
            rows_in.first()
            held[pl.ds(pl.multiple_of(chunk * STRIDE + LEAD, LEAD), BLOCK), :] = rows_ref[...]

        @pl.when(step == 2)
        def _():
            rows_in.second()
            rows_in.third()

        @pl.when(step == 4)
        def _():
            rows_in.fourth()

        for odd in (1, 3, 5, 7):
            @pl.when(step == odd)
            def _():
                for half in range(2):
                    rows_in.wait(odd, half)

        kept(chunk).start()
        rows = held[pl.ds(pl.multiple_of(chunk * STRIDE + LEAD, LEAD), BLOCK), :]
    else:
        chunk = step
        rows = rows_ref[LEAD:, :]

    qw, vw = heads * key_width, heads * value_width
    mixed = 2 * qw + vw
    masks = Masks(meta, docs, chunk)
    gate_ref[...] = dot(rows, wg_ref[...])
    small = dot(rows, ws_ref[...])
    small_ref[...] = small
    if cube:
        @pl.when(step == 0)
        def _():
            edges.spread()

        rows_ext = held[pl.ds(pl.multiple_of(chunk * STRIDE, LEAD), STRIDE), :]
    else:
        rows_ext = rows_ref[...]
    for span, ref in ((slice(0, qw), wq_ref), (slice(qw, 2 * qw), wk_ref), (slice(2 * qw, mixed), wv_ref)):
        pre = dot(rows_ext, ref[...])
        ext[:, span] = pre
        pre_ref[:, span] = pre[LEAD:, :]

    conv = jnp.zeros((BLOCK, mixed), f32)
    for lag in range(taps):
        keep = jnp.where(masks.offset >= lag, 1.0, 0.0)
        conv = conv + conv_ref[lag : lag + 1, :] * (ext[LEAD - lag : LEAD - lag + BLOCK, :] * keep)
    act_ref[...] = conv
    act = conv * sigmoid(conv)

    lane = lax.broadcasted_iota(jnp.int32, (BLOCK, LANES), 1)
    decay = dvec_ref[1:2, :] * softplus(small + dvec_ref[0:1, :])
    cumul = exact_left(masks.lower, decay)
    scal = jnp.where(lane < heads, cumul, sigmoid(small))
    scal_ref[...] = scal
    scal_t = scal.T

    held_heads = []
    for head in range(heads):
        act_q = act[:, head * key_width : (head + 1) * key_width]
        act_k = act[:, qw + head * key_width : qw + (head + 1) * key_width]
        value = act[:, 2 * qw + head * value_width : 2 * qw + (head + 1) * value_width].astype(bf16)
        norm_q = lax.rsqrt(jnp.sum(act_q * act_q, axis=1, keepdims=True) + epsilon)
        norm_k = lax.rsqrt(jnp.sum(act_k * act_k, axis=1, keepdims=True) + epsilon)
        query = (act_q * norm_q * key_width ** (-0.5)).astype(bf16)
        key = (act_k * norm_k).astype(bf16)
        qkv_ref[:, head * key_width : (head + 1) * key_width] = query
        qkv_ref[:, qw + head * key_width : qw + (head + 1) * key_width] = key
        qkv_ref[:, 2 * qw + head * value_width : 2 * qw + (head + 1) * value_width] = value
        within, entry, leave, through = decays(masks, scal, scal_t, head)
        beta = scal[:, heads + head : heads + head + 1]
        system = jnp.where(masks.strictly, beta * dot_nt(key, key) * within, 0.0)
        held_heads.append((system, key, value, beta, entry, leave, through))

    half = BLOCK // 2
    inverses = unit_lower_inverses([part[0] for part in held_heads])
    for head, (upper, corner, lower) in enumerate(inverses):
        inv_ref[0, head, :half, :half] = upper
        inv_ref[0, head, :half, half:] = jnp.zeros((half, half), bf16)
        inv_ref[0, head, half:, :half] = corner
        inv_ref[0, head, half:, half:] = lower
    for head, (_, key, value, beta, entry, leave, through) in enumerate(held_heads):
        inverse = inv_ref[0, head]
        key_f = key.astype(f32)
        w_part = dot(inverse, (beta * entry * key_f).astype(bf16)).astype(bf16)
        u_part = dot(inverse, (beta * value.astype(f32)).astype(bf16))
        w_out_ref[0, head] = w_part
        u_ref[0, head] = u_part
        tail_key = (leave * key_f).astype(bf16)
        drop = dot_tn(tail_key, w_part)
        drop_ref[0, head] = drop
        drops[chunk, head] = drop.astype(bf16)
        adds[chunk, head] = dot_tn(tail_key, u_part.astype(bf16))
        throughs[chunk, head] = jnp.broadcast_to(through, (8, LANES))

    @pl.when(step == chunks - 1)
    def _():
        shape = (key_width, key_width + value_width)
        ident = jnp.where(lax.broadcasted_iota(jnp.int32, shape, 0) == lax.broadcasted_iota(jnp.int32, shape, 1), 1.0, 0.0)
        for head in range(heads):
            state[head] = ident

        def pass_on(at, carry):
            for head in range(heads):
                before = state[head]
                starts_ref[at, head] = before
                after = throughs[at, head][0:1, 0:1] * before - dot(drops[at, head], before.astype(bf16))
                state[head] = after + jnp.concatenate(
                    [jnp.zeros((key_width, key_width), f32), adds[at, head]], axis=1
                )
            return carry

        lax.fori_loop(0, chunks, pass_on, 0)
        for head in range(heads):
            map_ref[head] = state[head]
        if cube:
            groups, group = lax.axis_size("seq"), lax.axis_index("seq")

            def hand_on(by, target):
                slot = groups - 1 - by
                return pltpu.make_async_remote_copy(
                    going, coming.at[slot], map_sem.at[0, slot], map_sem.at[1, slot],
                    device_id={"seq": target}, device_id_type=MESH,
                )

            for head in range(heads):
                going[head] = state[head].astype(bf16)
            for by in range(groups - 1, 0, -1):
                @pl.when(group + by < groups)
                def _():
                    hand_on(by, group + by).start()

            for by in range(groups - 1, 0, -1):
                slot = groups - 1 - by

                @pl.when(group >= by)
                def _():
                    hand_on(by, group - by).wait_recv()
                    earlier_ref[slot] = coming[slot]

                @pl.when(group < by)
                def _():
                    earlier_ref[slot] = jnp.zeros(earlier_ref.shape[1:], bf16)

            for by in range(groups - 1, 0, -1):
                @pl.when(group + by < groups)
                def _():
                    hand_on(by, group + by).wait_send()

            rows_in.last()
            edges.end()
            for block in range(chunks):
                kept(block).wait()


def output_kernel(
    heads, key_width, value_width, docs, others, cube,
    meta, maps_ref, starts_ref, w_in_ref, u_ref, qkv_ref, scal_ref, gate_ref, gain_ref, w_output_ref, *refs,
):
    if cube:
        inputs_ref, next_gain_ref, *refs = refs
    core_ref, gated_ref, fresh_ref, state_ref, mixed_ref, *refs = refs
    if cube:
        next_ref, *refs = refs
    incoming, *refs = refs
    step = pl.program_id(0)
    chunk = cube_order("head", 7 - step) if cube else step
    qw = heads * key_width

    @pl.when(step == 0)
    def _():
        for head in range(heads):
            state = jnp.zeros((key_width, value_width), f32)
            for other in range(others):
                passing = maps_ref[other, head, :, :key_width]
                top, low = halves(state)
                state = dot(passing, top) + dot(passing, low) + maps_ref[other, head, :, key_width:].astype(f32)
            incoming[head] = state

    masks = Masks(meta, docs, chunk)
    scal = scal_ref[...]
    scal_t = scal.T
    gain = gain_ref[...]
    for head in range(heads):
        query = qkv_ref[:, head * key_width : (head + 1) * key_width]
        key = qkv_ref[:, qw + head * key_width : qw + (head + 1) * key_width]
        within, entry, leave, through = decays(masks, scal, scal_t, head)
        begun = starts_ref[0, head]
        state = dot_fine(begun[:, :key_width], incoming[head]) + begun[:, key_width:]
        state_ref[0, head] = state
        state_low = state.astype(bf16)
        fresh = (u_ref[0, head] - dot(w_in_ref[0, head], state_low)).astype(bf16)
        fresh_ref[0, head] = fresh
        scores = (dot_nt(query, key) * within).astype(bf16)
        core = dot((query.astype(f32) * entry).astype(bf16), state_low) + dot(scores, fresh)
        span = slice(head * value_width, (head + 1) * value_width)
        core_ref[:, span] = core
        scale = lax.rsqrt(jnp.mean(core * core, axis=1, keepdims=True) + epsilon)
        gate = gate_ref[:, span]
        gated_ref[:, span] = (core * scale * gain * (gate * sigmoid(gate))).astype(bf16)
    mixed = dot(gated_ref[...], w_output_ref[...])
    if not cube:
        mixed_ref[...] = mixed.astype(bf16)
        return

    total, *refs = refs
    scatter_block(step, CubeScatter("head", total, *refs), mixed)

    @pl.when(step == 7)
    def _():
        hidden_in = inputs_ref[...].astype(f32) + total[...]
        mixed_ref[...] = hidden_in
        next_ref[...] = rms_scale(hidden_in, next_gain_ref[...]).astype(bf16)


def core_grad_kernel(
    heads, key_width, value_width, docs, chunks,
    meta, grad_ref, w_output_ref, core_ref, gate_ref, gain_ref, qkv_ref, scal_ref, w_in_ref, drop_ref,
    grad_core_ref, inner_ref, pull_ref, grad_gate_ref, grad_gain_ref, total_ref, chunk=None, later=None,
):
    step = pl.program_id(0)
    chunk = chunks - 1 - step if chunk is None else chunk
    qw = heads * key_width
    masks = Masks(meta, docs, chunk)
    scal = scal_ref[...]
    scal_t = scal.T
    gain = gain_ref[...]

    @pl.when(step == 0)
    def _():
        grad_gain_ref[...] = jnp.zeros_like(grad_gain_ref)
        total_ref[...] = jnp.zeros_like(total_ref)

    grad_gated = dot_nt(grad_ref[...], w_output_ref[...])
    for head in range(heads):
        span = slice(head * value_width, (head + 1) * value_width)
        core = core_ref[:, span]
        gate = gate_ref[:, span]
        grad_in = grad_gated[:, span]
        scale = lax.rsqrt(jnp.mean(core * core, axis=1, keepdims=True) + epsilon)
        sigma = sigmoid(gate)
        normed = core * scale
        grad_gate_ref[:, span] = (
            grad_in * (normed * gain) * (sigma * (1.0 + gate * (1.0 - sigma)))
        ).astype(bf16)
        grad_normed = grad_in * (gate * sigma)
        weighted = grad_normed * gain
        grad_core = scale * (weighted - normed * jnp.mean(weighted * normed, axis=1, keepdims=True))
        grad_gain_ref[0:1, :] += jnp.sum(grad_normed * normed, axis=0, keepdims=True)
        grad_core = grad_core.astype(bf16)
        grad_core_ref[0, head] = grad_core
        query = qkv_ref[:, head * key_width : (head + 1) * key_width]
        key = qkv_ref[:, qw + head * key_width : qw + (head + 1) * key_width]
        within, entry, leave, through = decays(masks, scal, scal_t, head)
        scores = (dot_nt(query, key) * within).astype(bf16)
        inner = dot_tn(scores, grad_core)
        inner_ref[0, head] = inner
        pull = dot_tn((query.astype(f32) * entry).astype(bf16), grad_core) - dot_tn(
            w_in_ref[0, head], inner.astype(bf16)
        )
        pull_ref[0, head] = pull
        if later is not None:
            pulls, drops, throughs = later
            pulls[chunk, head] = pull
            drops[chunk, head] = drop_ref[0, head].astype(bf16)
            throughs[chunk, head] = jnp.broadcast_to(through, (8, LANES))
            continue
        total = total_ref[head]
        total_ref[head] = (
            through * total - dot_tn(drop_ref[0, head].astype(bf16), total.astype(bf16)) + pull
        )


def backward_kernel(
    heads, key_width, value_width, docs, chunks, others, cube,
    meta, maps_ref, qkv_ref, act_ref, scal_ref, small_ref, inv_ref, fresh_ref, state_ref,
    grad_core_ref, inner_ref, pull_ref, drop_ref, dvec_ref, *refs,
):
    if cube:
        feed_ref, *refs = refs
    grad_conv_ref, grad_small_ref, sums_ref, edge_ref, *refs = refs
    if cube:
        feed_sum_ref, *refs = refs
    carried, edge_out, edge_in, edge_sem, *refs = refs
    step = pl.program_id(0)
    chunk = chunks - 1 - step

    @pl.when(step == 0)
    def _():
        line_barrier("seq", "head" if cube else None)

    if cube:
        rows = feed_ref.shape[0] // 8
        total, *refs = refs
        part = pl.ds(pl.multiple_of(cube_order("head", 7 - step) * rows, rows), rows)
        scatter = CubeScatter("head", total, *refs)
        scatter_block(step, scatter, feed_ref[part, :].astype(f32), inside=True)
    groups, group = lax.axis_size("seq"), lax.axis_index("seq")
    edge = pltpu.make_async_remote_copy(
        edge_out, edge_in, edge_sem.at[0], edge_sem.at[1],
        device_id={"seq": jnp.maximum(group - 1, 0)}, device_id_type=MESH,
    )

    qw = heads * key_width

    @pl.when(step == 0)
    def _():
        sums_ref[...] = jnp.zeros_like(sums_ref)
        for head in range(heads):
            state = jnp.zeros((key_width, value_width), f32)
            for other in range(others):
                passing = maps_ref[other, head, :, :key_width]
                top, low = halves(state)
                state = dot_tn(passing, top) + dot_tn(passing, low) + maps_ref[other, head, :, key_width:].astype(f32)
            carried[head] = state

    masks = Masks(meta, docs, chunk)
    scal = scal_ref[...]
    scal_t = scal.T
    lane = lax.broadcasted_iota(jnp.int32, (BLOCK, LANES), 1)
    slopes = jnp.zeros((BLOCK, LANES), f32)
    tails = jnp.zeros((1, LANES), f32)
    betas = jnp.zeros((BLOCK, LANES), f32)
    for head in range(heads):
        q_span = slice(head * key_width, (head + 1) * key_width)
        k_span = slice(qw + head * key_width, qw + (head + 1) * key_width)
        v_span = slice(2 * qw + head * value_width, 2 * qw + (head + 1) * value_width)
        query, key, value = qkv_ref[:, q_span], qkv_ref[:, k_span], qkv_ref[:, v_span]
        query_f, key_f = query.astype(f32), key.astype(f32)
        within, entry, leave, through = decays(masks, scal, scal_t, head)
        beta = scal[:, heads + head : heads + head + 1]
        later = carried[head]
        later_low = later.astype(bf16)
        state = state_ref[0, head]
        state_low = state.astype(bf16)
        grad_core = grad_core_ref[0, head]
        fresh = fresh_ref[0, head]
        carried[head] = through * later - dot_tn(drop_ref[0, head].astype(bf16), later_low) + pull_ref[0, head]
        grad_fresh = inner_ref[0, head] + dot((leave * key_f).astype(bf16), later_low)
        grad_x = dot_tn(inv_ref[0, head], grad_fresh.astype(bf16))
        grad_x_low = grad_x.astype(bf16)
        grad_x_beta = beta * grad_x
        recalled = dot(key, state_low)
        grad_beta = jnp.sum(grad_x * (value.astype(f32) - entry * recalled), axis=1, keepdims=True)
        from_state_q = dot_nt(grad_core, state_low)
        from_state_k = dot_nt(grad_x_beta.astype(bf16), state_low)
        grad_scores = (dot_nt(grad_core, fresh) * within).astype(bf16)
        gram = dot_nt(key, key)
        grad_system = jnp.where(masks.strictly, dot_nt(grad_x_low, fresh) * within, 0.0)
        grad_beta = grad_beta - jnp.sum(grad_system * gram, axis=1, keepdims=True)
        grad_gram = (-beta * grad_system).astype(bf16)
        grad_query = dot(grad_scores, key) + entry * from_state_q
        grad_row = dot(grad_gram, key) - entry * from_state_k
        passed = leave * dot_nt(fresh, later_low)
        grad_col = dot_tn(grad_gram, key) + dot_tn(grad_scores, query) + passed
        slope = jnp.sum(query_f * grad_query + key_f * (grad_row - grad_col), axis=1, keepdims=True)
        kept = jnp.sum(jnp.sum(state * later, axis=1, keepdims=True), axis=0, keepdims=True)
        moved = jnp.sum(jnp.sum(key_f * passed, axis=1, keepdims=True), axis=0, keepdims=True)
        tail = through * kept + moved
        slopes = jnp.where(lane == head, slope, slopes)
        tails = jnp.where(lane[0:1, :] == head, tail, tails)
        betas = jnp.where(lane == heads + head, grad_beta, betas)

        conv_q, conv_k, conv_v = act_ref[:, q_span], act_ref[:, k_span], act_ref[:, v_span]
        for span, conv, grad, factor in (
            (q_span, conv_q, grad_query, key_width ** (-0.5)),
            (k_span, conv_k, grad_row + grad_col, 1.0),
        ):
            sigma = sigmoid(conv)
            act = conv * sigma
            norm = lax.rsqrt(jnp.sum(act * act, axis=1, keepdims=True) + epsilon)
            unit = act * norm
            grad_act = (factor * norm) * (grad - unit * jnp.sum(grad * unit, axis=1, keepdims=True))
            grad_conv_ref[:, span] = grad_act * (sigma * (1.0 + conv * (1.0 - sigma)))
        grad_conv_ref[:, v_span] = grad_x_beta * silu_slope(conv_v)

    grad_decay = jnp.where(lane < heads, exact_left(masks.upper, slopes) + tails, 0.0)
    shifted = small_ref[...] + dvec_ref[0:1, :]
    rate = dvec_ref[1:2, :]
    grad_z = grad_decay * rate * sigmoid(shifted)
    sums_ref[0:1, :] += jnp.sum(grad_z, axis=0, keepdims=True)
    sums_ref[1:2, :] += jnp.sum(grad_decay * (rate * softplus(shifted)), axis=0, keepdims=True)
    strength = sigmoid(small_ref[...])
    grad_small_ref[...] = jnp.where(lane < heads, grad_z, betas * strength * (1.0 - strength)).astype(bf16)

    @pl.when(step == chunks - 1)
    def _():
        if cube:
            scatter.finish()
            feed_sum_ref[...] = total[...].astype(bf16)
        edge_out[...] = grad_conv_ref[0:HALO, :]

        @pl.when(group > 0)
        def _():
            edge.start()

        @pl.when(group < groups - 1)
        def _():
            edge.wait_recv()
            edge_ref[...] = edge_in[...]

        @pl.when(group == groups - 1)
        def _():
            edge_ref[...] = jnp.zeros(edge_ref.shape, f32)

        @pl.when(group > 0)
        def _():
            edge.wait_send()


def projection_grad_kernel(
    mixed, docs, chunks, taps, cube,
    meta, grad_conv_ref, later_ref, edge_ref, pre_ref, grad_gate_ref, grad_small_ref, conv_ref, rows_ref,
    wq_ref, wk_ref, wv_ref, wg_ref, ws_ref,
    grad_pre_ref, grad_taps_ref, grad_rows_ref, gain_sum_ref,
    ext, *refs,
):
    step = pl.program_id(0)
    chunk = cube_order("head", 7 - step) if cube else step

    @pl.when(step == 0)
    def _():
        grad_taps_ref[...] = jnp.zeros_like(grad_taps_ref)
        gain_sum_ref[...] = jnp.zeros_like(gain_sum_ref)

    ext[0:BLOCK, :] = grad_conv_ref[...]

    @pl.when(chunk == chunks - 1)
    def _():
        ext[BLOCK : BLOCK + HALO, :] = edge_ref[...]

    @pl.when(chunk < chunks - 1)
    def _():
        ext[BLOCK : BLOCK + HALO, :] = later_ref[...]

    place = meta[0] + chunk * BLOCK + lax.broadcasted_iota(jnp.int32, (BLOCK, 1), 0)
    pre = pre_ref[...]
    total = jnp.zeros((BLOCK, mixed), f32)
    for lag in range(taps):
        keep = jnp.where(offset_of(meta, docs, place + lag) >= lag, 1.0, 0.0)
        moved = ext[lag : lag + BLOCK, :] * keep
        total = total + conv_ref[lag : lag + 1, :] * moved
        grad_taps_ref[lag : lag + 1, :] += jnp.sum(pre * moved, axis=0, keepdims=True)
    width = grad_gate_ref.shape[1]
    grad_pre_ref[:, :mixed] = total.astype(bf16)
    grad_pre_ref[:, mixed : mixed + width] = grad_gate_ref[...]
    grad_pre_ref[:, mixed + width :] = grad_small_ref[...]
    grad = jnp.zeros(grad_rows_ref.shape, f32)
    begin = 0
    for ref in (wq_ref, wk_ref, wv_ref, wg_ref, ws_ref):
        grad = grad + dot_nt(grad_pre_ref[:, begin : begin + ref.shape[1]], ref[...])
        begin += ref.shape[1]
    gain_sum_ref[0:1, :] += jnp.sum(grad * rows_ref[...].astype(f32), axis=0, keepdims=True)
    if cube:
        scatter_block(step, CubeScatter("head", grad_rows_ref, *refs), grad)
    else:
        grad_rows_ref[...] = grad.astype(bf16)


MESH = pl.DeviceIdType.MESH
ANYWHERE = pl.BlockSpec(memory_space=pl.ANY)


def line_barrier(axis, cube=None):
    devices, place = lax.axis_size(axis), lax.axis_index(axis)
    barrier = pltpu.get_barrier_semaphore()

    @pl.when(place > 0)
    def _():
        pl.semaphore_signal(barrier, inc=1, device_id={axis: place - 1}, device_id_type=MESH)

    @pl.when(place < devices - 1)
    def _():
        pl.semaphore_signal(barrier, inc=1, device_id={axis: place + 1}, device_id_type=MESH)

    more = 0
    if cube is not None:
        for mask in (1, 2, 4):
            pl.semaphore_signal(
                barrier, inc=1, device_id={cube: flip(lax.axis_index(cube), mask)}, device_id_type=MESH
            )
        more = 3

    @pl.when((place > 0) & (place < devices - 1))
    def _():
        pl.semaphore_wait(barrier, 2 + more)

    @pl.when((place == 0) | (place == devices - 1))
    def _():
        pl.semaphore_wait(barrier, 1 + more)


class LineSum:
    skew = 2
    window = 4

    def __init__(self, axis, counts, depths, parts, passed, arrived, sums, reduce_sems, back_sems):
        self.axis, self.counts, self.depths = axis, counts, depths
        self.single = [array.shape[0] == depth for array, depth in zip(sums, depths)]
        self.parts, self.passed, self.arrived, self.sums = parts, passed, arrived, sums
        self.sems = (reduce_sems, back_sems)
        self.devices, self.place = lax.axis_size(axis), lax.axis_index(axis)
        self.steps = max(counts) + self.skew * (self.devices - 1)

    def rows_of(self, half, index, at):
        depth = self.depths[index]
        return pl.ds(pl.multiple_of((half * self.counts[index] + at) * depth, depth), depth)

    def copy(self, half, index, at, target, back):
        rows = self.rows_of(half, index, at)
        slot = half * self.counts[index] + at
        source, landing = (self.sums, self.sums) if back else (self.passed, self.arrived)
        sent, received = self.sems[back][2 * index], self.sems[back][2 * index + 1]
        return pltpu.make_async_remote_copy(
            source[index].at[rows, :], landing[index].at[rows, :], sent.at[slot], received.at[slot],
            device_id={self.axis: target}, device_id_type=MESH,
        )

    def send(self, half, index, at, target, back):
        @pl.when(at >= self.window)
        def _():
            self.copy(half, index, at - self.window, target, back).wait_send()

        self.copy(half, index, at, target, back).start()

    def each(self, handle):
        place, last = self.place, self.devices - 1
        for half in range(2):
            ends = (last, 0) if half == 0 else (0, last)
            toward = place - 1 if half == 0 else place + 1
            away = place + 1 if half == 0 else place - 1
            for index in range(len(self.counts)):
                if half == 0 or not self.single[index]:
                    handle(half, index, toward, away, place == ends[0], place == ends[1])

    def reduce(self, step):
        def handle(half, index, toward, away, begin, end):
            late = (self.devices - 1 - self.place) if half == 0 else self.place
            at = step - self.skew * late

            @pl.when((at >= 0) & (at < self.counts[index]))
            def _():
                rows = self.rows_of(half, index, at)

                @pl.when(begin)
                def _():
                    self.passed[index][rows, :] = self.parts[index][rows, :]
                    self.send(half, index, at, toward, 0)

                @pl.when(jnp.logical_not(begin))
                def _():
                    self.copy(half, index, at, toward, 0).wait_recv()
                    added = (
                        self.parts[index][rows, :].astype(f32) + self.arrived[index][rows, :].astype(f32)
                    ).astype(bf16)

                    @pl.when(jnp.logical_not(end))
                    def _():
                        self.passed[index][rows, :] = added
                        self.send(half, index, at, toward, 0)

                    @pl.when(end)
                    def _():
                        self.sums[index][rows, :] = added

        self.each(handle)

    def back(self, step, given=None):
        def handle(half, index, toward, away, begin, end):
            late = self.place if half == 0 else (self.devices - 1 - self.place)
            at = step - self.skew * late

            @pl.when((at >= 0) & (at < self.counts[index]))
            def _():
                if given is not None:
                    @pl.when(end)
                    def _():
                        rows = self.rows_of(half, index, at)
                        self.sums[index][rows, :] = given[index][rows, :]

                @pl.when(jnp.logical_not(end))
                def _():
                    self.copy(half, index, at, away, 1).wait_recv()

                @pl.when(jnp.logical_not(begin))
                def _():
                    self.send(half, index, at, away, 1)

        self.each(handle)

    def settle(self, back):
        def handle(half, index, toward, away, begin, end):
            count = self.counts[index]
            for at in range(max(count - self.window, 0), count):
                @pl.when(jnp.logical_not(begin if back else end))
                def _():
                    self.copy(half, index, at, away if back else toward, back).wait_send()

        self.each(handle)


def line_sum_kernel(axis, cube, counts, depths, *refs):
    total = len(counts)
    rows_ref, grads_ref, *refs = refs
    parts, refs = refs[: total - 2], refs[total - 2 :]
    if cube:
        block_ref, *refs = refs
    sums, refs = refs[:total], refs[total:]
    if cube:
        whole_ref, blocks_ref, *refs = refs
    product, turned, *refs = refs
    parts = (product, turned, *parts)
    width = product.shape[1]
    arrived, passed, refs = refs[:total], refs[total : 2 * total], refs[2 * total :]
    share = BLOCK // depths[0]
    tiles = counts[0] // share
    line = LineSum(axis, counts, depths, parts, passed, arrived, sums, refs[: 2 * total], refs[2 * total : 4 * total])
    line_barrier(axis, "head" if cube else None)

    begin = max(counts)
    if cube:
        final = CubeTotal(*refs[4 * total : 4 * total + 4])
        gather = CubeGather("head", block_ref, blocks_ref, *refs[4 * total + 4 :], enter=False)
        gather.first()

    turned[...] = dot_tn(grads_ref[:, width:], rows_ref[...])[: turned.shape[0], :].astype(bf16)

    def step_on(step, carry):
        @pl.when((step % share == 0) & (step < tiles * share))
        def _():
            for half in range(2):
                columns = pl.ds(pl.multiple_of((half * tiles + step // share) * BLOCK, BLOCK), BLOCK)
                product[columns, :] = dot_tn(rows_ref[:, columns], grads_ref[:, :width]).astype(bf16)

        @pl.when(step < line.steps)
        def _():
            line.reduce(step)

        @pl.when(step >= begin)
        def _():
            line.back(step - begin)

        if cube:
            for at, phase in ((begin // 2, gather.second), (begin * 3 // 4, gather.third), (begin, gather.fourth)):
                @pl.when(step == at)
                def _():
                    phase()

            after = begin + line.skew * line.devices
            for stage in range(4):
                @pl.when(step == after + 3 * stage)
                def _():
                    if stage:
                        final.end(stage - 1, whole_ref)
                    else:
                        final.held[0] = sums[-1][: whole_ref.shape[0], :].astype(f32)
                    if stage < 3:
                        final.copy(stage).start()

        return carry

    lax.fori_loop(0, begin + line.steps, step_on, 0)
    line.settle(0)
    line.settle(1)
    if cube:
        gather.last()


class CubeTotal:
    def __init__(self, held, arrived, send_sem, recv_sem):
        self.held, self.arrived, self.send_sem, self.recv_sem = held, arrived, send_sem, recv_sem

    def copy(self, stage):
        return pltpu.make_async_remote_copy(
            self.held.at[stage], self.arrived.at[stage], self.send_sem.at[stage], self.recv_sem.at[stage],
            device_id={"head": flip(lax.axis_index("head"), (1, 2, 4)[stage])}, device_id_type=MESH,
        )

    def end(self, stage, total_ref):
        self.copy(stage).wait()
        if stage < 2:
            self.held[stage + 1] = self.held[stage] + self.arrived[stage]
        else:
            total_ref[...] = self.held[stage] + self.arrived[stage]


def line_scratch(arrays, depths, moves):
    counts = tuple(max(array.shape[0] // (2 * depth), 1) for array, depth in zip(arrays, depths))
    semaphores = []
    for count in counts:
        semaphores += [pltpu.SemaphoreType.DMA((2 * count,))] * 2
    return counts, semaphores * moves


def line_sum(rows, grads, blocks, given, depths, axis, collective_id):
    cube = lax.axis_size("head") == 8
    arrays = (
        struct((rows.shape[1], grads.shape[1] - LANES), bf16), struct((2 * HALO, rows.shape[1]), bf16), *given,
    )
    counts, semaphores = line_scratch(arrays, depths, 2)
    vmem = pl.BlockSpec(memory_space=pltpu.VMEM)
    scratch = [pltpu.VMEM(array.shape, bf16) for array in (*arrays[:2], *arrays, *arrays)] + semaphores
    total = (8, arrays[-1].shape[1])
    if cube:
        scratch += [pltpu.VMEM((3,) + total, f32)] * 2 + [pltpu.SemaphoreType.DMA((3,))] * 2 + CUBE_SEMAPHORES
    results = pl.pallas_call(
        functools.partial(line_sum_kernel, axis, cube, counts, tuple(depths)),
        in_specs=[vmem] * len(arrays) + [ANYWHERE] * cube,
        out_specs=[vmem] * (len(arrays) + cube) + [ANYWHERE] * cube,
        out_shape=[struct(array.shape, bf16) for array in arrays]
        + [struct(total, f32)] * cube
        + [struct((8 * block.shape[0], block.shape[1]), bf16) for block in blocks],
        scratch_shapes=scratch,
        compiler_params=pltpu.CompilerParams(
            collective_id=collective_id, has_side_effects=True, vmem_limit_bytes=VMEM_LIMIT
        ),
        cost_estimate=pl.CostEstimate(flops=10**8, bytes_accessed=40 * 10**6, transcendentals=0),
        name="line_sum",
    )(rows, grads, *given, *blocks)
    if not cube:
        results = [*results, lax.psum(results[-1][:8].astype(f32), "head")]
    return results


def whole(shape):
    zeros = (0,) * len(shape)
    return pl.BlockSpec(tuple(shape), lambda step: zeros)


def held(shape):
    zeros = (0,) * len(shape)
    return pl.BlockSpec(tuple(shape), lambda step: zeros, pipeline_mode=pl.Buffered(1))


def by_rows(width, chunks=None):
    if chunks is None:
        return pl.BlockSpec((BLOCK, width), lambda step: (step, 0))
    return pl.BlockSpec((BLOCK, width), lambda step: (chunks - 1 - step, 0))


def by_chunk(shape, chunks=None):
    rest = (0,) * len(shape)
    if chunks is None:
        return pl.BlockSpec((1,) + tuple(shape), lambda step: (step,) + rest)
    return pl.BlockSpec((1,) + tuple(shape), lambda step: (chunks - 1 - step,) + rest)


SCALARS = pl.BlockSpec(memory_space=pltpu.SMEM)


def feed_kernel(
    axis, devices, rows,
    own_ref, *refs,
):
    given, kept, refs = refs[:4], refs[4:9], refs[9:]
    total_ref, *refs = refs
    hidden_ref, *refs = refs
    inside, refs = refs[:8], refs[8:]
    inside = (*inside, inside[0])
    grads_ref, w_gate_ref, w_up_ref, w_down_ref = inside[:4]
    blocks_ref, turned_ref, grad_gate_ref, grad_up_ref, part_ref = inside[4:]
    parts, arrived, gather_send, gather_recv, chain_send, chain_recv, load_sem, store_sem = refs
    place = lax.axis_index(axis)
    piece = rows // 2

    def load(index):
        return pltpu.make_async_copy(given[index], inside[index], load_sem.at[index])

    def store(index):
        return pltpu.make_async_copy(inside[4 + index], kept[index], store_sem.at[index])

    for index in (3, 0, 1, 2):
        load(index).start()
    line_barrier(axis)

    def span(block, half):
        return pl.ds(pl.multiple_of(block * rows + half * piece, piece), piece)

    def full(block):
        return pl.ds(pl.multiple_of(block * rows, rows), rows)

    def gather(owner, hop, way, half):
        target = place + 1 - 2 * way
        slot = (hop * 2 + way) * 2 + half
        return pltpu.make_async_remote_copy(
            blocks_ref.at[span(owner, half), :], blocks_ref.at[span(owner, half), :],
            gather_send.at[slot], gather_recv.at[slot], device_id={axis: target}, device_id_type=MESH,
        )

    def quarter(block, part):
        return pl.ds(pl.multiple_of(block * rows + part * (rows // 4), rows // 4), rows // 4)

    def chain(block, way, part, at):
        target = at + 1 - 2 * way
        landing = jnp.where((block == target) & (way == 0), devices, block)
        slot = (way * devices + block) * 4 + part
        return pltpu.make_async_remote_copy(
            parts.at[quarter(block, part), :], arrived.at[quarter(landing, part), :],
            chain_send.at[slot], chain_recv.at[slot], device_id={axis: target}, device_id_type=MESH,
        )

    blocks_ref[full(place), :] = own_ref[...]

    def event(step, carry):
        hop = (step + 1) // 2
        way = (step + 1) % 2
        owner = jnp.where(way == 0, place - hop, place + hop)

        @pl.when(step == 0)
        def _():
            for side in range(2):
                @pl.when((place + 1 - 2 * side >= 0) & (place + 1 - 2 * side < devices))
                def _():
                    for half in range(2):
                        gather(place, 0, side, half).start()

            for index in range(4):
                load(index).wait()

        @pl.when((step > 0) & (way == 0))
        def _():
            for side in range(2):
                come = place - hop if side == 0 else place + hop
                goes = place + 1 if side == 0 else place - 1

                @pl.when((come >= 0) & (come < devices))
                def _():
                    for half in range(2):
                        gather(come, hop - 1, side, half).wait_recv()

                        @pl.when((goes >= 0) & (goes < devices))
                        def _():
                            gather(come, hop, side, half).start()

        @pl.when((owner >= 0) & (owner < devices))
        def _():
            here = full(owner)
            grad_hidden = dot_nt(grads_ref[here, :], w_down_ref[...])

            block = blocks_ref[here, :]
            gate_pre = dot(block, w_gate_ref[...])
            up_pre = dot(block, w_up_ref[...])
            sigma = sigmoid(gate_pre)
            act = gate_pre * sigma
            hidden = (act * up_pre).astype(bf16)
            hidden_ref[here, :] = hidden
            turned_ref[:, full(owner)] = hidden.T
            grad_gate_ref[here, :] = (grad_hidden * up_pre * (sigma * (1.0 + gate_pre * (1.0 - sigma)))).astype(bf16)
            grad_up_ref[here, :] = (grad_hidden * act).astype(bf16)
            grad = dot_nt(grad_gate_ref[here, :], w_gate_ref[...]) + dot_nt(grad_up_ref[here, :], w_up_ref[...])

            @pl.when(step == 0)
            def _():
                total_ref[...] = grad

            @pl.when(step > 0)
            def _():
                parts[here, :] = grad.astype(bf16)

        @pl.when((way == 1) & (step > 0))
        def _():
            for part in range(4):
                for turn in range(2):
                    side = jnp.where(2 * place < devices, turn, 1 - turn)
                    block = jnp.where(side == 1, devices - 1 - hop, hop)
                    begins = place == jnp.where(side == 1, devices - 1, 0)
                    valid = jnp.where(side == 1, block < place, block > place)

                    @pl.when(valid)
                    def _():
                        @pl.when(jnp.logical_not(begins))
                        def _():
                            chain(block, side, part, place + 2 * side - 1).wait_recv()
                            at = quarter(block, part)
                            parts[at, :] = (parts[at, :].astype(f32) + arrived[at, :].astype(f32)).astype(bf16)

                        chain(block, side, part, place).start()

        return carry

    lax.fori_loop(0, 2 * devices - 1, event, 0)

    for index in range(4):
        store(index).start()

    def feed_part(block, carry):
        part_ref[full(block), :] = dot(hidden_ref[full(block), :], w_down_ref[...]).astype(bf16)
        return carry

    lax.fori_loop(0, devices, feed_part, 0)
    store(4).start()

    for side, landing, comes in ((1, place, place < devices - 1), (0, devices, place > 0)):
        @pl.when(comes)
        def _():
            for part in range(4):
                chain(place, side, part, place + 2 * side - 1).wait_recv()
                at = pl.ds(part * (rows // 4), rows // 4)
                total_ref[at, :] += arrived[quarter(landing, part), :].astype(f32)

    def gather_end(step, carry):
        hop = step // 2
        way = step % 2
        owner = jnp.where(way == 0, place - hop, place + hop)
        target = place + 1 - 2 * way

        @pl.when((owner >= 0) & (owner < devices) & (target >= 0) & (target < devices))
        def _():
            for half in range(2):
                gather(owner, hop, way, half).wait_send()

        return carry

    lax.fori_loop(0, 2 * (devices - 1), gather_end, 0)

    def chain_end(block, carry):
        @pl.when(block < place)
        def _():
            for part in range(4):
                chain(block, 1, part, place).wait_send()

        @pl.when(block > place)
        def _():
            for part in range(4):
                chain(block, 0, part, place).wait_send()

        return carry

    lax.fori_loop(0, devices, chain_end, 0)
    for index in range(5):
        store(index).wait()


def feed(own, grads, w_gate, w_up, w_down, axis, collective_id):
    devices = lax.axis_size(axis)
    rows, width = own.shape
    units = w_gate.shape[1]
    vmem = pl.BlockSpec(memory_space=pltpu.VMEM)
    moves = pltpu.SemaphoreType.DMA((4 * devices,))
    chains = pltpu.SemaphoreType.DMA((8 * devices,))
    given = (grads, w_gate, w_up, w_down)
    kept = [struct((devices * rows, width), bf16), struct((units, devices * rows), bf16)]
    kept += [struct((devices * rows, units), bf16)] * 2
    kept += [struct((devices * rows, width), bf16)]
    return pl.pallas_call(
        functools.partial(feed_kernel, axis, devices, rows),
        in_specs=[vmem] + [ANYWHERE] * 4,
        out_specs=[ANYWHERE] * 5 + [vmem],
        out_shape=kept + [struct((rows, width), f32)],
        scratch_shapes=[
            pltpu.VMEM((devices * rows, units), bf16),
            *(pltpu.VMEM(array.shape, array.dtype) for array in (*given, *kept[:4])),
            pltpu.VMEM((devices * rows, width), bf16), pltpu.VMEM(((devices + 1) * rows, width), bf16),
            moves, moves, chains, chains, pltpu.SemaphoreType.DMA((4,)), pltpu.SemaphoreType.DMA((5,)),
        ],
        compiler_params=pltpu.CompilerParams(
            collective_id=collective_id, has_side_effects=True, vmem_limit_bytes=61 * 1024 * 1024
        ),
        name="feed",
    )(own, grads, w_gate, w_up, w_down)


def flip(index, mask):
    for bit in (1, 2, 4):
        if mask & bit:
            index = index + bit * (1 - 2 * ((index // bit) % 2))
    return index


def cube_barrier(axis, place):
    barrier = pltpu.get_barrier_semaphore()
    for mask in (1, 2, 4):
        pl.semaphore_signal(barrier, inc=1, device_id={axis: flip(place, mask)}, device_id_type=MESH)
    pl.semaphore_wait(barrier, 3)


class CubeGather:
    FIRST = ((0, 0, 2), (0, 1, 4), (0, 1, 2), (0, 0, 4), (0, 0, 1), (0, 1, 1))
    SECOND = ((2, 0, 4), (4, 1, 2), (2, 0, 1), (4, 1, 1))
    THIRD = ((2, 1, 1), (4, 0, 1))
    FOURTH = ((6, 0, 1), (6, 1, 1))

    def __init__(self, axis, own_ref, all_ref, own_sem, send_sem, recv_sem, stride=None, lead=0, enter=True):
        self.axis, self.own_ref, self.all_ref = axis, own_ref, all_ref
        self.stride, self.lead, self.enter = stride or own_ref.shape[0], lead, enter
        self.own_sem, self.send_sem, self.recv_sem = own_sem, send_sem, recv_sem
        self.place = lax.axis_index(axis)
        self.rows = own_ref.shape[0]
        self.piece = self.rows // 2

    def part(self, mask, half):
        start = flip(self.place, mask) * self.stride + self.lead + half * self.piece
        return self.all_ref.at[pl.ds(pl.multiple_of(start, LEAD), self.piece), :]

    def copy(self, mask, half, toward):
        source = self.part(mask, half) if mask else self.own_ref.at[pl.ds(half * self.piece, self.piece), :]
        return pltpu.make_async_remote_copy(
            source, self.part(mask, half),
            self.send_sem.at[toward * 2 + half, mask // 2], self.recv_sem.at[(mask ^ toward) * 2 + half],
            device_id={self.axis: flip(self.place, toward)}, device_id_type=MESH,
        )

    def wait(self, mask, half):
        pltpu.make_async_remote_copy(
            self.part(mask, half), self.part(mask, half), self.send_sem.at[0, 0], self.recv_sem.at[mask * 2 + half],
            device_id={self.axis: flip(self.place, 1)}, device_id_type=MESH,
        ).wait_recv()

    def own(self):
        start = pl.multiple_of(self.place * self.rows, self.rows)
        return pltpu.make_async_copy(self.own_ref, self.all_ref.at[pl.ds(start, self.rows), :], self.own_sem)

    def first(self):
        if self.own_sem is not None:
            if self.enter:
                cube_barrier(self.axis, self.place)
            self.own().start()
        for move in self.FIRST:
            self.copy(*move).start()

    def second(self):
        self.wait(2, 0)
        self.copy(*self.SECOND[0]).start()
        self.wait(4, 1)
        for move in self.SECOND[1:]:
            self.copy(*move).start()

    def third(self):
        for move in self.THIRD:
            self.wait(*move[:2])
            self.copy(*move).start()

    def fourth(self):
        for move in self.FOURTH:
            self.wait(*move[:2])
            self.copy(*move).start()

    def last(self):
        if self.own_sem is not None:
            for mask in (1, 3, 5, 7):
                for half in range(2):
                    self.wait(mask, half)
            self.own().wait()
        for move in self.FIRST + self.SECOND + self.THIRD + self.FOURTH:
            self.copy(*move).wait_send()


CUBE_SEMAPHORES = [pltpu.SemaphoreType.DMA, pltpu.SemaphoreType.DMA((10, 4)), pltpu.SemaphoreType.DMA((16,))]


def feed_grads_kernel(
    blocks_ref, grads_ref, hidden_ref, grad_gate_ref, grad_up_ref, down_ref, gate_ref, up_ref,
):
    gate_ref[...] = dot_tn(blocks_ref[...], grad_gate_ref[...]).astype(bf16)
    up_ref[...] = dot_tn(blocks_ref[...], grad_up_ref[...]).astype(bf16)
    down_ref[...] = dot(hidden_ref[...], grads_ref[...]).astype(bf16)


def feed_grads(own, blocks, grads, hidden, grad_gate, grad_up, axis):
    rows, width = blocks.shape
    units = hidden.shape[0]
    tall = pl.BlockSpec((rows, BLOCK), lambda step: (0, step))
    down = pl.BlockSpec((units, BLOCK), lambda step: (0, step))
    flat = pl.BlockSpec((BLOCK, units), lambda step: (step, 0))
    fixed = held((rows, units))
    results = pl.pallas_call(
        feed_grads_kernel,
        grid=(width // BLOCK,),
        in_specs=[tall, tall, held(hidden.shape), fixed, fixed],
        out_specs=[down, flat, flat],
        out_shape=[
            struct((units, width), bf16), struct((width, units), bf16), struct((width, units), bf16),
        ],
        compiler_params=params(),
        name="feed_grads",
    )(blocks, grads, hidden, grad_gate, grad_up)
    return (*results, lax.all_gather(own, axis, axis=0, tiled=True))


def feed_core_kernel(
    sizes, chunks, axis, tiles,
    meta, total_in, hidden_in, low_ref, next_gain_ref, blocks_ref, grads_ref, hidden_ref, feed_gate_ref, feed_up_ref,
    w_output_ref, core_ref, gate_ref, gain_ref, qkv_ref, scal_ref, w_in_ref, drop_ref,
    down_out, gate_out, up_out, all_ref, *refs,
):
    outs, (grad_in_ref, gain_sum_ref, rows_ref, copy_sem, send_sem, recv_sem, *later) = refs[:6], refs[6:]
    step = pl.program_id(0)
    rows = total_in.shape[0]
    own = pl.ds(pl.multiple_of(lax.axis_index(axis) * rows, rows), rows)
    gather = CubeGather(axis, rows_ref.at[own, :], rows_ref, None, send_sem, recv_sem)

    @pl.when(step == 0)
    def _():
        grad_norm, gain_sum = rms_back(hidden_in[...], next_gain_ref[...], total_in[...])
        grad_in = low_ref[...].astype(f32) + grad_norm
        grad_in_ref[...] = grad_in
        gain_sum_ref[0:1, :] = gain_sum[None, :]
        rows_ref[own, :] = grad_in.astype(bf16)
        cube_barrier(axis, gather.place)
        gather.first()

    @pl.when(step == tiles - 1)
    def _():
        gather.second()
        gather.third()

    @pl.when(step == tiles + 3)
    def _():
        gather.fourth()

    for mask in (1, 3, 5, 7):
        @pl.when(step == (1 if mask == 1 else tiles + mask))
        def _():
            for half in range(2):
                gather.wait(mask, half)

    @pl.when((step >= 2) & (step < tiles + 2))
    def _():
        turned = blocks_ref[...].T
        gate_out[...] = dot(turned, feed_gate_ref[...]).astype(bf16)
        up_out[...] = dot(turned, feed_up_ref[...]).astype(bf16)
        down_out[...] = dot(hidden_ref[...], grads_ref[...]).astype(bf16)

    @pl.when((step < 2) | (step >= tiles + 2))
    def _():
        chunk = core_order(axis, step, tiles)
        core_grad_kernel(
            *sizes, chunks,
            meta, rows_ref.at[pl.ds(pl.multiple_of(chunk * BLOCK, BLOCK), BLOCK), :], w_output_ref,
            core_ref, gate_ref, gain_ref, qkv_ref, scal_ref, w_in_ref, drop_ref, *outs, chunk=chunk, later=later,
        )

    @pl.when(step == tiles + chunks - 1)
    def _():
        kept = pltpu.make_async_copy(rows_ref, all_ref, copy_sem)
        kept.start()
        total_ref = outs[5]
        pulls, drops, throughs = later

        def pass_on(at, carry):
            chunk = chunks - 1 - at
            for head in range(sizes[0]):
                total = total_ref[head]
                total_ref[head] = (
                    throughs[chunk, head][0:1, 0:1] * total
                    - dot_tn(drops[chunk, head], total.astype(bf16)) + pulls[chunk, head]
                )
            return carry

        lax.fori_loop(0, chunks, pass_on, 0)
        gather.last()
        kept.wait()


def core_order(axis, step, tiles):
    return cube_order(axis, jnp.where(step < 2, step, jnp.maximum(step - tiles, 1)))


class CubeScatter:
    def __init__(self, axis, total_ref, given, other, leaving, coming, waiting, send_sem, recv_sem):
        self.axis, self.total_ref = axis, total_ref
        self.given, self.other, self.leaving, self.coming, self.waiting = given, other, leaving, coming, waiting
        self.send_sem, self.recv_sem = send_sem, recv_sem
        self.place = lax.axis_index(axis)
        self.piece = total_ref.shape[0] // 2

    def slot(self, index, half):
        return pl.ds((2 * index + half) * self.piece, self.piece)

    def core_copy(self, mask, half):
        at = self.slot(mask // 2, half)
        return pltpu.make_async_remote_copy(
            self.given.at[at, :], self.other.at[at, :],
            self.send_sem.at[0, mask // 2, half], self.recv_sem.at[0, mask // 2, half],
            device_id={self.axis: flip(self.place, 1)}, device_id_type=MESH,
        )

    def landing(self, index, toward):
        return (toward // 2 - 1) * 2 + (1 if index else 0)

    def chip_copy(self, index, half, toward):
        return pltpu.make_async_remote_copy(
            self.leaving.at[self.slot(index, half), :],
            self.coming.at[self.slot(self.landing(index, toward), half), :],
            self.send_sem.at[toward // 2, index, half], self.recv_sem.at[toward // 2, 1 if index else 0, half],
            device_id={self.axis: flip(self.place, toward)}, device_id_type=MESH,
        )

    def arrived(self, index, half, toward):
        self.chip_copy(index, half, toward).wait_recv()
        return self.coming[self.slot(self.landing(index, toward), half), :].astype(f32)

    def send(self, index, half, toward, values):
        self.leaving[self.slot(index, half), :] = values.astype(bf16)
        self.chip_copy(index, half, toward).start()

    def take(self, mask, block):
        piece = self.piece
        if mask % 2:
            self.given[pl.ds(mask // 2 * 2 * piece, 2 * piece), :] = block.astype(bf16)
            for half in range(2):
                self.core_copy(mask, half).start()
            if mask == 1:
                self.send(2, 0, 4, self.waiting[0] + self.arrived(0, 0, 2))
                self.send(1, 1, 2, self.waiting[1] + self.arrived(0, 1, 4))
            return
        parts = []
        for half in range(2):
            self.core_copy(mask + 1, half).wait_recv()
            parts.append(
                block[half * piece : (half + 1) * piece, :]
                + self.other[self.slot(mask // 2, half), :].astype(f32)
            )
        if mask == 6:
            self.send(0, 0, 2, parts[0])
            self.send(0, 1, 4, parts[1])
        elif mask == 4:
            self.send(2, 1, 4, parts[1])
            self.waiting[0] = parts[0]
        elif mask == 2:
            self.send(1, 0, 2, parts[0])
            self.waiting[1] = parts[1]
        else:
            self.total_ref[0:piece, :] = parts[0]
            self.total_ref[piece:, :] = parts[1]

    def finish(self):
        piece = self.piece
        self.total_ref[0:piece, :] += self.arrived(1, 0, 2)
        self.total_ref[piece:, :] += self.arrived(2, 1, 4)
        self.total_ref[0:piece, :] += self.arrived(2, 0, 4)
        self.total_ref[piece:, :] += self.arrived(1, 1, 2)
        for mask in (7, 5, 3, 1):
            for half in range(2):
                self.core_copy(mask, half).wait_send()
        for index, half, toward in ((0, 0, 2), (0, 1, 4), (1, 0, 2), (2, 1, 4), (1, 1, 2), (2, 0, 4)):
            self.chip_copy(index, half, toward).wait_send()


def scatter_block(step, scatter, block, inside=False):
    if not inside:
        @pl.when(step == 0)
        def _():
            cube_barrier("head", scatter.place)

    for mask in range(8):
        @pl.when(step == 7 - mask)
        def _():
            scatter.take(mask, block)

    if not inside:
        @pl.when(step == 7)
        def _():
            scatter.finish()


def cube_scatter_scratch(rows, width):
    return [
        pltpu.VMEM((4 * rows, width), bf16), pltpu.VMEM((4 * rows, width), bf16),
        pltpu.VMEM((3 * rows, width), bf16), pltpu.VMEM((4 * rows, width), bf16),
        pltpu.VMEM((2, rows // 2, width), f32),
        pltpu.SemaphoreType.DMA((3, 4, 2)), pltpu.SemaphoreType.DMA((3, 4, 2)),
    ]


def params(collective_id=None):
    return pltpu.CompilerParams(
        dimension_semantics=("arbitrary",),
        vmem_limit_bytes=VMEM_LIMIT,
        collective_id=collective_id,
        has_side_effects=collective_id is not None,
    )


def widen_kernel(cuts, total, *refs):
    given, refs = refs[:total], refs[total:]
    if cuts:
        all_in, *refs = refs
        begin = 0
        for cut, result in zip(cuts, refs):
            result[...] = all_in[:, begin : begin + cut].astype(f32)
            begin += cut
        refs = refs[len(cuts) :]
    for source, result in zip(given, refs):
        result[...] = source[...].astype(f32)


def widen(given, columns=None, cuts=()):
    steps = 8 if given[0].shape[0] % 128 == 0 else 4
    sources = list(given)
    shapes = [array.shape for array in given]

    def part(shape):
        return pl.BlockSpec((shape[0] // steps, shape[1]), lambda step: (step, 0))

    specs = [part(shape) for shape in shapes]
    if cuts:
        sources.append(columns)
        cut_shapes = [(columns.shape[0], cut) for cut in cuts]
        specs = [part(shape) for shape in cut_shapes] + specs
        shapes = cut_shapes + shapes
    return pl.pallas_call(
        functools.partial(widen_kernel, cuts, len(given)),
        grid=(steps,),
        in_specs=[part(array.shape) for array in sources],
        out_specs=specs,
        out_shape=[struct(shape, f32) for shape in shapes],
        compiler_params=params(),
        name="widen",
    )(*sources)


def struct(shape, dtype):
    return jax.ShapeDtypeStruct(tuple(shape), dtype)


def from_earlier(array, axis):
    devices = lax.axis_size(axis)
    parts = [
        lax.ppermute(array, axis, [(i, i + by) for i in range(devices - by)])
        for by in range(devices - 1, 0, -1)
    ]
    return jnp.stack(parts) if parts else jnp.zeros((1,) + array.shape, array.dtype)


def from_later(array, axis):
    devices = lax.axis_size(axis)
    parts = [
        lax.ppermute(array, axis, [(i + by, i) for i in range(devices - by)])
        for by in range(devices - 1, 0, -1)
    ]
    return jnp.stack(parts) if parts else jnp.zeros((1,) + array.shape, array.dtype)


def shards(
    inputs,
    doc_lengths,
    first_gain,
    w_query,
    w_key,
    w_value,
    w_outgate,
    w_decay,
    w_beta,
    conv_query,
    conv_key,
    conv_value,
    decay_log,
    decay_bias,
    head_gain,
    w_output,
    second_gain,
    w_gate,
    w_up,
    w_down,
    cotangent,
):
    row_count, model_width = inputs.shape
    heads = decay_log.shape[0]
    qw, vw = w_query.shape[1], w_value.shape[1]
    key_width, value_width = qw // heads, vw // heads
    mixed_width = 2 * qw + vw
    taps = conv_query.shape[0]
    docs = doc_lengths.shape[0]
    seq_index = lax.axis_index("seq")
    head_index = lax.axis_index("head")
    head_total = lax.axis_size("head")
    seq_rows = row_count * head_total
    chunks = seq_rows // BLOCK
    others = max(lax.axis_size("seq") - 1, 1)
    sizes = (heads, key_width, value_width, docs)

    inputs_f = inputs.astype(f32)
    normed = rms_scale(inputs_f, first_gain).astype(bf16)
    meta = jnp.concatenate(
        [(seq_index * seq_rows).astype(jnp.int32)[None], slot_starts(doc_lengths)]
    )
    _, own_valid = layout(doc_lengths, (seq_index * head_total + head_index) * row_count, row_count)

    grad_out = cotangent.astype(f32) * own_valid.astype(f32)[:, None]
    grad_low = grad_out.astype(bf16)
    w_small = jnp.concatenate([w_decay, w_beta, jnp.zeros((model_width, LANES - 2 * heads), bf16)], axis=1)
    weights = (w_query, w_key, w_value, w_outgate, w_small)
    all_width = mixed_width + vw + LANES
    conv_all = jnp.concatenate([conv_query, conv_key, conv_value], axis=1)
    dvec = jnp.zeros((8, LANES), f32)
    dvec = dvec.at[0, :heads].set(decay_bias).at[1, :heads].set(-jnp.exp(decay_log))
    map_shape = (heads, key_width, key_width + value_width)

    cube = head_total == 8 and chunks == 8 and row_count == BLOCK
    if cube:
        rows_given, rows_spec = normed, held(normed.shape)

        def at_step(step):
            return cube_order("head", step)
    else:
        block_rows = lax.all_gather(normed, "head", axis=0, tiled=True)
        tail = from_previous(block_rows[seq_rows - LEAD :])
        blocks = block_rows.reshape(chunks, BLOCK, model_width)
        leads = jnp.concatenate([tail[None], blocks[:-1, BLOCK - LEAD :]], axis=0)
        rows_given = jnp.concatenate([leads, blocks], axis=1).reshape(chunks * STRIDE, model_width)
        rows_spec = pl.BlockSpec((STRIDE, model_width), lambda step: (step, 0))

        def at_step(step):
            return step

    def rows_out(width):
        return pl.BlockSpec((BLOCK, width), lambda step: (at_step(step), 0))

    def chunk_out(shape):
        return pl.BlockSpec((1,) + tuple(shape), lambda step: (at_step(step),) + (0,) * len(shape))

    results = pl.pallas_call(
        functools.partial(forward_kernel, *sizes, taps, chunks, cube),
        grid=(chunks,),
        in_specs=[
            SCALARS, rows_spec, *(held(weight.shape) for weight in weights), whole(conv_all.shape),
            whole(dvec.shape),
        ],
        out_specs=[
            rows_out(mixed_width), rows_out(mixed_width), rows_out(vw), rows_out(LANES), rows_out(LANES),
            rows_out(mixed_width),
            chunk_out((heads, BLOCK, BLOCK)), chunk_out((heads, BLOCK, key_width)),
            chunk_out((heads, BLOCK, value_width)), chunk_out((heads, key_width, key_width)),
            whole((chunks,) + map_shape), whole(map_shape),
        ] + [ANYWHERE, whole((others,) + map_shape)] * cube,
        out_shape=[
            struct((seq_rows, mixed_width), f32), struct((seq_rows, mixed_width), f32),
            struct((seq_rows, vw), f32), struct((seq_rows, LANES), f32), struct((seq_rows, LANES), f32),
            struct((seq_rows, mixed_width), bf16),
            struct((chunks, heads, BLOCK, BLOCK), bf16), struct((chunks, heads, BLOCK, key_width), bf16),
            struct((chunks, heads, BLOCK, value_width), f32),
            struct((chunks, heads, key_width, key_width), f32),
            struct((chunks,) + map_shape, f32), struct(map_shape, f32),
        ] + [struct((seq_rows, model_width), bf16), struct((others,) + map_shape, bf16)] * cube,
        scratch_shapes=[
            pltpu.VMEM((STRIDE, mixed_width), f32), pltpu.VMEM(map_shape, f32),
            pltpu.VMEM((chunks, heads, key_width, key_width), bf16),
            pltpu.VMEM((chunks, heads, key_width, value_width), f32),
            pltpu.VMEM((chunks, heads, 8, LANES), f32),
        ] + [
            pltpu.VMEM((chunks * STRIDE, model_width), bf16), pltpu.SemaphoreType.DMA((chunks,)),
            pltpu.VMEM((LEAD, model_width), bf16), pltpu.SemaphoreType.DMA((2,)),
            pltpu.SemaphoreType.DMA((8,)), pltpu.SemaphoreType.DMA((8,)), *CUBE_SEMAPHORES[1:],
            pltpu.VMEM(map_shape, bf16), pltpu.VMEM((others,) + map_shape, bf16),
            pltpu.SemaphoreType.DMA((2, others)),
        ] * cube,
        compiler_params=params(2 if cube else None),
        name="mixer_forward",
    )(meta, rows_given, *weights, conv_all, dvec)
    (pre, conv, gate, small, scal, qkv, inverse, w_part, u_part, drop, starts, block_map) = results[:12]
    if cube:
        block_rows, earlier = results[12:]
    else:
        earlier = from_earlier(block_map.astype(bf16), "seq")

    grad_block_two = lax.all_gather(grad_low, "seq", axis=0, tiled=True)
    gain_row = head_gain[None, :]
    def last_first(step):
        return cube_order("head", 7 - step) if cube else step

    def rows_back(width):
        return pl.BlockSpec((BLOCK, width), lambda step: (last_first(step), 0))

    def chunk_back(shape):
        return pl.BlockSpec((1,) + tuple(shape), lambda step: (last_first(step),) + (0,) * len(shape))

    second_row = second_gain[None, :]
    own_rows = (inputs, second_row) if cube else ()
    core, gated, fresh, states, *mixed_parts = pl.pallas_call(
        functools.partial(output_kernel, *sizes, others, cube),
        grid=(chunks,),
        in_specs=[
            SCALARS, whole(earlier.shape), chunk_back(map_shape), chunk_back((heads, BLOCK, key_width)),
            chunk_back((heads, BLOCK, value_width)), rows_back(mixed_width), rows_back(LANES), rows_back(vw),
            whole(gain_row.shape), held(w_output.shape), *(held(array.shape) for array in own_rows),
        ],
        out_specs=[
            rows_back(vw), rows_back(vw), chunk_back((heads, BLOCK, value_width)),
            chunk_back((heads, key_width, value_width)),
            *([whole((row_count, model_width))] * 2 if cube else [rows_back(model_width)]),
        ],
        out_shape=[
            struct((seq_rows, vw), f32), struct((seq_rows, vw), bf16),
            struct((chunks, heads, BLOCK, value_width), bf16),
            struct((chunks, heads, key_width, value_width), f32),
            *(
                [struct((row_count, model_width), f32), struct((row_count, model_width), bf16)]
                if cube else [struct((seq_rows, model_width), bf16)]
            ),
        ],
        scratch_shapes=[pltpu.VMEM((heads, key_width, value_width), f32)]
        + (
            [pltpu.VMEM((row_count, model_width), f32), *cube_scatter_scratch(row_count, model_width)]
            if cube else []
        ),
        compiler_params=params(5 if cube else None),
        name="mixer_output",
    )(meta, earlier, starts, w_part, u_part, qkv, scal, gate, gain_row, w_output, *own_rows)
    if cube:
        hidden_in, normed_two = mixed_parts
    else:
        mixer_out = lax.psum_scatter(mixed_parts[0], "head", scatter_dimension=0, tiled=True).astype(f32)
        hidden_in = inputs_f + mixer_out
        normed_two = rms_scale(hidden_in, second_gain).astype(bf16)

    mlp_block, hidden, grad_gate, grad_up, mlp_part, grad_normed_two = feed(
        normed_two, grad_block_two, w_gate, w_up, w_down, "seq", 3
    )
    mlp_out = lax.psum_scatter(mlp_part, "seq", scatter_dimension=0, tiled=True)
    core_shapes = [
        struct((chunks, heads, BLOCK, value_width), bf16), struct((chunks, heads, BLOCK, value_width), f32),
        struct((chunks, heads, key_width, value_width), f32), struct((seq_rows, vw), bf16),
        struct((8, value_width), f32), struct((heads, key_width, value_width), f32),
    ]
    if cube:
        tiles = model_width // BLOCK
        owned = (grad_normed_two, hidden_in, grad_low, second_row)
        units, mlp_rows = hidden.shape

        def tile(step):
            return jnp.clip(step - 2, 0, tiles - 1)

        def core_chunk(step):
            return core_order("head", step, tiles)

        def core_rows(width):
            return pl.BlockSpec((BLOCK, width), lambda step: (core_chunk(step), 0))

        def core_blocks(shape):
            return pl.BlockSpec((1,) + tuple(shape), lambda step: (core_chunk(step),) + (0,) * len(shape))

        tall = pl.BlockSpec((mlp_rows, BLOCK), lambda step: (0, tile(step)))
        down = pl.BlockSpec((units, BLOCK), lambda step: (0, tile(step)))
        flat = pl.BlockSpec((BLOCK, units), lambda step: (tile(step), 0))
        results = pl.pallas_call(
            functools.partial(feed_core_kernel, sizes, chunks, "head", tiles),
            grid=(tiles + chunks,),
            in_specs=[
                SCALARS, *(held(array.shape) for array in owned), tall, tall, *(held(array.shape) for array in (hidden, grad_gate, grad_up)),
                held(w_output.shape), core_rows(vw), core_rows(vw), whole(gain_row.shape), core_rows(mixed_width),
                core_rows(LANES), core_blocks((heads, BLOCK, key_width)), core_blocks((heads, key_width, key_width)),
            ],
            out_specs=[
                down, flat, flat, ANYWHERE,
                core_blocks((heads, BLOCK, value_width)), core_blocks((heads, BLOCK, value_width)),
                core_blocks((heads, key_width, value_width)), core_rows(vw),
                whole((8, value_width)), whole((heads, key_width, value_width)),
                whole((row_count, model_width)), whole((8, model_width)),
            ],
            out_shape=[
                struct((units, model_width), bf16), struct((model_width, units), bf16),
                struct((model_width, units), bf16), struct((seq_rows, model_width), bf16), *core_shapes,
                struct((row_count, model_width), f32), struct((8, model_width), f32),
            ],
            scratch_shapes=[
                pltpu.VMEM((seq_rows, model_width), bf16), pltpu.SemaphoreType.DMA, *CUBE_SEMAPHORES[1:],
                pltpu.VMEM((chunks, heads, key_width, value_width), f32),
                pltpu.VMEM((chunks, heads, key_width, key_width), bf16),
                pltpu.VMEM((chunks, heads, 8, LANES), f32),
            ],
            compiler_params=params(6),
            name="feed_core",
        )(
            meta, *owned, mlp_block, grad_block_two, hidden, grad_gate, grad_up,
            w_output, core, gate, gain_row, qkv, scal, w_part, drop,
        )
        ff_grads, grad_block = results[:3], results[3]
        grad_core, inner, pull, grad_gate_pre, grad_head, pulled, grad_hidden_in, grad_second = results[4:]
        grad_second = grad_second[0]
    else:
        grad_hidden_norm, grad_second = rms_back(hidden_in, second_gain, grad_normed_two)
        grad_hidden_in = grad_out + grad_hidden_norm
        grad_mix = grad_hidden_in.astype(bf16)
        *ff_grads, grad_block = feed_grads(
            grad_mix, mlp_block, grad_block_two, hidden, grad_gate, grad_up, "head"
        )
        grad_core, inner, pull, grad_gate_pre, grad_head, pulled = pl.pallas_call(
            functools.partial(core_grad_kernel, *sizes, chunks),
            grid=(chunks,),
            in_specs=[
                SCALARS, by_rows(model_width, chunks), whole(w_output.shape), by_rows(vw, chunks), by_rows(vw, chunks),
                whole(gain_row.shape), by_rows(mixed_width, chunks), by_rows(LANES, chunks),
                by_chunk((heads, BLOCK, key_width), chunks), by_chunk((heads, key_width, key_width), chunks),
            ],
            out_specs=[
                by_chunk((heads, BLOCK, value_width), chunks), by_chunk((heads, BLOCK, value_width), chunks),
                by_chunk((heads, key_width, value_width), chunks), by_rows(vw, chunks),
                whole((8, value_width)), whole((heads, key_width, value_width)),
            ],
            out_shape=core_shapes,
            compiler_params=params(),
            name="mixer_core_grad",
        )(meta, grad_block, w_output, core, gate, gain_row, qkv, scal, w_part, drop)
    grad_w_output = dot_tn(gated, grad_block).astype(bf16)
    later = from_later(
        jnp.concatenate([block_map[:, :, :key_width], pulled], axis=2).astype(bf16), "seq"
    )
    later, _ = lax.optimization_barrier((later, grad_w_output))
    mlp_out, grad_w_output = lax.optimization_barrier((mlp_out, grad_w_output))
    grad_w_output = lax.psum(grad_w_output, "seq")
    feed_part = (ff_grads[1],) if cube else ()
    grad_conv, grad_small, sums, edge, *feed_sum = pl.pallas_call(
        functools.partial(backward_kernel, *sizes, chunks, others, cube),
        grid=(chunks,),
        in_specs=[
            SCALARS, whole(later.shape), by_rows(mixed_width, chunks), by_rows(mixed_width, chunks),
            by_rows(LANES, chunks), by_rows(LANES, chunks), by_chunk((heads, BLOCK, BLOCK), chunks),
            by_chunk((heads, BLOCK, value_width), chunks), by_chunk((heads, key_width, value_width), chunks),
            by_chunk((heads, BLOCK, value_width), chunks), by_chunk((heads, BLOCK, value_width), chunks),
            by_chunk((heads, key_width, value_width), chunks), by_chunk((heads, key_width, key_width), chunks),
            whole(dvec.shape), *(held(array.shape) for array in feed_part),
        ],
        out_specs=[
            by_rows(mixed_width, chunks), by_rows(LANES, chunks), whole((8, LANES)), whole((HALO, mixed_width)),
            *(whole((array.shape[0] // 8, array.shape[1])) for array in feed_part),
        ],
        out_shape=[
            struct((seq_rows, mixed_width), f32), struct((seq_rows, LANES), bf16), struct((8, LANES), f32),
            struct((HALO, mixed_width), f32),
            *(struct((array.shape[0] // 8, array.shape[1]), bf16) for array in feed_part),
        ],
        scratch_shapes=[
            pltpu.VMEM((heads, key_width, value_width), f32), pltpu.VMEM((HALO, mixed_width), f32),
            pltpu.VMEM((HALO, mixed_width), f32), pltpu.SemaphoreType.DMA((2,)),
            *(
                scratch for array in feed_part for scratch in (
                    pltpu.VMEM((array.shape[0] // 8, array.shape[1]), f32),
                    *cube_scatter_scratch(array.shape[0] // 8, array.shape[1]),
                )
            ),
        ],
        compiler_params=params(9),
        name="mixer_backward",
    )(
        meta, later, qkv, conv, scal, small, inverse, fresh, states, grad_core, inner, pull, drop, dvec, *feed_part
    )

    if cube:
        ff_grads = [ff_grads[0], ff_grads[2]]
    grad_small, *ff_grads = lax.optimization_barrier((grad_small, *ff_grads))
    ff_grads = [lax.psum(part, "head") for part in ff_grads]
    step_rows = BLOCK // HALO
    last_halo = seq_rows // HALO - 1
    later_rows = pl.BlockSpec(
        (HALO, mixed_width), lambda step: (jnp.minimum((last_first(step) + 1) * step_rows, last_halo), 0)
    )
    grad_pre, grad_taps, grad_rows, gain_sum = pl.pallas_call(
        functools.partial(projection_grad_kernel, mixed_width, docs, chunks, taps, cube),
        grid=(chunks,),
        in_specs=[
            SCALARS, rows_back(mixed_width), later_rows, whole(edge.shape), rows_back(mixed_width), rows_back(vw),
            rows_back(LANES), whole(conv_all.shape), rows_back(model_width),
            *(held(weight.shape) for weight in weights),
        ],
        out_specs=[
            rows_back(all_width), whole((8, mixed_width)),
            whole((row_count, model_width)) if cube else rows_back(model_width), whole((8, model_width)),
        ],
        out_shape=[
            struct((seq_rows, all_width), bf16), struct((8, mixed_width), f32),
            struct((row_count, model_width), f32) if cube else struct((seq_rows, model_width), bf16),
            struct((8, model_width), f32),
        ],
        scratch_shapes=[pltpu.VMEM((BLOCK + HALO, mixed_width), f32)]
        + (cube_scatter_scratch(row_count, model_width) if cube else []),
        compiler_params=params(8 if cube else None),
        name="projection_grad",
    )(meta, grad_conv, grad_conv, edge, pre, grad_gate_pre, grad_small, conv_all, block_rows, *weights)

    if cube:
        grad_normed = grad_rows
    else:
        grad_normed = lax.psum_scatter(grad_rows, "head", scatter_dimension=0, tiled=True).astype(f32)
    grad_input_norm, _ = rms_back(inputs_f, first_gain, grad_normed)
    grad_inputs = grad_hidden_in + grad_input_norm
    gains = jnp.concatenate([gain_sum[0] / first_gain, grad_second, grad_head[0]]).reshape(2, -1)
    grad_w_all, grad_w_small, small_sums, _, gains, *gathered = line_sum(
        block_rows,
        grad_pre,
        feed_sum,
        (
            jnp.pad(
                jnp.concatenate([grad_taps, sums], axis=1), ((0, 8), (0, 0))
            ).astype(bf16),
            jnp.pad(gains, ((0, 14), (0, 0))).astype(bf16),
        ),
        (32, 16, 16, 16),
        "seq",
        1,
    )
    gains = gains[:2].reshape(-1)
    first_part, second_part = gains[:model_width], gains[model_width : 2 * model_width]
    head_part = gains[2 * model_width :]
    if cube:
        ff_grads = [ff_grads[0], *gathered, ff_grads[1]]
    grad_w_all, grad_w_output = lax.optimization_barrier((grad_w_all, grad_w_output))
    grad_w_all, grad_inputs, mlp_out, *ff_grads = lax.optimization_barrier(
        (grad_w_all, grad_inputs, mlp_out, *ff_grads)
    )
    (
        grad_w_query, grad_w_key, grad_w_value, grad_w_outgate, grad_w_down, grad_w_gate, grad_w_up, grad_w_output,
    ) = widen((*ff_grads, grad_w_output), grad_w_all, (qw, qw, vw, vw))
    grad_taps = small_sums[:taps, :mixed_width].astype(f32)
    sums = small_sums[:2, mixed_width : mixed_width + heads].astype(f32)
    output = (hidden_in + mlp_out.astype(f32)).astype(bf16)
    return (
        output,
        grad_inputs,
        first_part,
        grad_w_query,
        grad_w_key,
        grad_w_value,
        grad_w_outgate,
        grad_w_small[:heads].astype(f32).T,
        grad_w_small[heads : 2 * heads].astype(f32).T,
        grad_taps[:, :qw],
        grad_taps[:, qw : 2 * qw],
        grad_taps[:, 2 * qw :],
        sums[1],
        sums[0],
        head_part,
        grad_w_output,
        second_part,
        grad_w_gate,
        grad_w_up,
        grad_w_down,
    )


def from_previous(array):
    devices = lax.axis_size("seq")
    return lax.ppermute(array, "seq", [(i, i + 1) for i in range(devices - 1)])


def solution(mesh):
    in_specs = (
        P(("seq", "head"), None),
        P(),
        P(),
        P(None, "head"),
        P(None, "head"),
        P(None, "head"),
        P(None, "head"),
        P(None, "head"),
        P(None, "head"),
        P(None, "head"),
        P(None, "head"),
        P(None, "head"),
        P("head"),
        P("head"),
        P(),
        P("head", None),
        P(),
        P(None, "seq"),
        P(None, "seq"),
        P("seq", None),
        P(("seq", "head"), None),
    )
    out_specs = (
        P(("seq", "head"), None),
        P(("seq", "head"), None),
        P(),
        P(None, "head"),
        P(None, "head"),
        P(None, "head"),
        P(None, "head"),
        P(None, "head"),
        P(None, "head"),
        P(None, "head"),
        P(None, "head"),
        P(None, "head"),
        P("head"),
        P("head"),
        P(),
        P("head", None),
        P(),
        P(None, "seq"),
        P(None, "seq"),
        P("seq", None),
    )
    return jax.shard_map(shards, mesh=mesh, in_specs=in_specs, out_specs=out_specs, check_vma=False)
```

```python
import functools

import jax
import jax.numpy as jnp
from jax import lax
from jax.experimental import pallas as pl
from jax.experimental.pallas import tpu as pltpu
from jax.sharding import PartitionSpec as P

GROUP = 64
BLOCK = 256
LANES = 128
HALO = 8

epsilon = 1e-06
f32 = jnp.float32
bf16 = jnp.bfloat16
VMEM_LIMIT = 56 * 1024 * 1024


def dot(left, right):
    return jnp.dot(left, right, preferred_element_type=f32)


def dot_tn(left, right):
    return lax.dot_general(left, right, (((0,), (0,)), ((), ())), preferred_element_type=f32)


def dot_nt(left, right):
    return lax.dot_general(left, right, (((1,), (1,)), ((), ())), preferred_element_type=f32)


def halves(values):
    top = values.astype(bf16)
    return top, (values - top.astype(f32)).astype(bf16)


def exact_left(left, right):
    top = right.astype(bf16)
    rest = right - top.astype(f32)
    middle = rest.astype(bf16)
    low = (rest - middle.astype(f32)).astype(bf16)
    return dot(left, top) + dot(left, middle) + dot(left, low)


def dot_fine(left, right):
    left_top, left_low = halves(left)
    right_top, right_low = halves(right)
    return dot(left_top, right_top) + (dot(left_top, right_low) + dot(left_low, right_top))


def sigmoid(values):
    return jax.nn.sigmoid(values)


def silu_slope(values):
    sigma = sigmoid(values)
    return sigma * (1.0 + values * (1.0 - sigma))


def softplus(values):
    return jnp.maximum(values, 0.0) + jnp.log1p(jnp.exp(-jnp.abs(values)))


def slot_starts(doc_lengths):
    slot_sizes = (doc_lengths + (GROUP - 1)) // GROUP * GROUP
    return jnp.cumsum(slot_sizes, dtype=jnp.int32) - slot_sizes


def layout(doc_lengths, first_row, row_total):
    starts = slot_starts(doc_lengths)
    places = first_row + jnp.arange(row_total, dtype=jnp.int32)
    owners = jnp.sum(
        (places[:, None] >= starts[None, 1:]).astype(jnp.int32), axis=1, dtype=jnp.int32
    )
    picked = (owners[:, None] == jnp.arange(doc_lengths.shape[0], dtype=jnp.int32)[None, :]).astype(
        jnp.int32
    )
    begins = jnp.sum(picked * starts[None, :], axis=1, dtype=jnp.int32)
    length = jnp.sum(picked * doc_lengths[None, :], axis=1, dtype=jnp.int32)
    offset = places - begins
    return (offset, offset < length)


def rms_scale(values, gain):
    return values * lax.rsqrt(jnp.mean(values * values, axis=-1, keepdims=True) + epsilon) * gain


def rms_back(values, gain, grad_in):
    scale = lax.rsqrt(jnp.mean(values * values, axis=-1, keepdims=True) + epsilon)
    weighted = grad_in * gain
    grad_values = scale * weighted - values * scale**3 * jnp.mean(
        weighted * values, axis=-1, keepdims=True
    )
    grad_gain = jnp.sum((grad_in * values * scale).reshape(-1, values.shape[-1]), axis=0)
    return (grad_values, grad_gain)


def owner_of(meta, docs, places):
    total = jnp.zeros_like(places)
    for doc in range(1, docs):
        total = total + jnp.where(places >= meta[1 + doc], 1, 0)
    return total


def offset_of(meta, docs, places):
    begin = jnp.zeros_like(places)
    for doc in range(1, docs):
        begin = jnp.where(places >= meta[1 + doc], meta[1 + doc], begin)
    return places - begin


class Masks:
    def __init__(self, meta, docs, chunk):
        base = meta[0] + chunk * BLOCK
        rows = lax.broadcasted_iota(jnp.int32, (BLOCK, BLOCK), 0)
        cols = lax.broadcasted_iota(jnp.int32, (BLOCK, BLOCK), 1)
        same = owner_of(meta, docs, base + rows) == owner_of(meta, docs, base + cols)
        self.inclusive = same & (rows >= cols)
        self.strictly = same & (rows > cols)
        self.level = rows ^ cols
        self.lower = jnp.where(rows >= cols, 1.0, 0.0).astype(bf16)
        self.upper = jnp.where(rows <= cols, 1.0, 0.0).astype(bf16)
        self.eye = jnp.where(rows == cols, 1.0, 0.0)
        place = base + lax.broadcasted_iota(jnp.int32, (BLOCK, 1), 0)
        owner = owner_of(meta, docs, place)
        before = jnp.int32(0)
        last = jnp.int32(0)
        for doc in range(1, docs):
            before = before + jnp.where(base - 1 >= meta[1 + doc], 1, 0)
            last = last + jnp.where(base + BLOCK - 1 >= meta[1 + doc], 1, 0)
        self.enters = jnp.where(owner == before, 1.0, 0.0)
        self.leaves = jnp.where(owner == last, 1.0, 0.0)
        self.through = jnp.where(before == last, 1.0, 0.0).astype(f32)
        self.offset = offset_of(meta, docs, place)


def decays(masks, scal, scal_t, head):
    column = scal[:, head : head + 1]
    row = scal_t[head : head + 1, :]
    within = jnp.where(masks.inclusive, jnp.exp(jnp.minimum(column - row, 0.0)), 0.0)
    last = column[BLOCK - 1 : BLOCK, :]
    entry = jnp.exp(column) * masks.enters
    leave = jnp.exp(last - column) * masks.leaves
    through = jnp.exp(last) * masks.through
    return within, entry, leave, through


def unit_lower_inverses(systems):
    half = BLOCK // 2
    rows = lax.broadcasted_iota(jnp.int32, (half, half), 0)
    cols = lax.broadcasted_iota(jnp.int32, (half, half), 1)
    level = rows ^ cols
    eye = jnp.where(rows == cols, 1.0, 0.0)
    parts = [system[at : at + half, at : at + half] for system in systems for at in (0, half)]
    solved = [eye - jnp.where(level == 1, part, 0.0) for part in parts]
    width = 2
    while width < half:
        keep = (level >= width) & (level < 2 * width)
        low = [inverse.astype(bf16) for inverse in solved]
        moved = [dot(jnp.where(keep, part, 0.0).astype(bf16), inverse) for part, inverse in zip(parts, low)]
        solved = [
            whole_part - dot(inverse, part.astype(bf16))
            for whole_part, inverse, part in zip(solved, low, moved)
        ]
        width *= 2
    solved = [inverse.astype(bf16) for inverse in solved]
    results = []
    for index, system in enumerate(systems):
        upper, lower = solved[2 * index], solved[2 * index + 1]
        corner = -dot(lower, dot(system[half:, :half].astype(bf16), upper).astype(bf16))
        results.append((upper, corner.astype(bf16), lower))
    return results


LEAD = 2 * HALO
STRIDE = BLOCK + LEAD


def cube_order(axis, step):
    place = lax.axis_index(axis)
    chunk = 0
    for bit in (1, 2, 4):
        chunk = chunk + bit * ((place // bit + step // bit) % 2)
    return chunk


class EdgeRows:
    def __init__(self, line, axis, own_ref, rows_ref, edge_ref, line_sem, send_sem, recv_sem):
        self.line, self.axis = line, axis
        self.group, self.place = lax.axis_index(line), lax.axis_index(axis)
        self.groups, self.last = lax.axis_size(line), lax.axis_size(axis) - 1
        self.own_ref, self.rows_ref, self.edge_ref = own_ref, rows_ref, edge_ref
        self.line_sem, self.send_sem, self.recv_sem = line_sem, send_sem, recv_sem

    def enter(self):
        barrier = pltpu.get_barrier_semaphore()
        for mask in (1, 2, 4, 6):
            pl.semaphore_signal(barrier, inc=1, device_id={self.axis: flip(self.place, mask)}, device_id_type=MESH)
        for by in range(1, self.groups):
            other = lax.rem(self.group + by, self.groups)
            pl.semaphore_signal(barrier, inc=1, device_id={self.line: other}, device_id_type=MESH)
        pl.semaphore_wait(barrier, 3 + self.groups)

    def hands_on(self):
        return (self.place == self.last) & (self.group < self.groups - 1)

    def receives(self):
        return (self.place == self.last) & (self.group > 0)

    def landing(self, mask):
        block = lax.rem(flip(self.place, mask) + 1, self.last + 1)
        return self.rows_ref.at[pl.ds(pl.multiple_of(block * STRIDE, LEAD), LEAD), :]

    def onward(self):
        return pltpu.make_async_remote_copy(
            self.own_ref.at[pl.ds(BLOCK - LEAD, LEAD), :], self.edge_ref, self.line_sem.at[0], self.line_sem.at[1],
            device_id={self.line: self.group + 1}, device_id_type=MESH,
        )

    def copy(self, mask, toward):
        return pltpu.make_async_remote_copy(
            self.landing(mask) if mask else self.edge_ref, self.landing(mask),
            self.send_sem.at[mask + toward if mask else toward], self.recv_sem.at[mask ^ toward],
            device_id={self.axis: flip(self.place, toward)}, device_id_type=MESH,
        )

    def wait(self, mask):
        pltpu.make_async_remote_copy(
            self.landing(mask), self.landing(mask), self.send_sem.at[0], self.recv_sem.at[mask],
            device_id={self.axis: flip(self.place, 1)}, device_id_type=MESH,
        ).wait_recv()

    def start(self):
        @pl.when(self.hands_on())
        def _():
            self.onward().start()

        @pl.when(self.place < self.last)
        def _():
            self.edge_ref[...] = self.own_ref[BLOCK - LEAD :, :]

        @pl.when((self.place == self.last) & (self.group == 0))
        def _():
            self.edge_ref[...] = jnp.zeros(self.edge_ref.shape, bf16)

        @pl.when(self.receives())
        def _():
            pltpu.make_async_remote_copy(
                self.edge_ref, self.edge_ref, self.line_sem.at[0], self.line_sem.at[1],
                device_id={self.line: self.group - 1}, device_id_type=MESH,
            ).wait_recv()

        for toward in (6, 2, 4, 1):
            self.copy(0, toward).start()
        self.landing(0)[...] = self.edge_ref[...]

    def spread(self):
        for mask in (2, 4, 6):
            self.wait(mask)
            self.copy(mask, 1).start()
        for mask in (1, 3, 5, 7):
            self.wait(mask)

    def end(self):
        @pl.when(self.hands_on())
        def _():
            self.onward().wait_send()

        for toward in (6, 2, 4, 1):
            self.copy(0, toward).wait_send()
        for mask in (2, 4, 6):
            self.copy(mask, 1).wait_send()


class MapExchange:
    def __init__(self, going, coming, behind, sem):
        self.going, self.coming, self.behind, self.sem = going, coming, behind, sem
        self.groups, self.group = lax.axis_size("seq"), lax.axis_index("seq")
        self.width = going.shape[1]

    def copy(self, kind, by, target):
        slot = self.groups - 1 - by
        passing = pl.ds(0, self.width)
        span = pl.ds(self.width, self.going.shape[2] - self.width) if kind == 0 else passing
        landing = self.behind.at[slot] if kind == 2 else self.coming.at[slot, :, :, span]
        return pltpu.make_async_remote_copy(
            self.going.at[:, :, span], landing, self.sem.at[2 * kind, slot], self.sem.at[2 * kind + 1, slot],
            device_id={"seq": target}, device_id_type=MESH,
        )

    def moves(self):
        group, groups = self.group, self.groups
        for by in range(groups - 1, 0, -1):
            yield 0, by, group + by, group + by < groups, group - by, group >= by
            yield 1, by, group + by, (group + by < groups) & (group > 0), group - by, group > by
            yield 2, by, group - by, group >= by, group + by, group + by < groups

    def run(self):
        for kind, by, target, sends, source, comes in self.moves():
            @pl.when(sends)
            def _():
                self.copy(kind, by, target).start()

        for kind, by, target, sends, source, comes in self.moves():
            slot = self.groups - 1 - by

            @pl.when(comes)
            def _():
                self.copy(kind, by, source).wait_recv()

            @pl.when(jnp.logical_not(comes))
            def _():
                if kind == 0:
                    self.coming[slot, :, :, self.width :] = jnp.zeros(self.coming.shape[1:3] + (self.going.shape[2] - self.width,), bf16)
                elif kind == 1:
                    self.coming[slot, :, :, : self.width] = jnp.zeros(self.behind.shape[1:], bf16)
                else:
                    self.behind[slot] = jnp.zeros(self.behind.shape[1:], bf16)

        for kind, by, target, sends, source, comes in self.moves():
            @pl.when(sends)
            def _():
                self.copy(kind, by, target).wait_send()


def forward_kernel(
    heads, key_width, value_width, docs, taps, chunks, cube,
    meta, rows_ref, wq_ref, wk_ref, wv_ref, wg_ref, ws_ref, conv_ref, dvec_ref,
    pre_ref, act_ref, gate_ref, small_ref, scal_ref, qkv_ref, inv_ref, w_out_ref, u_ref, drop_ref,
    starts_ref, map_ref, *refs,
):
    step = pl.program_id(0)
    ext, state, drops, adds, throughs = refs[3 * cube : 3 * cube + 5]
    if cube:
        all_ref = refs[0]
        earlier_ref, later_ref, *refs = refs[1:]
        held, copy_sem, edge_ref, line_sem, edge_send, edge_recv, cube_send, cube_recv = refs[5:13]
        going, coming, behind, map_sem = refs[13:]
        chunk = cube_order("head", step)
        rows_in = CubeGather("head", rows_ref, held, None, cube_send, cube_recv, STRIDE, LEAD)
        edges = EdgeRows("seq", "head", rows_ref, held, edge_ref, line_sem, edge_send, edge_recv)

        def kept(block):
            start = pl.multiple_of(block * STRIDE + LEAD, LEAD)
            return pltpu.make_async_copy(
                held.at[pl.ds(start, BLOCK), :],
                all_ref.at[pl.ds(pl.multiple_of(block * BLOCK, BLOCK), BLOCK), :],
                copy_sem.at[block],
            )

        @pl.when(step == 0)
        def _():
            edges.enter()
            edges.start()
            rows_in.first()
            held[pl.ds(pl.multiple_of(chunk * STRIDE + LEAD, LEAD), BLOCK), :] = rows_ref[...]

        @pl.when(step == 2)
        def _():
            rows_in.second()
            rows_in.third()

        @pl.when(step == 4)
        def _():
            rows_in.fourth()

        for odd in (1, 3, 5, 7):
            @pl.when(step == odd)
            def _():
                for half in range(2):
                    rows_in.wait(odd, half)

        kept(chunk).start()
        rows = held[pl.ds(pl.multiple_of(chunk * STRIDE + LEAD, LEAD), BLOCK), :]
    else:
        chunk = step
        rows = rows_ref[LEAD:, :]

    qw, vw = heads * key_width, heads * value_width
    mixed = 2 * qw + vw
    masks = Masks(meta, docs, chunk)
    gate_ref[...] = dot(rows, wg_ref[...])
    small = dot(rows, ws_ref[...])
    small_ref[...] = small
    if cube:
        @pl.when(step == 0)
        def _():
            edges.spread()

        rows_ext = held[pl.ds(pl.multiple_of(chunk * STRIDE, LEAD), STRIDE), :]
    else:
        rows_ext = rows_ref[...]
    for span, ref in ((slice(0, qw), wq_ref), (slice(qw, 2 * qw), wk_ref), (slice(2 * qw, mixed), wv_ref)):
        pre = dot(rows_ext, ref[...])
        ext[:, span] = pre
        pre_ref[:, span] = pre[LEAD:, :]

    conv = jnp.zeros((BLOCK, mixed), f32)
    for lag in range(taps):
        keep = jnp.where(masks.offset >= lag, 1.0, 0.0)
        conv = conv + conv_ref[lag : lag + 1, :] * (ext[LEAD - lag : LEAD - lag + BLOCK, :] * keep)
    act_ref[...] = conv
    act = conv * sigmoid(conv)

    lane = lax.broadcasted_iota(jnp.int32, (BLOCK, LANES), 1)
    decay = dvec_ref[1:2, :] * softplus(small + dvec_ref[0:1, :])
    cumul = exact_left(masks.lower, decay)
    scal = jnp.where(lane < heads, cumul, sigmoid(small))
    scal_ref[...] = scal
    scal_t = scal.T

    held_heads = []
    for head in range(heads):
        act_q = act[:, head * key_width : (head + 1) * key_width]
        act_k = act[:, qw + head * key_width : qw + (head + 1) * key_width]
        value = act[:, 2 * qw + head * value_width : 2 * qw + (head + 1) * value_width].astype(bf16)
        norm_q = lax.rsqrt(jnp.sum(act_q * act_q, axis=1, keepdims=True) + epsilon)
        norm_k = lax.rsqrt(jnp.sum(act_k * act_k, axis=1, keepdims=True) + epsilon)
        query = (act_q * norm_q * key_width ** (-0.5)).astype(bf16)
        key = (act_k * norm_k).astype(bf16)
        qkv_ref[:, head * key_width : (head + 1) * key_width] = query
        qkv_ref[:, qw + head * key_width : qw + (head + 1) * key_width] = key
        qkv_ref[:, 2 * qw + head * value_width : 2 * qw + (head + 1) * value_width] = value
        within, entry, leave, through = decays(masks, scal, scal_t, head)
        beta = scal[:, heads + head : heads + head + 1]
        system = jnp.where(masks.strictly, beta * dot_nt(key, key) * within, 0.0)
        held_heads.append((system, key, value, beta, entry, leave, through))

    half = BLOCK // 2
    inverses = unit_lower_inverses([part[0] for part in held_heads])
    for head, (upper, corner, lower) in enumerate(inverses):
        inv_ref[0, head, :half, :half] = upper
        inv_ref[0, head, :half, half:] = jnp.zeros((half, half), bf16)
        inv_ref[0, head, half:, :half] = corner
        inv_ref[0, head, half:, half:] = lower
    for head, (_, key, value, beta, entry, leave, through) in enumerate(held_heads):
        inverse = inv_ref[0, head]
        key_f = key.astype(f32)
        w_part = dot(inverse, (beta * entry * key_f).astype(bf16)).astype(bf16)
        u_part = dot(inverse, (beta * value.astype(f32)).astype(bf16))
        w_out_ref[0, head] = w_part
        u_ref[0, head] = u_part
        tail_key = (leave * key_f).astype(bf16)
        drop = dot_tn(tail_key, w_part)
        drop_ref[0, head] = drop
        drops[chunk, head] = drop.astype(bf16)
        adds[chunk, head] = dot_tn(tail_key, u_part.astype(bf16))
        throughs[chunk, head] = jnp.broadcast_to(through, (8, LANES))

    @pl.when(step == chunks - 1)
    def _():
        shape = (key_width, key_width + value_width)
        ident = jnp.where(lax.broadcasted_iota(jnp.int32, shape, 0) == lax.broadcasted_iota(jnp.int32, shape, 1), 1.0, 0.0)
        for head in range(heads):
            state[head] = ident

        def pass_on(at, carry):
            for head in range(heads):
                before = state[head]
                starts_ref[at, head] = before
                after = throughs[at, head][0:1, 0:1] * before - dot(drops[at, head], before.astype(bf16))
                state[head] = after + jnp.concatenate(
                    [jnp.zeros((key_width, key_width), f32), adds[at, head]], axis=1
                )
            return carry

        lax.fori_loop(0, chunks, pass_on, 0)
        for head in range(heads):
            map_ref[head] = state[head]
        if cube:
            maps = MapExchange(going, coming, behind, map_sem)
            for head in range(heads):
                going[head] = state[head].astype(bf16)
            maps.run()
            earlier_ref[...] = coming[...]
            later_ref[...] = behind[...]
            rows_in.last()
            edges.end()
            for block in range(chunks):
                kept(block).wait()


def output_kernel(
    heads, key_width, value_width, docs, others, cube,
    meta, maps_ref, starts_ref, w_in_ref, u_ref, qkv_ref, scal_ref, gate_ref, gain_ref, w_output_ref, *refs,
):
    if cube:
        inputs_ref, next_gain_ref, *refs = refs
    core_ref, gated_ref, fresh_ref, state_ref, mixed_ref, *refs = refs
    if cube:
        next_ref, *refs = refs
    incoming, *refs = refs
    step = pl.program_id(0)
    chunk = cube_order("head", 7 - step) if cube else step
    qw = heads * key_width

    @pl.when(step == 0)
    def _():
        for head in range(heads):
            state = jnp.zeros((key_width, value_width), f32)
            for other in range(others):
                passing = maps_ref[other, head, :, :key_width]
                top, low = halves(state)
                state = dot(passing, top) + dot(passing, low) + maps_ref[other, head, :, key_width:].astype(f32)
            incoming[head] = state

    masks = Masks(meta, docs, chunk)
    scal = scal_ref[...]
    scal_t = scal.T
    gain = gain_ref[...]
    for head in range(heads):
        query = qkv_ref[:, head * key_width : (head + 1) * key_width]
        key = qkv_ref[:, qw + head * key_width : qw + (head + 1) * key_width]
        within, entry, leave, through = decays(masks, scal, scal_t, head)
        begun = starts_ref[0, head]
        state = dot_fine(begun[:, :key_width], incoming[head]) + begun[:, key_width:]
        state_ref[0, head] = state
        state_low = state.astype(bf16)
        fresh = (u_ref[0, head] - dot(w_in_ref[0, head], state_low)).astype(bf16)
        fresh_ref[0, head] = fresh
        scores = (dot_nt(query, key) * within).astype(bf16)
        core = dot((query.astype(f32) * entry).astype(bf16), state_low) + dot(scores, fresh)
        span = slice(head * value_width, (head + 1) * value_width)
        core_ref[:, span] = core
        scale = lax.rsqrt(jnp.mean(core * core, axis=1, keepdims=True) + epsilon)
        gate = gate_ref[:, span]
        gated_ref[:, span] = (core * scale * gain * (gate * sigmoid(gate))).astype(bf16)
    mixed = dot(gated_ref[...], w_output_ref[...])
    if not cube:
        mixed_ref[...] = mixed.astype(bf16)
        return

    total, *refs = refs
    scatter_block(step, CubeScatter("head", total, *refs), mixed)

    @pl.when(step == 7)
    def _():
        hidden_in = inputs_ref[...].astype(f32) + total[...]
        mixed_ref[...] = hidden_in
        next_ref[...] = rms_scale(hidden_in, next_gain_ref[...]).astype(bf16)


def core_grad_kernel(
    heads, key_width, value_width, docs, chunks,
    meta, grad_ref, w_output_ref, core_ref, gate_ref, gain_ref, qkv_ref, scal_ref, w_in_ref, drop_ref,
    grad_core_ref, inner_ref, pull_ref, grad_gate_ref, grad_gain_ref, total_ref, chunk=None, later=None,
):
    step = pl.program_id(0)
    chunk = chunks - 1 - step if chunk is None else chunk
    qw = heads * key_width
    masks = Masks(meta, docs, chunk)
    scal = scal_ref[...]
    scal_t = scal.T
    gain = gain_ref[...]

    @pl.when(step == 0)
    def _():
        grad_gain_ref[...] = jnp.zeros_like(grad_gain_ref)
        total_ref[...] = jnp.zeros_like(total_ref)

    grad_gated = dot_nt(grad_ref[...], w_output_ref[...])
    for head in range(heads):
        span = slice(head * value_width, (head + 1) * value_width)
        core = core_ref[:, span]
        gate = gate_ref[:, span]
        grad_in = grad_gated[:, span]
        scale = lax.rsqrt(jnp.mean(core * core, axis=1, keepdims=True) + epsilon)
        sigma = sigmoid(gate)
        normed = core * scale
        grad_gate_ref[:, span] = (
            grad_in * (normed * gain) * (sigma * (1.0 + gate * (1.0 - sigma)))
        ).astype(bf16)
        grad_normed = grad_in * (gate * sigma)
        weighted = grad_normed * gain
        grad_core = scale * (weighted - normed * jnp.mean(weighted * normed, axis=1, keepdims=True))
        grad_gain_ref[0:1, :] += jnp.sum(grad_normed * normed, axis=0, keepdims=True)
        grad_core = grad_core.astype(bf16)
        grad_core_ref[0, head] = grad_core
        query = qkv_ref[:, head * key_width : (head + 1) * key_width]
        key = qkv_ref[:, qw + head * key_width : qw + (head + 1) * key_width]
        within, entry, leave, through = decays(masks, scal, scal_t, head)
        scores = (dot_nt(query, key) * within).astype(bf16)
        inner = dot_tn(scores, grad_core)
        inner_ref[0, head] = inner
        pull = dot_tn((query.astype(f32) * entry).astype(bf16), grad_core) - dot_tn(
            w_in_ref[0, head], inner.astype(bf16)
        )
        pull_ref[0, head] = pull
        if later is not None:
            pulls, drops, throughs = later
            pulls[chunk, head] = pull
            drops[chunk, head] = drop_ref[0, head].astype(bf16)
            throughs[chunk, head] = jnp.broadcast_to(through, (8, LANES))
            continue
        total = total_ref[head]
        total_ref[head] = (
            through * total - dot_tn(drop_ref[0, head].astype(bf16), total.astype(bf16)) + pull
        )


def backward_kernel(
    heads, key_width, value_width, docs, chunks, others, cube,
    meta, passing_ref, later_ref, qkv_ref, act_ref, scal_ref, small_ref, inv_ref, fresh_ref, state_ref,
    grad_core_ref, inner_ref, pull_ref, drop_ref, dvec_ref, *refs,
):
    if cube:
        feed_ref, *refs = refs
    grad_conv_ref, grad_small_ref, sums_ref, edge_ref, *refs = refs
    if cube:
        feed_sum_ref, *refs = refs
    carried, edge_out, edge_in, edge_sem, *refs = refs
    step = pl.program_id(0)
    chunk = chunks - 1 - step

    @pl.when(step == 0)
    def _():
        line_barrier("seq", "head" if cube else None)

    if cube:
        rows = feed_ref.shape[0] // 8
        total, *refs = refs
        scatter = CubeScatter("head", total, *refs)
        for at, masks in enumerate(((7,), (6, 5), (4, 3), (2, 1), (0,))):
            @pl.when(step == at)
            def _():
                for mask in masks:
                    part = pl.ds(pl.multiple_of(flip(scatter.place, mask) * rows, rows), rows)
                    scatter.take(mask, feed_ref[part, :].astype(f32))
    groups, group = lax.axis_size("seq"), lax.axis_index("seq")
    edge = pltpu.make_async_remote_copy(
        edge_out, edge_in, edge_sem.at[0], edge_sem.at[1],
        device_id={"seq": jnp.maximum(group - 1, 0)}, device_id_type=MESH,
    )

    qw = heads * key_width

    @pl.when(step == 0)
    def _():
        sums_ref[...] = jnp.zeros_like(sums_ref)
        for head in range(heads):
            state = jnp.zeros((key_width, value_width), f32)
            for other in range(others):
                passing = passing_ref[other, head]
                top, low = halves(state)
                state = dot_tn(passing, top) + dot_tn(passing, low) + later_ref[other, head].astype(f32)
            carried[head] = state

    masks = Masks(meta, docs, chunk)
    scal = scal_ref[...]
    scal_t = scal.T
    lane = lax.broadcasted_iota(jnp.int32, (BLOCK, LANES), 1)
    slopes = jnp.zeros((BLOCK, LANES), f32)
    tails = jnp.zeros((1, LANES), f32)
    betas = jnp.zeros((BLOCK, LANES), f32)
    for head in range(heads):
        q_span = slice(head * key_width, (head + 1) * key_width)
        k_span = slice(qw + head * key_width, qw + (head + 1) * key_width)
        v_span = slice(2 * qw + head * value_width, 2 * qw + (head + 1) * value_width)
        query, key, value = qkv_ref[:, q_span], qkv_ref[:, k_span], qkv_ref[:, v_span]
        query_f, key_f = query.astype(f32), key.astype(f32)
        within, entry, leave, through = decays(masks, scal, scal_t, head)
        beta = scal[:, heads + head : heads + head + 1]
        later = carried[head]
        later_low = later.astype(bf16)
        state = state_ref[0, head]
        state_low = state.astype(bf16)
        grad_core = grad_core_ref[0, head]
        fresh = fresh_ref[0, head]
        carried[head] = through * later - dot_tn(drop_ref[0, head].astype(bf16), later_low) + pull_ref[0, head]
        grad_fresh = inner_ref[0, head] + dot((leave * key_f).astype(bf16), later_low)
        grad_x = dot_tn(inv_ref[0, head], grad_fresh.astype(bf16))
        grad_x_low = grad_x.astype(bf16)
        grad_x_beta = beta * grad_x
        recalled = dot(key, state_low)
        grad_beta = jnp.sum(grad_x * (value.astype(f32) - entry * recalled), axis=1, keepdims=True)
        from_state_q = dot_nt(grad_core, state_low)
        from_state_k = dot_nt(grad_x_beta.astype(bf16), state_low)
        grad_scores = (dot_nt(grad_core, fresh) * within).astype(bf16)
        gram = dot_nt(key, key)
        grad_system = jnp.where(masks.strictly, dot_nt(grad_x_low, fresh) * within, 0.0)
        grad_beta = grad_beta - jnp.sum(grad_system * gram, axis=1, keepdims=True)
        grad_gram = (-beta * grad_system).astype(bf16)
        grad_query = dot(grad_scores, key) + entry * from_state_q
        grad_row = dot(grad_gram, key) - entry * from_state_k
        passed = leave * dot_nt(fresh, later_low)
        grad_col = dot_tn(grad_gram, key) + dot_tn(grad_scores, query) + passed
        slope = jnp.sum(query_f * grad_query + key_f * (grad_row - grad_col), axis=1, keepdims=True)
        kept = jnp.sum(jnp.sum(state * later, axis=1, keepdims=True), axis=0, keepdims=True)
        moved = jnp.sum(jnp.sum(key_f * passed, axis=1, keepdims=True), axis=0, keepdims=True)
        tail = through * kept + moved
        slopes = jnp.where(lane == head, slope, slopes)
        tails = jnp.where(lane[0:1, :] == head, tail, tails)
        betas = jnp.where(lane == heads + head, grad_beta, betas)

        conv_q, conv_k, conv_v = act_ref[:, q_span], act_ref[:, k_span], act_ref[:, v_span]
        for span, conv, grad, factor in (
            (q_span, conv_q, grad_query, key_width ** (-0.5)),
            (k_span, conv_k, grad_row + grad_col, 1.0),
        ):
            sigma = sigmoid(conv)
            act = conv * sigma
            norm = lax.rsqrt(jnp.sum(act * act, axis=1, keepdims=True) + epsilon)
            unit = act * norm
            grad_act = (factor * norm) * (grad - unit * jnp.sum(grad * unit, axis=1, keepdims=True))
            grad_conv_ref[:, span] = grad_act * (sigma * (1.0 + conv * (1.0 - sigma)))
        grad_conv_ref[:, v_span] = grad_x_beta * silu_slope(conv_v)

    grad_decay = jnp.where(lane < heads, exact_left(masks.upper, slopes) + tails, 0.0)
    shifted = small_ref[...] + dvec_ref[0:1, :]
    rate = dvec_ref[1:2, :]
    grad_z = grad_decay * rate * sigmoid(shifted)
    sums_ref[0:1, :] += jnp.sum(grad_z, axis=0, keepdims=True)
    sums_ref[1:2, :] += jnp.sum(grad_decay * (rate * softplus(shifted)), axis=0, keepdims=True)
    strength = sigmoid(small_ref[...])
    grad_small_ref[...] = jnp.where(lane < heads, grad_z, betas * strength * (1.0 - strength)).astype(bf16)

    @pl.when(step == chunks - 1)
    def _():
        if cube:
            scatter.finish()
            feed_sum_ref[...] = total[...].astype(bf16)
        edge_out[...] = grad_conv_ref[0:HALO, :]

        @pl.when(group > 0)
        def _():
            edge.start()

        @pl.when(group < groups - 1)
        def _():
            edge.wait_recv()
            edge_ref[...] = edge_in[...]

        @pl.when(group == groups - 1)
        def _():
            edge_ref[...] = jnp.zeros(edge_ref.shape, f32)

        @pl.when(group > 0)
        def _():
            edge.wait_send()


def projection_grad_kernel(
    mixed, docs, chunks, taps, cube,
    meta, grad_conv_ref, later_ref, edge_ref, pre_ref, grad_gate_ref, grad_small_ref, conv_ref, rows_ref,
    wq_ref, wk_ref, wv_ref, wg_ref, ws_ref,
    grad_pre_ref, grad_taps_ref, grad_rows_ref, gain_sum_ref,
    ext, *refs,
):
    step = pl.program_id(0)
    chunk = cube_order("head", 7 - step) if cube else step

    @pl.when(step == 0)
    def _():
        grad_taps_ref[...] = jnp.zeros_like(grad_taps_ref)
        gain_sum_ref[...] = jnp.zeros_like(gain_sum_ref)

    ext[0:BLOCK, :] = grad_conv_ref[...]

    @pl.when(chunk == chunks - 1)
    def _():
        ext[BLOCK : BLOCK + HALO, :] = edge_ref[...]

    @pl.when(chunk < chunks - 1)
    def _():
        ext[BLOCK : BLOCK + HALO, :] = later_ref[...]

    place = meta[0] + chunk * BLOCK + lax.broadcasted_iota(jnp.int32, (BLOCK, 1), 0)
    pre = pre_ref[...]
    total = jnp.zeros((BLOCK, mixed), f32)
    for lag in range(taps):
        keep = jnp.where(offset_of(meta, docs, place + lag) >= lag, 1.0, 0.0)
        moved = ext[lag : lag + BLOCK, :] * keep
        total = total + conv_ref[lag : lag + 1, :] * moved
        grad_taps_ref[lag : lag + 1, :] += jnp.sum(pre * moved, axis=0, keepdims=True)
    width = grad_gate_ref.shape[1]
    grad_pre_ref[:, :mixed] = total.astype(bf16)
    grad_pre_ref[:, mixed : mixed + width] = grad_gate_ref[...]
    grad_pre_ref[:, mixed + width :] = grad_small_ref[...]
    grad = jnp.zeros(grad_rows_ref.shape, f32)
    begin = 0
    for ref in (wq_ref, wk_ref, wv_ref, wg_ref, ws_ref):
        grad = grad + dot_nt(grad_pre_ref[:, begin : begin + ref.shape[1]], ref[...])
        begin += ref.shape[1]
    gain_sum_ref[0:1, :] += jnp.sum(grad * rows_ref[...].astype(f32), axis=0, keepdims=True)
    if cube:
        scatter_block(step, CubeScatter("head", grad_rows_ref, *refs), grad)
    else:
        grad_rows_ref[...] = grad.astype(bf16)


MESH = pl.DeviceIdType.MESH
ANYWHERE = pl.BlockSpec(memory_space=pl.ANY)


def line_barrier(axis, cube=None):
    devices, place = lax.axis_size(axis), lax.axis_index(axis)
    barrier = pltpu.get_barrier_semaphore()

    @pl.when(place > 0)
    def _():
        pl.semaphore_signal(barrier, inc=1, device_id={axis: place - 1}, device_id_type=MESH)

    @pl.when(place < devices - 1)
    def _():
        pl.semaphore_signal(barrier, inc=1, device_id={axis: place + 1}, device_id_type=MESH)

    more = 0
    if cube is not None:
        for mask in (1, 2, 4):
            pl.semaphore_signal(
                barrier, inc=1, device_id={cube: flip(lax.axis_index(cube), mask)}, device_id_type=MESH
            )
        more = 3

    @pl.when((place > 0) & (place < devices - 1))
    def _():
        pl.semaphore_wait(barrier, 2 + more)

    @pl.when((place == 0) | (place == devices - 1))
    def _():
        pl.semaphore_wait(barrier, 1 + more)


class LineSum:
    skew = 2
    window = 4

    def __init__(self, axis, counts, depths, parts, passed, arrived, sums, reduce_sems, back_sems):
        self.axis, self.counts, self.depths = axis, counts, depths
        self.single = [array.shape[0] == depth for array, depth in zip(sums, depths)]
        self.parts, self.passed, self.arrived, self.sums = parts, passed, arrived, sums
        self.sems = (reduce_sems, back_sems)
        self.devices, self.place = lax.axis_size(axis), lax.axis_index(axis)
        self.steps = max(counts) + self.skew * (self.devices - 1)

    def rows_of(self, half, index, at):
        depth = self.depths[index]
        return pl.ds(pl.multiple_of((half * self.counts[index] + at) * depth, depth), depth)

    def copy(self, half, index, at, target, back):
        rows = self.rows_of(half, index, at)
        slot = half * self.counts[index] + at
        source, landing = (self.sums, self.sums) if back else (self.passed, self.arrived)
        sent, received = self.sems[back][2 * index], self.sems[back][2 * index + 1]
        return pltpu.make_async_remote_copy(
            source[index].at[rows, :], landing[index].at[rows, :], sent.at[slot], received.at[slot],
            device_id={self.axis: target}, device_id_type=MESH,
        )

    def send(self, half, index, at, target, back):
        @pl.when(at >= self.window)
        def _():
            self.copy(half, index, at - self.window, target, back).wait_send()

        self.copy(half, index, at, target, back).start()

    def each(self, handle):
        place, last = self.place, self.devices - 1
        for half in range(2):
            ends = (last, 0) if half == 0 else (0, last)
            toward = place - 1 if half == 0 else place + 1
            away = place + 1 if half == 0 else place - 1
            for index in range(len(self.counts)):
                if half == 0 or not self.single[index]:
                    handle(half, index, toward, away, place == ends[0], place == ends[1])

    def reduce(self, step):
        def handle(half, index, toward, away, begin, end):
            late = (self.devices - 1 - self.place) if half == 0 else self.place
            at = step - self.skew * late

            @pl.when((at >= 0) & (at < self.counts[index]))
            def _():
                rows = self.rows_of(half, index, at)

                @pl.when(begin)
                def _():
                    self.passed[index][rows, :] = self.parts[index][rows, :]
                    self.send(half, index, at, toward, 0)

                @pl.when(jnp.logical_not(begin))
                def _():
                    self.copy(half, index, at, toward, 0).wait_recv()
                    added = (
                        self.parts[index][rows, :].astype(f32) + self.arrived[index][rows, :].astype(f32)
                    ).astype(bf16)

                    @pl.when(jnp.logical_not(end))
                    def _():
                        self.passed[index][rows, :] = added
                        self.send(half, index, at, toward, 0)

                    @pl.when(end)
                    def _():
                        self.sums[index][rows, :] = added

        self.each(handle)

    def back(self, step, given=None):
        def handle(half, index, toward, away, begin, end):
            late = self.place if half == 0 else (self.devices - 1 - self.place)
            at = step - self.skew * late

            @pl.when((at >= 0) & (at < self.counts[index]))
            def _():
                if given is not None:
                    @pl.when(end)
                    def _():
                        rows = self.rows_of(half, index, at)
                        self.sums[index][rows, :] = given[index][rows, :]

                @pl.when(jnp.logical_not(end))
                def _():
                    self.copy(half, index, at, away, 1).wait_recv()

                @pl.when(jnp.logical_not(begin))
                def _():
                    self.send(half, index, at, away, 1)

        self.each(handle)

    def settle(self, back):
        def handle(half, index, toward, away, begin, end):
            count = self.counts[index]
            for at in range(max(count - self.window, 0), count):
                @pl.when(jnp.logical_not(begin if back else end))
                def _():
                    self.copy(half, index, at, away if back else toward, back).wait_send()

        self.each(handle)


def line_sum_kernel(axis, cube, counts, depths, *refs):
    total = len(counts)
    rows_ref, grads_ref, *refs = refs
    parts, refs = refs[: total - 2], refs[total - 2 :]
    if cube:
        block_ref, *refs = refs
    sums, refs = refs[:total], refs[total:]
    if cube:
        whole_ref, blocks_ref, *refs = refs
    product, turned, *refs = refs
    parts = (product, turned, *parts)
    width = product.shape[1]
    arrived, passed, refs = refs[:total], refs[total : 2 * total], refs[2 * total :]
    share = BLOCK // depths[0]
    tiles = counts[0] // share
    line = LineSum(axis, counts, depths, parts, passed, arrived, sums, refs[: 2 * total], refs[2 * total : 4 * total])
    line_barrier(axis, "head" if cube else None)

    begin = max(counts)
    if cube:
        final = CubeTotal(*refs[4 * total : 4 * total + 4])
        gather = CubeGather("head", block_ref, blocks_ref, *refs[4 * total + 4 :], enter=False)
        gather.first()

    turned[...] = dot_tn(grads_ref[:, width:], rows_ref[...])[: turned.shape[0], :].astype(bf16)

    def step_on(step, carry):
        @pl.when((step % share == 0) & (step < tiles * share))
        def _():
            for half in range(2):
                columns = pl.ds(pl.multiple_of((half * tiles + step // share) * BLOCK, BLOCK), BLOCK)
                product[columns, :] = dot_tn(rows_ref[:, columns], grads_ref[:, :width]).astype(bf16)

        @pl.when(step < line.steps)
        def _():
            line.reduce(step)

        @pl.when(step >= begin)
        def _():
            line.back(step - begin)

        if cube:
            for at, phase in ((begin // 2, gather.second), (begin * 3 // 4, gather.third), (begin, gather.fourth)):
                @pl.when(step == at)
                def _():
                    phase()

            after = begin + line.skew * line.devices
            for stage in range(4):
                @pl.when(step == after + 3 * stage)
                def _():
                    if stage:
                        final.end(stage - 1, whole_ref)
                    else:
                        final.held[0] = sums[-1][: whole_ref.shape[0], :].astype(f32)
                    if stage < 3:
                        final.copy(stage).start()

        return carry

    lax.fori_loop(0, begin + line.steps, step_on, 0)
    line.settle(0)
    line.settle(1)
    if cube:
        gather.last()


class CubeTotal:
    def __init__(self, held, arrived, send_sem, recv_sem):
        self.held, self.arrived, self.send_sem, self.recv_sem = held, arrived, send_sem, recv_sem

    def copy(self, stage):
        return pltpu.make_async_remote_copy(
            self.held.at[stage], self.arrived.at[stage], self.send_sem.at[stage], self.recv_sem.at[stage],
            device_id={"head": flip(lax.axis_index("head"), (1, 2, 4)[stage])}, device_id_type=MESH,
        )

    def end(self, stage, total_ref):
        self.copy(stage).wait()
        if stage < 2:
            self.held[stage + 1] = self.held[stage] + self.arrived[stage]
        else:
            total_ref[...] = self.held[stage] + self.arrived[stage]


def line_scratch(arrays, depths, moves):
    counts = tuple(max(array.shape[0] // (2 * depth), 1) for array, depth in zip(arrays, depths))
    semaphores = []
    for count in counts:
        semaphores += [pltpu.SemaphoreType.DMA((2 * count,))] * 2
    return counts, semaphores * moves


def line_sum(rows, grads, blocks, given, depths, axis, collective_id):
    cube = lax.axis_size("head") == 8
    arrays = (
        struct((rows.shape[1], grads.shape[1] - LANES), bf16), struct((2 * HALO, rows.shape[1]), bf16), *given,
    )
    counts, semaphores = line_scratch(arrays, depths, 2)
    vmem = pl.BlockSpec(memory_space=pltpu.VMEM)
    scratch = [pltpu.VMEM(array.shape, bf16) for array in (*arrays[:2], *arrays, *arrays)] + semaphores
    total = (8, arrays[-1].shape[1])
    if cube:
        scratch += [pltpu.VMEM((3,) + total, f32)] * 2 + [pltpu.SemaphoreType.DMA((3,))] * 2 + CUBE_SEMAPHORES
    results = pl.pallas_call(
        functools.partial(line_sum_kernel, axis, cube, counts, tuple(depths)),
        in_specs=[vmem] * len(arrays) + [ANYWHERE] * cube,
        out_specs=[vmem] * (len(arrays) + cube) + [ANYWHERE] * cube,
        out_shape=[struct(array.shape, bf16) for array in arrays]
        + [struct(total, f32)] * cube
        + [struct((8 * block.shape[0], block.shape[1]), bf16) for block in blocks],
        scratch_shapes=scratch,
        compiler_params=pltpu.CompilerParams(
            collective_id=collective_id, has_side_effects=True, vmem_limit_bytes=VMEM_LIMIT
        ),
        cost_estimate=pl.CostEstimate(flops=10**8, bytes_accessed=40 * 10**6, transcendentals=0),
        name="line_sum",
    )(rows, grads, *given, *blocks)
    if not cube:
        results = [*results, lax.psum(results[-1][:8].astype(f32), "head")]
    return results


def whole(shape):
    zeros = (0,) * len(shape)
    return pl.BlockSpec(tuple(shape), lambda step: zeros)


def held(shape):
    zeros = (0,) * len(shape)
    return pl.BlockSpec(tuple(shape), lambda step: zeros, pipeline_mode=pl.Buffered(1))


def by_rows(width, chunks=None):
    if chunks is None:
        return pl.BlockSpec((BLOCK, width), lambda step: (step, 0))
    return pl.BlockSpec((BLOCK, width), lambda step: (chunks - 1 - step, 0))


def by_chunk(shape, chunks=None):
    rest = (0,) * len(shape)
    if chunks is None:
        return pl.BlockSpec((1,) + tuple(shape), lambda step: (step,) + rest)
    return pl.BlockSpec((1,) + tuple(shape), lambda step: (chunks - 1 - step,) + rest)


SCALARS = pl.BlockSpec(memory_space=pltpu.SMEM)


def feed_kernel(
    axis, devices, rows, pieces,
    own_ref, *refs,
):
    given, kept, refs = refs[:4], refs[4:9], refs[9:]
    total_ref, *refs = refs
    hidden_ref, *refs = refs
    inside, refs = refs[:8], refs[8:]
    inside = (*inside, inside[0])
    grads_ref, w_gate_ref, w_up_ref, w_down_ref = inside[:4]
    blocks_ref, turned_ref, grad_gate_ref, grad_up_ref, part_ref = inside[4:]
    parts, arrived, gather_send, gather_recv, chain_send, chain_recv, load_sem, store_sem = refs
    place = lax.axis_index(axis)
    piece = rows // 2

    def load(index):
        return pltpu.make_async_copy(given[index], inside[index], load_sem.at[index])

    def store(index):
        return pltpu.make_async_copy(inside[4 + index], kept[index], store_sem.at[index])

    for index in (3, 0, 1, 2):
        load(index).start()
    line_barrier(axis)

    def span(block, half):
        return pl.ds(pl.multiple_of(block * rows + half * piece, piece), piece)

    def full(block):
        return pl.ds(pl.multiple_of(block * rows, rows), rows)

    def gather(owner, hop, way, half):
        target = place + 1 - 2 * way
        slot = (hop * 2 + way) * 2 + half
        return pltpu.make_async_remote_copy(
            blocks_ref.at[span(owner, half), :], blocks_ref.at[span(owner, half), :],
            gather_send.at[slot], gather_recv.at[slot], device_id={axis: target}, device_id_type=MESH,
        )

    bit = rows // pieces

    def strip(block, part):
        return pl.ds(pl.multiple_of(block * rows + part * bit, bit), bit)

    def chain(block, way, part, at):
        target = at + 1 - 2 * way
        landing = jnp.where((block == target) & (way == 0), devices, block)
        slot = (way * devices + block) * pieces + part
        return pltpu.make_async_remote_copy(
            parts.at[strip(block, part), :], arrived.at[strip(landing, part), :],
            chain_send.at[slot], chain_recv.at[slot], device_id={axis: target}, device_id_type=MESH,
        )

    blocks_ref[full(place), :] = own_ref[...]

    def event(step, carry):
        hop = (step + 1) // 2
        way = (step + 1) % 2
        owner = jnp.where(way == 0, place - hop, place + hop)

        @pl.when(step == 0)
        def _():
            for side in range(2):
                @pl.when((place + 1 - 2 * side >= 0) & (place + 1 - 2 * side < devices))
                def _():
                    for half in range(2):
                        gather(place, 0, side, half).start()

            for index in range(4):
                load(index).wait()

        @pl.when((step > 0) & (way == 0))
        def _():
            for side in range(2):
                come = place - hop if side == 0 else place + hop
                goes = place + 1 if side == 0 else place - 1

                @pl.when((come >= 0) & (come < devices))
                def _():
                    for half in range(2):
                        gather(come, hop - 1, side, half).wait_recv()

                        @pl.when((goes >= 0) & (goes < devices))
                        def _():
                            gather(come, hop, side, half).start()

        @pl.when((owner >= 0) & (owner < devices))
        def _():
            here = full(owner)
            grad_hidden = dot_nt(grads_ref[here, :], w_down_ref[...])

            block = blocks_ref[here, :]
            gate_pre = dot(block, w_gate_ref[...])
            up_pre = dot(block, w_up_ref[...])
            sigma = sigmoid(gate_pre)
            act = gate_pre * sigma
            hidden = (act * up_pre).astype(bf16)
            hidden_ref[here, :] = hidden
            turned_ref[:, full(owner)] = hidden.T
            grad_gate_ref[here, :] = (grad_hidden * up_pre * (sigma * (1.0 + gate_pre * (1.0 - sigma)))).astype(bf16)
            grad_up_ref[here, :] = (grad_hidden * act).astype(bf16)
            grad = dot_nt(grad_gate_ref[here, :], w_gate_ref[...]) + dot_nt(grad_up_ref[here, :], w_up_ref[...])

            @pl.when(step == 0)
            def _():
                total_ref[...] = grad

            @pl.when(step > 0)
            def _():
                parts[here, :] = grad.astype(bf16)

        @pl.when((way == 1) & (step > 0))
        def _():
            for part in range(pieces):
                for turn in range(2):
                    side = jnp.where(2 * place < devices, turn, 1 - turn)
                    block = jnp.where(side == 1, devices - 1 - hop, hop)
                    begins = place == jnp.where(side == 1, devices - 1, 0)
                    valid = jnp.where(side == 1, block < place, block > place)

                    @pl.when(valid)
                    def _():
                        @pl.when(jnp.logical_not(begins))
                        def _():
                            chain(block, side, part, place + 2 * side - 1).wait_recv()
                            at = strip(block, part)
                            parts[at, :] = (parts[at, :].astype(f32) + arrived[at, :].astype(f32)).astype(bf16)

                        chain(block, side, part, place).start()

        return carry

    lax.fori_loop(0, 2 * devices - 1, event, 0)

    for index in range(4):
        store(index).start()

    def feed_part(block, carry):
        part_ref[full(block), :] = dot(hidden_ref[full(block), :], w_down_ref[...]).astype(bf16)
        return carry

    lax.fori_loop(0, devices, feed_part, 0)
    store(4).start()

    for side, landing, comes in ((1, place, place < devices - 1), (0, devices, place > 0)):
        @pl.when(comes)
        def _():
            for part in range(pieces):
                chain(place, side, part, place + 2 * side - 1).wait_recv()
                at = pl.ds(part * bit, bit)
                total_ref[at, :] += arrived[strip(landing, part), :].astype(f32)

    def gather_end(step, carry):
        hop = step // 2
        way = step % 2
        owner = jnp.where(way == 0, place - hop, place + hop)
        target = place + 1 - 2 * way

        @pl.when((owner >= 0) & (owner < devices) & (target >= 0) & (target < devices))
        def _():
            for half in range(2):
                gather(owner, hop, way, half).wait_send()

        return carry

    lax.fori_loop(0, 2 * (devices - 1), gather_end, 0)

    def chain_end(block, carry):
        @pl.when(block < place)
        def _():
            for part in range(pieces):
                chain(block, 1, part, place).wait_send()

        @pl.when(block > place)
        def _():
            for part in range(pieces):
                chain(block, 0, part, place).wait_send()

        return carry

    lax.fori_loop(0, devices, chain_end, 0)
    for index in range(5):
        store(index).wait()


def feed(own, grads, w_gate, w_up, w_down, axis, collective_id):
    devices = lax.axis_size(axis)
    rows, width = own.shape
    units = w_gate.shape[1]
    vmem = pl.BlockSpec(memory_space=pltpu.VMEM)
    moves = pltpu.SemaphoreType.DMA((4 * devices,))
    pieces = 4
    chains = pltpu.SemaphoreType.DMA((2 * pieces * devices,))
    given = (grads, w_gate, w_up, w_down)
    kept = [struct((devices * rows, width), bf16), struct((units, devices * rows), bf16)]
    kept += [struct((devices * rows, units), bf16)] * 2
    kept += [struct((devices * rows, width), bf16)]
    return pl.pallas_call(
        functools.partial(feed_kernel, axis, devices, rows, pieces),
        in_specs=[vmem] + [ANYWHERE] * 4,
        out_specs=[ANYWHERE] * 5 + [vmem],
        out_shape=kept + [struct((rows, width), f32)],
        scratch_shapes=[
            pltpu.VMEM((devices * rows, units), bf16),
            *(pltpu.VMEM(array.shape, array.dtype) for array in (*given, *kept[:4])),
            pltpu.VMEM((devices * rows, width), bf16), pltpu.VMEM(((devices + 1) * rows, width), bf16),
            moves, moves, chains, chains, pltpu.SemaphoreType.DMA((4,)), pltpu.SemaphoreType.DMA((5,)),
        ],
        compiler_params=pltpu.CompilerParams(
            collective_id=collective_id, has_side_effects=True, vmem_limit_bytes=61 * 1024 * 1024
        ),
        name="feed",
    )(own, grads, w_gate, w_up, w_down)


def flip(index, mask):
    for bit in (1, 2, 4):
        if mask & bit:
            index = index + bit * (1 - 2 * ((index // bit) % 2))
    return index


def cube_barrier(axis, place):
    barrier = pltpu.get_barrier_semaphore()
    for mask in (1, 2, 4):
        pl.semaphore_signal(barrier, inc=1, device_id={axis: flip(place, mask)}, device_id_type=MESH)
    pl.semaphore_wait(barrier, 3)


class CubeGather:
    FIRST = ((0, 0, 2), (0, 1, 4), (0, 1, 2), (0, 0, 4), (0, 0, 1), (0, 1, 1))
    SECOND = ((2, 0, 4), (4, 1, 2), (2, 0, 1), (4, 1, 1))
    THIRD = ((2, 1, 1), (4, 0, 1))
    FOURTH = ((6, 0, 1), (6, 1, 1))

    def __init__(self, axis, own_ref, all_ref, own_sem, send_sem, recv_sem, stride=None, lead=0, enter=True):
        self.axis, self.own_ref, self.all_ref = axis, own_ref, all_ref
        self.stride, self.lead, self.enter = stride or own_ref.shape[0], lead, enter
        self.own_sem, self.send_sem, self.recv_sem = own_sem, send_sem, recv_sem
        self.place = lax.axis_index(axis)
        self.rows = own_ref.shape[0]
        self.piece = self.rows // 2

    def part(self, mask, half):
        start = flip(self.place, mask) * self.stride + self.lead + half * self.piece
        return self.all_ref.at[pl.ds(pl.multiple_of(start, LEAD), self.piece), :]

    def copy(self, mask, half, toward):
        source = self.part(mask, half) if mask else self.own_ref.at[pl.ds(half * self.piece, self.piece), :]
        return pltpu.make_async_remote_copy(
            source, self.part(mask, half),
            self.send_sem.at[toward * 2 + half, mask // 2], self.recv_sem.at[(mask ^ toward) * 2 + half],
            device_id={self.axis: flip(self.place, toward)}, device_id_type=MESH,
        )

    def wait(self, mask, half):
        pltpu.make_async_remote_copy(
            self.part(mask, half), self.part(mask, half), self.send_sem.at[0, 0], self.recv_sem.at[mask * 2 + half],
            device_id={self.axis: flip(self.place, 1)}, device_id_type=MESH,
        ).wait_recv()

    def own(self):
        start = pl.multiple_of(self.place * self.rows, self.rows)
        return pltpu.make_async_copy(self.own_ref, self.all_ref.at[pl.ds(start, self.rows), :], self.own_sem)

    def first(self):
        if self.own_sem is not None:
            if self.enter:
                cube_barrier(self.axis, self.place)
            self.own().start()
        for move in self.FIRST:
            self.copy(*move).start()

    def second(self):
        self.wait(2, 0)
        self.copy(*self.SECOND[0]).start()
        self.wait(4, 1)
        for move in self.SECOND[1:]:
            self.copy(*move).start()

    def third(self):
        for move in self.THIRD:
            self.wait(*move[:2])
            self.copy(*move).start()

    def fourth(self):
        for move in self.FOURTH:
            self.wait(*move[:2])
            self.copy(*move).start()

    def last(self):
        if self.own_sem is not None:
            for mask in (1, 3, 5, 7):
                for half in range(2):
                    self.wait(mask, half)
            self.own().wait()
        for move in self.FIRST + self.SECOND + self.THIRD + self.FOURTH:
            self.copy(*move).wait_send()


CUBE_SEMAPHORES = [pltpu.SemaphoreType.DMA, pltpu.SemaphoreType.DMA((10, 4)), pltpu.SemaphoreType.DMA((16,))]


def feed_grads_kernel(
    blocks_ref, grads_ref, hidden_ref, grad_gate_ref, grad_up_ref, down_ref, gate_ref, up_ref,
):
    gate_ref[...] = dot_tn(blocks_ref[...], grad_gate_ref[...]).astype(bf16)
    up_ref[...] = dot_tn(blocks_ref[...], grad_up_ref[...]).astype(bf16)
    down_ref[...] = dot(hidden_ref[...], grads_ref[...]).astype(bf16)


def feed_grads(own, blocks, grads, hidden, grad_gate, grad_up, axis):
    rows, width = blocks.shape
    units = hidden.shape[0]
    tall = pl.BlockSpec((rows, BLOCK), lambda step: (0, step))
    down = pl.BlockSpec((units, BLOCK), lambda step: (0, step))
    flat = pl.BlockSpec((BLOCK, units), lambda step: (step, 0))
    fixed = held((rows, units))
    results = pl.pallas_call(
        feed_grads_kernel,
        grid=(width // BLOCK,),
        in_specs=[tall, tall, held(hidden.shape), fixed, fixed],
        out_specs=[down, flat, flat],
        out_shape=[
            struct((units, width), bf16), struct((width, units), bf16), struct((width, units), bf16),
        ],
        compiler_params=params(),
        name="feed_grads",
    )(blocks, grads, hidden, grad_gate, grad_up)
    return (*results, lax.all_gather(own, axis, axis=0, tiled=True))


def feed_core_kernel(
    sizes, chunks, axis, tiles,
    meta, total_in, hidden_in, low_ref, next_gain_ref, blocks_ref, grads_ref, hidden_ref, feed_gate_ref, feed_up_ref,
    w_output_ref, core_ref, gate_ref, gain_ref, qkv_ref, scal_ref, w_in_ref, drop_ref,
    down_out, gate_out, up_out, all_ref, *refs,
):
    outs, (grad_in_ref, gain_sum_ref, rows_ref, copy_sem, send_sem, recv_sem, *later) = refs[:6], refs[6:]
    step = pl.program_id(0)
    rows = total_in.shape[0]
    own = pl.ds(pl.multiple_of(lax.axis_index(axis) * rows, rows), rows)
    gather = CubeGather(axis, rows_ref.at[own, :], rows_ref, None, send_sem, recv_sem)

    @pl.when(step == 0)
    def _():
        grad_norm, gain_sum = rms_back(hidden_in[...], next_gain_ref[...], total_in[...])
        grad_in = low_ref[...].astype(f32) + grad_norm
        grad_in_ref[...] = grad_in
        gain_sum_ref[0:1, :] = gain_sum[None, :]
        rows_ref[own, :] = grad_in.astype(bf16)
        cube_barrier(axis, gather.place)
        gather.first()

    @pl.when(step == tiles - 1)
    def _():
        gather.second()
        gather.third()

    @pl.when(step == tiles + 3)
    def _():
        gather.fourth()

    for mask in (1, 3, 5, 7):
        @pl.when(step == (1 if mask == 1 else tiles + mask))
        def _():
            for half in range(2):
                gather.wait(mask, half)

    @pl.when((step >= 2) & (step < tiles + 2))
    def _():
        turned = blocks_ref[...].T
        gate_out[...] = dot(turned, feed_gate_ref[...]).astype(bf16)
        up_out[...] = dot(turned, feed_up_ref[...]).astype(bf16)
        down_out[...] = dot(hidden_ref[...], grads_ref[...]).astype(bf16)

    @pl.when((step < 2) | (step >= tiles + 2))
    def _():
        chunk = core_order(axis, step, tiles)
        core_grad_kernel(
            *sizes, chunks,
            meta, rows_ref.at[pl.ds(pl.multiple_of(chunk * BLOCK, BLOCK), BLOCK), :], w_output_ref,
            core_ref, gate_ref, gain_ref, qkv_ref, scal_ref, w_in_ref, drop_ref, *outs, chunk=chunk, later=later,
        )

    @pl.when(step == tiles + chunks - 1)
    def _():
        kept = pltpu.make_async_copy(rows_ref, all_ref, copy_sem)
        kept.start()
        total_ref = outs[5]
        pulls, drops, throughs = later

        def pass_on(at, carry):
            chunk = chunks - 1 - at
            for head in range(sizes[0]):
                total = total_ref[head]
                total_ref[head] = (
                    throughs[chunk, head][0:1, 0:1] * total
                    - dot_tn(drops[chunk, head], total.astype(bf16)) + pulls[chunk, head]
                )
            return carry

        lax.fori_loop(0, chunks, pass_on, 0)
        gather.last()
        kept.wait()


def core_order(axis, step, tiles):
    return cube_order(axis, jnp.where(step < 2, step, jnp.maximum(step - tiles, 1)))


class CubeScatter:
    def __init__(self, axis, total_ref, given, other, leaving, coming, waiting, send_sem, recv_sem):
        self.axis, self.total_ref = axis, total_ref
        self.given, self.other, self.leaving, self.coming, self.waiting = given, other, leaving, coming, waiting
        self.send_sem, self.recv_sem = send_sem, recv_sem
        self.place = lax.axis_index(axis)
        self.piece = total_ref.shape[0] // 2

    def slot(self, index, half):
        return pl.ds((2 * index + half) * self.piece, self.piece)

    def core_copy(self, mask, half):
        at = self.slot(mask // 2, half)
        return pltpu.make_async_remote_copy(
            self.given.at[at, :], self.other.at[at, :],
            self.send_sem.at[0, mask // 2, half], self.recv_sem.at[0, mask // 2, half],
            device_id={self.axis: flip(self.place, 1)}, device_id_type=MESH,
        )

    def landing(self, index, toward):
        return (toward // 2 - 1) * 2 + (1 if index else 0)

    def chip_copy(self, index, half, toward):
        return pltpu.make_async_remote_copy(
            self.leaving.at[self.slot(index, half), :],
            self.coming.at[self.slot(self.landing(index, toward), half), :],
            self.send_sem.at[toward // 2, index, half], self.recv_sem.at[toward // 2, 1 if index else 0, half],
            device_id={self.axis: flip(self.place, toward)}, device_id_type=MESH,
        )

    def arrived(self, index, half, toward):
        self.chip_copy(index, half, toward).wait_recv()
        return self.coming[self.slot(self.landing(index, toward), half), :].astype(f32)

    def send(self, index, half, toward, values):
        self.leaving[self.slot(index, half), :] = values.astype(bf16)
        self.chip_copy(index, half, toward).start()

    def take(self, mask, block):
        piece = self.piece
        if mask % 2:
            self.given[pl.ds(mask // 2 * 2 * piece, 2 * piece), :] = block.astype(bf16)
            for half in range(2):
                self.core_copy(mask, half).start()
            if mask == 1:
                self.send(2, 0, 4, self.waiting[0] + self.arrived(0, 0, 2))
                self.send(1, 1, 2, self.waiting[1] + self.arrived(0, 1, 4))
            return
        parts = []
        for half in range(2):
            self.core_copy(mask + 1, half).wait_recv()
            parts.append(
                block[half * piece : (half + 1) * piece, :]
                + self.other[self.slot(mask // 2, half), :].astype(f32)
            )
        if mask == 6:
            self.send(0, 0, 2, parts[0])
            self.send(0, 1, 4, parts[1])
        elif mask == 4:
            self.send(2, 1, 4, parts[1])
            self.waiting[0] = parts[0]
        elif mask == 2:
            self.send(1, 0, 2, parts[0])
            self.waiting[1] = parts[1]
        else:
            self.total_ref[0:piece, :] = parts[0]
            self.total_ref[piece:, :] = parts[1]

    def finish(self):
        piece = self.piece
        self.total_ref[0:piece, :] += self.arrived(1, 0, 2)
        self.total_ref[piece:, :] += self.arrived(2, 1, 4)
        self.total_ref[0:piece, :] += self.arrived(2, 0, 4)
        self.total_ref[piece:, :] += self.arrived(1, 1, 2)
        for mask in (7, 5, 3, 1):
            for half in range(2):
                self.core_copy(mask, half).wait_send()
        for index, half, toward in ((0, 0, 2), (0, 1, 4), (1, 0, 2), (2, 1, 4), (1, 1, 2), (2, 0, 4)):
            self.chip_copy(index, half, toward).wait_send()


def scatter_block(step, scatter, block):
    @pl.when(step == 0)
    def _():
        cube_barrier("head", scatter.place)

    for mask in range(8):
        @pl.when(step == 7 - mask)
        def _():
            scatter.take(mask, block)

    @pl.when(step == 7)
    def _():
        scatter.finish()


def cube_scatter_scratch(rows, width):
    return [
        pltpu.VMEM((4 * rows, width), bf16), pltpu.VMEM((4 * rows, width), bf16),
        pltpu.VMEM((3 * rows, width), bf16), pltpu.VMEM((4 * rows, width), bf16),
        pltpu.VMEM((2, rows // 2, width), f32),
        pltpu.SemaphoreType.DMA((3, 4, 2)), pltpu.SemaphoreType.DMA((3, 4, 2)),
    ]


def params(collective_id=None):
    return pltpu.CompilerParams(
        dimension_semantics=("arbitrary",),
        vmem_limit_bytes=VMEM_LIMIT,
        collective_id=collective_id,
        has_side_effects=collective_id is not None,
    )


def finish_kernel(
    cuts, total, grad_ref, inputs_ref, gain_ref, grad_hidden_ref, hidden_ref, mlp_ref, taps_ref, all_in, *refs,
):
    given, refs = refs[:total], refs[total:]
    output_ref, grad_inputs_ref, taps_q, taps_k, taps_v, *refs = refs
    output_ref[...] = (hidden_ref[...] + mlp_ref[...].astype(f32)).astype(bf16)
    values = inputs_ref[...].astype(f32)
    scale = lax.rsqrt(jnp.mean(values * values, axis=-1, keepdims=True) + epsilon)
    weighted = grad_ref[...] * gain_ref[...]
    grad_inputs_ref[...] = grad_hidden_ref[...] + (
        scale * weighted - values * scale**3 * jnp.mean(weighted * values, axis=-1, keepdims=True)
    )
    begin = 0
    for result in (taps_q, taps_k, taps_v):
        count, width = result.shape
        result[...] = taps_ref[:, begin : begin + width].astype(f32)[:count, :]
        begin += width
    begin = 0
    for cut, result in zip(cuts, refs):
        result[...] = all_in[:, begin : begin + cut].astype(f32)
        begin += cut
    for source, result in zip(given, refs[len(cuts) :]):
        result[...] = source[...].astype(f32)


def finish(rows, gain, small, taps, columns, cuts, given):
    steps = 8 if given[0].shape[0] % 128 == 0 else 4

    def part(shape):
        return pl.BlockSpec((shape[0] // steps, shape[1]), lambda step: (step, 0))

    grad, inputs, grad_hidden, hidden, mlp = rows
    taps_shapes = [(taps, cut) for cut in cuts[:3]]
    shapes = [(columns.shape[0], cut) for cut in cuts] + [array.shape for array in given]
    return pl.pallas_call(
        functools.partial(finish_kernel, cuts, len(given)),
        grid=(steps,),
        in_specs=[
            part(grad.shape), part(inputs.shape), whole(gain.shape), part(grad_hidden.shape), part(hidden.shape),
            part(mlp.shape), whole(small.shape), part(columns.shape), *(part(array.shape) for array in given),
        ],
        out_specs=[
            part(inputs.shape), part(inputs.shape), *(whole(shape) for shape in taps_shapes),
            *(part(shape) for shape in shapes),
        ],
        out_shape=[
            struct(inputs.shape, bf16), struct(inputs.shape, f32), *(struct(shape, f32) for shape in taps_shapes),
            *(struct(shape, f32) for shape in shapes),
        ],
        compiler_params=params(),
        name="finish",
    )(grad, inputs, gain, grad_hidden, hidden, mlp, small, columns, *given)


def struct(shape, dtype):
    return jax.ShapeDtypeStruct(tuple(shape), dtype)


def from_earlier(array, axis):
    devices = lax.axis_size(axis)
    parts = [
        lax.ppermute(array, axis, [(i, i + by) for i in range(devices - by)])
        for by in range(devices - 1, 0, -1)
    ]
    return jnp.stack(parts) if parts else jnp.zeros((1,) + array.shape, array.dtype)


def from_later(array, axis):
    devices = lax.axis_size(axis)
    parts = [
        lax.ppermute(array, axis, [(i + by, i) for i in range(devices - by)])
        for by in range(devices - 1, 0, -1)
    ]
    return jnp.stack(parts) if parts else jnp.zeros((1,) + array.shape, array.dtype)


def shards(
    inputs,
    doc_lengths,
    first_gain,
    w_query,
    w_key,
    w_value,
    w_outgate,
    w_decay,
    w_beta,
    conv_query,
    conv_key,
    conv_value,
    decay_log,
    decay_bias,
    head_gain,
    w_output,
    second_gain,
    w_gate,
    w_up,
    w_down,
    cotangent,
):
    row_count, model_width = inputs.shape
    heads = decay_log.shape[0]
    qw, vw = w_query.shape[1], w_value.shape[1]
    key_width, value_width = qw // heads, vw // heads
    mixed_width = 2 * qw + vw
    taps = conv_query.shape[0]
    docs = doc_lengths.shape[0]
    seq_index = lax.axis_index("seq")
    head_index = lax.axis_index("head")
    head_total = lax.axis_size("head")
    seq_rows = row_count * head_total
    chunks = seq_rows // BLOCK
    others = max(lax.axis_size("seq") - 1, 1)
    sizes = (heads, key_width, value_width, docs)

    inputs_f = inputs.astype(f32)
    normed = rms_scale(inputs_f, first_gain).astype(bf16)
    meta = jnp.concatenate(
        [(seq_index * seq_rows).astype(jnp.int32)[None], slot_starts(doc_lengths)]
    )
    _, own_valid = layout(doc_lengths, (seq_index * head_total + head_index) * row_count, row_count)

    grad_out = cotangent.astype(f32) * own_valid.astype(f32)[:, None]
    grad_low = grad_out.astype(bf16)
    w_small = jnp.concatenate([w_decay, w_beta, jnp.zeros((model_width, LANES - 2 * heads), bf16)], axis=1)
    weights = (w_query, w_key, w_value, w_outgate, w_small)
    all_width = mixed_width + vw + LANES
    conv_all = jnp.concatenate([conv_query, conv_key, conv_value], axis=1)
    dvec = jnp.zeros((8, LANES), f32)
    dvec = dvec.at[0, :heads].set(decay_bias).at[1, :heads].set(-jnp.exp(decay_log))
    map_shape = (heads, key_width, key_width + value_width)
    passing_shape = (others, heads, key_width, key_width)

    cube = head_total == 8 and chunks == 8 and row_count == BLOCK
    if cube:
        rows_given, rows_spec = normed, held(normed.shape)

        def at_step(step):
            return cube_order("head", step)
    else:
        block_rows = lax.all_gather(normed, "head", axis=0, tiled=True)
        tail = from_previous(block_rows[seq_rows - LEAD :])
        blocks = block_rows.reshape(chunks, BLOCK, model_width)
        leads = jnp.concatenate([tail[None], blocks[:-1, BLOCK - LEAD :]], axis=0)
        rows_given = jnp.concatenate([leads, blocks], axis=1).reshape(chunks * STRIDE, model_width)
        rows_spec = pl.BlockSpec((STRIDE, model_width), lambda step: (step, 0))

        def at_step(step):
            return step

    def rows_out(width):
        return pl.BlockSpec((BLOCK, width), lambda step: (at_step(step), 0))

    def chunk_out(shape):
        return pl.BlockSpec((1,) + tuple(shape), lambda step: (at_step(step),) + (0,) * len(shape))

    results = pl.pallas_call(
        functools.partial(forward_kernel, *sizes, taps, chunks, cube),
        grid=(chunks,),
        in_specs=[
            SCALARS, rows_spec, *(held(weight.shape) for weight in weights), whole(conv_all.shape),
            whole(dvec.shape),
        ],
        out_specs=[
            rows_out(mixed_width), rows_out(mixed_width), rows_out(vw), rows_out(LANES), rows_out(LANES),
            rows_out(mixed_width),
            chunk_out((heads, BLOCK, BLOCK)), chunk_out((heads, BLOCK, key_width)),
            chunk_out((heads, BLOCK, value_width)), chunk_out((heads, key_width, key_width)),
            whole((chunks,) + map_shape), whole(map_shape),
        ] + [ANYWHERE, whole((others,) + map_shape), whole(passing_shape)] * cube,
        out_shape=[
            struct((seq_rows, mixed_width), f32), struct((seq_rows, mixed_width), f32),
            struct((seq_rows, vw), f32), struct((seq_rows, LANES), f32), struct((seq_rows, LANES), f32),
            struct((seq_rows, mixed_width), bf16),
            struct((chunks, heads, BLOCK, BLOCK), bf16), struct((chunks, heads, BLOCK, key_width), bf16),
            struct((chunks, heads, BLOCK, value_width), f32),
            struct((chunks, heads, key_width, key_width), f32),
            struct((chunks,) + map_shape, f32), struct(map_shape, f32),
        ] + [
            struct((seq_rows, model_width), bf16), struct((others,) + map_shape, bf16), struct(passing_shape, bf16),
        ] * cube,
        scratch_shapes=[
            pltpu.VMEM((STRIDE, mixed_width), f32), pltpu.VMEM(map_shape, f32),
            pltpu.VMEM((chunks, heads, key_width, key_width), bf16),
            pltpu.VMEM((chunks, heads, key_width, value_width), f32),
            pltpu.VMEM((chunks, heads, 8, LANES), f32),
        ] + [
            pltpu.VMEM((chunks * STRIDE, model_width), bf16), pltpu.SemaphoreType.DMA((chunks,)),
            pltpu.VMEM((LEAD, model_width), bf16), pltpu.SemaphoreType.DMA((2,)),
            pltpu.SemaphoreType.DMA((8,)), pltpu.SemaphoreType.DMA((8,)), *CUBE_SEMAPHORES[1:],
            pltpu.VMEM(map_shape, bf16), pltpu.VMEM((others,) + map_shape, bf16), pltpu.VMEM(passing_shape, bf16),
            pltpu.SemaphoreType.DMA((6, others)),
        ] * cube,
        compiler_params=params(2 if cube else None),
        name="mixer_forward",
    )(meta, rows_given, *weights, conv_all, dvec)
    (pre, conv, gate, small, scal, qkv, inverse, w_part, u_part, drop, starts, block_map) = results[:12]
    if cube:
        block_rows, earlier, passing = results[12:]
    else:
        earlier = from_earlier(block_map.astype(bf16), "seq")
        passing = from_later(block_map[:, :, :key_width].astype(bf16), "seq")

    grad_block_two = lax.all_gather(grad_low, "seq", axis=0, tiled=True)
    gain_row = head_gain[None, :]
    def last_first(step):
        return cube_order("head", 7 - step) if cube else step

    def rows_back(width):
        return pl.BlockSpec((BLOCK, width), lambda step: (last_first(step), 0))

    def chunk_back(shape):
        return pl.BlockSpec((1,) + tuple(shape), lambda step: (last_first(step),) + (0,) * len(shape))

    second_row = second_gain[None, :]
    own_rows = (inputs, second_row) if cube else ()
    core, gated, fresh, states, *mixed_parts = pl.pallas_call(
        functools.partial(output_kernel, *sizes, others, cube),
        grid=(chunks,),
        in_specs=[
            SCALARS, whole(earlier.shape), chunk_back(map_shape), chunk_back((heads, BLOCK, key_width)),
            chunk_back((heads, BLOCK, value_width)), rows_back(mixed_width), rows_back(LANES), rows_back(vw),
            whole(gain_row.shape), held(w_output.shape), *(held(array.shape) for array in own_rows),
        ],
        out_specs=[
            rows_back(vw), rows_back(vw), chunk_back((heads, BLOCK, value_width)),
            chunk_back((heads, key_width, value_width)),
            *([whole((row_count, model_width))] * 2 if cube else [rows_back(model_width)]),
        ],
        out_shape=[
            struct((seq_rows, vw), f32), struct((seq_rows, vw), bf16),
            struct((chunks, heads, BLOCK, value_width), bf16),
            struct((chunks, heads, key_width, value_width), f32),
            *(
                [struct((row_count, model_width), f32), struct((row_count, model_width), bf16)]
                if cube else [struct((seq_rows, model_width), bf16)]
            ),
        ],
        scratch_shapes=[pltpu.VMEM((heads, key_width, value_width), f32)]
        + (
            [pltpu.VMEM((row_count, model_width), f32), *cube_scatter_scratch(row_count, model_width)]
            if cube else []
        ),
        compiler_params=params(5 if cube else None),
        name="mixer_output",
    )(meta, earlier, starts, w_part, u_part, qkv, scal, gate, gain_row, w_output, *own_rows)
    if cube:
        hidden_in, normed_two = mixed_parts
    else:
        mixer_out = lax.psum_scatter(mixed_parts[0], "head", scatter_dimension=0, tiled=True).astype(f32)
        hidden_in = inputs_f + mixer_out
        normed_two = rms_scale(hidden_in, second_gain).astype(bf16)

    mlp_block, hidden, grad_gate, grad_up, mlp_part, grad_normed_two = feed(
        normed_two, grad_block_two, w_gate, w_up, w_down, "seq", 3
    )
    mlp_out = lax.psum_scatter(mlp_part, "seq", scatter_dimension=0, tiled=True)
    core_shapes = [
        struct((chunks, heads, BLOCK, value_width), bf16), struct((chunks, heads, BLOCK, value_width), f32),
        struct((chunks, heads, key_width, value_width), f32), struct((seq_rows, vw), bf16),
        struct((8, value_width), f32), struct((heads, key_width, value_width), f32),
    ]
    if cube:
        tiles = model_width // BLOCK
        owned = (grad_normed_two, hidden_in, grad_low, second_row)
        units, mlp_rows = hidden.shape

        def tile(step):
            return jnp.clip(step - 2, 0, tiles - 1)

        def core_chunk(step):
            return core_order("head", step, tiles)

        def core_rows(width):
            return pl.BlockSpec((BLOCK, width), lambda step: (core_chunk(step), 0))

        def core_blocks(shape):
            return pl.BlockSpec((1,) + tuple(shape), lambda step: (core_chunk(step),) + (0,) * len(shape))

        tall = pl.BlockSpec((mlp_rows, BLOCK), lambda step: (0, tile(step)))
        down = pl.BlockSpec((units, BLOCK), lambda step: (0, tile(step)))
        flat = pl.BlockSpec((BLOCK, units), lambda step: (tile(step), 0))
        results = pl.pallas_call(
            functools.partial(feed_core_kernel, sizes, chunks, "head", tiles),
            grid=(tiles + chunks,),
            in_specs=[
                SCALARS, *(held(array.shape) for array in owned), tall, tall, *(held(array.shape) for array in (hidden, grad_gate, grad_up)),
                held(w_output.shape), core_rows(vw), core_rows(vw), whole(gain_row.shape), core_rows(mixed_width),
                core_rows(LANES), core_blocks((heads, BLOCK, key_width)), core_blocks((heads, key_width, key_width)),
            ],
            out_specs=[
                down, flat, flat, ANYWHERE,
                core_blocks((heads, BLOCK, value_width)), core_blocks((heads, BLOCK, value_width)),
                core_blocks((heads, key_width, value_width)), core_rows(vw),
                whole((8, value_width)), whole((heads, key_width, value_width)),
                whole((row_count, model_width)), whole((8, model_width)),
            ],
            out_shape=[
                struct((units, model_width), bf16), struct((model_width, units), bf16),
                struct((model_width, units), bf16), struct((seq_rows, model_width), bf16), *core_shapes,
                struct((row_count, model_width), f32), struct((8, model_width), f32),
            ],
            scratch_shapes=[
                pltpu.VMEM((seq_rows, model_width), bf16), pltpu.SemaphoreType.DMA, *CUBE_SEMAPHORES[1:],
                pltpu.VMEM((chunks, heads, key_width, value_width), f32),
                pltpu.VMEM((chunks, heads, key_width, key_width), bf16),
                pltpu.VMEM((chunks, heads, 8, LANES), f32),
            ],
            compiler_params=params(6),
            name="feed_core",
        )(
            meta, *owned, mlp_block, grad_block_two, hidden, grad_gate, grad_up,
            w_output, core, gate, gain_row, qkv, scal, w_part, drop,
        )
        ff_grads, grad_block = results[:3], results[3]
        grad_core, inner, pull, grad_gate_pre, grad_head, pulled, grad_hidden_in, grad_second = results[4:]
        grad_second = grad_second[0]
    else:
        grad_hidden_norm, grad_second = rms_back(hidden_in, second_gain, grad_normed_two)
        grad_hidden_in = grad_out + grad_hidden_norm
        grad_mix = grad_hidden_in.astype(bf16)
        *ff_grads, grad_block = feed_grads(
            grad_mix, mlp_block, grad_block_two, hidden, grad_gate, grad_up, "head"
        )
        grad_core, inner, pull, grad_gate_pre, grad_head, pulled = pl.pallas_call(
            functools.partial(core_grad_kernel, *sizes, chunks),
            grid=(chunks,),
            in_specs=[
                SCALARS, by_rows(model_width, chunks), whole(w_output.shape), by_rows(vw, chunks), by_rows(vw, chunks),
                whole(gain_row.shape), by_rows(mixed_width, chunks), by_rows(LANES, chunks),
                by_chunk((heads, BLOCK, key_width), chunks), by_chunk((heads, key_width, key_width), chunks),
            ],
            out_specs=[
                by_chunk((heads, BLOCK, value_width), chunks), by_chunk((heads, BLOCK, value_width), chunks),
                by_chunk((heads, key_width, value_width), chunks), by_rows(vw, chunks),
                whole((8, value_width)), whole((heads, key_width, value_width)),
            ],
            out_shape=core_shapes,
            compiler_params=params(),
            name="mixer_core_grad",
        )(meta, grad_block, w_output, core, gate, gain_row, qkv, scal, w_part, drop)
    grad_w_output = dot_tn(gated, grad_block).astype(bf16)
    later = from_later(pulled.astype(bf16), "seq")
    later, _ = lax.optimization_barrier((later, grad_w_output))
    mlp_out, grad_w_output = lax.optimization_barrier((mlp_out, grad_w_output))
    grad_w_output = lax.psum(grad_w_output, "seq")
    feed_part = (ff_grads[1],) if cube else ()
    grad_conv, grad_small, sums, edge, *feed_sum = pl.pallas_call(
        functools.partial(backward_kernel, *sizes, chunks, others, cube),
        grid=(chunks,),
        in_specs=[
            SCALARS, whole(passing.shape), whole(later.shape), by_rows(mixed_width, chunks),
            by_rows(mixed_width, chunks),
            by_rows(LANES, chunks), by_rows(LANES, chunks), by_chunk((heads, BLOCK, BLOCK), chunks),
            by_chunk((heads, BLOCK, value_width), chunks), by_chunk((heads, key_width, value_width), chunks),
            by_chunk((heads, BLOCK, value_width), chunks), by_chunk((heads, BLOCK, value_width), chunks),
            by_chunk((heads, key_width, value_width), chunks), by_chunk((heads, key_width, key_width), chunks),
            whole(dvec.shape), *(held(array.shape) for array in feed_part),
        ],
        out_specs=[
            by_rows(mixed_width, chunks), by_rows(LANES, chunks), whole((8, LANES)), whole((HALO, mixed_width)),
            *(whole((array.shape[0] // 8, array.shape[1])) for array in feed_part),
        ],
        out_shape=[
            struct((seq_rows, mixed_width), f32), struct((seq_rows, LANES), bf16), struct((8, LANES), f32),
            struct((HALO, mixed_width), f32),
            *(struct((array.shape[0] // 8, array.shape[1]), bf16) for array in feed_part),
        ],
        scratch_shapes=[
            pltpu.VMEM((heads, key_width, value_width), f32), pltpu.VMEM((HALO, mixed_width), f32),
            pltpu.VMEM((HALO, mixed_width), f32), pltpu.SemaphoreType.DMA((2,)),
            *(
                scratch for array in feed_part for scratch in (
                    pltpu.VMEM((array.shape[0] // 8, array.shape[1]), f32),
                    *cube_scatter_scratch(array.shape[0] // 8, array.shape[1]),
                )
            ),
        ],
        compiler_params=params(9),
        name="mixer_backward",
    )(
        meta, passing, later, qkv, conv, scal, small, inverse, fresh, states, grad_core, inner, pull, drop, dvec, *feed_part
    )

    if cube:
        ff_grads = [ff_grads[0], ff_grads[2]]
    grad_small, *ff_grads = lax.optimization_barrier((grad_small, *ff_grads))
    ff_grads = [lax.psum(part, "head") for part in ff_grads]
    step_rows = BLOCK // HALO
    last_halo = seq_rows // HALO - 1
    later_rows = pl.BlockSpec(
        (HALO, mixed_width), lambda step: (jnp.minimum((last_first(step) + 1) * step_rows, last_halo), 0)
    )
    grad_pre, grad_taps, grad_rows, gain_sum = pl.pallas_call(
        functools.partial(projection_grad_kernel, mixed_width, docs, chunks, taps, cube),
        grid=(chunks,),
        in_specs=[
            SCALARS, rows_back(mixed_width), later_rows, whole(edge.shape), rows_back(mixed_width), rows_back(vw),
            rows_back(LANES), whole(conv_all.shape), rows_back(model_width),
            *(held(weight.shape) for weight in weights),
        ],
        out_specs=[
            rows_back(all_width), whole((8, mixed_width)),
            whole((row_count, model_width)) if cube else rows_back(model_width), whole((8, model_width)),
        ],
        out_shape=[
            struct((seq_rows, all_width), bf16), struct((8, mixed_width), f32),
            struct((row_count, model_width), f32) if cube else struct((seq_rows, model_width), bf16),
            struct((8, model_width), f32),
        ],
        scratch_shapes=[pltpu.VMEM((BLOCK + HALO, mixed_width), f32)]
        + (cube_scatter_scratch(row_count, model_width) if cube else []),
        compiler_params=params(8 if cube else None),
        name="projection_grad",
    )(meta, grad_conv, grad_conv, edge, pre, grad_gate_pre, grad_small, conv_all, block_rows, *weights)

    if cube:
        grad_normed = grad_rows
    else:
        grad_normed = lax.psum_scatter(grad_rows, "head", scatter_dimension=0, tiled=True).astype(f32)
    gains = jnp.concatenate([gain_sum[0] / first_gain, grad_second, grad_head[0]]).reshape(2, -1)
    grad_w_all, grad_w_small, small_sums, _, gains, *gathered = line_sum(
        block_rows,
        grad_pre,
        feed_sum,
        (
            jnp.pad(
                jnp.concatenate([grad_taps, sums], axis=1), ((0, 8), (0, 0))
            ).astype(bf16),
            jnp.pad(gains, ((0, 14), (0, 0))).astype(bf16),
        ),
        (32, 16, 16, 16),
        "seq",
        1,
    )
    gains = gains[:2].reshape(-1)
    first_part, second_part = gains[:model_width], gains[model_width : 2 * model_width]
    head_part = gains[2 * model_width :]
    if cube:
        ff_grads = [ff_grads[0], *gathered, ff_grads[1]]
    grad_w_all, grad_w_output = lax.optimization_barrier((grad_w_all, grad_w_output))
    grad_w_all, mlp_out, *ff_grads = lax.optimization_barrier((grad_w_all, mlp_out, *ff_grads))
    (
        output, grad_inputs, grad_conv_query, grad_conv_key, grad_conv_value,
        grad_w_query, grad_w_key, grad_w_value, grad_w_outgate, grad_w_down, grad_w_gate, grad_w_up, grad_w_output,
    ) = finish(
        (grad_normed, inputs, grad_hidden_in, hidden_in, mlp_out), first_gain[None, :], small_sums, taps,
        grad_w_all, (qw, qw, vw, vw), (*ff_grads, grad_w_output),
    )
    sums = small_sums[:2, mixed_width : mixed_width + heads].astype(f32)
    return (
        output,
        grad_inputs,
        first_part,
        grad_w_query,
        grad_w_key,
        grad_w_value,
        grad_w_outgate,
        grad_w_small[:heads].astype(f32).T,
        grad_w_small[heads : 2 * heads].astype(f32).T,
        grad_conv_query,
        grad_conv_key,
        grad_conv_value,
        sums[1],
        sums[0],
        head_part,
        grad_w_output,
        second_part,
        grad_w_gate,
        grad_w_up,
        grad_w_down,
    )


def from_previous(array):
    devices = lax.axis_size("seq")
    return lax.ppermute(array, "seq", [(i, i + 1) for i in range(devices - 1)])


def solution(mesh):
    in_specs = (
        P(("seq", "head"), None),
        P(),
        P(),
        P(None, "head"),
        P(None, "head"),
        P(None, "head"),
        P(None, "head"),
        P(None, "head"),
        P(None, "head"),
        P(None, "head"),
        P(None, "head"),
        P(None, "head"),
        P("head"),
        P("head"),
        P(),
        P("head", None),
        P(),
        P(None, "seq"),
        P(None, "seq"),
        P("seq", None),
        P(("seq", "head"), None),
    )
    out_specs = (
        P(("seq", "head"), None),
        P(("seq", "head"), None),
        P(),
        P(None, "head"),
        P(None, "head"),
        P(None, "head"),
        P(None, "head"),
        P(None, "head"),
        P(None, "head"),
        P(None, "head"),
        P(None, "head"),
        P(None, "head"),
        P("head"),
        P("head"),
        P(),
        P("head", None),
        P(),
        P(None, "seq"),
        P(None, "seq"),
        P("seq", None),
    )
    return jax.shard_map(shards, mesh=mesh, in_specs=in_specs, out_specs=out_specs, check_vma=False)
```

```python
import functools

import jax
import jax.numpy as jnp
from jax import lax
from jax.experimental import pallas as pl
from jax.experimental.pallas import tpu as pltpu
from jax.sharding import PartitionSpec as P

GROUP = 64
BLOCK = 256
LANES = 128
HALO = 8

epsilon = 1e-06
f32 = jnp.float32
bf16 = jnp.bfloat16
VMEM_LIMIT = 56 * 1024 * 1024


def dot(left, right):
    return jnp.dot(left, right, preferred_element_type=f32)


def dot_tn(left, right):
    return lax.dot_general(left, right, (((0,), (0,)), ((), ())), preferred_element_type=f32)


def dot_nt(left, right):
    return lax.dot_general(left, right, (((1,), (1,)), ((), ())), preferred_element_type=f32)


def halves(values):
    top = values.astype(bf16)
    return top, (values - top.astype(f32)).astype(bf16)


def exact_left(left, right):
    top = right.astype(bf16)
    rest = right - top.astype(f32)
    middle = rest.astype(bf16)
    low = (rest - middle.astype(f32)).astype(bf16)
    return dot(left, top) + dot(left, middle) + dot(left, low)


def dot_fine(left, right):
    left_top, left_low = halves(left)
    right_top, right_low = halves(right)
    return dot(left_top, right_top) + (dot(left_top, right_low) + dot(left_low, right_top))


def sigmoid(values):
    return jax.nn.sigmoid(values)


def silu_slope(values):
    sigma = sigmoid(values)
    return sigma * (1.0 + values * (1.0 - sigma))


def softplus(values):
    return jnp.maximum(values, 0.0) + jnp.log1p(jnp.exp(-jnp.abs(values)))


def slot_starts(doc_lengths):
    slot_sizes = (doc_lengths + (GROUP - 1)) // GROUP * GROUP
    return jnp.cumsum(slot_sizes, dtype=jnp.int32) - slot_sizes


def layout(doc_lengths, first_row, row_total):
    starts = slot_starts(doc_lengths)
    places = first_row + jnp.arange(row_total, dtype=jnp.int32)
    owners = jnp.sum(
        (places[:, None] >= starts[None, 1:]).astype(jnp.int32), axis=1, dtype=jnp.int32
    )
    picked = (owners[:, None] == jnp.arange(doc_lengths.shape[0], dtype=jnp.int32)[None, :]).astype(
        jnp.int32
    )
    begins = jnp.sum(picked * starts[None, :], axis=1, dtype=jnp.int32)
    length = jnp.sum(picked * doc_lengths[None, :], axis=1, dtype=jnp.int32)
    offset = places - begins
    return (offset, offset < length)


def rms_scale(values, gain):
    return values * lax.rsqrt(jnp.mean(values * values, axis=-1, keepdims=True) + epsilon) * gain


def rms_back(values, gain, grad_in):
    scale = lax.rsqrt(jnp.mean(values * values, axis=-1, keepdims=True) + epsilon)
    weighted = grad_in * gain
    grad_values = scale * weighted - values * scale**3 * jnp.mean(
        weighted * values, axis=-1, keepdims=True
    )
    grad_gain = jnp.sum((grad_in * values * scale).reshape(-1, values.shape[-1]), axis=0)
    return (grad_values, grad_gain)


def owner_of(meta, docs, places):
    total = jnp.zeros_like(places)
    for doc in range(1, docs):
        total = total + jnp.where(places >= meta[1 + doc], 1, 0)
    return total


def offset_of(meta, docs, places):
    begin = jnp.zeros_like(places)
    for doc in range(1, docs):
        begin = jnp.where(places >= meta[1 + doc], meta[1 + doc], begin)
    return places - begin


def valid_of(meta, docs, places):
    left = meta[1] + meta[1 + docs] - places
    for doc in range(1, docs):
        left = jnp.where(places >= meta[1 + doc], meta[1 + doc] + meta[1 + docs + doc] - places, left)
    return jnp.where(left > 0, 1.0, 0.0)


class Masks:
    def __init__(self, meta, docs, chunk):
        base = meta[0] + chunk * BLOCK
        rows = lax.broadcasted_iota(jnp.int32, (BLOCK, BLOCK), 0)
        cols = lax.broadcasted_iota(jnp.int32, (BLOCK, BLOCK), 1)
        same = owner_of(meta, docs, base + rows) == owner_of(meta, docs, base + cols)
        self.inclusive = same & (rows >= cols)
        self.strictly = same & (rows > cols)
        self.level = rows ^ cols
        self.lower = jnp.where(rows >= cols, 1.0, 0.0).astype(bf16)
        self.upper = jnp.where(rows <= cols, 1.0, 0.0).astype(bf16)
        self.eye = jnp.where(rows == cols, 1.0, 0.0)
        place = base + lax.broadcasted_iota(jnp.int32, (BLOCK, 1), 0)
        owner = owner_of(meta, docs, place)
        before = jnp.int32(0)
        last = jnp.int32(0)
        for doc in range(1, docs):
            before = before + jnp.where(base - 1 >= meta[1 + doc], 1, 0)
            last = last + jnp.where(base + BLOCK - 1 >= meta[1 + doc], 1, 0)
        self.enters = jnp.where(owner == before, 1.0, 0.0)
        self.leaves = jnp.where(owner == last, 1.0, 0.0)
        self.through = jnp.where(before == last, 1.0, 0.0).astype(f32)
        self.offset = offset_of(meta, docs, place)


def decays(masks, scal, scal_t, head):
    column = scal[:, head : head + 1]
    row = scal_t[head : head + 1, :]
    within = jnp.where(masks.inclusive, jnp.exp(jnp.minimum(column - row, 0.0)), 0.0)
    last = column[BLOCK - 1 : BLOCK, :]
    entry = jnp.exp(column) * masks.enters
    leave = jnp.exp(last - column) * masks.leaves
    through = jnp.exp(last) * masks.through
    return within, entry, leave, through


def unit_lower_inverses(systems):
    half = BLOCK // 2
    rows = lax.broadcasted_iota(jnp.int32, (half, half), 0)
    cols = lax.broadcasted_iota(jnp.int32, (half, half), 1)
    level = rows ^ cols
    eye = jnp.where(rows == cols, 1.0, 0.0)
    parts = [system[at : at + half, at : at + half] for system in systems for at in (0, half)]
    solved = [eye - jnp.where(level == 1, part, 0.0) for part in parts]
    width = 2
    while width < half:
        keep = (level >= width) & (level < 2 * width)
        low = [inverse.astype(bf16) for inverse in solved]
        moved = [dot(jnp.where(keep, part, 0.0).astype(bf16), inverse) for part, inverse in zip(parts, low)]
        solved = [
            whole_part - dot(inverse, part.astype(bf16))
            for whole_part, inverse, part in zip(solved, low, moved)
        ]
        width *= 2
    solved = [inverse.astype(bf16) for inverse in solved]
    results = []
    for index, system in enumerate(systems):
        upper, lower = solved[2 * index], solved[2 * index + 1]
        corner = -dot(lower, dot(system[half:, :half].astype(bf16), upper).astype(bf16))
        results.append((upper, corner.astype(bf16), lower))
    return results


LEAD = 2 * HALO
STRIDE = BLOCK + LEAD


def cube_order(axis, step):
    place = lax.axis_index(axis)
    chunk = 0
    for bit in (1, 2, 4):
        chunk = chunk + bit * ((place // bit + step // bit) % 2)
    return chunk


class EdgeRows:
    def __init__(self, line, axis, own_ref, rows_ref, edge_ref, line_sem, send_sem, recv_sem):
        self.line, self.axis = line, axis
        self.group, self.place = lax.axis_index(line), lax.axis_index(axis)
        self.groups, self.last = lax.axis_size(line), lax.axis_size(axis) - 1
        self.own_ref, self.rows_ref, self.edge_ref = own_ref, rows_ref, edge_ref
        self.line_sem, self.send_sem, self.recv_sem = line_sem, send_sem, recv_sem

    def enter(self):
        barrier = pltpu.get_barrier_semaphore()
        for mask in (1, 2, 4, 6):
            pl.semaphore_signal(barrier, inc=1, device_id={self.axis: flip(self.place, mask)}, device_id_type=MESH)
        for by in range(1, self.groups):
            other = lax.rem(self.group + by, self.groups)
            pl.semaphore_signal(barrier, inc=1, device_id={self.line: other}, device_id_type=MESH)
        pl.semaphore_wait(barrier, 3 + self.groups)

    def hands_on(self):
        return (self.place == self.last) & (self.group < self.groups - 1)

    def receives(self):
        return (self.place == self.last) & (self.group > 0)

    def landing(self, mask):
        block = lax.rem(flip(self.place, mask) + 1, self.last + 1)
        return self.rows_ref.at[pl.ds(pl.multiple_of(block * STRIDE, LEAD), LEAD), :]

    def onward(self):
        return pltpu.make_async_remote_copy(
            self.own_ref.at[pl.ds(BLOCK - LEAD, LEAD), :], self.edge_ref, self.line_sem.at[0], self.line_sem.at[1],
            device_id={self.line: self.group + 1}, device_id_type=MESH,
        )

    def copy(self, mask, toward):
        return pltpu.make_async_remote_copy(
            self.landing(mask) if mask else self.edge_ref, self.landing(mask),
            self.send_sem.at[mask + toward if mask else toward], self.recv_sem.at[mask ^ toward],
            device_id={self.axis: flip(self.place, toward)}, device_id_type=MESH,
        )

    def wait(self, mask):
        pltpu.make_async_remote_copy(
            self.landing(mask), self.landing(mask), self.send_sem.at[0], self.recv_sem.at[mask],
            device_id={self.axis: flip(self.place, 1)}, device_id_type=MESH,
        ).wait_recv()

    def start(self):
        @pl.when(self.hands_on())
        def _():
            self.onward().start()

        @pl.when(self.place < self.last)
        def _():
            self.edge_ref[...] = self.own_ref[BLOCK - LEAD :, :]

        @pl.when((self.place == self.last) & (self.group == 0))
        def _():
            self.edge_ref[...] = jnp.zeros(self.edge_ref.shape, bf16)

        @pl.when(self.receives())
        def _():
            pltpu.make_async_remote_copy(
                self.edge_ref, self.edge_ref, self.line_sem.at[0], self.line_sem.at[1],
                device_id={self.line: self.group - 1}, device_id_type=MESH,
            ).wait_recv()

        for toward in (6, 2, 4, 1):
            self.copy(0, toward).start()
        self.landing(0)[...] = self.edge_ref[...]

    def spread(self):
        for mask in (2, 4, 6):
            self.wait(mask)
            self.copy(mask, 1).start()
        for mask in (1, 3, 5, 7):
            self.wait(mask)

    def end(self):
        @pl.when(self.hands_on())
        def _():
            self.onward().wait_send()

        for toward in (6, 2, 4, 1):
            self.copy(0, toward).wait_send()
        for mask in (2, 4, 6):
            self.copy(mask, 1).wait_send()


class MapExchange:
    def __init__(self, going, coming, behind, sem):
        self.going, self.coming, self.behind, self.sem = going, coming, behind, sem
        self.groups, self.group = lax.axis_size("seq"), lax.axis_index("seq")
        self.width = going.shape[1]

    def copy(self, kind, by, target):
        slot = self.groups - 1 - by
        passing = pl.ds(0, self.width)
        span = pl.ds(self.width, self.going.shape[2] - self.width) if kind == 0 else passing
        landing = self.behind.at[slot] if kind == 2 else self.coming.at[slot, :, :, span]
        return pltpu.make_async_remote_copy(
            self.going.at[:, :, span], landing, self.sem.at[2 * kind, slot], self.sem.at[2 * kind + 1, slot],
            device_id={"seq": target}, device_id_type=MESH,
        )

    def moves(self):
        group, groups = self.group, self.groups
        for by in range(groups - 1, 0, -1):
            yield 0, by, group + by, group + by < groups, group - by, group >= by
            yield 1, by, group + by, (group + by < groups) & (group > 0), group - by, group > by
            yield 2, by, group - by, group >= by, group + by, group + by < groups

    def run(self):
        for kind, by, target, sends, source, comes in self.moves():
            @pl.when(sends)
            def _():
                self.copy(kind, by, target).start()

        for kind, by, target, sends, source, comes in self.moves():
            slot = self.groups - 1 - by

            @pl.when(comes)
            def _():
                self.copy(kind, by, source).wait_recv()

            @pl.when(jnp.logical_not(comes))
            def _():
                if kind == 0:
                    self.coming[slot, :, :, self.width :] = jnp.zeros(self.coming.shape[1:3] + (self.going.shape[2] - self.width,), bf16)
                elif kind == 1:
                    self.coming[slot, :, :, : self.width] = jnp.zeros(self.behind.shape[1:], bf16)
                else:
                    self.behind[slot] = jnp.zeros(self.behind.shape[1:], bf16)

        for kind, by, target, sends, source, comes in self.moves():
            @pl.when(sends)
            def _():
                self.copy(kind, by, target).wait_send()


def forward_kernel(
    heads, key_width, value_width, docs, taps, chunks, cube,
    meta, rows_ref, wq_ref, wk_ref, wv_ref, wg_ref, ws_ref, conv_ref, dvec_ref,
    pre_ref, act_ref, gate_ref, small_ref, scal_ref, qkv_ref, inv_ref, w_out_ref, u_ref, drop_ref,
    starts_ref, map_ref, *refs,
):
    step = pl.program_id(0)
    ext, state, drops, adds, throughs = refs[3 * cube : 3 * cube + 5]
    if cube:
        all_ref = refs[0]
        earlier_ref, later_ref, *refs = refs[1:]
        held, copy_sem, edge_ref, line_sem, edge_send, edge_recv, cube_send, cube_recv = refs[5:13]
        going, coming, behind, map_sem = refs[13:]
        chunk = cube_order("head", step)
        rows_in = CubeGather("head", rows_ref, held, None, cube_send, cube_recv, STRIDE, LEAD)
        edges = EdgeRows("seq", "head", rows_ref, held, edge_ref, line_sem, edge_send, edge_recv)

        def kept(block):
            start = pl.multiple_of(block * STRIDE + LEAD, LEAD)
            return pltpu.make_async_copy(
                held.at[pl.ds(start, BLOCK), :],
                all_ref.at[pl.ds(pl.multiple_of(block * BLOCK, BLOCK), BLOCK), :],
                copy_sem.at[block],
            )

        @pl.when(step == 0)
        def _():
            edges.enter()
            edges.start()
            rows_in.first()
            held[pl.ds(pl.multiple_of(chunk * STRIDE + LEAD, LEAD), BLOCK), :] = rows_ref[...]

        @pl.when(step == 2)
        def _():
            rows_in.second()
            rows_in.third()

        @pl.when(step == 4)
        def _():
            rows_in.fourth()

        for odd in (1, 3, 5, 7):
            @pl.when(step == odd)
            def _():
                for half in range(2):
                    rows_in.wait(odd, half)

        kept(chunk).start()
        rows = held[pl.ds(pl.multiple_of(chunk * STRIDE + LEAD, LEAD), BLOCK), :]
    else:
        chunk = step
        rows = rows_ref[LEAD:, :]

    qw, vw = heads * key_width, heads * value_width
    mixed = 2 * qw + vw
    masks = Masks(meta, docs, chunk)
    gate_ref[...] = dot(rows, wg_ref[...])
    small = dot(rows, ws_ref[...])
    small_ref[...] = small
    if cube:
        @pl.when(step == 0)
        def _():
            edges.spread()

        rows_ext = held[pl.ds(pl.multiple_of(chunk * STRIDE, LEAD), STRIDE), :]
    else:
        rows_ext = rows_ref[...]
    for span, ref in ((slice(0, qw), wq_ref), (slice(qw, 2 * qw), wk_ref), (slice(2 * qw, mixed), wv_ref)):
        pre = dot(rows_ext, ref[...])
        ext[:, span] = pre
        pre_ref[:, span] = pre[LEAD:, :]

    conv = jnp.zeros((BLOCK, mixed), f32)
    for lag in range(taps):
        keep = jnp.where(masks.offset >= lag, 1.0, 0.0)
        conv = conv + conv_ref[lag : lag + 1, :] * (ext[LEAD - lag : LEAD - lag + BLOCK, :] * keep)
    act_ref[...] = conv
    act = conv * sigmoid(conv)

    lane = lax.broadcasted_iota(jnp.int32, (BLOCK, LANES), 1)
    decay = dvec_ref[1:2, :] * softplus(small + dvec_ref[0:1, :])
    cumul = exact_left(masks.lower, decay)
    scal = jnp.where(lane < heads, cumul, sigmoid(small))
    scal_ref[...] = scal
    scal_t = scal.T

    held_heads = []
    for head in range(heads):
        act_q = act[:, head * key_width : (head + 1) * key_width]
        act_k = act[:, qw + head * key_width : qw + (head + 1) * key_width]
        value = act[:, 2 * qw + head * value_width : 2 * qw + (head + 1) * value_width].astype(bf16)
        norm_q = lax.rsqrt(jnp.sum(act_q * act_q, axis=1, keepdims=True) + epsilon)
        norm_k = lax.rsqrt(jnp.sum(act_k * act_k, axis=1, keepdims=True) + epsilon)
        query = (act_q * norm_q * key_width ** (-0.5)).astype(bf16)
        key = (act_k * norm_k).astype(bf16)
        qkv_ref[:, head * key_width : (head + 1) * key_width] = query
        qkv_ref[:, qw + head * key_width : qw + (head + 1) * key_width] = key
        qkv_ref[:, 2 * qw + head * value_width : 2 * qw + (head + 1) * value_width] = value
        within, entry, leave, through = decays(masks, scal, scal_t, head)
        beta = scal[:, heads + head : heads + head + 1]
        system = jnp.where(masks.strictly, beta * dot_nt(key, key) * within, 0.0)
        held_heads.append((system, key, value, beta, entry, leave, through))

    half = BLOCK // 2
    inverses = unit_lower_inverses([part[0] for part in held_heads])
    for head, (upper, corner, lower) in enumerate(inverses):
        inv_ref[0, head, :half, :half] = upper
        inv_ref[0, head, :half, half:] = jnp.zeros((half, half), bf16)
        inv_ref[0, head, half:, :half] = corner
        inv_ref[0, head, half:, half:] = lower
    for head, (_, key, value, beta, entry, leave, through) in enumerate(held_heads):
        inverse = inv_ref[0, head]
        key_f = key.astype(f32)
        w_part = dot(inverse, (beta * entry * key_f).astype(bf16)).astype(bf16)
        u_part = dot(inverse, (beta * value.astype(f32)).astype(bf16))
        w_out_ref[0, head] = w_part
        u_ref[0, head] = u_part
        tail_key = (leave * key_f).astype(bf16)
        drop = dot_tn(tail_key, w_part)
        drop_ref[0, head] = drop
        drops[chunk, head] = drop.astype(bf16)
        adds[chunk, head] = dot_tn(tail_key, u_part.astype(bf16))
        throughs[chunk, head] = jnp.broadcast_to(through, (8, LANES))

    @pl.when(step == chunks - 1)
    def _():
        shape = (key_width, key_width + value_width)
        ident = jnp.where(lax.broadcasted_iota(jnp.int32, shape, 0) == lax.broadcasted_iota(jnp.int32, shape, 1), 1.0, 0.0)
        for head in range(heads):
            state[head] = ident

        def pass_on(at, carry):
            for head in range(heads):
                before = state[head]
                starts_ref[at, head] = before
                after = throughs[at, head][0:1, 0:1] * before - dot(drops[at, head], before.astype(bf16))
                state[head] = after + jnp.concatenate(
                    [jnp.zeros((key_width, key_width), f32), adds[at, head]], axis=1
                )
            return carry

        lax.fori_loop(0, chunks, pass_on, 0)
        for head in range(heads):
            map_ref[head] = state[head]
        if cube:
            maps = MapExchange(going, coming, behind, map_sem)
            for head in range(heads):
                going[head] = state[head].astype(bf16)
            maps.run()
            earlier_ref[...] = coming[...]
            later_ref[...] = behind[...]
            rows_in.last()
            edges.end()
            for block in range(chunks):
                kept(block).wait()


def output_kernel(
    heads, key_width, value_width, docs, others, cube,
    meta, maps_ref, starts_ref, w_in_ref, u_ref, qkv_ref, scal_ref, gate_ref, gain_ref, w_output_ref, *refs,
):
    if cube:
        inputs_ref, next_gain_ref, *refs = refs
    core_ref, gated_ref, fresh_ref, state_ref, mixed_ref, *refs = refs
    if cube:
        next_ref, *refs = refs
    incoming, *refs = refs
    step = pl.program_id(0)
    chunk = cube_order("head", 7 - step) if cube else step
    qw = heads * key_width

    @pl.when(step == 0)
    def _():
        for head in range(heads):
            state = jnp.zeros((key_width, value_width), f32)
            for other in range(others):
                passing = maps_ref[other, head, :, :key_width]
                top, low = halves(state)
                state = dot(passing, top) + dot(passing, low) + maps_ref[other, head, :, key_width:].astype(f32)
            incoming[head] = state

    masks = Masks(meta, docs, chunk)
    scal = scal_ref[...]
    scal_t = scal.T
    gain = gain_ref[...]
    for head in range(heads):
        query = qkv_ref[:, head * key_width : (head + 1) * key_width]
        key = qkv_ref[:, qw + head * key_width : qw + (head + 1) * key_width]
        within, entry, leave, through = decays(masks, scal, scal_t, head)
        begun = starts_ref[0, head]
        state = dot_fine(begun[:, :key_width], incoming[head]) + begun[:, key_width:]
        state_ref[0, head] = state
        state_low = state.astype(bf16)
        fresh = (u_ref[0, head] - dot(w_in_ref[0, head], state_low)).astype(bf16)
        fresh_ref[0, head] = fresh
        scores = (dot_nt(query, key) * within).astype(bf16)
        core = dot((query.astype(f32) * entry).astype(bf16), state_low) + dot(scores, fresh)
        span = slice(head * value_width, (head + 1) * value_width)
        core_ref[:, span] = core
        scale = lax.rsqrt(jnp.mean(core * core, axis=1, keepdims=True) + epsilon)
        gate = gate_ref[:, span]
        gated_ref[:, span] = (core * scale * gain * (gate * sigmoid(gate))).astype(bf16)
    mixed = dot(gated_ref[...], w_output_ref[...])
    if not cube:
        mixed_ref[...] = mixed.astype(bf16)
        return

    total, *refs = refs
    scatter_block(step, CubeScatter("head", total, *refs), mixed)

    @pl.when(step == 7)
    def _():
        hidden_in = inputs_ref[...].astype(f32) + total[...]
        mixed_ref[...] = hidden_in
        next_ref[...] = rms_scale(hidden_in, next_gain_ref[...]).astype(bf16)


def core_grad_kernel(
    heads, key_width, value_width, docs, chunks,
    meta, grad_ref, w_output_ref, core_ref, gate_ref, gain_ref, qkv_ref, scal_ref, w_in_ref, drop_ref,
    grad_core_ref, inner_ref, pull_ref, grad_gate_ref, grad_gain_ref, total_ref, chunk=None, later=None,
):
    step = pl.program_id(0)
    chunk = chunks - 1 - step if chunk is None else chunk
    qw = heads * key_width
    masks = Masks(meta, docs, chunk)
    scal = scal_ref[...]
    scal_t = scal.T
    gain = gain_ref[...]

    @pl.when(step == 0)
    def _():
        grad_gain_ref[...] = jnp.zeros_like(grad_gain_ref)
        total_ref[...] = jnp.zeros_like(total_ref)

    grad_gated = dot_nt(grad_ref[...], w_output_ref[...])
    for head in range(heads):
        span = slice(head * value_width, (head + 1) * value_width)
        core = core_ref[:, span]
        gate = gate_ref[:, span]
        grad_in = grad_gated[:, span]
        scale = lax.rsqrt(jnp.mean(core * core, axis=1, keepdims=True) + epsilon)
        sigma = sigmoid(gate)
        normed = core * scale
        grad_gate_ref[:, span] = (
            grad_in * (normed * gain) * (sigma * (1.0 + gate * (1.0 - sigma)))
        ).astype(bf16)
        grad_normed = grad_in * (gate * sigma)
        weighted = grad_normed * gain
        grad_core = scale * (weighted - normed * jnp.mean(weighted * normed, axis=1, keepdims=True))
        grad_gain_ref[0:1, :] += jnp.sum(grad_normed * normed, axis=0, keepdims=True)
        grad_core = grad_core.astype(bf16)
        grad_core_ref[0, head] = grad_core
        query = qkv_ref[:, head * key_width : (head + 1) * key_width]
        key = qkv_ref[:, qw + head * key_width : qw + (head + 1) * key_width]
        within, entry, leave, through = decays(masks, scal, scal_t, head)
        scores = (dot_nt(query, key) * within).astype(bf16)
        inner = dot_tn(scores, grad_core)
        inner_ref[0, head] = inner
        pull = dot_tn((query.astype(f32) * entry).astype(bf16), grad_core) - dot_tn(
            w_in_ref[0, head], inner.astype(bf16)
        )
        pull_ref[0, head] = pull
        if later is not None:
            pulls, drops, throughs = later
            pulls[chunk, head] = pull
            drops[chunk, head] = drop_ref[0, head].astype(bf16)
            throughs[chunk, head] = jnp.broadcast_to(through, (8, LANES))
            continue
        total = total_ref[head]
        total_ref[head] = (
            through * total - dot_tn(drop_ref[0, head].astype(bf16), total.astype(bf16)) + pull
        )


def backward_kernel(
    heads, key_width, value_width, docs, chunks, others, cube,
    meta, passing_ref, later_ref, qkv_ref, act_ref, scal_ref, small_ref, inv_ref, fresh_ref, state_ref,
    grad_core_ref, inner_ref, pull_ref, drop_ref, dvec_ref, *refs,
):
    if cube:
        feed_ref, *refs = refs
    grad_conv_ref, grad_small_ref, sums_ref, edge_ref, *refs = refs
    if cube:
        feed_sum_ref, *refs = refs
    carried, edge_out, edge_in, edge_sem, *refs = refs
    step = pl.program_id(0)
    chunk = chunks - 1 - step

    @pl.when(step == 0)
    def _():
        line_barrier("seq", "head" if cube else None)

    if cube:
        rows = feed_ref.shape[0] // 8
        total, *refs = refs
        scatter = CubeScatter("head", total, *refs)
        for at, masks in enumerate(((7,), (6, 5), (4, 3), (2, 1), (0,))):
            @pl.when(step == at)
            def _():
                for mask in masks:
                    part = pl.ds(pl.multiple_of(flip(scatter.place, mask) * rows, rows), rows)
                    scatter.take(mask, feed_ref[part, :].astype(f32))
    groups, group = lax.axis_size("seq"), lax.axis_index("seq")
    edge = pltpu.make_async_remote_copy(
        edge_out, edge_in, edge_sem.at[0], edge_sem.at[1],
        device_id={"seq": jnp.maximum(group - 1, 0)}, device_id_type=MESH,
    )

    qw = heads * key_width

    @pl.when(step == 0)
    def _():
        sums_ref[...] = jnp.zeros_like(sums_ref)
        for head in range(heads):
            state = jnp.zeros((key_width, value_width), f32)
            for other in range(others):
                passing = passing_ref[other, head]
                top, low = halves(state)
                state = dot_tn(passing, top) + dot_tn(passing, low) + later_ref[other, head].astype(f32)
            carried[head] = state

    masks = Masks(meta, docs, chunk)
    scal = scal_ref[...]
    scal_t = scal.T
    lane = lax.broadcasted_iota(jnp.int32, (BLOCK, LANES), 1)
    slopes = jnp.zeros((BLOCK, LANES), f32)
    tails = jnp.zeros((1, LANES), f32)
    betas = jnp.zeros((BLOCK, LANES), f32)
    for head in range(heads):
        q_span = slice(head * key_width, (head + 1) * key_width)
        k_span = slice(qw + head * key_width, qw + (head + 1) * key_width)
        v_span = slice(2 * qw + head * value_width, 2 * qw + (head + 1) * value_width)
        query, key, value = qkv_ref[:, q_span], qkv_ref[:, k_span], qkv_ref[:, v_span]
        query_f, key_f = query.astype(f32), key.astype(f32)
        within, entry, leave, through = decays(masks, scal, scal_t, head)
        beta = scal[:, heads + head : heads + head + 1]
        later = carried[head]
        later_low = later.astype(bf16)
        state = state_ref[0, head]
        state_low = state.astype(bf16)
        grad_core = grad_core_ref[0, head]
        fresh = fresh_ref[0, head]
        carried[head] = through * later - dot_tn(drop_ref[0, head].astype(bf16), later_low) + pull_ref[0, head]
        grad_fresh = inner_ref[0, head] + dot((leave * key_f).astype(bf16), later_low)
        grad_x = dot_tn(inv_ref[0, head], grad_fresh.astype(bf16))
        grad_x_low = grad_x.astype(bf16)
        grad_x_beta = beta * grad_x
        recalled = dot(key, state_low)
        grad_beta = jnp.sum(grad_x * (value.astype(f32) - entry * recalled), axis=1, keepdims=True)
        from_state_q = dot_nt(grad_core, state_low)
        from_state_k = dot_nt(grad_x_beta.astype(bf16), state_low)
        grad_scores = (dot_nt(grad_core, fresh) * within).astype(bf16)
        gram = dot_nt(key, key)
        grad_system = jnp.where(masks.strictly, dot_nt(grad_x_low, fresh) * within, 0.0)
        grad_beta = grad_beta - jnp.sum(grad_system * gram, axis=1, keepdims=True)
        grad_gram = (-beta * grad_system).astype(bf16)
        grad_query = dot(grad_scores, key) + entry * from_state_q
        grad_row = dot(grad_gram, key) - entry * from_state_k
        passed = leave * dot_nt(fresh, later_low)
        grad_col = dot_tn(grad_gram, key) + dot_tn(grad_scores, query) + passed
        slope = jnp.sum(query_f * grad_query + key_f * (grad_row - grad_col), axis=1, keepdims=True)
        kept = jnp.sum(jnp.sum(state * later, axis=1, keepdims=True), axis=0, keepdims=True)
        moved = jnp.sum(jnp.sum(key_f * passed, axis=1, keepdims=True), axis=0, keepdims=True)
        tail = through * kept + moved
        slopes = jnp.where(lane == head, slope, slopes)
        tails = jnp.where(lane[0:1, :] == head, tail, tails)
        betas = jnp.where(lane == heads + head, grad_beta, betas)

        conv_q, conv_k, conv_v = act_ref[:, q_span], act_ref[:, k_span], act_ref[:, v_span]
        for span, conv, grad, factor in (
            (q_span, conv_q, grad_query, key_width ** (-0.5)),
            (k_span, conv_k, grad_row + grad_col, 1.0),
        ):
            sigma = sigmoid(conv)
            act = conv * sigma
            norm = lax.rsqrt(jnp.sum(act * act, axis=1, keepdims=True) + epsilon)
            unit = act * norm
            grad_act = (factor * norm) * (grad - unit * jnp.sum(grad * unit, axis=1, keepdims=True))
            grad_conv_ref[:, span] = grad_act * (sigma * (1.0 + conv * (1.0 - sigma)))
        grad_conv_ref[:, v_span] = grad_x_beta * silu_slope(conv_v)

    grad_decay = jnp.where(lane < heads, exact_left(masks.upper, slopes) + tails, 0.0)
    shifted = small_ref[...] + dvec_ref[0:1, :]
    rate = dvec_ref[1:2, :]
    grad_z = grad_decay * rate * sigmoid(shifted)
    sums_ref[0:1, :] += jnp.sum(grad_z, axis=0, keepdims=True)
    sums_ref[1:2, :] += jnp.sum(grad_decay * (rate * softplus(shifted)), axis=0, keepdims=True)
    strength = sigmoid(small_ref[...])
    grad_small_ref[...] = jnp.where(lane < heads, grad_z, betas * strength * (1.0 - strength)).astype(bf16)

    @pl.when(step == chunks - 1)
    def _():
        if cube:
            scatter.finish()
            feed_sum_ref[...] = total[...].astype(bf16)
        edge_out[...] = grad_conv_ref[0:HALO, :]

        @pl.when(group > 0)
        def _():
            edge.start()

        @pl.when(group < groups - 1)
        def _():
            edge.wait_recv()
            edge_ref[...] = edge_in[...]

        @pl.when(group == groups - 1)
        def _():
            edge_ref[...] = jnp.zeros(edge_ref.shape, f32)

        @pl.when(group > 0)
        def _():
            edge.wait_send()


def projection_grad_kernel(
    mixed, docs, chunks, taps, cube,
    meta, grad_conv_ref, later_ref, edge_ref, pre_ref, grad_gate_ref, grad_small_ref, conv_ref, rows_ref,
    wq_ref, wk_ref, wv_ref, wg_ref, ws_ref,
    grad_pre_ref, grad_taps_ref, grad_rows_ref, gain_sum_ref,
    ext, *refs,
):
    step = pl.program_id(0)
    chunk = cube_order("head", 7 - step) if cube else step

    @pl.when(step == 0)
    def _():
        grad_taps_ref[...] = jnp.zeros_like(grad_taps_ref)
        gain_sum_ref[...] = jnp.zeros_like(gain_sum_ref)

    ext[0:BLOCK, :] = grad_conv_ref[...]

    @pl.when(chunk == chunks - 1)
    def _():
        ext[BLOCK : BLOCK + HALO, :] = edge_ref[...]

    @pl.when(chunk < chunks - 1)
    def _():
        ext[BLOCK : BLOCK + HALO, :] = later_ref[...]

    place = meta[0] + chunk * BLOCK + lax.broadcasted_iota(jnp.int32, (BLOCK, 1), 0)
    pre = pre_ref[...]
    total = jnp.zeros((BLOCK, mixed), f32)
    for lag in range(taps):
        keep = jnp.where(offset_of(meta, docs, place + lag) >= lag, 1.0, 0.0)
        moved = ext[lag : lag + BLOCK, :] * keep
        total = total + conv_ref[lag : lag + 1, :] * moved
        grad_taps_ref[lag : lag + 1, :] += jnp.sum(pre * moved, axis=0, keepdims=True)
    width = grad_gate_ref.shape[1]
    grad_pre_ref[:, :mixed] = total.astype(bf16)
    grad_pre_ref[:, mixed : mixed + width] = grad_gate_ref[...]
    grad_pre_ref[:, mixed + width :] = grad_small_ref[...]
    grad = jnp.zeros(grad_rows_ref.shape, f32)
    begin = 0
    for ref in (wq_ref, wk_ref, wv_ref, wg_ref, ws_ref):
        grad = grad + dot_nt(grad_pre_ref[:, begin : begin + ref.shape[1]], ref[...])
        begin += ref.shape[1]
    gain_sum_ref[0:1, :] += jnp.sum(grad * rows_ref[...].astype(f32), axis=0, keepdims=True)
    if cube:
        scatter_block(step, CubeScatter("head", grad_rows_ref, *refs), grad)
    else:
        grad_rows_ref[...] = grad.astype(bf16)


MESH = pl.DeviceIdType.MESH
ANYWHERE = pl.BlockSpec(memory_space=pl.ANY)


def line_barrier(axis, cube=None):
    devices, place = lax.axis_size(axis), lax.axis_index(axis)
    barrier = pltpu.get_barrier_semaphore()

    @pl.when(place > 0)
    def _():
        pl.semaphore_signal(barrier, inc=1, device_id={axis: place - 1}, device_id_type=MESH)

    @pl.when(place < devices - 1)
    def _():
        pl.semaphore_signal(barrier, inc=1, device_id={axis: place + 1}, device_id_type=MESH)

    more = 0
    if cube is not None:
        for mask in (1, 2, 4):
            pl.semaphore_signal(
                barrier, inc=1, device_id={cube: flip(lax.axis_index(cube), mask)}, device_id_type=MESH
            )
        more = 3

    @pl.when((place > 0) & (place < devices - 1))
    def _():
        pl.semaphore_wait(barrier, 2 + more)

    @pl.when((place == 0) | (place == devices - 1))
    def _():
        pl.semaphore_wait(barrier, 1 + more)


class LineSum:
    skew = 2
    window = 4

    def __init__(self, axis, counts, depths, parts, passed, arrived, sums, reduce_sems, back_sems):
        self.axis, self.counts, self.depths = axis, counts, depths
        self.single = [array.shape[0] == depth for array, depth in zip(sums, depths)]
        self.parts, self.passed, self.arrived, self.sums = parts, passed, arrived, sums
        self.sems = (reduce_sems, back_sems)
        self.devices, self.place = lax.axis_size(axis), lax.axis_index(axis)
        self.steps = max(counts) + self.skew * (self.devices - 1)

    def rows_of(self, half, index, at):
        depth = self.depths[index]
        return pl.ds(pl.multiple_of((half * self.counts[index] + at) * depth, depth), depth)

    def copy(self, half, index, at, target, back):
        rows = self.rows_of(half, index, at)
        slot = half * self.counts[index] + at
        source, landing = (self.sums, self.sums) if back else (self.passed, self.arrived)
        sent, received = self.sems[back][2 * index], self.sems[back][2 * index + 1]
        return pltpu.make_async_remote_copy(
            source[index].at[rows, :], landing[index].at[rows, :], sent.at[slot], received.at[slot],
            device_id={self.axis: target}, device_id_type=MESH,
        )

    def send(self, half, index, at, target, back):
        @pl.when(at >= self.window)
        def _():
            self.copy(half, index, at - self.window, target, back).wait_send()

        self.copy(half, index, at, target, back).start()

    def each(self, handle):
        place, last = self.place, self.devices - 1
        for half in range(2):
            ends = (last, 0) if half == 0 else (0, last)
            toward = place - 1 if half == 0 else place + 1
            away = place + 1 if half == 0 else place - 1
            for index in range(len(self.counts)):
                if half == 0 or not self.single[index]:
                    handle(half, index, toward, away, place == ends[0], place == ends[1])

    def reduce(self, step):
        def handle(half, index, toward, away, begin, end):
            late = (self.devices - 1 - self.place) if half == 0 else self.place
            at = step - self.skew * late

            @pl.when((at >= 0) & (at < self.counts[index]))
            def _():
                rows = self.rows_of(half, index, at)

                @pl.when(begin)
                def _():
                    self.passed[index][rows, :] = self.parts[index][rows, :]
                    self.send(half, index, at, toward, 0)

                @pl.when(jnp.logical_not(begin))
                def _():
                    self.copy(half, index, at, toward, 0).wait_recv()
                    added = (
                        self.parts[index][rows, :].astype(f32) + self.arrived[index][rows, :].astype(f32)
                    ).astype(bf16)

                    @pl.when(jnp.logical_not(end))
                    def _():
                        self.passed[index][rows, :] = added
                        self.send(half, index, at, toward, 0)

                    @pl.when(end)
                    def _():
                        self.sums[index][rows, :] = added

        self.each(handle)

    def back(self, step, given=None):
        def handle(half, index, toward, away, begin, end):
            late = self.place if half == 0 else (self.devices - 1 - self.place)
            at = step - self.skew * late

            @pl.when((at >= 0) & (at < self.counts[index]))
            def _():
                if given is not None:
                    @pl.when(end)
                    def _():
                        rows = self.rows_of(half, index, at)
                        self.sums[index][rows, :] = given[index][rows, :]

                @pl.when(jnp.logical_not(end))
                def _():
                    self.copy(half, index, at, away, 1).wait_recv()

                @pl.when(jnp.logical_not(begin))
                def _():
                    self.send(half, index, at, away, 1)

        self.each(handle)

    def settle(self, back):
        def handle(half, index, toward, away, begin, end):
            count = self.counts[index]
            for at in range(max(count - self.window, 0), count):
                @pl.when(jnp.logical_not(begin if back else end))
                def _():
                    self.copy(half, index, at, away if back else toward, back).wait_send()

        self.each(handle)


def line_sum_kernel(axis, cube, counts, depths, *refs):
    total = len(counts)
    rows_ref, grads_ref, *refs = refs
    parts, refs = refs[: total - 2], refs[total - 2 :]
    if cube:
        block_ref, *refs = refs
    sums, refs = refs[:total], refs[total:]
    if cube:
        whole_ref, blocks_ref, *refs = refs
    product, turned, *refs = refs
    parts = (product, turned, *parts)
    width = product.shape[1]
    arrived, passed, refs = refs[:total], refs[total : 2 * total], refs[2 * total :]
    share = BLOCK // depths[0]
    tiles = counts[0] // share
    line = LineSum(axis, counts, depths, parts, passed, arrived, sums, refs[: 2 * total], refs[2 * total : 4 * total])
    line_barrier(axis, "head" if cube else None)

    begin = max(counts)
    if cube:
        final = CubeTotal(*refs[4 * total : 4 * total + 4])
        gather = CubeGather("head", block_ref, blocks_ref, *refs[4 * total + 4 :], enter=False)
        gather.first()

    turned[...] = dot_tn(grads_ref[:, width:], rows_ref[...])[: turned.shape[0], :].astype(bf16)

    def step_on(step, carry):
        @pl.when((step % share == 0) & (step < tiles * share))
        def _():
            for half in range(2):
                columns = pl.ds(pl.multiple_of((half * tiles + step // share) * BLOCK, BLOCK), BLOCK)
                product[columns, :] = dot_tn(rows_ref[:, columns], grads_ref[:, :width]).astype(bf16)

        @pl.when(step < line.steps)
        def _():
            line.reduce(step)

        @pl.when(step >= begin)
        def _():
            line.back(step - begin)

        if cube:
            for at, phase in ((begin // 2, gather.second), (begin * 3 // 4, gather.third), (begin, gather.fourth)):
                @pl.when(step == at)
                def _():
                    phase()

            after = begin + line.skew * line.devices
            for stage in range(4):
                @pl.when(step == after + 3 * stage)
                def _():
                    if stage:
                        final.end(stage - 1, whole_ref)
                    else:
                        final.held[0] = sums[-1][: whole_ref.shape[0], :].astype(f32)
                    if stage < 3:
                        final.copy(stage).start()

        return carry

    lax.fori_loop(0, begin + line.steps, step_on, 0)
    line.settle(0)
    line.settle(1)
    if cube:
        gather.last()


class CubeTotal:
    def __init__(self, held, arrived, send_sem, recv_sem):
        self.held, self.arrived, self.send_sem, self.recv_sem = held, arrived, send_sem, recv_sem

    def copy(self, stage):
        return pltpu.make_async_remote_copy(
            self.held.at[stage], self.arrived.at[stage], self.send_sem.at[stage], self.recv_sem.at[stage],
            device_id={"head": flip(lax.axis_index("head"), (1, 2, 4)[stage])}, device_id_type=MESH,
        )

    def end(self, stage, total_ref):
        self.copy(stage).wait()
        if stage < 2:
            self.held[stage + 1] = self.held[stage] + self.arrived[stage]
        else:
            total_ref[...] = self.held[stage] + self.arrived[stage]


def line_scratch(arrays, depths, moves):
    counts = tuple(max(array.shape[0] // (2 * depth), 1) for array, depth in zip(arrays, depths))
    semaphores = []
    for count in counts:
        semaphores += [pltpu.SemaphoreType.DMA((2 * count,))] * 2
    return counts, semaphores * moves


def line_sum(rows, grads, blocks, given, depths, axis, collective_id):
    cube = lax.axis_size("head") == 8
    arrays = (
        struct((rows.shape[1], grads.shape[1] - LANES), bf16), struct((2 * HALO, rows.shape[1]), bf16), *given,
    )
    counts, semaphores = line_scratch(arrays, depths, 2)
    vmem = pl.BlockSpec(memory_space=pltpu.VMEM)
    scratch = [pltpu.VMEM(array.shape, bf16) for array in (*arrays[:2], *arrays, *arrays)] + semaphores
    total = (8, arrays[-1].shape[1])
    if cube:
        scratch += [pltpu.VMEM((3,) + total, f32)] * 2 + [pltpu.SemaphoreType.DMA((3,))] * 2 + CUBE_SEMAPHORES
    results = pl.pallas_call(
        functools.partial(line_sum_kernel, axis, cube, counts, tuple(depths)),
        in_specs=[vmem] * len(arrays) + [ANYWHERE] * cube,
        out_specs=[vmem] * (len(arrays) + cube) + [ANYWHERE] * cube,
        out_shape=[struct(array.shape, bf16) for array in arrays]
        + [struct(total, f32)] * cube
        + [struct((8 * block.shape[0], block.shape[1]), bf16) for block in blocks],
        scratch_shapes=scratch,
        compiler_params=pltpu.CompilerParams(
            collective_id=collective_id, has_side_effects=True, vmem_limit_bytes=VMEM_LIMIT
        ),
        cost_estimate=pl.CostEstimate(flops=10**8, bytes_accessed=40 * 10**6, transcendentals=0),
        name="line_sum",
    )(rows, grads, *given, *blocks)
    if not cube:
        results = [*results, lax.psum(results[-1][:8].astype(f32), "head")]
    return results


def whole(shape):
    zeros = (0,) * len(shape)
    return pl.BlockSpec(tuple(shape), lambda step: zeros)


def held(shape):
    zeros = (0,) * len(shape)
    return pl.BlockSpec(tuple(shape), lambda step: zeros, pipeline_mode=pl.Buffered(1))


def by_rows(width, chunks=None):
    if chunks is None:
        return pl.BlockSpec((BLOCK, width), lambda step: (step, 0))
    return pl.BlockSpec((BLOCK, width), lambda step: (chunks - 1 - step, 0))


def by_chunk(shape, chunks=None):
    rest = (0,) * len(shape)
    if chunks is None:
        return pl.BlockSpec((1,) + tuple(shape), lambda step: (step,) + rest)
    return pl.BlockSpec((1,) + tuple(shape), lambda step: (chunks - 1 - step,) + rest)


SCALARS = pl.BlockSpec(memory_space=pltpu.SMEM)


def feed_kernel(
    axis, devices, rows, pieces, docs,
    meta, own_ref, *refs,
):
    given, kept, refs = refs[:4], refs[4:9], refs[9:]
    total_ref, *refs = refs
    hidden_ref, *refs = refs
    inside, refs = refs[:8], refs[8:]
    inside = (*inside, inside[0])
    grads_ref, w_gate_ref, w_up_ref, w_down_ref = inside[:4]
    blocks_ref, turned_ref, grad_gate_ref, grad_up_ref, part_ref = inside[4:]
    parts, arrived, gather_send, gather_recv, chain_send, chain_recv, load_sem, store_sem = refs
    place = lax.axis_index(axis)
    piece = rows // 2

    def load(index):
        return pltpu.make_async_copy(given[index], inside[index], load_sem.at[index])

    def store(index):
        return pltpu.make_async_copy(inside[4 + index], kept[index], store_sem.at[index])

    for index in (3, 0, 1, 2):
        load(index).start()
    line_barrier(axis)

    def span(block, half):
        return pl.ds(pl.multiple_of(block * rows + half * piece, piece), piece)

    def full(block):
        return pl.ds(pl.multiple_of(block * rows, rows), rows)

    def gather(owner, hop, way, half):
        target = place + 1 - 2 * way
        slot = (hop * 2 + way) * 2 + half
        return pltpu.make_async_remote_copy(
            blocks_ref.at[span(owner, half), :], blocks_ref.at[span(owner, half), :],
            gather_send.at[slot], gather_recv.at[slot], device_id={axis: target}, device_id_type=MESH,
        )

    bit = rows // pieces

    def strip(block, part):
        return pl.ds(pl.multiple_of(block * rows + part * bit, bit), bit)

    def chain(block, way, part, at):
        target = at + 1 - 2 * way
        landing = jnp.where((block == target) & (way == 0), devices, block)
        slot = (way * devices + block) * pieces + part
        return pltpu.make_async_remote_copy(
            parts.at[strip(block, part), :], arrived.at[strip(landing, part), :],
            chain_send.at[slot], chain_recv.at[slot], device_id={axis: target}, device_id_type=MESH,
        )

    blocks_ref[full(place), :] = own_ref[...]

    def event(step, carry):
        hop = (step + 1) // 2
        way = (step + 1) % 2
        owner = jnp.where(way == 0, place - hop, place + hop)

        @pl.when(step == 0)
        def _():
            for side in range(2):
                @pl.when((place + 1 - 2 * side >= 0) & (place + 1 - 2 * side < devices))
                def _():
                    for half in range(2):
                        gather(place, 0, side, half).start()

            for index in range(4):
                load(index).wait()

        @pl.when((step > 0) & (way == 0))
        def _():
            for side in range(2):
                come = place - hop if side == 0 else place + hop
                goes = place + 1 if side == 0 else place - 1

                @pl.when((come >= 0) & (come < devices))
                def _():
                    for half in range(2):
                        gather(come, hop - 1, side, half).wait_recv()

                        @pl.when((goes >= 0) & (goes < devices))
                        def _():
                            gather(come, hop, side, half).start()

        @pl.when((owner >= 0) & (owner < devices))
        def _():
            here = full(owner)
            first = (owner * lax.axis_size("head") + lax.axis_index("head")) * rows
            valid = valid_of(meta, docs, first + lax.broadcasted_iota(jnp.int32, (rows, 1), 0))
            grad_hidden = valid * dot_nt(grads_ref[here, :], w_down_ref[...])
            block = blocks_ref[here, :]
            gate_pre = dot(block, w_gate_ref[...])
            up_pre = dot(block, w_up_ref[...])
            sigma = sigmoid(gate_pre)
            act = gate_pre * sigma
            hidden = act * up_pre
            hidden_ref[here, :] = hidden.astype(bf16)
            turned_ref[:, full(owner)] = (valid * hidden).astype(bf16).T
            grad_gate_ref[here, :] = (grad_hidden * up_pre * (sigma * (1.0 + gate_pre * (1.0 - sigma)))).astype(bf16)
            grad_up_ref[here, :] = (grad_hidden * act).astype(bf16)
            grad = dot_nt(grad_gate_ref[here, :], w_gate_ref[...]) + dot_nt(grad_up_ref[here, :], w_up_ref[...])

            @pl.when(step == 0)
            def _():
                total_ref[...] = grad

            @pl.when(step > 0)
            def _():
                parts[here, :] = grad.astype(bf16)

        @pl.when((way == 1) & (step > 0))
        def _():
            for part in range(pieces):
                for turn in range(2):
                    side = jnp.where(2 * place < devices, turn, 1 - turn)
                    block = jnp.where(side == 1, devices - 1 - hop, hop)
                    begins = place == jnp.where(side == 1, devices - 1, 0)
                    valid = jnp.where(side == 1, block < place, block > place)

                    @pl.when(valid)
                    def _():
                        @pl.when(jnp.logical_not(begins))
                        def _():
                            chain(block, side, part, place + 2 * side - 1).wait_recv()
                            at = strip(block, part)
                            parts[at, :] = (parts[at, :].astype(f32) + arrived[at, :].astype(f32)).astype(bf16)

                        chain(block, side, part, place).start()

        return carry

    lax.fori_loop(0, 2 * devices - 1, event, 0)

    for index in range(4):
        store(index).start()

    def feed_part(block, carry):
        part_ref[full(block), :] = dot(hidden_ref[full(block), :], w_down_ref[...]).astype(bf16)
        return carry

    lax.fori_loop(0, devices, feed_part, 0)
    store(4).start()

    for side, landing, comes in ((1, place, place < devices - 1), (0, devices, place > 0)):
        @pl.when(comes)
        def _():
            for part in range(pieces):
                chain(place, side, part, place + 2 * side - 1).wait_recv()
                at = pl.ds(part * bit, bit)
                total_ref[at, :] += arrived[strip(landing, part), :].astype(f32)

    def gather_end(step, carry):
        hop = step // 2
        way = step % 2
        owner = jnp.where(way == 0, place - hop, place + hop)
        target = place + 1 - 2 * way

        @pl.when((owner >= 0) & (owner < devices) & (target >= 0) & (target < devices))
        def _():
            for half in range(2):
                gather(owner, hop, way, half).wait_send()

        return carry

    lax.fori_loop(0, 2 * (devices - 1), gather_end, 0)

    def chain_end(block, carry):
        @pl.when(block < place)
        def _():
            for part in range(pieces):
                chain(block, 1, part, place).wait_send()

        @pl.when(block > place)
        def _():
            for part in range(pieces):
                chain(block, 0, part, place).wait_send()

        return carry

    lax.fori_loop(0, devices, chain_end, 0)
    for index in range(5):
        store(index).wait()


def feed(meta, docs, own, grads, w_gate, w_up, w_down, axis, collective_id):
    devices = lax.axis_size(axis)
    rows, width = own.shape
    units = w_gate.shape[1]
    vmem = pl.BlockSpec(memory_space=pltpu.VMEM)
    moves = pltpu.SemaphoreType.DMA((4 * devices,))
    pieces = 4
    chains = pltpu.SemaphoreType.DMA((2 * pieces * devices,))
    given = (grads, w_gate, w_up, w_down)
    kept = [struct((devices * rows, width), bf16), struct((units, devices * rows), bf16)]
    kept += [struct((devices * rows, units), bf16)] * 2
    kept += [struct((devices * rows, width), bf16)]
    return pl.pallas_call(
        functools.partial(feed_kernel, axis, devices, rows, pieces, docs),
        in_specs=[SCALARS, vmem] + [ANYWHERE] * 4,
        out_specs=[ANYWHERE] * 5 + [vmem],
        out_shape=kept + [struct((rows, width), f32)],
        scratch_shapes=[
            pltpu.VMEM((devices * rows, units), bf16),
            *(pltpu.VMEM(array.shape, array.dtype) for array in (*given, *kept[:4])),
            pltpu.VMEM((devices * rows, width), bf16), pltpu.VMEM(((devices + 1) * rows, width), bf16),
            moves, moves, chains, chains, pltpu.SemaphoreType.DMA((4,)), pltpu.SemaphoreType.DMA((5,)),
        ],
        compiler_params=pltpu.CompilerParams(
            collective_id=collective_id, has_side_effects=True, vmem_limit_bytes=61 * 1024 * 1024
        ),
        name="feed",
    )(meta, own, grads, w_gate, w_up, w_down)


def flip(index, mask):
    for bit in (1, 2, 4):
        if mask & bit:
            index = index + bit * (1 - 2 * ((index // bit) % 2))
    return index


def cube_barrier(axis, place):
    barrier = pltpu.get_barrier_semaphore()
    for mask in (1, 2, 4):
        pl.semaphore_signal(barrier, inc=1, device_id={axis: flip(place, mask)}, device_id_type=MESH)
    pl.semaphore_wait(barrier, 3)


class CubeGather:
    FIRST = ((0, 0, 2), (0, 1, 4), (0, 1, 2), (0, 0, 4), (0, 0, 1), (0, 1, 1))
    SECOND = ((2, 0, 4), (4, 1, 2), (2, 0, 1), (4, 1, 1))
    THIRD = ((2, 1, 1), (4, 0, 1))
    FOURTH = ((6, 0, 1), (6, 1, 1))

    def __init__(self, axis, own_ref, all_ref, own_sem, send_sem, recv_sem, stride=None, lead=0, enter=True):
        self.axis, self.own_ref, self.all_ref = axis, own_ref, all_ref
        self.stride, self.lead, self.enter = stride or own_ref.shape[0], lead, enter
        self.own_sem, self.send_sem, self.recv_sem = own_sem, send_sem, recv_sem
        self.place = lax.axis_index(axis)
        self.rows = own_ref.shape[0]
        self.piece = self.rows // 2

    def part(self, mask, half):
        start = flip(self.place, mask) * self.stride + self.lead + half * self.piece
        return self.all_ref.at[pl.ds(pl.multiple_of(start, LEAD), self.piece), :]

    def copy(self, mask, half, toward):
        source = self.part(mask, half) if mask else self.own_ref.at[pl.ds(half * self.piece, self.piece), :]
        return pltpu.make_async_remote_copy(
            source, self.part(mask, half),
            self.send_sem.at[toward * 2 + half, mask // 2], self.recv_sem.at[(mask ^ toward) * 2 + half],
            device_id={self.axis: flip(self.place, toward)}, device_id_type=MESH,
        )

    def wait(self, mask, half):
        pltpu.make_async_remote_copy(
            self.part(mask, half), self.part(mask, half), self.send_sem.at[0, 0], self.recv_sem.at[mask * 2 + half],
            device_id={self.axis: flip(self.place, 1)}, device_id_type=MESH,
        ).wait_recv()

    def own(self):
        start = pl.multiple_of(self.place * self.rows, self.rows)
        return pltpu.make_async_copy(self.own_ref, self.all_ref.at[pl.ds(start, self.rows), :], self.own_sem)

    def first(self):
        if self.own_sem is not None:
            if self.enter:
                cube_barrier(self.axis, self.place)
            self.own().start()
        for move in self.FIRST:
            self.copy(*move).start()

    def second(self):
        self.wait(2, 0)
        self.copy(*self.SECOND[0]).start()
        self.wait(4, 1)
        for move in self.SECOND[1:]:
            self.copy(*move).start()

    def third(self):
        for move in self.THIRD:
            self.wait(*move[:2])
            self.copy(*move).start()

    def fourth(self):
        for move in self.FOURTH:
            self.wait(*move[:2])
            self.copy(*move).start()

    def last(self):
        if self.own_sem is not None:
            for mask in (1, 3, 5, 7):
                for half in range(2):
                    self.wait(mask, half)
            self.own().wait()
        for move in self.FIRST + self.SECOND + self.THIRD + self.FOURTH:
            self.copy(*move).wait_send()


CUBE_SEMAPHORES = [pltpu.SemaphoreType.DMA, pltpu.SemaphoreType.DMA((10, 4)), pltpu.SemaphoreType.DMA((16,))]


def feed_grads_kernel(
    blocks_ref, grads_ref, hidden_ref, grad_gate_ref, grad_up_ref, down_ref, gate_ref, up_ref,
):
    gate_ref[...] = dot_tn(blocks_ref[...], grad_gate_ref[...]).astype(bf16)
    up_ref[...] = dot_tn(blocks_ref[...], grad_up_ref[...]).astype(bf16)
    down_ref[...] = dot(hidden_ref[...], grads_ref[...]).astype(bf16)


def feed_grads(own, blocks, grads, hidden, grad_gate, grad_up, axis):
    rows, width = blocks.shape
    units = hidden.shape[0]
    tall = pl.BlockSpec((rows, BLOCK), lambda step: (0, step))
    down = pl.BlockSpec((units, BLOCK), lambda step: (0, step))
    flat = pl.BlockSpec((BLOCK, units), lambda step: (step, 0))
    fixed = held((rows, units))
    results = pl.pallas_call(
        feed_grads_kernel,
        grid=(width // BLOCK,),
        in_specs=[tall, tall, held(hidden.shape), fixed, fixed],
        out_specs=[down, flat, flat],
        out_shape=[
            struct((units, width), bf16), struct((width, units), bf16), struct((width, units), bf16),
        ],
        compiler_params=params(),
        name="feed_grads",
    )(blocks, grads, hidden, grad_gate, grad_up)
    return (*results, lax.all_gather(own, axis, axis=0, tiled=True))


def feed_core_kernel(
    sizes, chunks, axis, tiles,
    meta, total_in, hidden_in, low_ref, next_gain_ref, blocks_ref, grads_ref, hidden_ref, feed_gate_ref, feed_up_ref,
    w_output_ref, core_ref, gate_ref, gain_ref, qkv_ref, scal_ref, w_in_ref, drop_ref,
    down_out, gate_out, up_out, all_ref, *refs,
):
    outs, (grad_in_ref, gain_sum_ref, rows_ref, copy_sem, send_sem, recv_sem, *later) = refs[:6], refs[6:]
    step = pl.program_id(0)
    rows = total_in.shape[0]
    own = pl.ds(pl.multiple_of(lax.axis_index(axis) * rows, rows), rows)
    gather = CubeGather(axis, rows_ref.at[own, :], rows_ref, None, send_sem, recv_sem)

    @pl.when(step == 0)
    def _():
        grad_norm, gain_sum = rms_back(hidden_in[...], next_gain_ref[...], total_in[...])
        first = meta[0] + lax.axis_index(axis) * rows
        valid = valid_of(meta, sizes[3], first + lax.broadcasted_iota(jnp.int32, (rows, 1), 0))
        grad_in = valid * low_ref[...].astype(f32) + grad_norm
        grad_in_ref[...] = grad_in
        gain_sum_ref[0:1, :] = gain_sum[None, :]
        rows_ref[own, :] = grad_in.astype(bf16)
        cube_barrier(axis, gather.place)
        gather.first()

    @pl.when(step == tiles - 1)
    def _():
        gather.second()
        gather.third()

    @pl.when(step == tiles + 3)
    def _():
        gather.fourth()

    for mask in (1, 3, 5, 7):
        @pl.when(step == (1 if mask == 1 else tiles + mask))
        def _():
            for half in range(2):
                gather.wait(mask, half)

    @pl.when((step >= 2) & (step < tiles + 2))
    def _():
        turned = blocks_ref[...].T
        gate_out[...] = dot(turned, feed_gate_ref[...]).astype(bf16)
        up_out[...] = dot(turned, feed_up_ref[...]).astype(bf16)
        down_out[...] = dot(hidden_ref[...], grads_ref[...]).astype(bf16)

    @pl.when((step < 2) | (step >= tiles + 2))
    def _():
        chunk = core_order(axis, step, tiles)
        core_grad_kernel(
            *sizes, chunks,
            meta, rows_ref.at[pl.ds(pl.multiple_of(chunk * BLOCK, BLOCK), BLOCK), :], w_output_ref,
            core_ref, gate_ref, gain_ref, qkv_ref, scal_ref, w_in_ref, drop_ref, *outs, chunk=chunk, later=later,
        )

    @pl.when(step == tiles + chunks - 1)
    def _():
        kept = pltpu.make_async_copy(rows_ref, all_ref, copy_sem)
        kept.start()
        total_ref = outs[5]
        pulls, drops, throughs = later

        def pass_on(at, carry):
            chunk = chunks - 1 - at
            for head in range(sizes[0]):
                total = total_ref[head]
                total_ref[head] = (
                    throughs[chunk, head][0:1, 0:1] * total
                    - dot_tn(drops[chunk, head], total.astype(bf16)) + pulls[chunk, head]
                )
            return carry

        lax.fori_loop(0, chunks, pass_on, 0)
        gather.last()
        kept.wait()


def core_order(axis, step, tiles):
    return cube_order(axis, jnp.where(step < 2, step, jnp.maximum(step - tiles, 1)))


class CubeScatter:
    def __init__(self, axis, total_ref, given, other, leaving, coming, waiting, send_sem, recv_sem):
        self.axis, self.total_ref = axis, total_ref
        self.given, self.other, self.leaving, self.coming, self.waiting = given, other, leaving, coming, waiting
        self.send_sem, self.recv_sem = send_sem, recv_sem
        self.place = lax.axis_index(axis)
        self.piece = total_ref.shape[0] // 2

    def slot(self, index, half):
        return pl.ds((2 * index + half) * self.piece, self.piece)

    def core_copy(self, mask, half):
        at = self.slot(mask // 2, half)
        return pltpu.make_async_remote_copy(
            self.given.at[at, :], self.other.at[at, :],
            self.send_sem.at[0, mask // 2, half], self.recv_sem.at[0, mask // 2, half],
            device_id={self.axis: flip(self.place, 1)}, device_id_type=MESH,
        )

    def landing(self, index, toward):
        return (toward // 2 - 1) * 2 + (1 if index else 0)

    def chip_copy(self, index, half, toward):
        return pltpu.make_async_remote_copy(
            self.leaving.at[self.slot(index, half), :],
            self.coming.at[self.slot(self.landing(index, toward), half), :],
            self.send_sem.at[toward // 2, index, half], self.recv_sem.at[toward // 2, 1 if index else 0, half],
            device_id={self.axis: flip(self.place, toward)}, device_id_type=MESH,
        )

    def arrived(self, index, half, toward):
        self.chip_copy(index, half, toward).wait_recv()
        return self.coming[self.slot(self.landing(index, toward), half), :].astype(f32)

    def send(self, index, half, toward, values):
        self.leaving[self.slot(index, half), :] = values.astype(bf16)
        self.chip_copy(index, half, toward).start()

    def take(self, mask, block):
        piece = self.piece
        if mask % 2:
            self.given[pl.ds(mask // 2 * 2 * piece, 2 * piece), :] = block.astype(bf16)
            for half in range(2):
                self.core_copy(mask, half).start()
            if mask == 1:
                self.send(2, 0, 4, self.waiting[0] + self.arrived(0, 0, 2))
                self.send(1, 1, 2, self.waiting[1] + self.arrived(0, 1, 4))
            return
        parts = []
        for half in range(2):
            self.core_copy(mask + 1, half).wait_recv()
            parts.append(
                block[half * piece : (half + 1) * piece, :]
                + self.other[self.slot(mask // 2, half), :].astype(f32)
            )
        if mask == 6:
            self.send(0, 0, 2, parts[0])
            self.send(0, 1, 4, parts[1])
        elif mask == 4:
            self.send(2, 1, 4, parts[1])
            self.waiting[0] = parts[0]
        elif mask == 2:
            self.send(1, 0, 2, parts[0])
            self.waiting[1] = parts[1]
        else:
            self.total_ref[0:piece, :] = parts[0]
            self.total_ref[piece:, :] = parts[1]

    def finish(self):
        piece = self.piece
        self.total_ref[0:piece, :] += self.arrived(1, 0, 2)
        self.total_ref[piece:, :] += self.arrived(2, 1, 4)
        self.total_ref[0:piece, :] += self.arrived(2, 0, 4)
        self.total_ref[piece:, :] += self.arrived(1, 1, 2)
        for mask in (7, 5, 3, 1):
            for half in range(2):
                self.core_copy(mask, half).wait_send()
        for index, half, toward in ((0, 0, 2), (0, 1, 4), (1, 0, 2), (2, 1, 4), (1, 1, 2), (2, 0, 4)):
            self.chip_copy(index, half, toward).wait_send()


def scatter_block(step, scatter, block):
    @pl.when(step == 0)
    def _():
        cube_barrier("head", scatter.place)

    for mask in range(8):
        @pl.when(step == 7 - mask)
        def _():
            scatter.take(mask, block)

    @pl.when(step == 7)
    def _():
        scatter.finish()


def cube_scatter_scratch(rows, width):
    return [
        pltpu.VMEM((4 * rows, width), bf16), pltpu.VMEM((4 * rows, width), bf16),
        pltpu.VMEM((3 * rows, width), bf16), pltpu.VMEM((4 * rows, width), bf16),
        pltpu.VMEM((2, rows // 2, width), f32),
        pltpu.SemaphoreType.DMA((3, 4, 2)), pltpu.SemaphoreType.DMA((3, 4, 2)),
    ]


def params(collective_id=None):
    return pltpu.CompilerParams(
        dimension_semantics=("arbitrary",),
        vmem_limit_bytes=VMEM_LIMIT,
        collective_id=collective_id,
        has_side_effects=collective_id is not None,
    )


def finish_kernel(
    cuts, total, grad_ref, inputs_ref, gain_ref, grad_hidden_ref, hidden_ref, mlp_ref, taps_ref, all_in, *refs,
):
    given, refs = refs[:total], refs[total:]
    output_ref, grad_inputs_ref, taps_q, taps_k, taps_v, *refs = refs
    output_ref[...] = (hidden_ref[...] + mlp_ref[...].astype(f32)).astype(bf16)
    values = inputs_ref[...].astype(f32)
    scale = lax.rsqrt(jnp.mean(values * values, axis=-1, keepdims=True) + epsilon)
    weighted = grad_ref[...] * gain_ref[...]
    grad_inputs_ref[...] = grad_hidden_ref[...] + (
        scale * weighted - values * scale**3 * jnp.mean(weighted * values, axis=-1, keepdims=True)
    )
    begin = 0
    for result in (taps_q, taps_k, taps_v):
        count, width = result.shape
        result[...] = taps_ref[:, begin : begin + width].astype(f32)[:count, :]
        begin += width
    begin = 0
    for cut, result in zip(cuts, refs):
        result[...] = all_in[:, begin : begin + cut].astype(f32)
        begin += cut
    for source, result in zip(given, refs[len(cuts) :]):
        result[...] = source[...].astype(f32)


def finish(rows, gain, small, taps, columns, cuts, given):
    steps = 8 if given[0].shape[0] % 128 == 0 else 4

    def part(shape):
        return pl.BlockSpec((shape[0] // steps, shape[1]), lambda step: (step, 0))

    grad, inputs, grad_hidden, hidden, mlp = rows
    taps_shapes = [(taps, cut) for cut in cuts[:3]]
    shapes = [(columns.shape[0], cut) for cut in cuts] + [array.shape for array in given]
    return pl.pallas_call(
        functools.partial(finish_kernel, cuts, len(given)),
        grid=(steps,),
        in_specs=[
            part(grad.shape), part(inputs.shape), whole(gain.shape), part(grad_hidden.shape), part(hidden.shape),
            part(mlp.shape), whole(small.shape), part(columns.shape), *(part(array.shape) for array in given),
        ],
        out_specs=[
            part(inputs.shape), part(inputs.shape), *(whole(shape) for shape in taps_shapes),
            *(part(shape) for shape in shapes),
        ],
        out_shape=[
            struct(inputs.shape, bf16), struct(inputs.shape, f32), *(struct(shape, f32) for shape in taps_shapes),
            *(struct(shape, f32) for shape in shapes),
        ],
        compiler_params=params(),
        name="finish",
    )(grad, inputs, gain, grad_hidden, hidden, mlp, small, columns, *given)


def struct(shape, dtype):
    return jax.ShapeDtypeStruct(tuple(shape), dtype)


def from_earlier(array, axis):
    devices = lax.axis_size(axis)
    parts = [
        lax.ppermute(array, axis, [(i, i + by) for i in range(devices - by)])
        for by in range(devices - 1, 0, -1)
    ]
    return jnp.stack(parts) if parts else jnp.zeros((1,) + array.shape, array.dtype)


def from_later(array, axis):
    devices = lax.axis_size(axis)
    parts = [
        lax.ppermute(array, axis, [(i + by, i) for i in range(devices - by)])
        for by in range(devices - 1, 0, -1)
    ]
    return jnp.stack(parts) if parts else jnp.zeros((1,) + array.shape, array.dtype)


def shards(
    inputs,
    doc_lengths,
    first_gain,
    w_query,
    w_key,
    w_value,
    w_outgate,
    w_decay,
    w_beta,
    conv_query,
    conv_key,
    conv_value,
    decay_log,
    decay_bias,
    head_gain,
    w_output,
    second_gain,
    w_gate,
    w_up,
    w_down,
    cotangent,
):
    row_count, model_width = inputs.shape
    heads = decay_log.shape[0]
    qw, vw = w_query.shape[1], w_value.shape[1]
    key_width, value_width = qw // heads, vw // heads
    mixed_width = 2 * qw + vw
    taps = conv_query.shape[0]
    docs = doc_lengths.shape[0]
    seq_index = lax.axis_index("seq")
    head_index = lax.axis_index("head")
    head_total = lax.axis_size("head")
    seq_rows = row_count * head_total
    chunks = seq_rows // BLOCK
    others = max(lax.axis_size("seq") - 1, 1)
    sizes = (heads, key_width, value_width, docs)

    inputs_f = inputs.astype(f32)
    normed = rms_scale(inputs_f, first_gain).astype(bf16)
    meta = jnp.concatenate(
        [(seq_index * seq_rows).astype(jnp.int32)[None], slot_starts(doc_lengths), doc_lengths]
    )

    w_small = jnp.concatenate([w_decay, w_beta, jnp.zeros((model_width, LANES - 2 * heads), bf16)], axis=1)
    weights = (w_query, w_key, w_value, w_outgate, w_small)
    all_width = mixed_width + vw + LANES
    conv_all = jnp.concatenate([conv_query, conv_key, conv_value], axis=1)
    dvec = jnp.zeros((8, LANES), f32)
    dvec = dvec.at[0, :heads].set(decay_bias).at[1, :heads].set(-jnp.exp(decay_log))
    map_shape = (heads, key_width, key_width + value_width)
    passing_shape = (others, heads, key_width, key_width)

    cube = head_total == 8 and chunks == 8 and row_count == BLOCK
    if cube:
        rows_given, rows_spec = normed, held(normed.shape)

        def at_step(step):
            return cube_order("head", step)
    else:
        block_rows = lax.all_gather(normed, "head", axis=0, tiled=True)
        tail = from_previous(block_rows[seq_rows - LEAD :])
        blocks = block_rows.reshape(chunks, BLOCK, model_width)
        leads = jnp.concatenate([tail[None], blocks[:-1, BLOCK - LEAD :]], axis=0)
        rows_given = jnp.concatenate([leads, blocks], axis=1).reshape(chunks * STRIDE, model_width)
        rows_spec = pl.BlockSpec((STRIDE, model_width), lambda step: (step, 0))

        def at_step(step):
            return step

    def rows_out(width):
        return pl.BlockSpec((BLOCK, width), lambda step: (at_step(step), 0))

    def chunk_out(shape):
        return pl.BlockSpec((1,) + tuple(shape), lambda step: (at_step(step),) + (0,) * len(shape))

    results = pl.pallas_call(
        functools.partial(forward_kernel, *sizes, taps, chunks, cube),
        grid=(chunks,),
        in_specs=[
            SCALARS, rows_spec, *(held(weight.shape) for weight in weights), whole(conv_all.shape),
            whole(dvec.shape),
        ],
        out_specs=[
            rows_out(mixed_width), rows_out(mixed_width), rows_out(vw), rows_out(LANES), rows_out(LANES),
            rows_out(mixed_width),
            chunk_out((heads, BLOCK, BLOCK)), chunk_out((heads, BLOCK, key_width)),
            chunk_out((heads, BLOCK, value_width)), chunk_out((heads, key_width, key_width)),
            whole((chunks,) + map_shape), whole(map_shape),
        ] + [ANYWHERE, whole((others,) + map_shape), whole(passing_shape)] * cube,
        out_shape=[
            struct((seq_rows, mixed_width), f32), struct((seq_rows, mixed_width), f32),
            struct((seq_rows, vw), f32), struct((seq_rows, LANES), f32), struct((seq_rows, LANES), f32),
            struct((seq_rows, mixed_width), bf16),
            struct((chunks, heads, BLOCK, BLOCK), bf16), struct((chunks, heads, BLOCK, key_width), bf16),
            struct((chunks, heads, BLOCK, value_width), f32),
            struct((chunks, heads, key_width, key_width), f32),
            struct((chunks,) + map_shape, f32), struct(map_shape, f32),
        ] + [
            struct((seq_rows, model_width), bf16), struct((others,) + map_shape, bf16), struct(passing_shape, bf16),
        ] * cube,
        scratch_shapes=[
            pltpu.VMEM((STRIDE, mixed_width), f32), pltpu.VMEM(map_shape, f32),
            pltpu.VMEM((chunks, heads, key_width, key_width), bf16),
            pltpu.VMEM((chunks, heads, key_width, value_width), f32),
            pltpu.VMEM((chunks, heads, 8, LANES), f32),
        ] + [
            pltpu.VMEM((chunks * STRIDE, model_width), bf16), pltpu.SemaphoreType.DMA((chunks,)),
            pltpu.VMEM((LEAD, model_width), bf16), pltpu.SemaphoreType.DMA((2,)),
            pltpu.SemaphoreType.DMA((8,)), pltpu.SemaphoreType.DMA((8,)), *CUBE_SEMAPHORES[1:],
            pltpu.VMEM(map_shape, bf16), pltpu.VMEM((others,) + map_shape, bf16), pltpu.VMEM(passing_shape, bf16),
            pltpu.SemaphoreType.DMA((6, others)),
        ] * cube,
        compiler_params=params(2 if cube else None),
        name="mixer_forward",
    )(meta, rows_given, *weights, conv_all, dvec)
    (pre, conv, gate, small, scal, qkv, inverse, w_part, u_part, drop, starts, block_map) = results[:12]
    if cube:
        block_rows, earlier, passing = results[12:]
    else:
        earlier = from_earlier(block_map.astype(bf16), "seq")
        passing = from_later(block_map[:, :, :key_width].astype(bf16), "seq")

    grad_block_two = lax.all_gather(cotangent, "seq", axis=0, tiled=True)
    gain_row = head_gain[None, :]
    def last_first(step):
        return cube_order("head", 7 - step) if cube else step

    def rows_back(width):
        return pl.BlockSpec((BLOCK, width), lambda step: (last_first(step), 0))

    def chunk_back(shape):
        return pl.BlockSpec((1,) + tuple(shape), lambda step: (last_first(step),) + (0,) * len(shape))

    second_row = second_gain[None, :]
    own_rows = (inputs, second_row) if cube else ()
    core, gated, fresh, states, *mixed_parts = pl.pallas_call(
        functools.partial(output_kernel, *sizes, others, cube),
        grid=(chunks,),
        in_specs=[
            SCALARS, whole(earlier.shape), chunk_back(map_shape), chunk_back((heads, BLOCK, key_width)),
            chunk_back((heads, BLOCK, value_width)), rows_back(mixed_width), rows_back(LANES), rows_back(vw),
            whole(gain_row.shape), held(w_output.shape), *(held(array.shape) for array in own_rows),
        ],
        out_specs=[
            rows_back(vw), rows_back(vw), chunk_back((heads, BLOCK, value_width)),
            chunk_back((heads, key_width, value_width)),
            *([whole((row_count, model_width))] * 2 if cube else [rows_back(model_width)]),
        ],
        out_shape=[
            struct((seq_rows, vw), f32), struct((seq_rows, vw), bf16),
            struct((chunks, heads, BLOCK, value_width), bf16),
            struct((chunks, heads, key_width, value_width), f32),
            *(
                [struct((row_count, model_width), f32), struct((row_count, model_width), bf16)]
                if cube else [struct((seq_rows, model_width), bf16)]
            ),
        ],
        scratch_shapes=[pltpu.VMEM((heads, key_width, value_width), f32)]
        + (
            [pltpu.VMEM((row_count, model_width), f32), *cube_scatter_scratch(row_count, model_width)]
            if cube else []
        ),
        compiler_params=params(5 if cube else None),
        name="mixer_output",
    )(meta, earlier, starts, w_part, u_part, qkv, scal, gate, gain_row, w_output, *own_rows)
    if cube:
        hidden_in, normed_two = mixed_parts
    else:
        mixer_out = lax.psum_scatter(mixed_parts[0], "head", scatter_dimension=0, tiled=True).astype(f32)
        hidden_in = inputs_f + mixer_out
        normed_two = rms_scale(hidden_in, second_gain).astype(bf16)

    mlp_block, hidden, grad_gate, grad_up, mlp_part, grad_normed_two = feed(
        meta, docs, normed_two, grad_block_two, w_gate, w_up, w_down, "seq", 3
    )
    mlp_out = lax.psum_scatter(mlp_part, "seq", scatter_dimension=0, tiled=True)
    core_shapes = [
        struct((chunks, heads, BLOCK, value_width), bf16), struct((chunks, heads, BLOCK, value_width), f32),
        struct((chunks, heads, key_width, value_width), f32), struct((seq_rows, vw), bf16),
        struct((8, value_width), f32), struct((heads, key_width, value_width), f32),
    ]
    if cube:
        tiles = model_width // BLOCK
        owned = (grad_normed_two, hidden_in, cotangent, second_row)
        units, mlp_rows = hidden.shape

        def tile(step):
            return jnp.clip(step - 2, 0, tiles - 1)

        def core_chunk(step):
            return core_order("head", step, tiles)

        def core_rows(width):
            return pl.BlockSpec((BLOCK, width), lambda step: (core_chunk(step), 0))

        def core_blocks(shape):
            return pl.BlockSpec((1,) + tuple(shape), lambda step: (core_chunk(step),) + (0,) * len(shape))

        tall = pl.BlockSpec((mlp_rows, BLOCK), lambda step: (0, tile(step)))
        down = pl.BlockSpec((units, BLOCK), lambda step: (0, tile(step)))
        flat = pl.BlockSpec((BLOCK, units), lambda step: (tile(step), 0))
        results = pl.pallas_call(
            functools.partial(feed_core_kernel, sizes, chunks, "head", tiles),
            grid=(tiles + chunks,),
            in_specs=[
                SCALARS, *(held(array.shape) for array in owned), tall, tall, *(held(array.shape) for array in (hidden, grad_gate, grad_up)),
                held(w_output.shape), core_rows(vw), core_rows(vw), whole(gain_row.shape), core_rows(mixed_width),
                core_rows(LANES), core_blocks((heads, BLOCK, key_width)), core_blocks((heads, key_width, key_width)),
            ],
            out_specs=[
                down, flat, flat, ANYWHERE,
                core_blocks((heads, BLOCK, value_width)), core_blocks((heads, BLOCK, value_width)),
                core_blocks((heads, key_width, value_width)), core_rows(vw),
                whole((8, value_width)), whole((heads, key_width, value_width)),
                whole((row_count, model_width)), whole((8, model_width)),
            ],
            out_shape=[
                struct((units, model_width), bf16), struct((model_width, units), bf16),
                struct((model_width, units), bf16), struct((seq_rows, model_width), bf16), *core_shapes,
                struct((row_count, model_width), f32), struct((8, model_width), f32),
            ],
            scratch_shapes=[
                pltpu.VMEM((seq_rows, model_width), bf16), pltpu.SemaphoreType.DMA, *CUBE_SEMAPHORES[1:],
                pltpu.VMEM((chunks, heads, key_width, value_width), f32),
                pltpu.VMEM((chunks, heads, key_width, key_width), bf16),
                pltpu.VMEM((chunks, heads, 8, LANES), f32),
            ],
            compiler_params=params(6),
            name="feed_core",
        )(
            meta, *owned, mlp_block, grad_block_two, hidden, grad_gate, grad_up,
            w_output, core, gate, gain_row, qkv, scal, w_part, drop,
        )
        ff_grads, grad_block = results[:3], results[3]
        grad_core, inner, pull, grad_gate_pre, grad_head, pulled, grad_hidden_in, grad_second = results[4:]
        grad_second = grad_second[0]
    else:
        grad_hidden_norm, grad_second = rms_back(hidden_in, second_gain, grad_normed_two)
        _, own_valid = layout(doc_lengths, (seq_index * head_total + head_index) * row_count, row_count)
        grad_hidden_in = cotangent.astype(f32) * own_valid.astype(f32)[:, None] + grad_hidden_norm
        grad_mix = grad_hidden_in.astype(bf16)
        *ff_grads, grad_block = feed_grads(
            grad_mix, mlp_block, grad_block_two, hidden, grad_gate, grad_up, "head"
        )
        grad_core, inner, pull, grad_gate_pre, grad_head, pulled = pl.pallas_call(
            functools.partial(core_grad_kernel, *sizes, chunks),
            grid=(chunks,),
            in_specs=[
                SCALARS, by_rows(model_width, chunks), whole(w_output.shape), by_rows(vw, chunks), by_rows(vw, chunks),
                whole(gain_row.shape), by_rows(mixed_width, chunks), by_rows(LANES, chunks),
                by_chunk((heads, BLOCK, key_width), chunks), by_chunk((heads, key_width, key_width), chunks),
            ],
            out_specs=[
                by_chunk((heads, BLOCK, value_width), chunks), by_chunk((heads, BLOCK, value_width), chunks),
                by_chunk((heads, key_width, value_width), chunks), by_rows(vw, chunks),
                whole((8, value_width)), whole((heads, key_width, value_width)),
            ],
            out_shape=core_shapes,
            compiler_params=params(),
            name="mixer_core_grad",
        )(meta, grad_block, w_output, core, gate, gain_row, qkv, scal, w_part, drop)
    grad_w_output = dot_tn(gated, grad_block).astype(bf16)
    later = from_later(pulled.astype(bf16), "seq")
    later, _ = lax.optimization_barrier((later, grad_w_output))
    mlp_out, grad_w_output = lax.optimization_barrier((mlp_out, grad_w_output))
    grad_w_output = lax.psum(grad_w_output, "seq")
    feed_part = (ff_grads[1],) if cube else ()
    grad_conv, grad_small, sums, edge, *feed_sum = pl.pallas_call(
        functools.partial(backward_kernel, *sizes, chunks, others, cube),
        grid=(chunks,),
        in_specs=[
            SCALARS, whole(passing.shape), whole(later.shape), by_rows(mixed_width, chunks),
            by_rows(mixed_width, chunks),
            by_rows(LANES, chunks), by_rows(LANES, chunks), by_chunk((heads, BLOCK, BLOCK), chunks),
            by_chunk((heads, BLOCK, value_width), chunks), by_chunk((heads, key_width, value_width), chunks),
            by_chunk((heads, BLOCK, value_width), chunks), by_chunk((heads, BLOCK, value_width), chunks),
            by_chunk((heads, key_width, value_width), chunks), by_chunk((heads, key_width, key_width), chunks),
            whole(dvec.shape), *(held(array.shape) for array in feed_part),
        ],
        out_specs=[
            by_rows(mixed_width, chunks), by_rows(LANES, chunks), whole((8, LANES)), whole((HALO, mixed_width)),
            *(whole((array.shape[0] // 8, array.shape[1])) for array in feed_part),
        ],
        out_shape=[
            struct((seq_rows, mixed_width), f32), struct((seq_rows, LANES), bf16), struct((8, LANES), f32),
            struct((HALO, mixed_width), f32),
            *(struct((array.shape[0] // 8, array.shape[1]), bf16) for array in feed_part),
        ],
        scratch_shapes=[
            pltpu.VMEM((heads, key_width, value_width), f32), pltpu.VMEM((HALO, mixed_width), f32),
            pltpu.VMEM((HALO, mixed_width), f32), pltpu.SemaphoreType.DMA((2,)),
            *(
                scratch for array in feed_part for scratch in (
                    pltpu.VMEM((array.shape[0] // 8, array.shape[1]), f32),
                    *cube_scatter_scratch(array.shape[0] // 8, array.shape[1]),
                )
            ),
        ],
        compiler_params=params(9),
        name="mixer_backward",
    )(
        meta, passing, later, qkv, conv, scal, small, inverse, fresh, states, grad_core, inner, pull, drop, dvec, *feed_part
    )

    if cube:
        ff_grads = [ff_grads[0], ff_grads[2]]
    grad_small, *ff_grads = lax.optimization_barrier((grad_small, *ff_grads))
    ff_grads = [lax.psum(part, "head") for part in ff_grads]
    step_rows = BLOCK // HALO
    last_halo = seq_rows // HALO - 1
    later_rows = pl.BlockSpec(
        (HALO, mixed_width), lambda step: (jnp.minimum((last_first(step) + 1) * step_rows, last_halo), 0)
    )
    grad_pre, grad_taps, grad_rows, gain_sum = pl.pallas_call(
        functools.partial(projection_grad_kernel, mixed_width, docs, chunks, taps, cube),
        grid=(chunks,),
        in_specs=[
            SCALARS, rows_back(mixed_width), later_rows, whole(edge.shape), rows_back(mixed_width), rows_back(vw),
            rows_back(LANES), whole(conv_all.shape), rows_back(model_width),
            *(held(weight.shape) for weight in weights),
        ],
        out_specs=[
            rows_back(all_width), whole((8, mixed_width)),
            whole((row_count, model_width)) if cube else rows_back(model_width), whole((8, model_width)),
        ],
        out_shape=[
            struct((seq_rows, all_width), bf16), struct((8, mixed_width), f32),
            struct((row_count, model_width), f32) if cube else struct((seq_rows, model_width), bf16),
            struct((8, model_width), f32),
        ],
        scratch_shapes=[pltpu.VMEM((BLOCK + HALO, mixed_width), f32)]
        + (cube_scatter_scratch(row_count, model_width) if cube else []),
        compiler_params=params(8 if cube else None),
        name="projection_grad",
    )(meta, grad_conv, grad_conv, edge, pre, grad_gate_pre, grad_small, conv_all, block_rows, *weights)

    if cube:
        grad_normed = grad_rows
    else:
        grad_normed = lax.psum_scatter(grad_rows, "head", scatter_dimension=0, tiled=True).astype(f32)
    gains = jnp.concatenate([gain_sum[0] / first_gain, grad_second, grad_head[0]]).reshape(2, -1)
    grad_w_all, grad_w_small, small_sums, _, gains, *gathered = line_sum(
        block_rows,
        grad_pre,
        feed_sum,
        (
            jnp.pad(
                jnp.concatenate([grad_taps, sums], axis=1), ((0, 8), (0, 0))
            ).astype(bf16),
            jnp.pad(gains, ((0, 14), (0, 0))).astype(bf16),
        ),
        (32, 16, 16, 16),
        "seq",
        1,
    )
    gains = gains[:2].reshape(-1)
    first_part, second_part = gains[:model_width], gains[model_width : 2 * model_width]
    head_part = gains[2 * model_width :]
    if cube:
        ff_grads = [ff_grads[0], *gathered, ff_grads[1]]
    grad_w_all, grad_w_output = lax.optimization_barrier((grad_w_all, grad_w_output))
    grad_w_all, mlp_out, *ff_grads = lax.optimization_barrier((grad_w_all, mlp_out, *ff_grads))
    (
        output, grad_inputs, grad_conv_query, grad_conv_key, grad_conv_value,
        grad_w_query, grad_w_key, grad_w_value, grad_w_outgate, grad_w_down, grad_w_gate, grad_w_up, grad_w_output,
    ) = finish(
        (grad_normed, inputs, grad_hidden_in, hidden_in, mlp_out), first_gain[None, :], small_sums, taps,
        grad_w_all, (qw, qw, vw, vw), (*ff_grads, grad_w_output),
    )
    sums = small_sums[:2, mixed_width : mixed_width + heads].astype(f32)
    return (
        output,
        grad_inputs,
        first_part,
        grad_w_query,
        grad_w_key,
        grad_w_value,
        grad_w_outgate,
        grad_w_small[:heads].astype(f32).T,
        grad_w_small[heads : 2 * heads].astype(f32).T,
        grad_conv_query,
        grad_conv_key,
        grad_conv_value,
        sums[1],
        sums[0],
        head_part,
        grad_w_output,
        second_part,
        grad_w_gate,
        grad_w_up,
        grad_w_down,
    )


def from_previous(array):
    devices = lax.axis_size("seq")
    return lax.ppermute(array, "seq", [(i, i + 1) for i in range(devices - 1)])


def solution(mesh):
    in_specs = (
        P(("seq", "head"), None),
        P(),
        P(),
        P(None, "head"),
        P(None, "head"),
        P(None, "head"),
        P(None, "head"),
        P(None, "head"),
        P(None, "head"),
        P(None, "head"),
        P(None, "head"),
        P(None, "head"),
        P("head"),
        P("head"),
        P(),
        P("head", None),
        P(),
        P(None, "seq"),
        P(None, "seq"),
        P("seq", None),
        P(("seq", "head"), None),
    )
    out_specs = (
        P(("seq", "head"), None),
        P(("seq", "head"), None),
        P(),
        P(None, "head"),
        P(None, "head"),
        P(None, "head"),
        P(None, "head"),
        P(None, "head"),
        P(None, "head"),
        P(None, "head"),
        P(None, "head"),
        P(None, "head"),
        P("head"),
        P("head"),
        P(),
        P("head", None),
        P(),
        P(None, "seq"),
        P(None, "seq"),
        P("seq", None),
    )
    return jax.shard_map(shards, mesh=mesh, in_specs=in_specs, out_specs=out_specs, check_vma=False)
```
